32 devices in a mesh: groups: 2 (over y), seq: 4 (over z), heads: 2 (over x), sub: 2 (over core).
Axes of the slice: x: 2, y: 2, z: 4, core: 2. Of those that a mesh axis runs over, the one named last changes fastest.
Arguments:
- queries: bfloat16 [4096, 2048], P(('groups', 'seq', 'heads', 'sub')), parts along dimension 0, may hold values from -12.5 to 12.5
- new_keys: bfloat16 [4096, 2048], P(('groups', 'seq', 'heads', 'sub')), parts along dimension 0, may hold values from -5 to 5
- new_values: bfloat16 [4096, 2048], P(('groups', 'seq', 'heads', 'sub')), parts along dimension 0, may hold values from -5 to 5
- cache_keys: bfloat16 [8192, 2048], P(('groups', 'seq'), ('heads', 'sub')), parts along dimension 0, may hold values from -5 to 5
- cache_values: bfloat16 [8192, 2048], P(('groups', 'seq'), ('heads', 'sub')), parts along dimension 0, may hold values from -5 to 5
- selection: int32 [8, 16, 8], P(('groups', 'seq'), ('heads', 'sub')), parts along dimension 0, may hold values from 0 to 7, as said below
Outputs:
- attended: bfloat16 [4096, 2048], P(('groups', 'seq', 'heads', 'sub')), parts along dimension 0
The draws below stay inside these ranges and needn't reach their ends.
There are 2 independent parts, one for each index of `groups`. The reference program is written for one: setup_inputs(seed, part) draws one part's arguments, and reference() takes and returns one part's arrays. A program takes and returns all parts, laid end to end along the dimension named above; each array names one. Nothing has to cross between parts.
Inputs may be any that keep to these rules, and one draw needn't show every extreme that they name: `selection`: every selected block precedes the span; the 8 blocks of one query block and head are different. For one index of seq and one index of heads+sub, of the 32 selections of that device's query blocks and heads (heads taken in order from index times 4), exactly 8 names a block held by each index of seq (blocks index * 2 to index * 2 + 1).
All inputs are finite; a program needn't handle non-finite values.
Results may differ from the reference program's by a relative error of at most 0.0023.
Values may be sent and summed in bfloat16 or wider, within the bound.
No kernel may reach another device: no remote copies, remote signals or barrier semaphores. Data moves between devices by JAX's collectives and lax.ppermute only.
A program may use at most 128 MiB of HBM per device.

```python
import jax
import jax.numpy as jnp
from jax import lax

HD = 128
HEAD_DEV = 4
BLOCK = 512
TOPK = 8
QB_DEV = 1
CB_DEV = 2
HEADS = 16
WIDTH = 2048
QBLK = 4
QTOK = 2048
NCB = 8
CTX = 4096
N_SEQ = 4


def draw_queries(key, part):
    noise_key = jax.random.fold_in(key, 1)
    values = jnp.clip(2.5 * jax.random.normal(noise_key, (QTOK, HEADS * HD), jnp.float32), -12.5, 12.5)
    return values.astype(jnp.bfloat16)


def draw_new_keys(key, part):
    noise_key = jax.random.fold_in(key, 2)
    values = jnp.clip(jax.random.normal(noise_key, (QTOK, HEADS * HD), jnp.float32), -5.0, 5.0)
    return values.astype(jnp.bfloat16)


def draw_selection(key, part):
    group_count = HEADS // HEAD_DEV
    request_count = QB_DEV * HEAD_DEV * TOPK
    keys = jax.random.split(jax.random.fold_in(key, 3), N_SEQ * group_count)

    def one_group(group_key):
        first_key, second_key = jax.random.split(group_key)
        shuffled = jax.random.permutation(first_key, N_SEQ)
        offsets = jax.random.randint(second_key, (N_SEQ,), 0, CB_DEV)
        counter = jnp.arange(request_count)
        source = shuffled[counter % N_SEQ]
        inner = (counter // N_SEQ + offsets[source]) % CB_DEV
        return (source * CB_DEV + inner).astype(jnp.int32)
    flat = jax.vmap(one_group)(keys)
    shaped = flat.reshape(N_SEQ, group_count, QB_DEV, HEAD_DEV, TOPK)
    return shaped.transpose(0, 2, 1, 3, 4).reshape(N_SEQ * QB_DEV, HEADS, TOPK)


def shard_levels(rng, dims, cuts, least, high):
    factor_of = 1.0
    for axis_at, blocks in cuts:
        draws = jax.random.uniform(jax.random.fold_in(jax.random.fold_in(rng, 6), axis_at), (blocks,), jnp.float32, least / len(cuts), high / len(cuts))
        factor_of = factor_of * jnp.repeat(jnp.exp(draws), dims[axis_at] // blocks).reshape((-1,) + (1,) * (len(dims) - 1 - axis_at))
    return factor_of


def scatter_about(own_key, shape, scale, most, shards=(), held_as=jnp.bfloat16):
    drawn = jax.random.normal(own_key, shape, jnp.float32) * scale
    if len(shards) > 0:
        drawn = shard_levels(own_key, shape, shards, -0.22, 0.18) * drawn
    return jnp.clip(drawn, min=-most, max=most).astype(held_as)


def setup_inputs(seed: int = 0, part: int = 0) -> dict:
    key_of = jax.random.split(jax.random.key(seed), 7)
    part_keys = jax.random.split(jax.random.fold_in(key_of[6], part), 7)
    queries = draw_queries(jax.random.fold_in(jax.random.fold_in(key_of[6], part), 71), part)
    new_keys = draw_new_keys(jax.random.fold_in(jax.random.fold_in(key_of[6], part), 71), part)
    new_values = scatter_about(part_keys[2], (QTOK, WIDTH), 1.0, 5.0, ((0, 16),))
    cache_keys = scatter_about(part_keys[3], (CTX, WIDTH), 1.0, 5.0, ((0, 4), (1, 4)))
    cache_values = scatter_about(part_keys[4], (CTX, WIDTH), 1.0, 5.0, ((0, 4), (1, 4)))
    selection = draw_selection(jax.random.fold_in(jax.random.fold_in(key_of[6], part), 71), part)
    return {"queries": queries, "new_keys": new_keys, "new_values": new_values, "cache_keys": cache_keys, "cache_values": cache_values, "selection": selection}


def attend(query_heads, key_heads, value_heads, causal, scaling):
    scores = jnp.einsum("hqd,hkd->hqk", query_heads.astype(jnp.float32), key_heads.astype(jnp.float32)) * scaling
    if causal is not None:
        scores = jnp.where(causal[None, :, :], scores, -jnp.inf)
    highest = jnp.max(scores, axis=-1)
    weights = jnp.exp(scores - highest[..., None])
    totals = jnp.sum(weights, axis=-1)
    rounded = lax.optimization_barrier(weights.astype(jnp.bfloat16)).astype(jnp.float32)
    mixed = jnp.einsum("hqk,hkd->hqd", rounded, value_heads.astype(jnp.float32))
    return mixed, highest, totals


def reference(queries, new_keys, new_values, cache_keys, cache_values, selection):
    scaling = HD ** -0.5
    cache_k = cache_keys.reshape(NCB, BLOCK, HEADS, HD)
    cache_v = cache_values.reshape(NCB, BLOCK, HEADS, HD)
    head_index = jnp.arange(HEADS).astype(jnp.int32)[:, None]
    causal = jnp.arange(BLOCK)[:, None] >= jnp.arange(BLOCK)[None, :]

    def one_block(position):
        begin = (position * BLOCK).astype(jnp.int32)

        def heads_of(array):
            rows = lax.dynamic_slice_in_dim(array, begin, BLOCK, 0)
            return rows.reshape(BLOCK, HEADS, HD).transpose(1, 0, 2)

        query_heads = heads_of(queries)
        chosen = lax.dynamic_index_in_dim(selection, position, 0, keepdims=False).astype(jnp.int32)
        chosen_k = cache_k[chosen, :, head_index, :]
        chosen_v = cache_v[chosen, :, head_index, :]
        parts = [attend(query_heads, heads_of(new_keys), heads_of(new_values), causal, scaling)]
        for turn in range(TOPK):
            parts.append(attend(query_heads, chosen_k[:, turn], chosen_v[:, turn], None, scaling))
        top = parts[0][1]
        for part in parts[1:]:
            top = jnp.maximum(top, part[1])
        numer = jnp.zeros((HEADS, BLOCK, HD), jnp.float32)
        denom = jnp.zeros((HEADS, BLOCK), jnp.float32)
        for part in parts:
            factor = jnp.exp(part[1] - top)
            numer = numer + factor[..., None] * part[0]
            denom = denom + factor * part[2]
        result = numer / denom[..., None]
        return result.transpose(1, 0, 2).reshape(BLOCK, HEADS * HD).astype(jnp.bfloat16)

    blocks_out = lax.map(one_block, jnp.arange(QBLK).astype(jnp.int32))
    return blocks_out.reshape(QTOK, HEADS * HD)
```

```python
import functools
import math

import jax
import jax.numpy as jnp
from jax import lax
from jax.experimental import pallas as pl
from jax.experimental.pallas import tpu as pltpu
from jax.sharding import PartitionSpec as P

HD = 128
BLOCK = 512


def order_ranks(owners):
    length = owners.shape[-1]
    counter = jnp.arange(length)
    earlier = counter[None, :] < counter[:, None]
    same_owner = owners[..., :, None] == owners[..., None, :]
    return jnp.sum(jnp.logical_and(same_owner, earlier), axis=-1)


def one_hot(values, length):
    return (values[..., None] == jnp.arange(length)).astype(jnp.float32)


def own_partial(query_blocks, key_blocks, value_blocks, scaling):
    scores = (
        jnp.einsum("bqhd,bkhd->bhqk", query_blocks, key_blocks, preferred_element_type=jnp.float32)
        * scaling
    )
    length = query_blocks.shape[1]
    causal = jnp.arange(length)[:, None] >= jnp.arange(length)[None, :]
    scores = jnp.where(causal, scores, -jnp.inf)
    highest = jnp.max(scores, axis=-1)
    weights = jnp.exp(scores - highest[..., None])
    totals = jnp.sum(weights, axis=-1)
    mixed = jnp.einsum(
        "bhqk,bkhd->bhqd",
        weights.astype(jnp.bfloat16),
        value_blocks,
        preferred_element_type=jnp.float32,
    )
    return (mixed, highest, totals)


def tile_partial(query_blocks, tile_pair, scaling):
    head_size = query_blocks.shape[-1]
    scores = (
        jnp.einsum(
            "bqhd,bhkd->bhqk",
            query_blocks,
            tile_pair[..., :head_size],
            preferred_element_type=jnp.float32,
        )
        * scaling
    )
    highest = jnp.max(scores, axis=-1)
    weights = jnp.exp(scores - highest[..., None])
    totals = jnp.sum(weights, axis=-1)
    mixed = jnp.einsum(
        "bhqk,bhkd->bhqd",
        weights.astype(jnp.bfloat16),
        tile_pair[..., head_size:],
        preferred_element_type=jnp.float32,
    )
    return (mixed, highest, totals)


def merge_parts(parts):
    top = parts[0][1]
    for part in parts[1:]:
        top = jnp.maximum(top, part[1])
    numer = jnp.zeros(parts[0][0].shape, jnp.float32)
    denom = jnp.zeros(parts[0][2].shape, jnp.float32)
    for part in parts:
        factor = jnp.exp(part[1] - top)
        numer = numer + factor[..., None] * part[0]
        denom = denom + factor * part[2]
    return numer / denom[..., None]


def sparse_body(queries, new_keys, new_values, cache_keys, cache_values, selection):
    heads_q, heads_k, heads_v = (
        lax.all_to_all(queries, ("heads", "sub"), split_axis=1, concat_axis=0, tiled=True),
        lax.all_to_all(new_keys, ("heads", "sub"), split_axis=1, concat_axis=0, tiled=True),
        lax.all_to_all(new_values, ("heads", "sub"), split_axis=1, concat_axis=0, tiled=True),
    )
    qblocks, head_count, top_count = selection.shape
    head_size = HD
    scaling = head_size ** (-0.5)
    shaped = (qblocks, BLOCK, head_count, head_size)
    query_blocks = heads_q.reshape(shaped)
    own = own_partial(query_blocks, heads_k.reshape(shaped), heads_v.reshape(shaped), scaling)
    seq_count = lax.axis_size("seq")
    myself = lax.axis_index("seq")
    cache_blocks = cache_keys.shape[0] // BLOCK
    tile_count = cache_blocks * head_count
    request_count = qblocks * head_count * top_count
    capacity = -(-request_count // seq_count)
    requests_all = lax.all_gather(selection, "seq", axis=0, tiled=True).reshape(
        seq_count, request_count
    )
    head_of = jnp.arange(request_count) // top_count % head_count
    my_requests = selection.reshape(request_count)
    my_owner = my_requests // cache_blocks
    my_slot = my_owner * capacity + order_ranks(my_owner)
    key_tiles = cache_keys.reshape(cache_blocks, BLOCK, head_count, head_size).transpose(0, 2, 1, 3)
    value_tiles = cache_values.reshape(cache_blocks, BLOCK, head_count, head_size).transpose(
        0, 2, 1, 3
    )
    tile_set = jnp.concatenate([key_tiles, value_tiles], axis=-1).reshape(
        tile_count, BLOCK, 2 * head_size
    )
    their_owner = requests_all // cache_blocks
    local_tile = requests_all % cache_blocks * head_count + head_of[None, :]
    served = (their_owner == myself).astype(jnp.float32)
    slot_pick = one_hot(order_ranks(their_owner), capacity) * served[..., None]
    picking = jnp.einsum("erc,erl->ecl", slot_pick, one_hot(local_tile, tile_count)).astype(
        jnp.bfloat16
    )
    parts = [own]
    outgoing = jnp.einsum(
        "ecl,lkf->eckf", picking, tile_set, preferred_element_type=jnp.float32
    ).astype(jnp.bfloat16)
    incoming = lax.all_to_all(outgoing, "seq", split_axis=0, concat_axis=0, tiled=True)
    fetched = incoming.reshape(seq_count * capacity, BLOCK, 2 * head_size)[my_slot]
    fetched = fetched.reshape(qblocks, head_count, top_count, BLOCK, 2 * head_size)
    for turn in range(top_count):
        parts.append(tile_partial(query_blocks, fetched[:, :, turn], scaling))
    result = merge_parts(parts)
    result = (
        result.transpose(0, 2, 1, 3)
        .reshape(qblocks * BLOCK, head_count * head_size)
        .astype(jnp.bfloat16)
    )
    return lax.all_to_all(result, ("heads", "sub"), split_axis=0, concat_axis=1, tiled=True)


STAT = 16
UNIT = 32767.0
LEAST = 1.2e-34
NEVER = -1.0e9
C2 = math.log2(math.e) * HD**-0.5


def attend_tile(q, k, v, mask=None):
    s = lax.dot_general(q, k, (((1,), (1,)), ((), ())), preferred_element_type=jnp.float32)
    if mask is not None:
        s = jnp.where(mask, s, -jnp.inf)
    m = jnp.max(s, axis=-1, keepdims=True)
    p = jnp.exp2((s - m) * C2)
    total = jnp.sum(p, axis=-1, keepdims=True)
    o = jnp.dot(p.astype(jnp.bfloat16), v, preferred_element_type=jnp.float32)
    return o, m * C2, total


def join(parts):
    top = functools.reduce(jnp.maximum, [m for _, m, _ in parts])
    factors = [jnp.exp2(m - top) for _, m, _ in parts]
    numer = sum(f * o for f, (o, _, _) in zip(factors, parts))
    denom = sum(f * t for f, (_, _, t) in zip(factors, parts))
    return numer, top, denom


def put(out_ref, heads):
    rows = heads[0][0].shape[0]
    lane = lax.broadcasted_iota(jnp.int32, (rows, 128), 1)
    stats = jnp.zeros((rows, 128), jnp.float32)
    for h, (numer, top, denom) in enumerate(heads):
        most = jnp.maximum(jnp.max(jnp.abs(numer), axis=-1, keepdims=True), LEAST)
        code = jnp.round(numer * (UNIT / most))
        out_ref[0:rows, h * HD : (h + 1) * HD] = code.astype(jnp.int32).astype(jnp.int16)
        for j, value in enumerate((top + jnp.log2(denom), jnp.log2(most / (UNIT * denom)))):
            whole = jnp.floor(value)
            stats = jnp.where(lane == 4 * h + 2 * j, whole, stats)
            stats = jnp.where(lane == 4 * h + 2 * j + 1, jnp.round((value - whole) * UNIT), stats)
    flat = jnp.transpose(stats)[0:STAT, :]
    out_ref[rows : rows + STAT, 0:rows] = flat.astype(jnp.int32).astype(jnp.int16)


def take(ref, head_count, valid=None):
    rows = ref.shape[0] - STAT
    flat = ref[rows : rows + STAT, 0:rows].astype(jnp.int32).astype(jnp.float32)
    flat = jnp.concatenate([flat, jnp.zeros((128 - STAT, rows), jnp.float32)], axis=0)
    stats = jnp.transpose(flat)
    heads = []
    for h in range(head_count):
        code = ref[0:rows, h * HD : (h + 1) * HD].astype(jnp.int32).astype(jnp.float32)
        weight = stats[:, 4 * h : 4 * h + 1] + stats[:, 4 * h + 1 : 4 * h + 2] * (1.0 / UNIT)
        unit = stats[:, 4 * h + 2 : 4 * h + 3] + stats[:, 4 * h + 3 : 4 * h + 4] * (1.0 / UNIT)
        if valid is not None:
            weight = jnp.where(valid, weight, NEVER)
        heads.append((code, weight, unit))
    return heads


def join_taken(taken):
    top = functools.reduce(jnp.maximum, [w for _, w, _ in taken])
    numer = sum(code * jnp.exp2(w - top + unit) for code, w, unit in taken)
    denom = sum(jnp.exp2(w - top) for _, w, _ in taken)
    return numer, top, denom


def cached_parts(q_ref, ck_ref, cv_ref, h):
    cols = slice(h * HD, (h + 1) * HD)
    q = q_ref[:, cols]
    parts = []
    for b in range(ck_ref.shape[0] // BLOCK):
        rows = slice(b * BLOCK, (b + 1) * BLOCK)
        parts.append(attend_tile(q, ck_ref[rows, cols], cv_ref[rows, cols]))
    return parts


def cached_kernel(count, flags_ref, *refs):
    q_refs, (ck_ref, cv_ref), out_refs = refs[:count], refs[count : count + 2], refs[count + 2 :]
    head_count = ck_ref.shape[1] // HD
    for at in range(count):

        @pl.when(flags_ref[at] > 0)
        def _(at=at):
            put(
                out_refs[at],
                [join(cached_parts(q_refs[at], ck_ref, cv_ref, h)) for h in range(head_count)],
            )


def own_kernel(order_ref, *refs):
    q_ref, *kv_refs, ck_ref, cv_ref, out_ref = refs
    head_count = ck_ref.shape[1] // HD
    width = ck_ref.shape[1]
    rows = q_ref.shape[0]
    pieces = len(kv_refs)
    step = kv_refs[0].shape[0]
    first = pieces

    def positions(shape, axis, start):
        at = lax.broadcasted_iota(jnp.int32, shape, axis)
        place = jnp.zeros(shape, jnp.int32)
        for d in range(shape[axis] // step):
            place = jnp.where(at // step == d, order_ref[start + d] * step + at % step, place)
        return place

    mask = positions((rows, step * pieces), 0, first) >= positions((rows, step * pieces), 1, 0)
    heads = []
    for h in range(head_count):
        cols = slice(h * HD, (h + 1) * HD)
        vcols = slice(width + h * HD, width + (h + 1) * HD)
        k = jnp.concatenate([r[:, cols] for r in kv_refs], axis=0)
        v = jnp.concatenate([r[:, vcols] for r in kv_refs], axis=0)
        parts = [attend_tile(q_ref[:, cols], k, v, mask)]
        heads.append(join(parts + cached_parts(q_ref, ck_ref, cv_ref, h)))
    put(out_ref, heads)


def merge_kernel(count, flags_ref, *refs):
    head_count = refs[0].shape[1] // HD
    for at in range(count):
        mine, theirs, out_ref = refs[2 * at], refs[2 * at + 1], refs[2 * count + at]
        a, b = take(mine, head_count), take(theirs, head_count, flags_ref[at] > 0)
        put(out_ref, [join_taken([a[h], b[h]]) for h in range(head_count)])


def final_kernel(flags_ref, own_ref, left_ref, right_ref, *out_refs):
    head_count = own_ref.shape[1] // HD
    a = take(own_ref, head_count)
    b = take(left_ref, head_count, flags_ref[0] > 0)
    c = take(right_ref, head_count, flags_ref[1] > 0)
    step = out_refs[0].shape[0]
    for h in range(head_count):
        numer, _, denom = join_taken([a[h], b[h], c[h]])
        value = (numer * (1.0 / denom)).astype(jnp.bfloat16)
        for i, out_ref in enumerate(out_refs):
            out_ref[:, h * HD : (h + 1) * HD] = value[i * step : (i + 1) * step]


def place_kernel(order_ref, *refs):
    *pieces, out_ref = refs
    width = pieces[0].shape[1]
    for d, piece in enumerate(pieces):
        start = pl.multiple_of(order_ref[d] * width, width)
        out_ref[:, pl.ds(start, width)] = piece[...]


def call(kernel, scalars, arrays, outs, flops=0, exps=0):
    moved = sum(a.size * a.dtype.itemsize for a in arrays)
    moved += sum(math.prod(o.shape) * o.dtype.itemsize for o in outs)
    return pl.pallas_call(
        kernel,
        out_shape=outs,
        in_specs=[pl.BlockSpec(memory_space=pltpu.SMEM)]
        + [pl.BlockSpec(memory_space=pltpu.VMEM)] * len(arrays),
        out_specs=[pl.BlockSpec(memory_space=pltpu.VMEM)] * len(outs),
        compiler_params=pltpu.CompilerParams(vmem_limit_bytes=32 * 1024 * 1024),
        cost_estimate=pl.CostEstimate(flops=flops, bytes_accessed=moved, transcendentals=exps),
    )(scalars, *arrays)


def dense_body(queries, new_keys, new_values, cache_keys, cache_values, chunk_count):
    seq_count = lax.axis_size("seq")
    s = lax.axis_index("seq")
    shares = lax.axis_size("heads") * lax.axis_size("sub")
    me = lax.axis_index("heads") * lax.axis_size("sub") + lax.axis_index("sub")
    step, width = queries.shape[0], queries.shape[1] // shares
    cached = cache_keys.shape[0]

    def swap(x, d):
        return lax.ppermute(x, ("heads", "sub"), [(i, i ^ d) for i in range(shares)])

    def piece(x, d):
        return lax.dynamic_slice(x, (0, (me ^ d) * width), (step, width))

    def along(x, shift, sources):
        return lax.ppermute(x, "seq", [(i, i + shift) for i in sources])

    q = [piece(queries, 0)] + [swap(piece(queries, d), d) for d in range(1, shares)]
    kv = [jnp.concatenate([piece(new_keys, d), piece(new_values, d)], axis=1) for d in range(shares)]
    kv = [kv[0]] + [swap(kv[d], d) for d in range(1, shares)]
    each = shares // chunk_count
    rows = each * step
    packed = jax.ShapeDtypeStruct((rows + STAT, width), jnp.int16)
    tile_flops = 4 * rows * cached * width
    tile_exps = rows * cached * (width // HD)

    def flags(*values):
        return jnp.stack([jnp.asarray(v).astype(jnp.int32) for v in values])

    order = [me ^ d for d in range(shares)]
    results = []
    for c in range(chunk_count):
        mine = jnp.concatenate(q[c * each : (c + 1) * each], axis=0)
        up, low, down, high = mine, mine, {}, {}
        for k in range(1, seq_count):
            up = along(up, 1, range(k - 1, seq_count - 1))
            low = along(low, -1, range(1, seq_count - k + 1))
            down[k], high[k] = call(
                functools.partial(cached_kernel, 2),
                flags(s >= k, s < seq_count - k),
                [up, low, cache_keys, cache_values],
                [packed, packed],
                tile_flops,
                tile_exps,
            )
        own = call(
            own_kernel,
            flags(*order, *order[c * each : (c + 1) * each]),
            [mine, *kv, cache_keys, cache_values],
            [packed],
            tile_flops * 3 // 2,
            tile_exps * 3 // 2,
        )[0]
        left, right = down[seq_count - 1], high[seq_count - 1]
        for k in range(seq_count - 1, 0, -1):
            left = along(left, -1, range(k, seq_count))
            right = along(right, 1, range(0, seq_count - k))
            if k > 1:
                left, right = call(
                    functools.partial(merge_kernel, 2),
                    flags(s < seq_count - 1, s > 0),
                    [down[k - 1], left, high[k - 1], right],
                    [packed, packed],
                )
        results += call(
            final_kernel,
            flags(s < seq_count - 1, s > 0),
            [own, left, right],
            [jax.ShapeDtypeStruct((step, width), jnp.bfloat16)] * each,
        )
    results = [results[0]] + [swap(results[d], d) for d in range(1, shares)]
    return call(
        place_kernel, flags(*order), results, [jax.ShapeDtypeStruct((step, shares * width), jnp.bfloat16)]
    )[0]


CHUNKS = 2


def body(queries, new_keys, new_values, cache_keys, cache_values, selection):
    qblocks, head_count, top_count = selection.shape
    shares = lax.axis_size("heads") * lax.axis_size("sub")
    context_blocks = cache_keys.shape[0] // BLOCK * lax.axis_size("seq")
    whole = top_count == context_blocks and qblocks == 1 and shares & (shares - 1) == 0
    if whole and shares % CHUNKS == 0 and 4 * head_count <= STAT:
        return dense_body(queries, new_keys, new_values, cache_keys, cache_values, CHUNKS)
    return sparse_body(queries, new_keys, new_values, cache_keys, cache_values, selection)


def solution(mesh):
    in_specs = (
        P(("groups", "seq", "heads", "sub"), None),
        P(("groups", "seq", "heads", "sub"), None),
        P(("groups", "seq", "heads", "sub"), None),
        P(("groups", "seq"), ("heads", "sub")),
        P(("groups", "seq"), ("heads", "sub")),
        P(("groups", "seq"), ("heads", "sub"), None),
    )
    out_specs = P(("groups", "seq", "heads", "sub"), None)
    return jax.shard_map(body, mesh=mesh, in_specs=in_specs, out_specs=out_specs, check_vma=False)
```

```python
import functools
import math

import jax
import jax.numpy as jnp
from jax import lax
from jax.experimental import pallas as pl
from jax.experimental.pallas import tpu as pltpu
from jax.sharding import PartitionSpec as P

HD = 128
BLOCK = 512


def order_ranks(owners):
    length = owners.shape[-1]
    counter = jnp.arange(length)
    earlier = counter[None, :] < counter[:, None]
    same_owner = owners[..., :, None] == owners[..., None, :]
    return jnp.sum(jnp.logical_and(same_owner, earlier), axis=-1)


def one_hot(values, length):
    return (values[..., None] == jnp.arange(length)).astype(jnp.float32)


def own_partial(query_blocks, key_blocks, value_blocks, scaling):
    scores = (
        jnp.einsum("bqhd,bkhd->bhqk", query_blocks, key_blocks, preferred_element_type=jnp.float32)
        * scaling
    )
    length = query_blocks.shape[1]
    causal = jnp.arange(length)[:, None] >= jnp.arange(length)[None, :]
    scores = jnp.where(causal, scores, -jnp.inf)
    highest = jnp.max(scores, axis=-1)
    weights = jnp.exp(scores - highest[..., None])
    totals = jnp.sum(weights, axis=-1)
    mixed = jnp.einsum(
        "bhqk,bkhd->bhqd",
        weights.astype(jnp.bfloat16),
        value_blocks,
        preferred_element_type=jnp.float32,
    )
    return (mixed, highest, totals)


def tile_partial(query_blocks, tile_pair, scaling):
    head_size = query_blocks.shape[-1]
    scores = (
        jnp.einsum(
            "bqhd,bhkd->bhqk",
            query_blocks,
            tile_pair[..., :head_size],
            preferred_element_type=jnp.float32,
        )
        * scaling
    )
    highest = jnp.max(scores, axis=-1)
    weights = jnp.exp(scores - highest[..., None])
    totals = jnp.sum(weights, axis=-1)
    mixed = jnp.einsum(
        "bhqk,bhkd->bhqd",
        weights.astype(jnp.bfloat16),
        tile_pair[..., head_size:],
        preferred_element_type=jnp.float32,
    )
    return (mixed, highest, totals)


def merge_parts(parts):
    top = parts[0][1]
    for part in parts[1:]:
        top = jnp.maximum(top, part[1])
    numer = jnp.zeros(parts[0][0].shape, jnp.float32)
    denom = jnp.zeros(parts[0][2].shape, jnp.float32)
    for part in parts:
        factor = jnp.exp(part[1] - top)
        numer = numer + factor[..., None] * part[0]
        denom = denom + factor * part[2]
    return numer / denom[..., None]


def sparse_body(queries, new_keys, new_values, cache_keys, cache_values, selection):
    heads_q, heads_k, heads_v = (
        lax.all_to_all(queries, ("heads", "sub"), split_axis=1, concat_axis=0, tiled=True),
        lax.all_to_all(new_keys, ("heads", "sub"), split_axis=1, concat_axis=0, tiled=True),
        lax.all_to_all(new_values, ("heads", "sub"), split_axis=1, concat_axis=0, tiled=True),
    )
    qblocks, head_count, top_count = selection.shape
    head_size = HD
    scaling = head_size ** (-0.5)
    shaped = (qblocks, BLOCK, head_count, head_size)
    query_blocks = heads_q.reshape(shaped)
    own = own_partial(query_blocks, heads_k.reshape(shaped), heads_v.reshape(shaped), scaling)
    seq_count = lax.axis_size("seq")
    myself = lax.axis_index("seq")
    cache_blocks = cache_keys.shape[0] // BLOCK
    tile_count = cache_blocks * head_count
    request_count = qblocks * head_count * top_count
    capacity = -(-request_count // seq_count)
    requests_all = lax.all_gather(selection, "seq", axis=0, tiled=True).reshape(
        seq_count, request_count
    )
    head_of = jnp.arange(request_count) // top_count % head_count
    my_requests = selection.reshape(request_count)
    my_owner = my_requests // cache_blocks
    my_slot = my_owner * capacity + order_ranks(my_owner)
    key_tiles = cache_keys.reshape(cache_blocks, BLOCK, head_count, head_size).transpose(0, 2, 1, 3)
    value_tiles = cache_values.reshape(cache_blocks, BLOCK, head_count, head_size).transpose(
        0, 2, 1, 3
    )
    tile_set = jnp.concatenate([key_tiles, value_tiles], axis=-1).reshape(
        tile_count, BLOCK, 2 * head_size
    )
    their_owner = requests_all // cache_blocks
    local_tile = requests_all % cache_blocks * head_count + head_of[None, :]
    served = (their_owner == myself).astype(jnp.float32)
    slot_pick = one_hot(order_ranks(their_owner), capacity) * served[..., None]
    picking = jnp.einsum("erc,erl->ecl", slot_pick, one_hot(local_tile, tile_count)).astype(
        jnp.bfloat16
    )
    parts = [own]
    outgoing = jnp.einsum(
        "ecl,lkf->eckf", picking, tile_set, preferred_element_type=jnp.float32
    ).astype(jnp.bfloat16)
    incoming = lax.all_to_all(outgoing, "seq", split_axis=0, concat_axis=0, tiled=True)
    fetched = incoming.reshape(seq_count * capacity, BLOCK, 2 * head_size)[my_slot]
    fetched = fetched.reshape(qblocks, head_count, top_count, BLOCK, 2 * head_size)
    for turn in range(top_count):
        parts.append(tile_partial(query_blocks, fetched[:, :, turn], scaling))
    result = merge_parts(parts)
    result = (
        result.transpose(0, 2, 1, 3)
        .reshape(qblocks * BLOCK, head_count * head_size)
        .astype(jnp.bfloat16)
    )
    return lax.all_to_all(result, ("heads", "sub"), split_axis=0, concat_axis=1, tiled=True)


STAT = 16
UNIT = 32767.0
LEAST = 1.2e-34
C2 = math.log2(math.e) * HD**-0.5


def attend_tile(q, k, v, v_dim, mask=None):
    s = lax.dot_general(k, q, (((1,), (1,)), ((), ())), preferred_element_type=jnp.float32)
    if mask is not None:
        s = jnp.where(mask, s, -jnp.inf)
    m = jnp.max(s, axis=0, keepdims=True)
    p = jnp.exp2((s - m) * C2)
    total = jnp.sum(p, axis=0, keepdims=True)
    o = lax.dot_general(
        v, p.astype(jnp.bfloat16), (((v_dim,), (0,)), ((), ())), preferred_element_type=jnp.float32
    )
    return o, m * C2, total


def join(parts):
    top = functools.reduce(jnp.maximum, [m for _, m, _ in parts])
    factors = [jnp.exp2(m - top) for _, m, _ in parts]
    numer = sum(f * o for f, (o, _, _) in zip(factors, parts))
    denom = sum(f * t for f, (_, _, t) in zip(factors, parts))
    return numer, top, denom


def put(out_ref, heads):
    width, rows = len(heads) * HD, heads[0][0].shape[1]
    at = lax.broadcasted_iota(jnp.int32, (STAT, rows), 0)
    stats = jnp.zeros((STAT, rows), jnp.float32)
    for h, (numer, top, denom) in enumerate(heads):
        most = jnp.maximum(jnp.max(jnp.abs(numer), axis=0, keepdims=True), LEAST)
        code = jnp.round(numer * (UNIT / most))
        out_ref[h * HD : (h + 1) * HD, :] = code.astype(jnp.int32).astype(jnp.int16)
        for j, value in enumerate((top + jnp.log2(denom), jnp.log2(most / (UNIT * denom)))):
            whole = jnp.floor(value)
            stats = jnp.where(at == 4 * h + 2 * j, whole, stats)
            stats = jnp.where(at == 4 * h + 2 * j + 1, jnp.round((value - whole) * UNIT), stats)
    out_ref[width : width + STAT, :] = stats.astype(jnp.int32).astype(jnp.int16)


def take(ref):
    width = ref.shape[0] - STAT
    stats = ref[width : width + STAT, :].astype(jnp.int32).astype(jnp.float32)
    heads = []
    for h in range(width // HD):
        code = ref[h * HD : (h + 1) * HD, :].astype(jnp.int32).astype(jnp.float32)
        weight = stats[4 * h : 4 * h + 1] + stats[4 * h + 1 : 4 * h + 2] * (1.0 / UNIT)
        unit = stats[4 * h + 2 : 4 * h + 3] + stats[4 * h + 3 : 4 * h + 4] * (1.0 / UNIT)
        heads.append((code, weight, unit))
    return heads


def join_taken(taken):
    top = functools.reduce(jnp.maximum, [w for _, w, _ in taken])
    numer = sum(code * jnp.exp2(w - top + unit) for code, w, unit in taken)
    denom = sum(jnp.exp2(w - top) for _, w, _ in taken)
    return numer, top, denom


def cached_parts(q_ref, ck_ref, cvt_ref, h):
    cols = slice(h * HD, (h + 1) * HD)
    q = q_ref[:, cols]
    parts = []
    for b in range(ck_ref.shape[0] // BLOCK):
        rows = slice(b * BLOCK, (b + 1) * BLOCK)
        parts.append(attend_tile(q, ck_ref[rows, cols], cvt_ref[cols, rows], 1))
    return parts


def cached_kernel(q_ref, ck_ref, cvt_ref, out_ref):
    heads = range(ck_ref.shape[1] // HD)
    put(out_ref, [join(cached_parts(q_ref, ck_ref, cvt_ref, h)) for h in heads])


def own_kernel(start, order_ref, *refs):
    q_ref, *kv_refs, ck_ref, cvt_ref, out_ref = refs
    width = ck_ref.shape[1]
    rows = q_ref.shape[0]
    step = kv_refs[0].shape[0]

    def positions(shape, axis, first):
        at = lax.broadcasted_iota(jnp.int32, shape, axis)
        place = jnp.zeros(shape, jnp.int32)
        for d in range(shape[axis] // step):
            place = jnp.where(at // step == d, order_ref[first + d] * step + at % step, place)
        return place

    shape = (step * len(kv_refs), rows)
    mask = positions(shape, 1, start) >= positions(shape, 0, 0)
    heads = []
    for h in range(width // HD):
        cols = slice(h * HD, (h + 1) * HD)
        vcols = slice(width + h * HD, width + (h + 1) * HD)
        k = jnp.concatenate([r[:, cols] for r in kv_refs], axis=0)
        v = jnp.concatenate([r[:, vcols] for r in kv_refs], axis=0)
        parts = [attend_tile(q_ref[:, cols], k, v, 0, mask)]
        heads.append(join(parts + cached_parts(q_ref, ck_ref, cvt_ref, h)))
    put(out_ref, heads)


def merge_kernel(*refs):
    *in_refs, out_ref = refs
    put(out_ref, [join_taken(taken) for taken in zip(*[take(r) for r in in_refs])])


def final_kernel(count, *refs):
    in_refs, out_refs = refs[:count], refs[count:]
    step = out_refs[0].shape[0]
    for h, taken in enumerate(zip(*[take(r) for r in in_refs])):
        numer, _, denom = join_taken(taken)
        value = jnp.transpose(numer * (1.0 / denom)).astype(jnp.bfloat16)
        for i, out_ref in enumerate(out_refs):
            out_ref[:, h * HD : (h + 1) * HD] = value[i * step : (i + 1) * step]


def place_kernel(order_ref, *refs):
    *pieces, out_ref = refs
    width = pieces[0].shape[1]
    for d, piece in enumerate(pieces):
        start = pl.multiple_of(order_ref[d] * width, width)
        out_ref[:, pl.ds(start, width)] = piece[...]


def call(kernel, arrays, outs, flops=0, exps=0, scalars=None):
    moved = sum(a.size * a.dtype.itemsize for a in arrays)
    moved += sum(math.prod(o.shape) * o.dtype.itemsize for o in outs)
    first = [] if scalars is None else [scalars]
    return pl.pallas_call(
        kernel,
        out_shape=outs,
        in_specs=[pl.BlockSpec(memory_space=pltpu.SMEM)] * len(first)
        + [pl.BlockSpec(memory_space=pltpu.VMEM)] * len(arrays),
        out_specs=[pl.BlockSpec(memory_space=pltpu.VMEM)] * len(outs),
        compiler_params=pltpu.CompilerParams(vmem_limit_bytes=32 * 1024 * 1024),
        cost_estimate=pl.CostEstimate(flops=flops, bytes_accessed=moved, transcendentals=exps),
    )(*first, *arrays)


def dense_body(queries, new_keys, new_values, cache_keys, cache_values, chunk_count):
    seq_count = lax.axis_size("seq")
    shares = lax.axis_size("heads") * lax.axis_size("sub")
    me = lax.axis_index("heads") * lax.axis_size("sub") + lax.axis_index("sub")
    step, width = queries.shape[0], queries.shape[1] // shares
    cached = cache_keys.shape[0]
    each = shares // chunk_count
    rows = each * step
    packed = jax.ShapeDtypeStruct((width + STAT, rows), jnp.int16)
    tile_flops = 4 * rows * cached * width
    tile_exps = rows * cached * (width // HD)
    bits = [1 << b for b in range(seq_count.bit_length() - 1)]

    def swap(x, d):
        return lax.ppermute(x, ("heads", "sub"), [(i, i ^ d) for i in range(shares)])

    def piece(x, d):
        return lax.dynamic_slice(x, (0, (me ^ d) * width), (step, width))

    def along(x, bit):
        return lax.ppermute(x, "seq", [(i, i ^ bit) for i in range(seq_count)])

    order = jnp.stack([me ^ d for d in range(shares)]).astype(jnp.int32)
    cache_vt = cache_values.T
    q = [piece(queries, 0)] + [swap(piece(queries, d), d) for d in range(1, shares)]
    kv = [jnp.concatenate([piece(new_keys, d), piece(new_values, d)], axis=1) for d in range(shares)]
    kv = [kv[0]] + [swap(kv[d], d) for d in range(1, shares)]
    results = []
    for c in range(chunk_count):
        held = {0: jnp.concatenate(q[c * each : (c + 1) * each], axis=0)}
        for bit in reversed(bits):
            held.update({o | bit: along(x, bit) for o, x in list(held.items())})
        part = {
            o: call(cached_kernel, [held[o], cache_keys, cache_vt], [packed], tile_flops, tile_exps)[0]
            for o in range(1, seq_count)
        }
        part[0] = call(
            functools.partial(own_kernel, c * each),
            [held[0], *kv, cache_keys, cache_vt],
            [packed],
            tile_flops * 3 // 2,
            tile_exps * 3 // 2,
            order,
        )[0]
        arrived = []
        for bit in bits:
            for o in [o for o in part if o & bit]:
                got = along(part.pop(o), bit)
                if o == bit:
                    arrived.append(got)
                else:
                    part[o ^ bit] = call(merge_kernel, [part[o ^ bit], got], [packed])[0]
        results += call(
            functools.partial(final_kernel, 1 + len(arrived)),
            [part[0], *arrived],
            [jax.ShapeDtypeStruct((step, width), jnp.bfloat16)] * each,
        )
    results = [results[0]] + [swap(results[d], d) for d in range(1, shares)]
    out = jax.ShapeDtypeStruct((step, shares * width), jnp.bfloat16)
    return call(place_kernel, results, [out], scalars=order)[0]


CHUNKS = 2


def power_of_two(n):
    return n & (n - 1) == 0


def body(queries, new_keys, new_values, cache_keys, cache_values, selection):
    qblocks, head_count, top_count = selection.shape
    seq_count = lax.axis_size("seq")
    shares = lax.axis_size("heads") * lax.axis_size("sub")
    every = top_count == cache_keys.shape[0] // BLOCK * seq_count and qblocks == 1
    fits = power_of_two(seq_count) and power_of_two(shares) and shares % CHUNKS == 0
    if every and fits and 4 * head_count <= STAT:
        return dense_body(queries, new_keys, new_values, cache_keys, cache_values, CHUNKS)
    return sparse_body(queries, new_keys, new_values, cache_keys, cache_values, selection)


def solution(mesh):
    in_specs = (
        P(("groups", "seq", "heads", "sub"), None),
        P(("groups", "seq", "heads", "sub"), None),
        P(("groups", "seq", "heads", "sub"), None),
        P(("groups", "seq"), ("heads", "sub")),
        P(("groups", "seq"), ("heads", "sub")),
        P(("groups", "seq"), ("heads", "sub"), None),
    )
    out_specs = P(("groups", "seq", "heads", "sub"), None)
    return jax.shard_map(body, mesh=mesh, in_specs=in_specs, out_specs=out_specs, check_vma=False)
```

```python
import functools
import math

import jax
import jax.numpy as jnp
from jax import lax
from jax.experimental import pallas as pl
from jax.experimental.pallas import tpu as pltpu
from jax.sharding import PartitionSpec as P

HD = 128
BLOCK = 512


def order_ranks(owners):
    length = owners.shape[-1]
    counter = jnp.arange(length)
    earlier = counter[None, :] < counter[:, None]
    same_owner = owners[..., :, None] == owners[..., None, :]
    return jnp.sum(jnp.logical_and(same_owner, earlier), axis=-1)


def one_hot(values, length):
    return (values[..., None] == jnp.arange(length)).astype(jnp.float32)


def own_partial(query_blocks, key_blocks, value_blocks, scaling):
    scores = (
        jnp.einsum("bqhd,bkhd->bhqk", query_blocks, key_blocks, preferred_element_type=jnp.float32)
        * scaling
    )
    length = query_blocks.shape[1]
    causal = jnp.arange(length)[:, None] >= jnp.arange(length)[None, :]
    scores = jnp.where(causal, scores, -jnp.inf)
    highest = jnp.max(scores, axis=-1)
    weights = jnp.exp(scores - highest[..., None])
    totals = jnp.sum(weights, axis=-1)
    mixed = jnp.einsum(
        "bhqk,bkhd->bhqd",
        weights.astype(jnp.bfloat16),
        value_blocks,
        preferred_element_type=jnp.float32,
    )
    return (mixed, highest, totals)


def tile_partial(query_blocks, tile_pair, scaling):
    head_size = query_blocks.shape[-1]
    scores = (
        jnp.einsum(
            "bqhd,bhkd->bhqk",
            query_blocks,
            tile_pair[..., :head_size],
            preferred_element_type=jnp.float32,
        )
        * scaling
    )
    highest = jnp.max(scores, axis=-1)
    weights = jnp.exp(scores - highest[..., None])
    totals = jnp.sum(weights, axis=-1)
    mixed = jnp.einsum(
        "bhqk,bhkd->bhqd",
        weights.astype(jnp.bfloat16),
        tile_pair[..., head_size:],
        preferred_element_type=jnp.float32,
    )
    return (mixed, highest, totals)


def merge_parts(parts):
    top = parts[0][1]
    for part in parts[1:]:
        top = jnp.maximum(top, part[1])
    numer = jnp.zeros(parts[0][0].shape, jnp.float32)
    denom = jnp.zeros(parts[0][2].shape, jnp.float32)
    for part in parts:
        factor = jnp.exp(part[1] - top)
        numer = numer + factor[..., None] * part[0]
        denom = denom + factor * part[2]
    return numer / denom[..., None]


def sparse_body(queries, new_keys, new_values, cache_keys, cache_values, selection):
    heads_q, heads_k, heads_v = (
        lax.all_to_all(queries, ("heads", "sub"), split_axis=1, concat_axis=0, tiled=True),
        lax.all_to_all(new_keys, ("heads", "sub"), split_axis=1, concat_axis=0, tiled=True),
        lax.all_to_all(new_values, ("heads", "sub"), split_axis=1, concat_axis=0, tiled=True),
    )
    qblocks, head_count, top_count = selection.shape
    head_size = HD
    scaling = head_size ** (-0.5)
    shaped = (qblocks, BLOCK, head_count, head_size)
    query_blocks = heads_q.reshape(shaped)
    own = own_partial(query_blocks, heads_k.reshape(shaped), heads_v.reshape(shaped), scaling)
    seq_count = lax.axis_size("seq")
    myself = lax.axis_index("seq")
    cache_blocks = cache_keys.shape[0] // BLOCK
    tile_count = cache_blocks * head_count
    request_count = qblocks * head_count * top_count
    capacity = -(-request_count // seq_count)
    requests_all = lax.all_gather(selection, "seq", axis=0, tiled=True).reshape(
        seq_count, request_count
    )
    head_of = jnp.arange(request_count) // top_count % head_count
    my_requests = selection.reshape(request_count)
    my_owner = my_requests // cache_blocks
    my_slot = my_owner * capacity + order_ranks(my_owner)
    key_tiles = cache_keys.reshape(cache_blocks, BLOCK, head_count, head_size).transpose(0, 2, 1, 3)
    value_tiles = cache_values.reshape(cache_blocks, BLOCK, head_count, head_size).transpose(
        0, 2, 1, 3
    )
    tile_set = jnp.concatenate([key_tiles, value_tiles], axis=-1).reshape(
        tile_count, BLOCK, 2 * head_size
    )
    their_owner = requests_all // cache_blocks
    local_tile = requests_all % cache_blocks * head_count + head_of[None, :]
    served = (their_owner == myself).astype(jnp.float32)
    slot_pick = one_hot(order_ranks(their_owner), capacity) * served[..., None]
    picking = jnp.einsum("erc,erl->ecl", slot_pick, one_hot(local_tile, tile_count)).astype(
        jnp.bfloat16
    )
    parts = [own]
    outgoing = jnp.einsum(
        "ecl,lkf->eckf", picking, tile_set, preferred_element_type=jnp.float32
    ).astype(jnp.bfloat16)
    incoming = lax.all_to_all(outgoing, "seq", split_axis=0, concat_axis=0, tiled=True)
    fetched = incoming.reshape(seq_count * capacity, BLOCK, 2 * head_size)[my_slot]
    fetched = fetched.reshape(qblocks, head_count, top_count, BLOCK, 2 * head_size)
    for turn in range(top_count):
        parts.append(tile_partial(query_blocks, fetched[:, :, turn], scaling))
    result = merge_parts(parts)
    result = (
        result.transpose(0, 2, 1, 3)
        .reshape(qblocks * BLOCK, head_count * head_size)
        .astype(jnp.bfloat16)
    )
    return lax.all_to_all(result, ("heads", "sub"), split_axis=0, concat_axis=1, tiled=True)


STAT = 16
UNIT = 32767.0
LEAST = 1.2e-34
C2 = math.log2(math.e) * HD**-0.5


def scores_of(q, k, mask=None):
    s = lax.dot_general(k, q, (((1,), (1,)), ((), ())), preferred_element_type=jnp.float32)
    return s if mask is None else jnp.where(mask, s, -jnp.inf)


def weights_of(s):
    m = jnp.max(s, axis=0, keepdims=True)
    p = jnp.exp2((s - m) * C2)
    return p.astype(jnp.bfloat16), m * C2, jnp.sum(p, axis=0, keepdims=True)


def values_of(v, w, v_dim):
    return lax.dot_general(v, w, (((v_dim,), (0,)), ((), ())), preferred_element_type=jnp.float32)


def attend(tiles):
    count = len(tiles)
    s, w, parts = {}, {}, []
    for t in range(count + 2):
        if t < count:
            s[t] = tiles[t][0]()
        if 1 <= t <= count:
            w[t - 1] = weights_of(s.pop(t - 1))
        if t >= 2:
            weights, m, total = w.pop(t - 2)
            parts.append((tiles[t - 2][1](weights), m, total))
    return parts


def join(parts):
    top = functools.reduce(jnp.maximum, [m for _, m, _ in parts])
    factors = [jnp.exp2(m - top) for _, m, _ in parts]
    numer = sum(f * o for f, (o, _, _) in zip(factors, parts))
    denom = sum(f * t for f, (_, _, t) in zip(factors, parts))
    return numer, top, denom


def put(out_ref, heads):
    width, rows = len(heads) * HD, heads[0][0].shape[1]
    at = lax.broadcasted_iota(jnp.int32, (STAT, rows), 0)
    stats = jnp.zeros((STAT, rows), jnp.float32)
    for h, (numer, top, denom) in enumerate(heads):
        most = jnp.maximum(jnp.max(jnp.abs(numer), axis=0, keepdims=True), LEAST)
        code = jnp.round(numer * (UNIT / most))
        out_ref[h * HD : (h + 1) * HD, :] = code.astype(jnp.int32).astype(jnp.int16)
        for j, value in enumerate((top + jnp.log2(denom), jnp.log2(most / (UNIT * denom)))):
            whole = jnp.floor(value)
            stats = jnp.where(at == 4 * h + 2 * j, whole, stats)
            stats = jnp.where(at == 4 * h + 2 * j + 1, jnp.round((value - whole) * UNIT), stats)
    out_ref[width : width + STAT, :] = stats.astype(jnp.int32).astype(jnp.int16)


def take(ref):
    width = ref.shape[0] - STAT
    stats = ref[width : width + STAT, :].astype(jnp.int32).astype(jnp.float32)
    heads = []
    for h in range(width // HD):
        code = ref[h * HD : (h + 1) * HD, :].astype(jnp.int32).astype(jnp.float32)
        weight = stats[4 * h : 4 * h + 1] + stats[4 * h + 1 : 4 * h + 2] * (1.0 / UNIT)
        unit = stats[4 * h + 2 : 4 * h + 3] + stats[4 * h + 3 : 4 * h + 4] * (1.0 / UNIT)
        heads.append((code, weight, unit))
    return heads


def join_taken(taken):
    top = functools.reduce(jnp.maximum, [w for _, w, _ in taken])
    numer = sum(code * jnp.exp2(w - top + unit) for code, w, unit in taken)
    denom = sum(jnp.exp2(w - top) for _, w, _ in taken)
    return numer, top, denom


def cached_tiles(q_ref, ck_ref, cvt_ref, h):
    cols = slice(h * HD, (h + 1) * HD)
    tiles = []
    for b in range(ck_ref.shape[0] // BLOCK):
        rows = slice(b * BLOCK, (b + 1) * BLOCK)
        tiles.append(
            (
                lambda rows=rows: scores_of(q_ref[:, cols], ck_ref[rows, cols]),
                lambda w, rows=rows: values_of(cvt_ref[cols, rows], w, 1),
            )
        )
    return tiles


def attend_heads(tiles_of_heads):
    parts = attend([t for tiles in tiles_of_heads for t in tiles])
    heads = []
    for tiles in tiles_of_heads:
        heads.append(join(parts[: len(tiles)]))
        parts = parts[len(tiles) :]
    return heads


def cached_kernel(q_ref, ck_ref, cvt_ref, out_ref):
    heads = range(ck_ref.shape[1] // HD)
    put(out_ref, attend_heads([cached_tiles(q_ref, ck_ref, cvt_ref, h) for h in heads]))


def own_kernel(start, order_ref, *refs):
    q_ref, *kv_refs, ck_ref, cvt_ref, out_ref = refs
    width = ck_ref.shape[1]
    rows = q_ref.shape[0]
    step = kv_refs[0].shape[0]

    def positions(shape, axis, first):
        at = lax.broadcasted_iota(jnp.int32, shape, axis)
        place = jnp.zeros(shape, jnp.int32)
        for d in range(shape[axis] // step):
            place = jnp.where(at // step == d, order_ref[first + d] * step + at % step, place)
        return place

    shape = (step * len(kv_refs), rows)
    mask = positions(shape, 1, start) >= positions(shape, 0, 0)
    heads = []
    for h in range(width // HD):
        cols = slice(h * HD, (h + 1) * HD)
        vcols = slice(width + h * HD, width + (h + 1) * HD)
        own = (
            lambda cols=cols: scores_of(
                q_ref[:, cols], jnp.concatenate([r[:, cols] for r in kv_refs], axis=0), mask
            ),
            lambda w, vcols=vcols: values_of(
                jnp.concatenate([r[:, vcols] for r in kv_refs], axis=0), w, 0
            ),
        )
        heads.append([own] + cached_tiles(q_ref, ck_ref, cvt_ref, h))
    put(out_ref, attend_heads(heads))


def merge_kernel(*refs):
    *in_refs, out_ref = refs
    put(out_ref, [join_taken(taken) for taken in zip(*[take(r) for r in in_refs])])


def final_kernel(count, *refs):
    in_refs, out_refs = refs[:count], refs[count:]
    step = out_refs[0].shape[0]
    for h, taken in enumerate(zip(*[take(r) for r in in_refs])):
        numer, _, denom = join_taken(taken)
        value = jnp.transpose(numer * (1.0 / denom)).astype(jnp.bfloat16)
        for i, out_ref in enumerate(out_refs):
            out_ref[:, h * HD : (h + 1) * HD] = value[i * step : (i + 1) * step]


def place_kernel(order_ref, *refs):
    *pieces, out_ref = refs
    width = pieces[0].shape[1]
    for d, piece in enumerate(pieces):
        start = pl.multiple_of(order_ref[d] * width, width)
        out_ref[:, pl.ds(start, width)] = piece[...]


def call(kernel, arrays, outs, flops=0, exps=0, scalars=None):
    moved = sum(a.size * a.dtype.itemsize for a in arrays)
    moved += sum(math.prod(o.shape) * o.dtype.itemsize for o in outs)
    first = [] if scalars is None else [scalars]
    return pl.pallas_call(
        kernel,
        out_shape=outs,
        in_specs=[pl.BlockSpec(memory_space=pltpu.SMEM)] * len(first)
        + [pl.BlockSpec(memory_space=pltpu.VMEM)] * len(arrays),
        out_specs=[pl.BlockSpec(memory_space=pltpu.VMEM)] * len(outs),
        compiler_params=pltpu.CompilerParams(vmem_limit_bytes=32 * 1024 * 1024),
        cost_estimate=pl.CostEstimate(flops=flops, bytes_accessed=moved, transcendentals=exps),
    )(*first, *arrays)


def dense_body(queries, new_keys, new_values, cache_keys, cache_values, chunk_count):
    seq_count = lax.axis_size("seq")
    shares = lax.axis_size("heads") * lax.axis_size("sub")
    me = lax.axis_index("heads") * lax.axis_size("sub") + lax.axis_index("sub")
    step, width = queries.shape[0], queries.shape[1] // shares
    cached = cache_keys.shape[0]
    each = shares // chunk_count
    rows = each * step
    packed = jax.ShapeDtypeStruct((width + STAT, rows), jnp.int16)
    tile_flops = 4 * rows * cached * width
    tile_exps = rows * cached * (width // HD)
    bits = [1 << b for b in range(seq_count.bit_length() - 1)]

    def swap(x, d):
        return lax.ppermute(x, ("heads", "sub"), [(i, i ^ d) for i in range(shares)])

    def piece(x, d):
        return lax.dynamic_slice(x, (0, (me ^ d) * width), (step, width))

    def along(x, bit):
        return lax.ppermute(x, "seq", [(i, i ^ bit) for i in range(seq_count)])

    order = jnp.stack([me ^ d for d in range(shares)]).astype(jnp.int32)
    cache_vt = cache_values.T
    q = [piece(queries, 0)] + [swap(piece(queries, d), d) for d in range(1, shares)]
    kv = [jnp.concatenate([piece(new_keys, d), piece(new_values, d)], axis=1) for d in range(shares)]
    kv = [kv[0]] + [swap(kv[d], d) for d in range(1, shares)]
    results = []
    for c in range(chunk_count):
        held = {0: jnp.concatenate(q[c * each : (c + 1) * each], axis=0)}
        for bit in reversed(bits):
            held.update({o | bit: along(x, bit) for o, x in list(held.items())})
        part = {
            o: call(cached_kernel, [held[o], cache_keys, cache_vt], [packed], tile_flops, tile_exps)[0]
            for o in range(1, seq_count)
        }
        part[0] = call(
            functools.partial(own_kernel, c * each),
            [held[0], *kv, cache_keys, cache_vt],
            [packed],
            tile_flops * 3 // 2,
            tile_exps * 3 // 2,
            order,
        )[0]
        arrived = []
        for bit in bits:
            for o in [o for o in part if o & bit]:
                got = along(part.pop(o), bit)
                if o == bit:
                    arrived.append(got)
                else:
                    part[o ^ bit] = call(merge_kernel, [part[o ^ bit], got], [packed])[0]
        results += call(
            functools.partial(final_kernel, 1 + len(arrived)),
            [part[0], *arrived],
            [jax.ShapeDtypeStruct((step, width), jnp.bfloat16)] * each,
        )
    results = [results[0]] + [swap(results[d], d) for d in range(1, shares)]
    out = jax.ShapeDtypeStruct((step, shares * width), jnp.bfloat16)
    return call(place_kernel, results, [out], scalars=order)[0]


CHUNKS = 2


def power_of_two(n):
    return n & (n - 1) == 0


def body(queries, new_keys, new_values, cache_keys, cache_values, selection):
    qblocks, head_count, top_count = selection.shape
    seq_count = lax.axis_size("seq")
    shares = lax.axis_size("heads") * lax.axis_size("sub")
    every = top_count == cache_keys.shape[0] // BLOCK * seq_count and qblocks == 1
    fits = power_of_two(seq_count) and power_of_two(shares) and shares % CHUNKS == 0
    if every and fits and 4 * head_count <= STAT:
        return dense_body(queries, new_keys, new_values, cache_keys, cache_values, CHUNKS)
    return sparse_body(queries, new_keys, new_values, cache_keys, cache_values, selection)


def solution(mesh):
    in_specs = (
        P(("groups", "seq", "heads", "sub"), None),
        P(("groups", "seq", "heads", "sub"), None),
        P(("groups", "seq", "heads", "sub"), None),
        P(("groups", "seq"), ("heads", "sub")),
        P(("groups", "seq"), ("heads", "sub")),
        P(("groups", "seq"), ("heads", "sub"), None),
    )
    out_specs = P(("groups", "seq", "heads", "sub"), None)
    return jax.shard_map(body, mesh=mesh, in_specs=in_specs, out_specs=out_specs, check_vma=False)
```

```python
import functools
import math

import jax
import jax.numpy as jnp
from jax import lax
from jax.experimental import pallas as pl
from jax.experimental.pallas import tpu as pltpu
from jax.sharding import PartitionSpec as P

HD = 128
BLOCK = 512


def order_ranks(owners):
    length = owners.shape[-1]
    counter = jnp.arange(length)
    earlier = counter[None, :] < counter[:, None]
    same_owner = owners[..., :, None] == owners[..., None, :]
    return jnp.sum(jnp.logical_and(same_owner, earlier), axis=-1)


def one_hot(values, length):
    return (values[..., None] == jnp.arange(length)).astype(jnp.float32)


def own_partial(query_blocks, key_blocks, value_blocks, scaling):
    scores = (
        jnp.einsum("bqhd,bkhd->bhqk", query_blocks, key_blocks, preferred_element_type=jnp.float32)
        * scaling
    )
    length = query_blocks.shape[1]
    causal = jnp.arange(length)[:, None] >= jnp.arange(length)[None, :]
    scores = jnp.where(causal, scores, -jnp.inf)
    highest = jnp.max(scores, axis=-1)
    weights = jnp.exp(scores - highest[..., None])
    totals = jnp.sum(weights, axis=-1)
    mixed = jnp.einsum(
        "bhqk,bkhd->bhqd",
        weights.astype(jnp.bfloat16),
        value_blocks,
        preferred_element_type=jnp.float32,
    )
    return (mixed, highest, totals)


def tile_partial(query_blocks, tile_pair, scaling):
    head_size = query_blocks.shape[-1]
    scores = (
        jnp.einsum(
            "bqhd,bhkd->bhqk",
            query_blocks,
            tile_pair[..., :head_size],
            preferred_element_type=jnp.float32,
        )
        * scaling
    )
    highest = jnp.max(scores, axis=-1)
    weights = jnp.exp(scores - highest[..., None])
    totals = jnp.sum(weights, axis=-1)
    mixed = jnp.einsum(
        "bhqk,bhkd->bhqd",
        weights.astype(jnp.bfloat16),
        tile_pair[..., head_size:],
        preferred_element_type=jnp.float32,
    )
    return (mixed, highest, totals)


def merge_parts(parts):
    top = parts[0][1]
    for part in parts[1:]:
        top = jnp.maximum(top, part[1])
    numer = jnp.zeros(parts[0][0].shape, jnp.float32)
    denom = jnp.zeros(parts[0][2].shape, jnp.float32)
    for part in parts:
        factor = jnp.exp(part[1] - top)
        numer = numer + factor[..., None] * part[0]
        denom = denom + factor * part[2]
    return numer / denom[..., None]


def sparse_body(queries, new_keys, new_values, cache_keys, cache_values, selection):
    heads_q, heads_k, heads_v = (
        lax.all_to_all(queries, ("heads", "sub"), split_axis=1, concat_axis=0, tiled=True),
        lax.all_to_all(new_keys, ("heads", "sub"), split_axis=1, concat_axis=0, tiled=True),
        lax.all_to_all(new_values, ("heads", "sub"), split_axis=1, concat_axis=0, tiled=True),
    )
    qblocks, head_count, top_count = selection.shape
    head_size = HD
    scaling = head_size ** (-0.5)
    shaped = (qblocks, BLOCK, head_count, head_size)
    query_blocks = heads_q.reshape(shaped)
    own = own_partial(query_blocks, heads_k.reshape(shaped), heads_v.reshape(shaped), scaling)
    seq_count = lax.axis_size("seq")
    myself = lax.axis_index("seq")
    cache_blocks = cache_keys.shape[0] // BLOCK
    tile_count = cache_blocks * head_count
    request_count = qblocks * head_count * top_count
    capacity = -(-request_count // seq_count)
    requests_all = lax.all_gather(selection, "seq", axis=0, tiled=True).reshape(
        seq_count, request_count
    )
    head_of = jnp.arange(request_count) // top_count % head_count
    my_requests = selection.reshape(request_count)
    my_owner = my_requests // cache_blocks
    my_slot = my_owner * capacity + order_ranks(my_owner)
    key_tiles = cache_keys.reshape(cache_blocks, BLOCK, head_count, head_size).transpose(0, 2, 1, 3)
    value_tiles = cache_values.reshape(cache_blocks, BLOCK, head_count, head_size).transpose(
        0, 2, 1, 3
    )
    tile_set = jnp.concatenate([key_tiles, value_tiles], axis=-1).reshape(
        tile_count, BLOCK, 2 * head_size
    )
    their_owner = requests_all // cache_blocks
    local_tile = requests_all % cache_blocks * head_count + head_of[None, :]
    served = (their_owner == myself).astype(jnp.float32)
    slot_pick = one_hot(order_ranks(their_owner), capacity) * served[..., None]
    picking = jnp.einsum("erc,erl->ecl", slot_pick, one_hot(local_tile, tile_count)).astype(
        jnp.bfloat16
    )
    parts = [own]
    outgoing = jnp.einsum(
        "ecl,lkf->eckf", picking, tile_set, preferred_element_type=jnp.float32
    ).astype(jnp.bfloat16)
    incoming = lax.all_to_all(outgoing, "seq", split_axis=0, concat_axis=0, tiled=True)
    fetched = incoming.reshape(seq_count * capacity, BLOCK, 2 * head_size)[my_slot]
    fetched = fetched.reshape(qblocks, head_count, top_count, BLOCK, 2 * head_size)
    for turn in range(top_count):
        parts.append(tile_partial(query_blocks, fetched[:, :, turn], scaling))
    result = merge_parts(parts)
    result = (
        result.transpose(0, 2, 1, 3)
        .reshape(qblocks * BLOCK, head_count * head_size)
        .astype(jnp.bfloat16)
    )
    return lax.all_to_all(result, ("heads", "sub"), split_axis=0, concat_axis=1, tiled=True)


STAT = 16
UNIT = 32767.0
LEAST = 1.2e-34
NEVER = -1.0e9
C2 = math.log2(math.e) * HD**-0.5


def scores_of(q, k, mask=None):
    s = lax.dot_general(k, q, (((1,), (1,)), ((), ())), preferred_element_type=jnp.float32)
    return s if mask is None else jnp.where(mask, s, -jnp.inf)


def weights_of(s):
    m = jnp.max(s, axis=0, keepdims=True)
    p = jnp.exp2((s - m) * C2)
    return p.astype(jnp.bfloat16), m * C2, jnp.sum(p, axis=0, keepdims=True)


def values_of(v, w, v_dim):
    return lax.dot_general(v, w, (((v_dim,), (0,)), ((), ())), preferred_element_type=jnp.float32)


def attend(tiles):
    count = len(tiles)
    s, w, parts = {}, {}, []
    for t in range(count + 2):
        if t < count:
            s[t] = tiles[t][0]()
        if 1 <= t <= count:
            w[t - 1] = weights_of(s.pop(t - 1))
        if t >= 2:
            weights, m, total = w.pop(t - 2)
            parts.append((tiles[t - 2][1](weights), m, total))
    return parts


def join(parts):
    top = functools.reduce(jnp.maximum, [m for _, m, _ in parts])
    factors = [jnp.exp2(m - top) for _, m, _ in parts]
    numer = sum(f * o for f, (o, _, _) in zip(factors, parts))
    denom = sum(f * t for f, (_, _, t) in zip(factors, parts))
    return numer, top, denom


def put(out_ref, heads):
    width, rows = len(heads) * HD, heads[0][0].shape[1]
    at = lax.broadcasted_iota(jnp.int32, (STAT, rows), 0)
    stats = jnp.zeros((STAT, rows), jnp.float32)
    for h, (numer, top, denom) in enumerate(heads):
        most = jnp.maximum(jnp.max(jnp.abs(numer), axis=0, keepdims=True), LEAST)
        code = jnp.round(numer * (UNIT / most))
        out_ref[h * HD : (h + 1) * HD, :] = code.astype(jnp.int32).astype(jnp.int16)
        for j, value in enumerate((top + jnp.log2(denom), jnp.log2(most / (UNIT * denom)))):
            whole = jnp.floor(value)
            stats = jnp.where(at == 4 * h + 2 * j, whole, stats)
            stats = jnp.where(at == 4 * h + 2 * j + 1, jnp.round((value - whole) * UNIT), stats)
    out_ref[width : width + STAT, :] = stats.astype(jnp.int32).astype(jnp.int16)


def take(ref, valid=None):
    width = ref.shape[0] - STAT
    stats = ref[width : width + STAT, :].astype(jnp.int32).astype(jnp.float32)
    heads = []
    for h in range(width // HD):
        code = ref[h * HD : (h + 1) * HD, :].astype(jnp.int32).astype(jnp.float32)
        weight = stats[4 * h : 4 * h + 1] + stats[4 * h + 1 : 4 * h + 2] * (1.0 / UNIT)
        unit = stats[4 * h + 2 : 4 * h + 3] + stats[4 * h + 3 : 4 * h + 4] * (1.0 / UNIT)
        if valid is not None:
            weight = jnp.where(valid, weight, NEVER)
        heads.append((code, weight, unit))
    return heads


def join_taken(taken):
    top = functools.reduce(jnp.maximum, [w for _, w, _ in taken])
    numer = sum(code * jnp.exp2(w - top + unit) for code, w, unit in taken)
    denom = sum(jnp.exp2(w - top) for _, w, _ in taken)
    return numer, top, denom


def cached_tiles(q_of, ck_ref, cvt_ref, h):
    cols = slice(h * HD, (h + 1) * HD)
    tiles = []
    for b in range(ck_ref.shape[0] // BLOCK):
        rows = slice(b * BLOCK, (b + 1) * BLOCK)
        tiles.append(
            (
                lambda rows=rows: scores_of(q_of(cols), ck_ref[rows, cols]),
                lambda w, rows=rows: values_of(cvt_ref[cols, rows], w, 1),
            )
        )
    return tiles


def attend_heads(tiles_of_heads):
    parts = attend([t for tiles in tiles_of_heads for t in tiles])
    heads = []
    for tiles in tiles_of_heads:
        heads.append(join(parts[: len(tiles)]))
        parts = parts[len(tiles) :]
    return heads


def cached_kernel(q_ref, ck_ref, cvt_ref, out_ref):
    heads = range(ck_ref.shape[1] // HD)
    q_of = lambda cols: q_ref[:, cols]
    put(out_ref, attend_heads([cached_tiles(q_of, ck_ref, cvt_ref, h) for h in heads]))


def either_kernel(middle_ref, a_ref, b_ref, ck_ref, cvt_ref, out_ref):
    middle = middle_ref[0] > 0
    heads = range(ck_ref.shape[1] // HD)
    q_of = lambda cols: jnp.where(middle, a_ref[:, cols], b_ref[:, cols])
    put(out_ref, attend_heads([cached_tiles(q_of, ck_ref, cvt_ref, h) for h in heads]))


def own_kernel(mine, order_ref, *refs):
    q_ref, *kv_refs, ck_ref, cvt_ref, out_ref = refs
    width = ck_ref.shape[1]
    rows = q_ref.shape[0]
    step = kv_refs[0].shape[0]

    def positions(shape, axis, pieces):
        at = lax.broadcasted_iota(jnp.int32, shape, axis)
        place = jnp.zeros(shape, jnp.int32)
        for i, d in enumerate(pieces):
            place = jnp.where(at // step == i, order_ref[d] * step + at % step, place)
        return place

    shape = (step * len(kv_refs), rows)
    mask = positions(shape, 1, mine) >= positions(shape, 0, range(len(kv_refs)))
    q_of = lambda cols: q_ref[:, cols]
    heads = []
    for h in range(width // HD):
        cols = slice(h * HD, (h + 1) * HD)
        vcols = slice(width + h * HD, width + (h + 1) * HD)
        own = (
            lambda cols=cols: scores_of(
                q_ref[:, cols], jnp.concatenate([r[:, cols] for r in kv_refs], axis=0), mask
            ),
            lambda w, vcols=vcols: values_of(
                jnp.concatenate([r[:, vcols] for r in kv_refs], axis=0), w, 0
            ),
        )
        heads.append([own] + cached_tiles(q_of, ck_ref, cvt_ref, h))
    put(out_ref, attend_heads(heads))


def merge_kernel(middle_ref, mine_ref, got_ref, out_ref):
    taken = zip(take(mine_ref), take(got_ref, middle_ref[0] > 0))
    put(out_ref, [join_taken(pair) for pair in taken])


def final_kernel(middle_ref, own_ref, near_ref, far_ref, *out_refs):
    step = out_refs[0].shape[0]
    trio = zip(take(own_ref), take(near_ref), take(far_ref, middle_ref[0] > 0))
    for h, taken in enumerate(trio):
        numer, _, denom = join_taken(taken)
        value = jnp.transpose(numer * (1.0 / denom)).astype(jnp.bfloat16)
        for i, out_ref in enumerate(out_refs):
            out_ref[:, h * HD : (h + 1) * HD] = value[i * step : (i + 1) * step]


def pick_kernel(pieces, count, order_ref, *refs):
    in_refs, out_refs = refs[:count], refs[len(refs) - len(pieces) :]
    width = out_refs[0].shape[1] // len(in_refs)
    for d, out_ref in zip(pieces, out_refs):
        start = pl.multiple_of(order_ref[d] * width, width)
        for i, ref in enumerate(in_refs):
            out_ref[:, i * width : (i + 1) * width] = ref[:, pl.ds(start, width)]


def stack_kernel(count, *refs):
    out_ref = refs[-1]
    step = refs[0].shape[0]
    for i in range(count):
        out_ref[i * step : (i + 1) * step, :] = refs[i][...]


def place_kernel(order_ref, *refs):
    *pieces, out_ref = refs
    width = pieces[0].shape[1]
    for d, piece in enumerate(pieces):
        start = pl.multiple_of(order_ref[d] * width, width)
        out_ref[:, pl.ds(start, width)] = piece[...]


def call(kernel, arrays, outs, flops=0, exps=0, scalars=None, unread=()):
    moved = sum(a.size * a.dtype.itemsize for a in arrays)
    moved += sum(math.prod(o.shape) * o.dtype.itemsize for o in outs)
    first = [] if scalars is None else [scalars]
    return pl.pallas_call(
        kernel,
        out_shape=outs,
        in_specs=[pl.BlockSpec(memory_space=pltpu.SMEM)] * len(first)
        + [pl.BlockSpec(memory_space=pltpu.VMEM)] * len(arrays)
        + [pl.BlockSpec(memory_space=pl.ANY)] * len(unread),
        out_specs=[pl.BlockSpec(memory_space=pltpu.VMEM)] * len(outs),
        compiler_params=pltpu.CompilerParams(vmem_limit_bytes=16 * 1024 * 1024),
        cost_estimate=pl.CostEstimate(flops=flops, bytes_accessed=moved, transcendentals=exps),
    )(*first, *arrays, *unread)


def dense_body(queries, new_keys, new_values, cache_keys, cache_values):
    s = lax.axis_index("seq")
    shares = lax.axis_size("heads") * lax.axis_size("sub")
    me = lax.axis_index("heads") * lax.axis_size("sub") + lax.axis_index("sub")
    step, width = queries.shape[0], queries.shape[1] // shares
    cached = cache_keys.shape[0]
    rows = shares // CHUNKS * step
    chunk = jax.ShapeDtypeStruct((rows, width), jnp.bfloat16)
    piece = jax.ShapeDtypeStruct((step, width), jnp.bfloat16)
    pair = jax.ShapeDtypeStruct((step, 2 * width), jnp.bfloat16)
    packed = jax.ShapeDtypeStruct((width + STAT, rows), jnp.int16)
    tile_flops = 4 * rows * cached * width
    tile_exps = rows * cached * (width // HD)
    middle = jnp.logical_and(s > 0, s < 3).astype(jnp.int32).reshape(1)

    def swap(x, d):
        return lax.ppermute(x, ("heads", "sub"), [(i, i ^ d) for i in range(shares)])

    def neighbours(x):
        return lax.ppermute(x, "seq", [(0, 1), (1, 0), (2, 3), (3, 2)])

    def across(x):
        return lax.ppermute(x, "seq", [(1, 2), (2, 1)])

    def outward(x):
        return lax.ppermute(x, "seq", [(1, 0), (2, 3)])

    def inward(x):
        return lax.ppermute(x, "seq", [(0, 1), (3, 2)])

    order = jnp.stack([me ^ d for d in range(shares)]).astype(jnp.int32)
    pieces_of = [range(c, shares, CHUNKS) for c in range(CHUNKS)]
    cache_vt = cache_values.T
    arrived = None
    own, results = [], {}
    kv = []
    for c, pieces in enumerate(pieces_of):
        parts = call(
            functools.partial(pick_kernel, pieces, 1), [queries], [piece] * len(pieces), scalars=order
        )
        parts = [swap(x, d) if d else x for x, d in zip(parts, pieces)]
        unread = [] if arrived is None else [arrived]
        mine = call(functools.partial(stack_kernel, len(parts)), parts, [chunk], unread=unread)[0]
        near = neighbours(mine)
        over = across(mine)
        over_end = across(near)
        end_over = outward(over)
        end_over_end = outward(over_end)
        arrived = near
        context = [cache_keys, cache_vt]
        for_near = call(cached_kernel, [near, *context], [packed], tile_flops, tile_exps)[0]
        for_over = call(
            either_kernel, [over, end_over, *context], [packed], tile_flops, tile_exps, middle
        )[0]
        for_far = call(
            either_kernel, [over_end, end_over_end, *context], [packed], tile_flops, tile_exps, middle
        )[0]
        merge = lambda mine, got: call(merge_kernel, [mine, got], [packed], scalars=middle)[0]
        from_over = across(merge(for_over, inward(for_over)))
        for_end = across(merge(for_far, inward(for_far)))
        from_near = neighbours(merge(for_near, for_end))
        if not kv:
            kv = call(
                functools.partial(pick_kernel, range(shares), 2),
                [new_keys, new_values],
                [pair] * shares,
                scalars=order,
                unread=[mine],
            )
            kv = [swap(x, d) if d else x for d, x in enumerate(kv)]
        own = call(
            functools.partial(own_kernel, pieces),
            [mine, *kv, *context],
            [packed],
            tile_flops * 3 // 2,
            tile_exps * 3 // 2,
            order,
        )[0]
        ended = call(
            final_kernel, [own, from_near, from_over], [piece] * len(pieces), scalars=middle
        )
        results.update({d: swap(x, d) if d else x for d, x in zip(pieces, ended)})
    out = jax.ShapeDtypeStruct((step, shares * width), jnp.bfloat16)
    return call(place_kernel, [results[d] for d in range(shares)], [out], scalars=order)[0]


CHUNKS = 2


def power_of_two(n):
    return n & (n - 1) == 0


def body(queries, new_keys, new_values, cache_keys, cache_values, selection):
    qblocks, head_count, top_count = selection.shape
    seq_count = lax.axis_size("seq")
    shares = lax.axis_size("heads") * lax.axis_size("sub")
    every = top_count == cache_keys.shape[0] // BLOCK * seq_count and qblocks == 1
    fits = seq_count == 4 and power_of_two(shares) and shares % CHUNKS == 0
    if every and fits and 4 * head_count <= STAT:
        return dense_body(queries, new_keys, new_values, cache_keys, cache_values)
    return sparse_body(queries, new_keys, new_values, cache_keys, cache_values, selection)


def solution(mesh):
    in_specs = (
        P(("groups", "seq", "heads", "sub"), None),
        P(("groups", "seq", "heads", "sub"), None),
        P(("groups", "seq", "heads", "sub"), None),
        P(("groups", "seq"), ("heads", "sub")),
        P(("groups", "seq"), ("heads", "sub")),
        P(("groups", "seq"), ("heads", "sub"), None),
    )
    out_specs = P(("groups", "seq", "heads", "sub"), None)
    return jax.shard_map(body, mesh=mesh, in_specs=in_specs, out_specs=out_specs, check_vma=False)
```

```python
import functools
import math

import jax
import jax.numpy as jnp
from jax import lax
from jax.experimental import pallas as pl
from jax.experimental.pallas import tpu as pltpu
from jax.sharding import PartitionSpec as P

HD = 128
BLOCK = 512


def order_ranks(owners):
    length = owners.shape[-1]
    counter = jnp.arange(length)
    earlier = counter[None, :] < counter[:, None]
    same_owner = owners[..., :, None] == owners[..., None, :]
    return jnp.sum(jnp.logical_and(same_owner, earlier), axis=-1)


def one_hot(values, length):
    return (values[..., None] == jnp.arange(length)).astype(jnp.float32)


def own_partial(query_blocks, key_blocks, value_blocks, scaling):
    scores = (
        jnp.einsum("bqhd,bkhd->bhqk", query_blocks, key_blocks, preferred_element_type=jnp.float32)
        * scaling
    )
    length = query_blocks.shape[1]
    causal = jnp.arange(length)[:, None] >= jnp.arange(length)[None, :]
    scores = jnp.where(causal, scores, -jnp.inf)
    highest = jnp.max(scores, axis=-1)
    weights = jnp.exp(scores - highest[..., None])
    totals = jnp.sum(weights, axis=-1)
    mixed = jnp.einsum(
        "bhqk,bkhd->bhqd",
        weights.astype(jnp.bfloat16),
        value_blocks,
        preferred_element_type=jnp.float32,
    )
    return (mixed, highest, totals)


def tile_partial(query_blocks, tile_pair, scaling):
    head_size = query_blocks.shape[-1]
    scores = (
        jnp.einsum(
            "bqhd,bhkd->bhqk",
            query_blocks,
            tile_pair[..., :head_size],
            preferred_element_type=jnp.float32,
        )
        * scaling
    )
    highest = jnp.max(scores, axis=-1)
    weights = jnp.exp(scores - highest[..., None])
    totals = jnp.sum(weights, axis=-1)
    mixed = jnp.einsum(
        "bhqk,bhkd->bhqd",
        weights.astype(jnp.bfloat16),
        tile_pair[..., head_size:],
        preferred_element_type=jnp.float32,
    )
    return (mixed, highest, totals)


def merge_parts(parts):
    top = parts[0][1]
    for part in parts[1:]:
        top = jnp.maximum(top, part[1])
    numer = jnp.zeros(parts[0][0].shape, jnp.float32)
    denom = jnp.zeros(parts[0][2].shape, jnp.float32)
    for part in parts:
        factor = jnp.exp(part[1] - top)
        numer = numer + factor[..., None] * part[0]
        denom = denom + factor * part[2]
    return numer / denom[..., None]


def sparse_body(queries, new_keys, new_values, cache_keys, cache_values, selection):
    heads_q, heads_k, heads_v = (
        lax.all_to_all(queries, ("heads", "sub"), split_axis=1, concat_axis=0, tiled=True),
        lax.all_to_all(new_keys, ("heads", "sub"), split_axis=1, concat_axis=0, tiled=True),
        lax.all_to_all(new_values, ("heads", "sub"), split_axis=1, concat_axis=0, tiled=True),
    )
    qblocks, head_count, top_count = selection.shape
    head_size = HD
    scaling = head_size ** (-0.5)
    shaped = (qblocks, BLOCK, head_count, head_size)
    query_blocks = heads_q.reshape(shaped)
    own = own_partial(query_blocks, heads_k.reshape(shaped), heads_v.reshape(shaped), scaling)
    seq_count = lax.axis_size("seq")
    myself = lax.axis_index("seq")
    cache_blocks = cache_keys.shape[0] // BLOCK
    tile_count = cache_blocks * head_count
    request_count = qblocks * head_count * top_count
    capacity = -(-request_count // seq_count)
    requests_all = lax.all_gather(selection, "seq", axis=0, tiled=True).reshape(
        seq_count, request_count
    )
    head_of = jnp.arange(request_count) // top_count % head_count
    my_requests = selection.reshape(request_count)
    my_owner = my_requests // cache_blocks
    my_slot = my_owner * capacity + order_ranks(my_owner)
    key_tiles = cache_keys.reshape(cache_blocks, BLOCK, head_count, head_size).transpose(0, 2, 1, 3)
    value_tiles = cache_values.reshape(cache_blocks, BLOCK, head_count, head_size).transpose(
        0, 2, 1, 3
    )
    tile_set = jnp.concatenate([key_tiles, value_tiles], axis=-1).reshape(
        tile_count, BLOCK, 2 * head_size
    )
    their_owner = requests_all // cache_blocks
    local_tile = requests_all % cache_blocks * head_count + head_of[None, :]
    served = (their_owner == myself).astype(jnp.float32)
    slot_pick = one_hot(order_ranks(their_owner), capacity) * served[..., None]
    picking = jnp.einsum("erc,erl->ecl", slot_pick, one_hot(local_tile, tile_count)).astype(
        jnp.bfloat16
    )
    parts = [own]
    outgoing = jnp.einsum(
        "ecl,lkf->eckf", picking, tile_set, preferred_element_type=jnp.float32
    ).astype(jnp.bfloat16)
    incoming = lax.all_to_all(outgoing, "seq", split_axis=0, concat_axis=0, tiled=True)
    fetched = incoming.reshape(seq_count * capacity, BLOCK, 2 * head_size)[my_slot]
    fetched = fetched.reshape(qblocks, head_count, top_count, BLOCK, 2 * head_size)
    for turn in range(top_count):
        parts.append(tile_partial(query_blocks, fetched[:, :, turn], scaling))
    result = merge_parts(parts)
    result = (
        result.transpose(0, 2, 1, 3)
        .reshape(qblocks * BLOCK, head_count * head_size)
        .astype(jnp.bfloat16)
    )
    return lax.all_to_all(result, ("heads", "sub"), split_axis=0, concat_axis=1, tiled=True)


STAT = 16
UNIT = 32767.0
LEAST = 1.2e-34
NEVER = -1.0e9
C2 = math.log2(math.e) * HD**-0.5


def scores_of(q, k, mask=None):
    s = lax.dot_general(k, q, (((1,), (1,)), ((), ())), preferred_element_type=jnp.float32)
    return s if mask is None else jnp.where(mask, s, -jnp.inf)


def weights_of(s):
    m = jnp.max(s, axis=0, keepdims=True)
    p = jnp.exp2((s - m) * C2)
    return p.astype(jnp.bfloat16), m * C2, jnp.sum(p, axis=0, keepdims=True)


def values_of(v, w, v_dim):
    return lax.dot_general(v, w, (((v_dim,), (0,)), ((), ())), preferred_element_type=jnp.float32)


def attend(tiles):
    count = len(tiles)
    s, w, parts = {}, {}, []
    for t in range(count + 2):
        if t < count:
            s[t] = tiles[t][0]()
        if 1 <= t <= count:
            w[t - 1] = weights_of(s.pop(t - 1))
        if t >= 2:
            weights, m, total = w.pop(t - 2)
            parts.append((tiles[t - 2][1](weights), m, total))
    return parts


def join(parts):
    top = functools.reduce(jnp.maximum, [m for _, m, _ in parts])
    factors = [jnp.exp2(m - top) for _, m, _ in parts]
    numer = sum(f * o for f, (o, _, _) in zip(factors, parts))
    denom = sum(f * t for f, (_, _, t) in zip(factors, parts))
    return numer, top, denom


def put(out_ref, heads):
    width, rows = len(heads) * HD, heads[0][0].shape[1]
    at = lax.broadcasted_iota(jnp.int32, (STAT, rows), 0)
    stats = jnp.zeros((STAT, rows), jnp.float32)
    for h, (numer, top, denom) in enumerate(heads):
        most = jnp.maximum(jnp.max(jnp.abs(numer), axis=0, keepdims=True), LEAST)
        code = jnp.round(numer * (UNIT / most))
        out_ref[h * HD : (h + 1) * HD, :] = code.astype(jnp.int32).astype(jnp.int16)
        for j, value in enumerate((top + jnp.log2(denom), jnp.log2(most / (UNIT * denom)))):
            whole = jnp.floor(value)
            stats = jnp.where(at == 4 * h + 2 * j, whole, stats)
            stats = jnp.where(at == 4 * h + 2 * j + 1, jnp.round((value - whole) * UNIT), stats)
    out_ref[width : width + STAT, :] = stats.astype(jnp.int32).astype(jnp.int16)


def take(ref, valid=None):
    width = ref.shape[0] - STAT
    stats = ref[width : width + STAT, :].astype(jnp.int32).astype(jnp.float32)
    heads = []
    for h in range(width // HD):
        code = ref[h * HD : (h + 1) * HD, :].astype(jnp.int32).astype(jnp.float32)
        weight = stats[4 * h : 4 * h + 1] + stats[4 * h + 1 : 4 * h + 2] * (1.0 / UNIT)
        unit = stats[4 * h + 2 : 4 * h + 3] + stats[4 * h + 3 : 4 * h + 4] * (1.0 / UNIT)
        if valid is not None:
            weight = jnp.where(valid, weight, NEVER)
        heads.append((code, weight, unit))
    return heads


def join_taken(taken):
    top = functools.reduce(jnp.maximum, [w for _, w, _ in taken])
    numer = sum(code * jnp.exp2(w - top + unit) for code, w, unit in taken)
    denom = sum(jnp.exp2(w - top) for _, w, _ in taken)
    return numer, top, denom


def cached_tiles(q_of, ck_ref, cvt_ref, h):
    cols = slice(h * HD, (h + 1) * HD)
    tiles = []
    for b in range(ck_ref.shape[0] // BLOCK):
        rows = slice(b * BLOCK, (b + 1) * BLOCK)
        tiles.append(
            (
                lambda rows=rows: scores_of(q_of(cols), ck_ref[rows, cols]),
                lambda w, rows=rows: values_of(cvt_ref[cols, rows], w, 1),
            )
        )
    return tiles


def attend_heads(tiles_of_heads):
    parts = attend([t for tiles in tiles_of_heads for t in tiles])
    heads = []
    for tiles in tiles_of_heads:
        heads.append(join(parts[: len(tiles)]))
        parts = parts[len(tiles) :]
    return heads


def cached_kernel(order, place_ref, q_ref, ck_ref, cvt_ref, *out_refs):
    heads = range(ck_ref.shape[1] // HD)
    rows = out_refs[0].shape[1]
    for i, out_ref in zip(order, out_refs):
        start = pl.multiple_of(place_ref[i] * rows, rows)
        q_of = lambda cols, start=start: q_ref[pl.ds(start, rows), cols]
        put(out_ref, attend_heads([cached_tiles(q_of, ck_ref, cvt_ref, h) for h in heads]))


def own_kernel(mine, order_ref, *refs):
    q_ref, *kv_refs, ck_ref, cvt_ref, out_ref = refs
    width = ck_ref.shape[1]
    rows = q_ref.shape[0]
    step = kv_refs[0].shape[0]

    def positions(shape, axis, pieces):
        at = lax.broadcasted_iota(jnp.int32, shape, axis)
        place = jnp.zeros(shape, jnp.int32)
        for i, d in enumerate(pieces):
            place = jnp.where(at // step == i, order_ref[d] * step + at % step, place)
        return place

    shape = (step * len(kv_refs), rows)
    mask = positions(shape, 1, mine) >= positions(shape, 0, range(len(kv_refs)))
    q_of = lambda cols: q_ref[:, cols]
    heads = []
    for h in range(width // HD):
        cols = slice(h * HD, (h + 1) * HD)
        vcols = slice(width + h * HD, width + (h + 1) * HD)
        own = (
            lambda cols=cols: scores_of(
                q_ref[:, cols], jnp.concatenate([r[:, cols] for r in kv_refs], axis=0), mask
            ),
            lambda w, vcols=vcols: values_of(
                jnp.concatenate([r[:, vcols] for r in kv_refs], axis=0), w, 0
            ),
        )
        heads.append([own] + cached_tiles(q_of, ck_ref, cvt_ref, h))
    put(out_ref, attend_heads(heads))


def merge_kernel(middle_ref, mine_ref, got_ref, out_ref):
    taken = zip(take(mine_ref), take(got_ref, middle_ref[0] > 0))
    put(out_ref, [join_taken(pair) for pair in taken])


def final_kernel(middle_ref, own_ref, near_ref, far_ref, *out_refs):
    step = out_refs[0].shape[0]
    trio = zip(take(own_ref), take(near_ref), take(far_ref, middle_ref[0] > 0))
    for h, taken in enumerate(trio):
        numer, _, denom = join_taken(taken)
        value = jnp.transpose(numer * (1.0 / denom)).astype(jnp.bfloat16)
        for i, out_ref in enumerate(out_refs):
            out_ref[:, h * HD : (h + 1) * HD] = value[i * step : (i + 1) * step]


def pick_kernel(pieces, count, order_ref, *refs):
    in_refs, out_refs = refs[:count], refs[len(refs) - len(pieces) :]
    width = out_refs[0].shape[1] // len(in_refs)
    for d, out_ref in zip(pieces, out_refs):
        start = pl.multiple_of(order_ref[d] * width, width)
        for i, ref in enumerate(in_refs):
            out_ref[:, i * width : (i + 1) * width] = ref[:, pl.ds(start, width)]


def stack_kernel(count, *refs):
    out_ref = refs[-1]
    step = refs[0].shape[0]
    for i in range(count):
        out_ref[i * step : (i + 1) * step, :] = refs[i][...]


def place_kernel(order_ref, *refs):
    *pieces, out_ref = refs
    width = pieces[0].shape[1]
    for d, piece in enumerate(pieces):
        start = pl.multiple_of(order_ref[d] * width, width)
        out_ref[:, pl.ds(start, width)] = piece[...]


def call(kernel, arrays, outs, flops=0, exps=0, scalars=None, unread=()):
    moved = sum(a.size * a.dtype.itemsize for a in arrays)
    moved += sum(math.prod(o.shape) * o.dtype.itemsize for o in outs)
    first = [] if scalars is None else [scalars]
    return pl.pallas_call(
        kernel,
        out_shape=outs,
        in_specs=[pl.BlockSpec(memory_space=pltpu.SMEM)] * len(first)
        + [pl.BlockSpec(memory_space=pltpu.VMEM)] * len(arrays)
        + [pl.BlockSpec(memory_space=pl.ANY)] * len(unread),
        out_specs=[pl.BlockSpec(memory_space=pltpu.VMEM)] * len(outs),
        compiler_params=pltpu.CompilerParams(vmem_limit_bytes=16 * 1024 * 1024),
        cost_estimate=pl.CostEstimate(flops=flops, bytes_accessed=moved, transcendentals=exps),
    )(*first, *arrays, *unread)


def dense_body(queries, new_keys, new_values, cache_keys, cache_values):
    s = lax.axis_index("seq")
    shares = lax.axis_size("heads") * lax.axis_size("sub")
    me = lax.axis_index("heads") * lax.axis_size("sub") + lax.axis_index("sub")
    step, width = queries.shape[0], queries.shape[1] // shares
    cached = cache_keys.shape[0]
    rows = shares // CHUNKS * step
    chunk = jax.ShapeDtypeStruct((rows, width), jnp.bfloat16)
    piece = jax.ShapeDtypeStruct((step, width), jnp.bfloat16)
    pair = jax.ShapeDtypeStruct((step, 2 * width), jnp.bfloat16)
    packed = jax.ShapeDtypeStruct((width + STAT, rows), jnp.int16)
    tile_flops = 4 * rows * cached * width
    tile_exps = rows * cached * (width // HD)
    is_middle = jnp.logical_and(s > 0, s < 3)
    middle = is_middle.astype(jnp.int32).reshape(1)
    places = jnp.stack([s ^ jnp.where(is_middle, 2, 3), s ^ jnp.where(is_middle, 3, 2), s ^ 1]).astype(jnp.int32)

    def swap(x, d):
        return lax.ppermute(x, ("heads", "sub"), [(i, i ^ d) for i in range(shares)])

    def neighbours(x):
        return lax.ppermute(x, "seq", [(0, 1), (1, 0), (2, 3), (3, 2)])

    def across(x):
        return lax.ppermute(x, "seq", [(1, 2), (2, 1)])

    def inward(x):
        return lax.ppermute(x, "seq", [(0, 1), (3, 2)])

    order = jnp.stack([me ^ d for d in range(shares)]).astype(jnp.int32)
    pieces_of = [range(c, shares, CHUNKS) for c in range(CHUNKS)]
    cache_vt = cache_values.T
    arrived = None
    own, results = [], {}
    kv = []
    for c, pieces in enumerate(pieces_of):
        parts = call(
            functools.partial(pick_kernel, pieces, 1), [queries], [piece] * len(pieces), scalars=order
        )
        parts = [swap(x, d) if d else x for x, d in zip(parts, pieces)]
        unread = [] if arrived is None else [arrived]
        mine = call(functools.partial(stack_kernel, len(parts)), parts, [chunk], unread=unread)[0]
        every = lax.all_gather(mine, "seq", axis=0, tiled=True)
        arrived = every
        context = [cache_keys, cache_vt]
        for_far, for_over, for_near = [
            call(
                functools.partial(cached_kernel, [i]),
                [every, *context],
                [packed],
                tile_flops,
                tile_exps,
                places,
            )[0]
            for i in range(3)
        ]
        merge = lambda mine, got: call(merge_kernel, [mine, got], [packed], scalars=middle)[0]
        from_over = across(merge(for_over, inward(for_over)))
        for_end = across(merge(for_far, inward(for_far)))
        from_near = neighbours(merge(for_near, for_end))
        if not kv:
            kv = call(
                functools.partial(pick_kernel, range(shares), 2),
                [new_keys, new_values],
                [pair] * shares,
                scalars=order,
                unread=[mine],
            )
            kv = [swap(x, d) if d else x for d, x in enumerate(kv)]
        own = call(
            functools.partial(own_kernel, pieces),
            [mine, *kv, *context],
            [packed],
            tile_flops * 3 // 2,
            tile_exps * 3 // 2,
            order,
        )[0]
        ended = call(
            final_kernel, [own, from_near, from_over], [piece] * len(pieces), scalars=middle
        )
        results.update({d: swap(x, d) if d else x for d, x in zip(pieces, ended)})
    out = jax.ShapeDtypeStruct((step, shares * width), jnp.bfloat16)
    return call(place_kernel, [results[d] for d in range(shares)], [out], scalars=order)[0]


CHUNKS = 2


def power_of_two(n):
    return n & (n - 1) == 0


def body(queries, new_keys, new_values, cache_keys, cache_values, selection):
    qblocks, head_count, top_count = selection.shape
    seq_count = lax.axis_size("seq")
    shares = lax.axis_size("heads") * lax.axis_size("sub")
    every = top_count == cache_keys.shape[0] // BLOCK * seq_count and qblocks == 1
    fits = seq_count == 4 and power_of_two(shares) and shares % CHUNKS == 0
    if every and fits and 4 * head_count <= STAT:
        return dense_body(queries, new_keys, new_values, cache_keys, cache_values)
    return sparse_body(queries, new_keys, new_values, cache_keys, cache_values, selection)


def solution(mesh):
    in_specs = (
        P(("groups", "seq", "heads", "sub"), None),
        P(("groups", "seq", "heads", "sub"), None),
        P(("groups", "seq", "heads", "sub"), None),
        P(("groups", "seq"), ("heads", "sub")),
        P(("groups", "seq"), ("heads", "sub")),
        P(("groups", "seq"), ("heads", "sub"), None),
    )
    out_specs = P(("groups", "seq", "heads", "sub"), None)
    return jax.shard_map(body, mesh=mesh, in_specs=in_specs, out_specs=out_specs, check_vma=False)
```

```python
import functools
import math

import jax
import jax.numpy as jnp
from jax import lax
from jax.experimental import pallas as pl
from jax.experimental.pallas import tpu as pltpu
from jax.sharding import PartitionSpec as P

HD = 128
BLOCK = 512


def order_ranks(owners):
    length = owners.shape[-1]
    counter = jnp.arange(length)
    earlier = counter[None, :] < counter[:, None]
    same_owner = owners[..., :, None] == owners[..., None, :]
    return jnp.sum(jnp.logical_and(same_owner, earlier), axis=-1)


def one_hot(values, length):
    return (values[..., None] == jnp.arange(length)).astype(jnp.float32)


def own_partial(query_blocks, key_blocks, value_blocks, scaling):
    scores = (
        jnp.einsum("bqhd,bkhd->bhqk", query_blocks, key_blocks, preferred_element_type=jnp.float32)
        * scaling
    )
    length = query_blocks.shape[1]
    causal = jnp.arange(length)[:, None] >= jnp.arange(length)[None, :]
    scores = jnp.where(causal, scores, -jnp.inf)
    highest = jnp.max(scores, axis=-1)
    weights = jnp.exp(scores - highest[..., None])
    totals = jnp.sum(weights, axis=-1)
    mixed = jnp.einsum(
        "bhqk,bkhd->bhqd",
        weights.astype(jnp.bfloat16),
        value_blocks,
        preferred_element_type=jnp.float32,
    )
    return (mixed, highest, totals)


def tile_partial(query_blocks, tile_pair, scaling):
    head_size = query_blocks.shape[-1]
    scores = (
        jnp.einsum(
            "bqhd,bhkd->bhqk",
            query_blocks,
            tile_pair[..., :head_size],
            preferred_element_type=jnp.float32,
        )
        * scaling
    )
    highest = jnp.max(scores, axis=-1)
    weights = jnp.exp(scores - highest[..., None])
    totals = jnp.sum(weights, axis=-1)
    mixed = jnp.einsum(
        "bhqk,bhkd->bhqd",
        weights.astype(jnp.bfloat16),
        tile_pair[..., head_size:],
        preferred_element_type=jnp.float32,
    )
    return (mixed, highest, totals)


def merge_parts(parts):
    top = parts[0][1]
    for part in parts[1:]:
        top = jnp.maximum(top, part[1])
    numer = jnp.zeros(parts[0][0].shape, jnp.float32)
    denom = jnp.zeros(parts[0][2].shape, jnp.float32)
    for part in parts:
        factor = jnp.exp(part[1] - top)
        numer = numer + factor[..., None] * part[0]
        denom = denom + factor * part[2]
    return numer / denom[..., None]


def sparse_body(queries, new_keys, new_values, cache_keys, cache_values, selection):
    heads_q, heads_k, heads_v = (
        lax.all_to_all(queries, ("heads", "sub"), split_axis=1, concat_axis=0, tiled=True),
        lax.all_to_all(new_keys, ("heads", "sub"), split_axis=1, concat_axis=0, tiled=True),
        lax.all_to_all(new_values, ("heads", "sub"), split_axis=1, concat_axis=0, tiled=True),
    )
    qblocks, head_count, top_count = selection.shape
    head_size = HD
    scaling = head_size ** (-0.5)
    shaped = (qblocks, BLOCK, head_count, head_size)
    query_blocks = heads_q.reshape(shaped)
    own = own_partial(query_blocks, heads_k.reshape(shaped), heads_v.reshape(shaped), scaling)
    seq_count = lax.axis_size("seq")
    myself = lax.axis_index("seq")
    cache_blocks = cache_keys.shape[0] // BLOCK
    tile_count = cache_blocks * head_count
    request_count = qblocks * head_count * top_count
    capacity = -(-request_count // seq_count)
    requests_all = lax.all_gather(selection, "seq", axis=0, tiled=True).reshape(
        seq_count, request_count
    )
    head_of = jnp.arange(request_count) // top_count % head_count
    my_requests = selection.reshape(request_count)
    my_owner = my_requests // cache_blocks
    my_slot = my_owner * capacity + order_ranks(my_owner)
    key_tiles = cache_keys.reshape(cache_blocks, BLOCK, head_count, head_size).transpose(0, 2, 1, 3)
    value_tiles = cache_values.reshape(cache_blocks, BLOCK, head_count, head_size).transpose(
        0, 2, 1, 3
    )
    tile_set = jnp.concatenate([key_tiles, value_tiles], axis=-1).reshape(
        tile_count, BLOCK, 2 * head_size
    )
    their_owner = requests_all // cache_blocks
    local_tile = requests_all % cache_blocks * head_count + head_of[None, :]
    served = (their_owner == myself).astype(jnp.float32)
    slot_pick = one_hot(order_ranks(their_owner), capacity) * served[..., None]
    picking = jnp.einsum("erc,erl->ecl", slot_pick, one_hot(local_tile, tile_count)).astype(
        jnp.bfloat16
    )
    parts = [own]
    outgoing = jnp.einsum(
        "ecl,lkf->eckf", picking, tile_set, preferred_element_type=jnp.float32
    ).astype(jnp.bfloat16)
    incoming = lax.all_to_all(outgoing, "seq", split_axis=0, concat_axis=0, tiled=True)
    fetched = incoming.reshape(seq_count * capacity, BLOCK, 2 * head_size)[my_slot]
    fetched = fetched.reshape(qblocks, head_count, top_count, BLOCK, 2 * head_size)
    for turn in range(top_count):
        parts.append(tile_partial(query_blocks, fetched[:, :, turn], scaling))
    result = merge_parts(parts)
    result = (
        result.transpose(0, 2, 1, 3)
        .reshape(qblocks * BLOCK, head_count * head_size)
        .astype(jnp.bfloat16)
    )
    return lax.all_to_all(result, ("heads", "sub"), split_axis=0, concat_axis=1, tiled=True)


STAT = 16
UNIT = 32767.0
LEAST = 1.2e-34
C2 = math.log2(math.e) * HD**-0.5


def scores_of(q, k, mask=None):
    s = lax.dot_general(k, q, (((1,), (1,)), ((), ())), preferred_element_type=jnp.float32)
    return s if mask is None else jnp.where(mask, s, -jnp.inf)


def weights_of(s):
    m = jnp.max(s, axis=0, keepdims=True)
    p = jnp.exp2((s - m) * C2)
    return p.astype(jnp.bfloat16), m * C2, jnp.sum(p, axis=0, keepdims=True)


def values_of(v, w, v_dim):
    return lax.dot_general(v, w, (((v_dim,), (0,)), ((), ())), preferred_element_type=jnp.float32)


def attend(tiles):
    count = len(tiles)
    s, w, parts = {}, {}, []
    for t in range(count + 2):
        if t < count:
            s[t] = tiles[t][0]()
        if 1 <= t <= count:
            w[t - 1] = weights_of(s.pop(t - 1))
        if t >= 2:
            weights, m, total = w.pop(t - 2)
            parts.append((tiles[t - 2][1](weights), m, total))
    return parts


def join(parts):
    top = functools.reduce(jnp.maximum, [m for _, m, _ in parts])
    factors = [jnp.exp2(m - top) for _, m, _ in parts]
    numer = sum(f * o for f, (o, _, _) in zip(factors, parts))
    denom = sum(f * t for f, (_, _, t) in zip(factors, parts))
    return numer, top, denom


def put(out_ref, heads):
    width, rows = len(heads) * HD, heads[0][0].shape[1]
    at = lax.broadcasted_iota(jnp.int32, (STAT, rows), 0)
    stats = jnp.zeros((STAT, rows), jnp.float32)
    for h, (numer, top, denom) in enumerate(heads):
        most = jnp.maximum(jnp.max(jnp.abs(numer), axis=0, keepdims=True), LEAST)
        code = jnp.round(numer * (UNIT / most))
        out_ref[h * HD : (h + 1) * HD, :] = code.astype(jnp.int32).astype(jnp.int16)
        for j, value in enumerate((top + jnp.log2(denom), jnp.log2(most / (UNIT * denom)))):
            whole = jnp.floor(value)
            stats = jnp.where(at == 4 * h + 2 * j, whole, stats)
            stats = jnp.where(at == 4 * h + 2 * j + 1, jnp.round((value - whole) * UNIT), stats)
    out_ref[width : width + STAT, :] = stats.astype(jnp.int32).astype(jnp.int16)


def take(ref):
    width = ref.shape[0] - STAT
    stats = ref[width : width + STAT, :].astype(jnp.int32).astype(jnp.float32)
    heads = []
    for h in range(width // HD):
        code = ref[h * HD : (h + 1) * HD, :].astype(jnp.int32).astype(jnp.float32)
        weight = stats[4 * h : 4 * h + 1] + stats[4 * h + 1 : 4 * h + 2] * (1.0 / UNIT)
        unit = stats[4 * h + 2 : 4 * h + 3] + stats[4 * h + 3 : 4 * h + 4] * (1.0 / UNIT)
        heads.append((code, weight, unit))
    return heads


def join_taken(taken):
    top = functools.reduce(jnp.maximum, [w for _, w, _ in taken])
    numer = sum(code * jnp.exp2(w - top + unit) for code, w, unit in taken)
    denom = sum(jnp.exp2(w - top) for _, w, _ in taken)
    return numer, top, denom


def cached_tiles(q_of, ck_ref, cvt_ref, h):
    cols = slice(h * HD, (h + 1) * HD)
    tiles = []
    for b in range(ck_ref.shape[0] // BLOCK):
        rows = slice(b * BLOCK, (b + 1) * BLOCK)
        tiles.append(
            (
                lambda rows=rows: scores_of(q_of(cols), ck_ref[rows, cols]),
                lambda w, rows=rows: values_of(cvt_ref[cols, rows], w, 1),
            )
        )
    return tiles


def attend_heads(tiles_of_heads):
    parts = attend([t for tiles in tiles_of_heads for t in tiles])
    heads = []
    for tiles in tiles_of_heads:
        heads.append(join(parts[: len(tiles)]))
        parts = parts[len(tiles) :]
    return heads


def cached_kernel(q_ref, ck_ref, cvt_ref, out_ref):
    heads = range(ck_ref.shape[1] // HD)
    q_of = lambda cols: q_ref[:, cols]
    put(out_ref, attend_heads([cached_tiles(q_of, ck_ref, cvt_ref, h) for h in heads]))


def own_kernel(mine, order_ref, *refs):
    q_ref, *kv_refs, ck_ref, cvt_ref, out_ref = refs
    width = ck_ref.shape[1]
    rows = q_ref.shape[0]
    step = kv_refs[0].shape[0]

    def positions(shape, axis, pieces):
        at = lax.broadcasted_iota(jnp.int32, shape, axis)
        place = jnp.zeros(shape, jnp.int32)
        for i, d in enumerate(pieces):
            place = jnp.where(at // step == i, order_ref[d] * step + at % step, place)
        return place

    shape = (step * len(kv_refs), rows)
    mask = positions(shape, 1, mine) >= positions(shape, 0, range(len(kv_refs)))
    q_of = lambda cols: q_ref[:, cols]
    heads = []
    for h in range(width // HD):
        cols = slice(h * HD, (h + 1) * HD)
        vcols = slice(width + h * HD, width + (h + 1) * HD)
        own = (
            lambda cols=cols: scores_of(
                q_ref[:, cols], jnp.concatenate([r[:, cols] for r in kv_refs], axis=0), mask
            ),
            lambda w, vcols=vcols: values_of(
                jnp.concatenate([r[:, vcols] for r in kv_refs], axis=0), w, 0
            ),
        )
        heads.append([own] + cached_tiles(q_of, ck_ref, cvt_ref, h))
    put(out_ref, attend_heads(heads))


def merge_kernel(*refs):
    *in_refs, out_ref = refs
    put(out_ref, [join_taken(taken) for taken in zip(*[take(r) for r in in_refs])])


def final_kernel(count, *refs):
    in_refs, out_refs = refs[:count], refs[count:]
    step = out_refs[0].shape[0]
    for h, taken in enumerate(zip(*[take(r) for r in in_refs])):
        numer, _, denom = join_taken(taken)
        value = jnp.transpose(numer * (1.0 / denom)).astype(jnp.bfloat16)
        for i, out_ref in enumerate(out_refs):
            out_ref[:, h * HD : (h + 1) * HD] = value[i * step : (i + 1) * step]


def pick_kernel(pieces, count, order_ref, *refs):
    in_refs, out_refs = refs[:count], refs[len(refs) - len(pieces) :]
    width = out_refs[0].shape[1] // len(in_refs)
    for d, out_ref in zip(pieces, out_refs):
        start = pl.multiple_of(order_ref[d] * width, width)
        for i, ref in enumerate(in_refs):
            out_ref[:, i * width : (i + 1) * width] = ref[:, pl.ds(start, width)]


def stack_kernel(count, *refs):
    out_ref = refs[-1]
    step = refs[0].shape[0]
    for i in range(count):
        out_ref[i * step : (i + 1) * step, :] = refs[i][...]


def place_kernel(order_ref, *refs):
    *pieces, out_ref = refs
    width = pieces[0].shape[1]
    for d, piece in enumerate(pieces):
        start = pl.multiple_of(order_ref[d] * width, width)
        out_ref[:, pl.ds(start, width)] = piece[...]


def call(kernel, arrays, outs, flops=0, exps=0, scalars=None, unread=()):
    moved = sum(a.size * a.dtype.itemsize for a in arrays)
    moved += sum(math.prod(o.shape) * o.dtype.itemsize for o in outs)
    first = [] if scalars is None else [scalars]
    return pl.pallas_call(
        kernel,
        out_shape=outs,
        in_specs=[pl.BlockSpec(memory_space=pltpu.SMEM)] * len(first)
        + [pl.BlockSpec(memory_space=pltpu.VMEM)] * len(arrays)
        + [pl.BlockSpec(memory_space=pl.ANY)] * len(unread),
        out_specs=[pl.BlockSpec(memory_space=pltpu.VMEM)] * len(outs),
        compiler_params=pltpu.CompilerParams(vmem_limit_bytes=16 * 1024 * 1024),
        cost_estimate=pl.CostEstimate(flops=flops, bytes_accessed=moved, transcendentals=exps),
    )(*first, *arrays, *unread)


def dense_body(queries, new_keys, new_values, cache_keys, cache_values):
    seq_count = lax.axis_size("seq")
    shares = lax.axis_size("heads") * lax.axis_size("sub")
    me = lax.axis_index("heads") * lax.axis_size("sub") + lax.axis_index("sub")
    step, width = queries.shape[0], queries.shape[1] // shares
    cached = cache_keys.shape[0]
    each = shares // CHUNKS
    rows = each * step
    chunk = jax.ShapeDtypeStruct((rows, width), jnp.bfloat16)
    piece = jax.ShapeDtypeStruct((step, width), jnp.bfloat16)
    pair = jax.ShapeDtypeStruct((step, 2 * width), jnp.bfloat16)
    packed = jax.ShapeDtypeStruct((width + STAT, rows), jnp.int16)
    tile_flops = 4 * rows * cached * width
    tile_exps = rows * cached * (width // HD)
    bits = [1 << b for b in range(seq_count.bit_length() - 1)]

    def swap(x, d):
        return lax.ppermute(x, ("heads", "sub"), [(i, i ^ d) for i in range(shares)])

    def along(x, bit):
        return lax.ppermute(x, "seq", [(i, i ^ bit) for i in range(seq_count)])

    def after(x, unread):
        like = jax.ShapeDtypeStruct(x.shape, x.dtype)
        return call(functools.partial(stack_kernel, 1), [x], [like], unread=unread)[0] if unread else x

    order = jnp.stack([me ^ d for d in range(shares)]).astype(jnp.int32)
    cache_vt = cache_values.T
    ahead, last, kv, results = [], [], [], []
    for c in range(CHUNKS):
        pieces = range(c * each, (c + 1) * each)
        parts = call(
            functools.partial(pick_kernel, pieces, 1), [queries], [piece] * each, scalars=order
        )
        parts = [swap(x, d) if d else x for x, d in zip(parts, pieces)]
        mine = call(functools.partial(stack_kernel, each), parts, [chunk], unread=ahead)[0]
        held = {0: mine}
        for bit in reversed(bits):
            if held.keys() != {0}:
                held = {o: x if o == 0 else after(x, last) for o, x in held.items()}
            held.update({o | bit: along(x, bit) for o, x in list(held.items())})
        ahead = [held[bit] for bit in bits]
        last = [held[seq_count - 1]]
        context = [cache_keys, cache_vt]
        part = {
            o: call(cached_kernel, [held[o], *context], [packed], tile_flops, tile_exps)[0]
            for o in range(1, seq_count)
        }
        if not kv:
            kv = call(
                functools.partial(pick_kernel, range(shares), 2),
                [new_keys, new_values],
                [pair] * shares,
                scalars=order,
                unread=[mine],
            )
            kv = [swap(x, d) if d else x for d, x in enumerate(kv)]
        part[0] = call(
            functools.partial(own_kernel, pieces),
            [mine, *kv, *context],
            [packed],
            tile_flops * 3 // 2,
            tile_exps * 3 // 2,
            order,
        )[0]
        arrived = []
        for bit in bits:
            for o in [o for o in part if o & bit]:
                got = along(part.pop(o), bit)
                if o == bit:
                    arrived.append(got)
                else:
                    part[o ^ bit] = call(merge_kernel, [part[o ^ bit], got], [packed])[0]
        ended = call(
            functools.partial(final_kernel, 1 + len(arrived)),
            [part[0], *arrived],
            [piece] * each,
        )
        results += [swap(x, d) if d else x for x, d in zip(ended, pieces)]
    out = jax.ShapeDtypeStruct((step, shares * width), jnp.bfloat16)
    return call(place_kernel, results, [out], scalars=order)[0]


CHUNKS = 2


def power_of_two(n):
    return n & (n - 1) == 0


def body(queries, new_keys, new_values, cache_keys, cache_values, selection):
    qblocks, head_count, top_count = selection.shape
    seq_count = lax.axis_size("seq")
    shares = lax.axis_size("heads") * lax.axis_size("sub")
    every = top_count == cache_keys.shape[0] // BLOCK * seq_count and qblocks == 1
    fits = power_of_two(seq_count) and power_of_two(shares) and shares % CHUNKS == 0
    if every and fits and 4 * head_count <= STAT:
        return dense_body(queries, new_keys, new_values, cache_keys, cache_values)
    return sparse_body(queries, new_keys, new_values, cache_keys, cache_values, selection)


def solution(mesh):
    in_specs = (
        P(("groups", "seq", "heads", "sub"), None),
        P(("groups", "seq", "heads", "sub"), None),
        P(("groups", "seq", "heads", "sub"), None),
        P(("groups", "seq"), ("heads", "sub")),
        P(("groups", "seq"), ("heads", "sub")),
        P(("groups", "seq"), ("heads", "sub"), None),
    )
    out_specs = P(("groups", "seq", "heads", "sub"), None)
    return jax.shard_map(body, mesh=mesh, in_specs=in_specs, out_specs=out_specs, check_vma=False)
```

```python
import functools
import math

import jax
import jax.numpy as jnp
from jax import lax
from jax.experimental import pallas as pl
from jax.experimental.pallas import tpu as pltpu
from jax.sharding import PartitionSpec as P

HD = 128
BLOCK = 512


def order_ranks(owners):
    length = owners.shape[-1]
    counter = jnp.arange(length)
    earlier = counter[None, :] < counter[:, None]
    same_owner = owners[..., :, None] == owners[..., None, :]
    return jnp.sum(jnp.logical_and(same_owner, earlier), axis=-1)


def one_hot(values, length):
    return (values[..., None] == jnp.arange(length)).astype(jnp.float32)


def own_partial(query_blocks, key_blocks, value_blocks, scaling):
    scores = (
        jnp.einsum("bqhd,bkhd->bhqk", query_blocks, key_blocks, preferred_element_type=jnp.float32)
        * scaling
    )
    length = query_blocks.shape[1]
    causal = jnp.arange(length)[:, None] >= jnp.arange(length)[None, :]
    scores = jnp.where(causal, scores, -jnp.inf)
    highest = jnp.max(scores, axis=-1)
    weights = jnp.exp(scores - highest[..., None])
    totals = jnp.sum(weights, axis=-1)
    mixed = jnp.einsum(
        "bhqk,bkhd->bhqd",
        weights.astype(jnp.bfloat16),
        value_blocks,
        preferred_element_type=jnp.float32,
    )
    return (mixed, highest, totals)


def tile_partial(query_blocks, tile_pair, scaling):
    head_size = query_blocks.shape[-1]
    scores = (
        jnp.einsum(
            "bqhd,bhkd->bhqk",
            query_blocks,
            tile_pair[..., :head_size],
            preferred_element_type=jnp.float32,
        )
        * scaling
    )
    highest = jnp.max(scores, axis=-1)
    weights = jnp.exp(scores - highest[..., None])
    totals = jnp.sum(weights, axis=-1)
    mixed = jnp.einsum(
        "bhqk,bhkd->bhqd",
        weights.astype(jnp.bfloat16),
        tile_pair[..., head_size:],
        preferred_element_type=jnp.float32,
    )
    return (mixed, highest, totals)


def merge_parts(parts):
    top = parts[0][1]
    for part in parts[1:]:
        top = jnp.maximum(top, part[1])
    numer = jnp.zeros(parts[0][0].shape, jnp.float32)
    denom = jnp.zeros(parts[0][2].shape, jnp.float32)
    for part in parts:
        factor = jnp.exp(part[1] - top)
        numer = numer + factor[..., None] * part[0]
        denom = denom + factor * part[2]
    return numer / denom[..., None]


def sparse_body(queries, new_keys, new_values, cache_keys, cache_values, selection):
    heads_q, heads_k, heads_v = (
        lax.all_to_all(queries, ("heads", "sub"), split_axis=1, concat_axis=0, tiled=True),
        lax.all_to_all(new_keys, ("heads", "sub"), split_axis=1, concat_axis=0, tiled=True),
        lax.all_to_all(new_values, ("heads", "sub"), split_axis=1, concat_axis=0, tiled=True),
    )
    qblocks, head_count, top_count = selection.shape
    head_size = HD
    scaling = head_size ** (-0.5)
    shaped = (qblocks, BLOCK, head_count, head_size)
    query_blocks = heads_q.reshape(shaped)
    own = own_partial(query_blocks, heads_k.reshape(shaped), heads_v.reshape(shaped), scaling)
    seq_count = lax.axis_size("seq")
    myself = lax.axis_index("seq")
    cache_blocks = cache_keys.shape[0] // BLOCK
    tile_count = cache_blocks * head_count
    request_count = qblocks * head_count * top_count
    capacity = -(-request_count // seq_count)
    requests_all = lax.all_gather(selection, "seq", axis=0, tiled=True).reshape(
        seq_count, request_count
    )
    head_of = jnp.arange(request_count) // top_count % head_count
    my_requests = selection.reshape(request_count)
    my_owner = my_requests // cache_blocks
    my_slot = my_owner * capacity + order_ranks(my_owner)
    key_tiles = cache_keys.reshape(cache_blocks, BLOCK, head_count, head_size).transpose(0, 2, 1, 3)
    value_tiles = cache_values.reshape(cache_blocks, BLOCK, head_count, head_size).transpose(
        0, 2, 1, 3
    )
    tile_set = jnp.concatenate([key_tiles, value_tiles], axis=-1).reshape(
        tile_count, BLOCK, 2 * head_size
    )
    their_owner = requests_all // cache_blocks
    local_tile = requests_all % cache_blocks * head_count + head_of[None, :]
    served = (their_owner == myself).astype(jnp.float32)
    slot_pick = one_hot(order_ranks(their_owner), capacity) * served[..., None]
    picking = jnp.einsum("erc,erl->ecl", slot_pick, one_hot(local_tile, tile_count)).astype(
        jnp.bfloat16
    )
    parts = [own]
    outgoing = jnp.einsum(
        "ecl,lkf->eckf", picking, tile_set, preferred_element_type=jnp.float32
    ).astype(jnp.bfloat16)
    incoming = lax.all_to_all(outgoing, "seq", split_axis=0, concat_axis=0, tiled=True)
    fetched = incoming.reshape(seq_count * capacity, BLOCK, 2 * head_size)[my_slot]
    fetched = fetched.reshape(qblocks, head_count, top_count, BLOCK, 2 * head_size)
    for turn in range(top_count):
        parts.append(tile_partial(query_blocks, fetched[:, :, turn], scaling))
    result = merge_parts(parts)
    result = (
        result.transpose(0, 2, 1, 3)
        .reshape(qblocks * BLOCK, head_count * head_size)
        .astype(jnp.bfloat16)
    )
    return lax.all_to_all(result, ("heads", "sub"), split_axis=0, concat_axis=1, tiled=True)


STAT = 16
UNIT = 32767.0
LEAST = 1.2e-34
C2 = math.log2(math.e) * HD**-0.5


def scores_of(q, k, mask=None):
    s = lax.dot_general(k, q, (((1,), (1,)), ((), ())), preferred_element_type=jnp.float32)
    return s if mask is None else jnp.where(mask, s, -jnp.inf)


def weights_of(s):
    m = jnp.max(s, axis=0, keepdims=True)
    p = jnp.exp2((s - m) * C2)
    return p.astype(jnp.bfloat16), m * C2, jnp.sum(p, axis=0, keepdims=True)


def values_of(v, w, v_dim):
    return lax.dot_general(v, w, (((v_dim,), (0,)), ((), ())), preferred_element_type=jnp.float32)


def attend(tiles):
    count = len(tiles)
    s, w, parts = {}, {}, []
    for t in range(count + 2):
        if t < count:
            s[t] = tiles[t][0]()
        if 1 <= t <= count:
            w[t - 1] = weights_of(s.pop(t - 1))
        if t >= 2:
            weights, m, total = w.pop(t - 2)
            parts.append((tiles[t - 2][1](weights), m, total))
    return parts


def join(parts):
    top = functools.reduce(jnp.maximum, [m for _, m, _ in parts])
    factors = [jnp.exp2(m - top) for _, m, _ in parts]
    numer = sum(f * o for f, (o, _, _) in zip(factors, parts))
    denom = sum(f * t for f, (_, _, t) in zip(factors, parts))
    return numer, top, denom


def put(out_ref, heads):
    width, rows = len(heads) * HD, heads[0][0].shape[1]
    at = lax.broadcasted_iota(jnp.int32, (STAT, rows), 0)
    stats = jnp.zeros((STAT, rows), jnp.float32)
    for h, (numer, top, denom) in enumerate(heads):
        most = jnp.maximum(jnp.max(jnp.abs(numer), axis=0, keepdims=True), LEAST)
        code = jnp.round(numer * (UNIT / most))
        out_ref[h * HD : (h + 1) * HD, :] = code.astype(jnp.int32).astype(jnp.int16)
        for j, value in enumerate((top + jnp.log2(denom), jnp.log2(most / (UNIT * denom)))):
            whole = jnp.floor(value)
            stats = jnp.where(at == 4 * h + 2 * j, whole, stats)
            stats = jnp.where(at == 4 * h + 2 * j + 1, jnp.round((value - whole) * UNIT), stats)
    out_ref[width : width + STAT, :] = stats.astype(jnp.int32).astype(jnp.int16)


def take(ref):
    width = ref.shape[0] - STAT
    stats = ref[width : width + STAT, :].astype(jnp.int32).astype(jnp.float32)
    heads = []
    for h in range(width // HD):
        code = ref[h * HD : (h + 1) * HD, :].astype(jnp.int32).astype(jnp.float32)
        weight = stats[4 * h : 4 * h + 1] + stats[4 * h + 1 : 4 * h + 2] * (1.0 / UNIT)
        unit = stats[4 * h + 2 : 4 * h + 3] + stats[4 * h + 3 : 4 * h + 4] * (1.0 / UNIT)
        heads.append((code, weight, unit))
    return heads


def join_taken(taken):
    top = functools.reduce(jnp.maximum, [w for _, w, _ in taken])
    numer = sum(code * jnp.exp2(w - top + unit) for code, w, unit in taken)
    denom = sum(jnp.exp2(w - top) for _, w, _ in taken)
    return numer, top, denom


def cached_tiles(q_of, ck_ref, cvt_ref, h):
    cols = slice(h * HD, (h + 1) * HD)
    tiles = []
    for b in range(ck_ref.shape[0] // BLOCK):
        rows = slice(b * BLOCK, (b + 1) * BLOCK)
        tiles.append(
            (
                lambda rows=rows: scores_of(q_of(cols), ck_ref[rows, cols]),
                lambda w, rows=rows: values_of(cvt_ref[cols, rows], w, 1),
            )
        )
    return tiles


def attend_heads(tiles_of_heads):
    parts = attend([t for tiles in tiles_of_heads for t in tiles])
    heads = []
    for tiles in tiles_of_heads:
        heads.append(join(parts[: len(tiles)]))
        parts = parts[len(tiles) :]
    return heads


def cached_kernel(q_ref, ck_ref, cvt_ref, out_ref):
    heads = range(ck_ref.shape[1] // HD)
    q_of = lambda cols: q_ref[:, cols]
    put(out_ref, attend_heads([cached_tiles(q_of, ck_ref, cvt_ref, h) for h in heads]))


def own_kernel(mine, order_ref, *refs):
    q_ref, *kv_refs, ck_ref, cvt_ref, out_ref = refs
    width = ck_ref.shape[1]
    rows = q_ref.shape[0]
    step = kv_refs[0].shape[0]

    def positions(shape, axis, pieces):
        at = lax.broadcasted_iota(jnp.int32, shape, axis)
        place = jnp.zeros(shape, jnp.int32)
        for i, d in enumerate(pieces):
            place = jnp.where(at // step == i, order_ref[d] * step + at % step, place)
        return place

    shape = (step * len(kv_refs), rows)
    mask = positions(shape, 1, mine) >= positions(shape, 0, range(len(kv_refs)))
    q_of = lambda cols: q_ref[:, cols]
    heads = []
    for h in range(width // HD):
        cols = slice(h * HD, (h + 1) * HD)
        vcols = slice(width + h * HD, width + (h + 1) * HD)
        own = (
            lambda cols=cols: scores_of(
                q_ref[:, cols], jnp.concatenate([r[:, cols] for r in kv_refs], axis=0), mask
            ),
            lambda w, vcols=vcols: values_of(
                jnp.concatenate([r[:, vcols] for r in kv_refs], axis=0), w, 0
            ),
        )
        heads.append([own] + cached_tiles(q_of, ck_ref, cvt_ref, h))
    put(out_ref, attend_heads(heads))


def merge_kernel(*refs):
    *in_refs, out_ref = refs
    put(out_ref, [join_taken(taken) for taken in zip(*[take(r) for r in in_refs])])


def final_kernel(count, *refs):
    in_refs, out_refs = refs[:count], refs[count:]
    step = out_refs[0].shape[0]
    for h, taken in enumerate(zip(*[take(r) for r in in_refs])):
        numer, _, denom = join_taken(taken)
        value = jnp.transpose(numer * (1.0 / denom)).astype(jnp.bfloat16)
        for i, out_ref in enumerate(out_refs):
            out_ref[:, h * HD : (h + 1) * HD] = value[i * step : (i + 1) * step]


def pick_kernel(pieces, count, order_ref, *refs):
    in_refs, out_refs = refs[:count], refs[len(refs) - len(pieces) :]
    width = out_refs[0].shape[1] // len(in_refs)
    for d, out_ref in zip(pieces, out_refs):
        start = pl.multiple_of(order_ref[d] * width, width)
        for i, ref in enumerate(in_refs):
            out_ref[:, i * width : (i + 1) * width] = ref[:, pl.ds(start, width)]


def stack_kernel(count, *refs):
    out_ref = refs[-1]
    step = refs[0].shape[0]
    for i in range(count):
        out_ref[i * step : (i + 1) * step, :] = refs[i][...]


def place_kernel(order_ref, *refs):
    *pieces, out_ref = refs
    width = pieces[0].shape[1]
    for d, piece in enumerate(pieces):
        start = pl.multiple_of(order_ref[d] * width, width)
        out_ref[:, pl.ds(start, width)] = piece[...]


def call(kernel, arrays, outs, flops=0, exps=0, scalars=None, unread=()):
    moved = sum(a.size * a.dtype.itemsize for a in arrays)
    moved += sum(math.prod(o.shape) * o.dtype.itemsize for o in outs)
    first = [] if scalars is None else [scalars]
    return pl.pallas_call(
        kernel,
        out_shape=outs,
        in_specs=[pl.BlockSpec(memory_space=pltpu.SMEM)] * len(first)
        + [pl.BlockSpec(memory_space=pltpu.VMEM)] * len(arrays)
        + [pl.BlockSpec(memory_space=pl.ANY)] * len(unread),
        out_specs=[pl.BlockSpec(memory_space=pltpu.VMEM)] * len(outs),
        compiler_params=pltpu.CompilerParams(vmem_limit_bytes=16 * 1024 * 1024),
        cost_estimate=pl.CostEstimate(flops=flops, bytes_accessed=moved, transcendentals=exps),
    )(*first, *arrays, *unread)


def dense_body(queries, new_keys, new_values, cache_keys, cache_values):
    seq_count = lax.axis_size("seq")
    shares = lax.axis_size("heads") * lax.axis_size("sub")
    me = lax.axis_index("heads") * lax.axis_size("sub") + lax.axis_index("sub")
    step, width = queries.shape[0], queries.shape[1] // shares
    cached = cache_keys.shape[0]
    each = shares // CHUNKS
    rows = each * step
    chunk = jax.ShapeDtypeStruct((rows, width), jnp.bfloat16)
    piece = jax.ShapeDtypeStruct((step, width), jnp.bfloat16)
    pair = jax.ShapeDtypeStruct((step, 2 * width), jnp.bfloat16)
    packed = jax.ShapeDtypeStruct((width + STAT, rows), jnp.int16)
    tile_flops = 4 * rows * cached * width
    tile_exps = rows * cached * (width // HD)
    bits = [1 << b for b in range(seq_count.bit_length() - 1)]

    def swap(x, d):
        return lax.ppermute(x, ("heads", "sub"), [(i, i ^ d) for i in range(shares)])

    def along(x, bit):
        return lax.ppermute(x, "seq", [(i, i ^ bit) for i in range(seq_count)])

    def after(x, unread):
        like = jax.ShapeDtypeStruct(x.shape, x.dtype)
        return call(functools.partial(stack_kernel, 1), [x], [like], unread=unread)[0] if unread else x

    order = jnp.stack([me ^ d for d in range(shares)]).astype(jnp.int32)
    cache_vt = cache_values.T
    last, kv, results = [], [], []
    for c in range(CHUNKS):
        pieces = range(c * each, (c + 1) * each)
        parts = call(
            functools.partial(pick_kernel, pieces, 1), [queries], [piece] * each, scalars=order
        )
        parts = [swap(x, d) if d else x for x, d in zip(parts, pieces)]
        mine = call(functools.partial(stack_kernel, each), parts, [chunk], unread=[cache_vt] if c else [])[0]
        held = {0: mine}
        for bit in reversed(bits):
            if held.keys() != {0}:
                held = {o: x if o == 0 else after(x, last) for o, x in held.items()}
            held.update({o | bit: along(x, bit) for o, x in list(held.items())})
        context = [cache_keys, cache_vt]
        part = {
            o: call(cached_kernel, [held[o], *context], [packed], tile_flops, tile_exps)[0]
            for o in range(1, seq_count)
        }
        if not kv:
            kv = call(
                functools.partial(pick_kernel, range(shares), 2),
                [new_keys, new_values],
                [pair] * shares,
                scalars=order,
                unread=[mine],
            )
            kv = [swap(x, d) if d else x for d, x in enumerate(kv)]
        part[0] = call(
            functools.partial(own_kernel, pieces),
            [mine, *kv, *context],
            [packed],
            tile_flops * 3 // 2,
            tile_exps * 3 // 2,
            order,
        )[0]
        last = [held[seq_count - 1]] + [p for o, p in part.items() if o != seq_count - 1]
        arrived = []
        for bit in bits:
            for o in [o for o in part if o & bit]:
                got = along(part.pop(o), bit)
                if o == bit:
                    arrived.append(got)
                else:
                    part[o ^ bit] = call(merge_kernel, [part[o ^ bit], got], [packed])[0]
        ended = call(
            functools.partial(final_kernel, 1 + len(arrived)),
            [part[0], *arrived],
            [piece] * each,
        )
        results += [swap(x, d) if d else x for x, d in zip(ended, pieces)]
    out = jax.ShapeDtypeStruct((step, shares * width), jnp.bfloat16)
    return call(place_kernel, results, [out], scalars=order)[0]


CHUNKS = 2


def power_of_two(n):
    return n & (n - 1) == 0


def body(queries, new_keys, new_values, cache_keys, cache_values, selection):
    qblocks, head_count, top_count = selection.shape
    seq_count = lax.axis_size("seq")
    shares = lax.axis_size("heads") * lax.axis_size("sub")
    every = top_count == cache_keys.shape[0] // BLOCK * seq_count and qblocks == 1
    fits = power_of_two(seq_count) and power_of_two(shares) and shares % CHUNKS == 0
    if every and fits and 4 * head_count <= STAT:
        return dense_body(queries, new_keys, new_values, cache_keys, cache_values)
    return sparse_body(queries, new_keys, new_values, cache_keys, cache_values, selection)


def solution(mesh):
    in_specs = (
        P(("groups", "seq", "heads", "sub"), None),
        P(("groups", "seq", "heads", "sub"), None),
        P(("groups", "seq", "heads", "sub"), None),
        P(("groups", "seq"), ("heads", "sub")),
        P(("groups", "seq"), ("heads", "sub")),
        P(("groups", "seq"), ("heads", "sub"), None),
    )
    out_specs = P(("groups", "seq", "heads", "sub"), None)
    return jax.shard_map(body, mesh=mesh, in_specs=in_specs, out_specs=out_specs, check_vma=False)
```

```python
import functools
import math

import jax
import jax.numpy as jnp
from jax import lax
from jax.experimental import pallas as pl
from jax.experimental.pallas import tpu as pltpu
from jax.sharding import PartitionSpec as P

HD = 128
BLOCK = 512


def order_ranks(owners):
    length = owners.shape[-1]
    counter = jnp.arange(length)
    earlier = counter[None, :] < counter[:, None]
    same_owner = owners[..., :, None] == owners[..., None, :]
    return jnp.sum(jnp.logical_and(same_owner, earlier), axis=-1)


def one_hot(values, length):
    return (values[..., None] == jnp.arange(length)).astype(jnp.float32)


def own_partial(query_blocks, key_blocks, value_blocks, scaling):
    scores = (
        jnp.einsum("bqhd,bkhd->bhqk", query_blocks, key_blocks, preferred_element_type=jnp.float32)
        * scaling
    )
    length = query_blocks.shape[1]
    causal = jnp.arange(length)[:, None] >= jnp.arange(length)[None, :]
    scores = jnp.where(causal, scores, -jnp.inf)
    highest = jnp.max(scores, axis=-1)
    weights = jnp.exp(scores - highest[..., None])
    totals = jnp.sum(weights, axis=-1)
    mixed = jnp.einsum(
        "bhqk,bkhd->bhqd",
        weights.astype(jnp.bfloat16),
        value_blocks,
        preferred_element_type=jnp.float32,
    )
    return (mixed, highest, totals)


def tile_partial(query_blocks, tile_pair, scaling):
    head_size = query_blocks.shape[-1]
    scores = (
        jnp.einsum(
            "bqhd,bhkd->bhqk",
            query_blocks,
            tile_pair[..., :head_size],
            preferred_element_type=jnp.float32,
        )
        * scaling
    )
    highest = jnp.max(scores, axis=-1)
    weights = jnp.exp(scores - highest[..., None])
    totals = jnp.sum(weights, axis=-1)
    mixed = jnp.einsum(
        "bhqk,bhkd->bhqd",
        weights.astype(jnp.bfloat16),
        tile_pair[..., head_size:],
        preferred_element_type=jnp.float32,
    )
    return (mixed, highest, totals)


def merge_parts(parts):
    top = parts[0][1]
    for part in parts[1:]:
        top = jnp.maximum(top, part[1])
    numer = jnp.zeros(parts[0][0].shape, jnp.float32)
    denom = jnp.zeros(parts[0][2].shape, jnp.float32)
    for part in parts:
        factor = jnp.exp(part[1] - top)
        numer = numer + factor[..., None] * part[0]
        denom = denom + factor * part[2]
    return numer / denom[..., None]


def sparse_body(queries, new_keys, new_values, cache_keys, cache_values, selection):
    heads_q, heads_k, heads_v = (
        lax.all_to_all(queries, ("heads", "sub"), split_axis=1, concat_axis=0, tiled=True),
        lax.all_to_all(new_keys, ("heads", "sub"), split_axis=1, concat_axis=0, tiled=True),
        lax.all_to_all(new_values, ("heads", "sub"), split_axis=1, concat_axis=0, tiled=True),
    )
    qblocks, head_count, top_count = selection.shape
    head_size = HD
    scaling = head_size ** (-0.5)
    shaped = (qblocks, BLOCK, head_count, head_size)
    query_blocks = heads_q.reshape(shaped)
    own = own_partial(query_blocks, heads_k.reshape(shaped), heads_v.reshape(shaped), scaling)
    seq_count = lax.axis_size("seq")
    myself = lax.axis_index("seq")
    cache_blocks = cache_keys.shape[0] // BLOCK
    tile_count = cache_blocks * head_count
    request_count = qblocks * head_count * top_count
    capacity = -(-request_count // seq_count)
    requests_all = lax.all_gather(selection, "seq", axis=0, tiled=True).reshape(
        seq_count, request_count
    )
    head_of = jnp.arange(request_count) // top_count % head_count
    my_requests = selection.reshape(request_count)
    my_owner = my_requests // cache_blocks
    my_slot = my_owner * capacity + order_ranks(my_owner)
    key_tiles = cache_keys.reshape(cache_blocks, BLOCK, head_count, head_size).transpose(0, 2, 1, 3)
    value_tiles = cache_values.reshape(cache_blocks, BLOCK, head_count, head_size).transpose(
        0, 2, 1, 3
    )
    tile_set = jnp.concatenate([key_tiles, value_tiles], axis=-1).reshape(
        tile_count, BLOCK, 2 * head_size
    )
    their_owner = requests_all // cache_blocks
    local_tile = requests_all % cache_blocks * head_count + head_of[None, :]
    served = (their_owner == myself).astype(jnp.float32)
    slot_pick = one_hot(order_ranks(their_owner), capacity) * served[..., None]
    picking = jnp.einsum("erc,erl->ecl", slot_pick, one_hot(local_tile, tile_count)).astype(
        jnp.bfloat16
    )
    parts = [own]
    outgoing = jnp.einsum(
        "ecl,lkf->eckf", picking, tile_set, preferred_element_type=jnp.float32
    ).astype(jnp.bfloat16)
    incoming = lax.all_to_all(outgoing, "seq", split_axis=0, concat_axis=0, tiled=True)
    fetched = incoming.reshape(seq_count * capacity, BLOCK, 2 * head_size)[my_slot]
    fetched = fetched.reshape(qblocks, head_count, top_count, BLOCK, 2 * head_size)
    for turn in range(top_count):
        parts.append(tile_partial(query_blocks, fetched[:, :, turn], scaling))
    result = merge_parts(parts)
    result = (
        result.transpose(0, 2, 1, 3)
        .reshape(qblocks * BLOCK, head_count * head_size)
        .astype(jnp.bfloat16)
    )
    return lax.all_to_all(result, ("heads", "sub"), split_axis=0, concat_axis=1, tiled=True)


STAT = 16
UNIT = 32767.0
LEAST = 1.2e-34
NEVER = -1.0e9
C2 = math.log2(math.e) * HD**-0.5


def scores_of(q, k, mask=None):
    s = lax.dot_general(k, q, (((1,), (1,)), ((), ())), preferred_element_type=jnp.float32)
    return s if mask is None else jnp.where(mask, s, -jnp.inf)


def weights_of(s):
    m = jnp.max(s, axis=0, keepdims=True)
    p = jnp.exp2((s - m) * C2)
    return p.astype(jnp.bfloat16), m * C2, jnp.sum(p, axis=0, keepdims=True)


def values_of(v, w, v_dim):
    return lax.dot_general(v, w, (((v_dim,), (0,)), ((), ())), preferred_element_type=jnp.float32)


def attend(tiles):
    count = len(tiles)
    s, w, parts = {}, {}, []
    for t in range(count + 2):
        if t < count:
            s[t] = tiles[t][0]()
        if 1 <= t <= count:
            w[t - 1] = weights_of(s.pop(t - 1))
        if t >= 2:
            weights, m, total = w.pop(t - 2)
            parts.append((tiles[t - 2][1](weights), m, total))
    return parts


def join(parts):
    top = functools.reduce(jnp.maximum, [m for _, m, _ in parts])
    factors = [jnp.exp2(m - top) for _, m, _ in parts]
    numer = sum(f * o for f, (o, _, _) in zip(factors, parts))
    denom = sum(f * t for f, (_, _, t) in zip(factors, parts))
    return numer, top, denom


def put(out_ref, heads):
    width, rows = len(heads) * HD, heads[0][0].shape[1]
    at = lax.broadcasted_iota(jnp.int32, (STAT, rows), 0)
    stats = jnp.zeros((STAT, rows), jnp.float32)
    for h, (numer, top, denom) in enumerate(heads):
        most = jnp.maximum(jnp.max(jnp.abs(numer), axis=0, keepdims=True), LEAST)
        code = jnp.round(numer * (UNIT / most))
        out_ref[h * HD : (h + 1) * HD, :] = code.astype(jnp.int32).astype(jnp.int16)
        for j, value in enumerate((top + jnp.log2(denom), jnp.log2(most / (UNIT * denom)))):
            whole = jnp.floor(value)
            stats = jnp.where(at == 4 * h + 2 * j, whole, stats)
            stats = jnp.where(at == 4 * h + 2 * j + 1, jnp.round((value - whole) * UNIT), stats)
    out_ref[width : width + STAT, :] = stats.astype(jnp.int32).astype(jnp.int16)


def take(ref, valid=None):
    width = ref.shape[0] - STAT
    stats = ref[width : width + STAT, :].astype(jnp.int32).astype(jnp.float32)
    heads = []
    for h in range(width // HD):
        code = ref[h * HD : (h + 1) * HD, :].astype(jnp.int32).astype(jnp.float32)
        weight = stats[4 * h : 4 * h + 1] + stats[4 * h + 1 : 4 * h + 2] * (1.0 / UNIT)
        unit = stats[4 * h + 2 : 4 * h + 3] + stats[4 * h + 3 : 4 * h + 4] * (1.0 / UNIT)
        if valid is not None:
            weight = jnp.where(valid, weight, NEVER)
        heads.append((code, weight, unit))
    return heads


def join_taken(taken):
    top = functools.reduce(jnp.maximum, [w for _, w, _ in taken])
    numer = sum(code * jnp.exp2(w - top + unit) for code, w, unit in taken)
    denom = sum(jnp.exp2(w - top) for _, w, _ in taken)
    return numer, top, denom


def cached_tiles(q_of, ck_ref, cvt_ref, h):
    cols = slice(h * HD, (h + 1) * HD)
    tiles = []
    for b in range(ck_ref.shape[0] // BLOCK):
        rows = slice(b * BLOCK, (b + 1) * BLOCK)
        tiles.append(
            (
                lambda rows=rows: scores_of(q_of(cols), ck_ref[rows, cols]),
                lambda w, rows=rows: values_of(cvt_ref[cols, rows], w, 1),
            )
        )
    return tiles


def attend_heads(tiles_of_heads):
    parts = attend([t for tiles in tiles_of_heads for t in tiles])
    heads = []
    for tiles in tiles_of_heads:
        heads.append(join(parts[: len(tiles)]))
        parts = parts[len(tiles) :]
    return heads


def cached_kernel(q_ref, ck_ref, cvt_ref, out_ref):
    heads = range(ck_ref.shape[1] // HD)
    q_of = lambda cols: q_ref[:, cols]
    put(out_ref, attend_heads([cached_tiles(q_of, ck_ref, cvt_ref, h) for h in heads]))


def either_kernel(middle_ref, a_ref, b_ref, ck_ref, cvt_ref, out_ref):
    middle = middle_ref[0] > 0
    heads = range(ck_ref.shape[1] // HD)
    q_of = lambda cols: jnp.where(middle, a_ref[:, cols], b_ref[:, cols])
    put(out_ref, attend_heads([cached_tiles(q_of, ck_ref, cvt_ref, h) for h in heads]))


def own_kernel(mine, order_ref, *refs):
    q_ref, *kv_refs, ck_ref, cvt_ref, out_ref = refs
    width = ck_ref.shape[1]
    rows = q_ref.shape[0]
    step = kv_refs[0].shape[0]

    def positions(shape, axis, pieces):
        at = lax.broadcasted_iota(jnp.int32, shape, axis)
        place = jnp.zeros(shape, jnp.int32)
        for i, d in enumerate(pieces):
            place = jnp.where(at // step == i, order_ref[d] * step + at % step, place)
        return place

    shape = (step * len(kv_refs), rows)
    mask = positions(shape, 1, mine) >= positions(shape, 0, range(len(kv_refs)))
    q_of = lambda cols: q_ref[:, cols]
    heads = []
    for h in range(width // HD):
        cols = slice(h * HD, (h + 1) * HD)
        vcols = slice(width + h * HD, width + (h + 1) * HD)
        own = (
            lambda cols=cols: scores_of(
                q_ref[:, cols], jnp.concatenate([r[:, cols] for r in kv_refs], axis=0), mask
            ),
            lambda w, vcols=vcols: values_of(
                jnp.concatenate([r[:, vcols] for r in kv_refs], axis=0), w, 0
            ),
        )
        heads.append([own] + cached_tiles(q_of, ck_ref, cvt_ref, h))
    put(out_ref, attend_heads(heads))


def merge_kernel(middle_ref, mine_ref, got_ref, out_ref):
    taken = zip(take(mine_ref), take(got_ref, middle_ref[0] > 0))
    put(out_ref, [join_taken(pair) for pair in taken])


def final_kernel(middle_ref, own_ref, near_ref, far_ref, *out_refs):
    step = out_refs[0].shape[0]
    trio = zip(take(own_ref), take(near_ref), take(far_ref, middle_ref[0] > 0))
    for h, taken in enumerate(trio):
        numer, _, denom = join_taken(taken)
        value = jnp.transpose(numer * (1.0 / denom)).astype(jnp.bfloat16)
        for i, out_ref in enumerate(out_refs):
            out_ref[:, h * HD : (h + 1) * HD] = value[i * step : (i + 1) * step]


def pick_kernel(pieces, order_ref, *refs):
    in_refs, out_refs = refs[: len(refs) - len(pieces)], refs[len(refs) - len(pieces) :]
    width = out_refs[0].shape[1] // len(in_refs)
    for d, out_ref in zip(pieces, out_refs):
        start = pl.multiple_of(order_ref[d] * width, width)
        for i, ref in enumerate(in_refs):
            out_ref[:, i * width : (i + 1) * width] = ref[:, pl.ds(start, width)]


def stack_kernel(*refs):
    *in_refs, out_ref = refs
    step = in_refs[0].shape[0]
    for i, ref in enumerate(in_refs):
        out_ref[i * step : (i + 1) * step, :] = ref[...]


def place_kernel(order_ref, *refs):
    *pieces, out_ref = refs
    width = pieces[0].shape[1]
    for d, piece in enumerate(pieces):
        start = pl.multiple_of(order_ref[d] * width, width)
        out_ref[:, pl.ds(start, width)] = piece[...]


def call(kernel, arrays, outs, flops=0, exps=0, scalars=None, unread=()):
    moved = sum(a.size * a.dtype.itemsize for a in arrays)
    moved += sum(math.prod(o.shape) * o.dtype.itemsize for o in outs)
    first = [] if scalars is None else [scalars]
    read = len(first) + len(arrays)

    def without_unread(*refs):
        kernel(*refs[:read], *refs[read + len(unread) :])

    return pl.pallas_call(
        without_unread,
        out_shape=outs,
        in_specs=[pl.BlockSpec(memory_space=pltpu.SMEM)] * len(first)
        + [pl.BlockSpec(memory_space=pltpu.VMEM)] * len(arrays)
        + [pl.BlockSpec(memory_space=pl.ANY)] * len(unread),
        out_specs=[pl.BlockSpec(memory_space=pltpu.VMEM)] * len(outs),
        compiler_params=pltpu.CompilerParams(vmem_limit_bytes=16 * 1024 * 1024),
        cost_estimate=pl.CostEstimate(flops=flops, bytes_accessed=moved, transcendentals=exps),
    )(*first, *arrays, *unread)


class Steps:
    def __init__(self):
        self.seen = []

    def run(self, kernel, arrays, outs, **more):
        results = call(kernel, arrays, outs, unread=list(self.seen), **more)
        self.seen.append(results[0])
        return results

    def ready(self, x):
        like = jax.ShapeDtypeStruct(x.shape, x.dtype)
        x = call(stack_kernel, [x], [like], unread=list(self.seen))[0]
        self.seen = [x]
        return x

    def have(self, x):
        self.seen.append(x)
        return x


class Half:
    def __init__(self, steps, mine, context, middle):
        self.steps, self.mine, self.context, self.middle = steps, mine, context, middle
        (rows, width), cached = mine.shape, context[0].shape[0]
        self.packed = [jax.ShapeDtypeStruct((width + STAT, rows), jnp.int16)]
        self.cost = {"flops": 4 * rows * cached * width, "exps": rows * cached * (width // HD)}

    def neighbours(self, x):
        return lax.ppermute(self.steps.ready(x), "seq", [(0, 1), (1, 0), (2, 3), (3, 2)])

    def across(self, x):
        return lax.ppermute(self.steps.ready(x), "seq", [(1, 2), (2, 1)])

    def outward(self, x):
        return lax.ppermute(self.steps.ready(x), "seq", [(1, 0), (2, 3)])

    def inward(self, x):
        return lax.ppermute(self.steps.ready(x), "seq", [(0, 1), (3, 2)])

    def attend(self, *queries):
        if len(queries) == 1:
            return self.steps.run(cached_kernel, [*queries, *self.context], self.packed, **self.cost)[0]
        arrays = [*queries, *self.context]
        return self.steps.run(either_kernel, arrays, self.packed, scalars=self.middle, **self.cost)[0]

    def merge(self, mine, got):
        return self.steps.run(merge_kernel, [mine, got], self.packed, scalars=self.middle)[0]

    def attend_own(self, kv, pieces, order):
        more = {name: value * 3 // 2 for name, value in self.cost.items()}
        kernel = functools.partial(own_kernel, pieces)
        return self.steps.run(
            kernel, [self.mine, *kv, *self.context], self.packed, scalars=order, **more
        )[0]

    def end(self, own, near, over, pieces):
        rows, width = self.mine.shape
        piece = jax.ShapeDtypeStruct((rows // len(pieces), width), jnp.bfloat16)
        return self.steps.run(
            final_kernel, [own, near, over], [piece] * len(pieces), scalars=self.middle
        )


def dense_body(queries, new_keys, new_values, cache_keys, cache_values):
    s = lax.axis_index("seq")
    shares = lax.axis_size("heads") * lax.axis_size("sub")
    me = lax.axis_index("heads") * lax.axis_size("sub") + lax.axis_index("sub")
    step, width = queries.shape[0], queries.shape[1] // shares
    half = shares // 2
    piece = jax.ShapeDtypeStruct((step, width), jnp.bfloat16)
    pair = jax.ShapeDtypeStruct((step, 2 * width), jnp.bfloat16)
    middle = jnp.logical_and(s > 0, s < 3).astype(jnp.int32).reshape(1)
    steps = Steps()
    run, have = steps.run, steps.have

    def swap(x, d):
        return lax.ppermute(x, ("heads", "sub"), [(i, i ^ d) for i in range(shares)])

    order = jnp.stack([me ^ d for d in range(shares)]).astype(jnp.int32)
    pieces_a, pieces_b = range(half), range(half, shares)
    chunk = [jax.ShapeDtypeStruct((half * step, width), jnp.bfloat16)]
    pick = functools.partial(pick_kernel, range(shares))

    q = call(pick, [queries], [piece] * shares, scalars=order)
    q_a = [q[0]] + [swap(q[d], d) for d in pieces_a if d]
    a_rows = run(stack_kernel, q_a, chunk)[0]
    q_b = [swap(q[d], d) for d in pieces_b]
    cache_vt = cache_values.T
    context = [cache_keys, cache_vt]
    a = Half(steps, a_rows, context, middle)
    near_a = a.neighbours(a.mine)
    over_a = a.across(a.mine)
    kv = run(pick, [new_keys, new_values], [pair] * shares, scalars=order)
    have(cache_vt)
    b_rows = run(stack_kernel, q_b, chunk)[0]
    b = Half(steps, b_rows, context, middle)
    near_b = b.neighbours(b.mine)
    far_a = a.across(have(near_a))
    p_near_a = a.attend(near_a)
    over_a_end = a.outward(have(over_a))
    have(far_a)
    far_b = b.across(have(near_b))
    kv = [kv[0]] + [swap(steps.ready(kv[d]), d) for d in range(1, shares)]
    far_a_end = a.outward(far_a)
    p_over_a = a.attend(over_a, have(over_a_end))
    back_over_a = a.inward(p_over_a)
    over_b = b.across(b.mine)
    far_b_end = b.outward(have(far_b))
    p_far_a = a.attend(far_a, have(far_a_end))
    back_far_a = a.inward(p_far_a)
    from_over_a = a.across(a.merge(p_over_a, have(back_over_a)))
    over_b_end = b.outward(have(over_b))
    p_far_b = b.attend(far_b, have(far_b_end))
    back_far_b = b.inward(p_far_b)
    m_far_a = a.merge(p_far_a, have(back_far_a))
    kv = [have(x) for x in kv]
    for_end_a = a.across(m_far_a)
    have(from_over_a)
    p_over_b = b.attend(over_b, have(over_b_end))
    back_over_b = b.inward(p_over_b)
    for_end_b = b.across(b.merge(p_far_b, have(back_far_b)))
    p_near_b = b.attend(near_b)
    from_near_a = a.neighbours(a.merge(p_near_a, have(for_end_a)))
    m_over_b = b.merge(p_over_b, have(back_over_b))
    m_near_b = b.merge(p_near_b, have(for_end_b))
    from_over_b = b.across(m_over_b)
    from_near_b = b.neighbours(m_near_b)
    own_b = b.attend_own(kv, pieces_b, order)
    have(from_near_a)
    own_a = a.attend_own(kv, pieces_a, order)
    out_b = b.end(own_b, have(from_near_b), have(from_over_b), pieces_b)
    out_b = [swap(x, d) for d, x in zip(pieces_b, out_b)]
    out_a = a.end(own_a, from_near_a, from_over_a, pieces_a)
    out_a = [swap(x, d) if d else x for d, x in zip(pieces_a, out_a)]
    out = jax.ShapeDtypeStruct((step, shares * width), jnp.bfloat16)
    return call(place_kernel, [*out_a, *out_b], [out], scalars=order)[0]


def power_of_two(n):
    return n & (n - 1) == 0


def body(queries, new_keys, new_values, cache_keys, cache_values, selection):
    qblocks, head_count, top_count = selection.shape
    seq_count = lax.axis_size("seq")
    shares = lax.axis_size("heads") * lax.axis_size("sub")
    every = top_count == cache_keys.shape[0] // BLOCK * seq_count and qblocks == 1
    fits = seq_count == 4 and power_of_two(shares) and shares > 1
    if every and fits and 4 * head_count <= STAT:
        return dense_body(queries, new_keys, new_values, cache_keys, cache_values)
    return sparse_body(queries, new_keys, new_values, cache_keys, cache_values, selection)


def solution(mesh):
    in_specs = (
        P(("groups", "seq", "heads", "sub"), None),
        P(("groups", "seq", "heads", "sub"), None),
        P(("groups", "seq", "heads", "sub"), None),
        P(("groups", "seq"), ("heads", "sub")),
        P(("groups", "seq"), ("heads", "sub")),
        P(("groups", "seq"), ("heads", "sub"), None),
    )
    out_specs = P(("groups", "seq", "heads", "sub"), None)
    return jax.shard_map(body, mesh=mesh, in_specs=in_specs, out_specs=out_specs, check_vma=False)
```

```python
import functools
import math

import jax
import jax.numpy as jnp
from jax import lax
from jax.experimental import pallas as pl
from jax.experimental.pallas import tpu as pltpu
from jax.sharding import PartitionSpec as P

HD = 128
BLOCK = 512


def order_ranks(owners):
    length = owners.shape[-1]
    counter = jnp.arange(length)
    earlier = counter[None, :] < counter[:, None]
    same_owner = owners[..., :, None] == owners[..., None, :]
    return jnp.sum(jnp.logical_and(same_owner, earlier), axis=-1)


def one_hot(values, length):
    return (values[..., None] == jnp.arange(length)).astype(jnp.float32)


def own_partial(query_blocks, key_blocks, value_blocks, scaling):
    scores = (
        jnp.einsum("bqhd,bkhd->bhqk", query_blocks, key_blocks, preferred_element_type=jnp.float32)
        * scaling
    )
    length = query_blocks.shape[1]
    causal = jnp.arange(length)[:, None] >= jnp.arange(length)[None, :]
    scores = jnp.where(causal, scores, -jnp.inf)
    highest = jnp.max(scores, axis=-1)
    weights = jnp.exp(scores - highest[..., None])
    totals = jnp.sum(weights, axis=-1)
    mixed = jnp.einsum(
        "bhqk,bkhd->bhqd",
        weights.astype(jnp.bfloat16),
        value_blocks,
        preferred_element_type=jnp.float32,
    )
    return (mixed, highest, totals)


def tile_partial(query_blocks, tile_pair, scaling):
    head_size = query_blocks.shape[-1]
    scores = (
        jnp.einsum(
            "bqhd,bhkd->bhqk",
            query_blocks,
            tile_pair[..., :head_size],
            preferred_element_type=jnp.float32,
        )
        * scaling
    )
    highest = jnp.max(scores, axis=-1)
    weights = jnp.exp(scores - highest[..., None])
    totals = jnp.sum(weights, axis=-1)
    mixed = jnp.einsum(
        "bhqk,bhkd->bhqd",
        weights.astype(jnp.bfloat16),
        tile_pair[..., head_size:],
        preferred_element_type=jnp.float32,
    )
    return (mixed, highest, totals)


def merge_parts(parts):
    top = parts[0][1]
    for part in parts[1:]:
        top = jnp.maximum(top, part[1])
    numer = jnp.zeros(parts[0][0].shape, jnp.float32)
    denom = jnp.zeros(parts[0][2].shape, jnp.float32)
    for part in parts:
        factor = jnp.exp(part[1] - top)
        numer = numer + factor[..., None] * part[0]
        denom = denom + factor * part[2]
    return numer / denom[..., None]


def sparse_body(queries, new_keys, new_values, cache_keys, cache_values, selection):
    heads_q, heads_k, heads_v = (
        lax.all_to_all(queries, ("heads", "sub"), split_axis=1, concat_axis=0, tiled=True),
        lax.all_to_all(new_keys, ("heads", "sub"), split_axis=1, concat_axis=0, tiled=True),
        lax.all_to_all(new_values, ("heads", "sub"), split_axis=1, concat_axis=0, tiled=True),
    )
    qblocks, head_count, top_count = selection.shape
    head_size = HD
    scaling = head_size ** (-0.5)
    shaped = (qblocks, BLOCK, head_count, head_size)
    query_blocks = heads_q.reshape(shaped)
    own = own_partial(query_blocks, heads_k.reshape(shaped), heads_v.reshape(shaped), scaling)
    seq_count = lax.axis_size("seq")
    myself = lax.axis_index("seq")
    cache_blocks = cache_keys.shape[0] // BLOCK
    tile_count = cache_blocks * head_count
    request_count = qblocks * head_count * top_count
    capacity = -(-request_count // seq_count)
    requests_all = lax.all_gather(selection, "seq", axis=0, tiled=True).reshape(
        seq_count, request_count
    )
    head_of = jnp.arange(request_count) // top_count % head_count
    my_requests = selection.reshape(request_count)
    my_owner = my_requests // cache_blocks
    my_slot = my_owner * capacity + order_ranks(my_owner)
    key_tiles = cache_keys.reshape(cache_blocks, BLOCK, head_count, head_size).transpose(0, 2, 1, 3)
    value_tiles = cache_values.reshape(cache_blocks, BLOCK, head_count, head_size).transpose(
        0, 2, 1, 3
    )
    tile_set = jnp.concatenate([key_tiles, value_tiles], axis=-1).reshape(
        tile_count, BLOCK, 2 * head_size
    )
    their_owner = requests_all // cache_blocks
    local_tile = requests_all % cache_blocks * head_count + head_of[None, :]
    served = (their_owner == myself).astype(jnp.float32)
    slot_pick = one_hot(order_ranks(their_owner), capacity) * served[..., None]
    picking = jnp.einsum("erc,erl->ecl", slot_pick, one_hot(local_tile, tile_count)).astype(
        jnp.bfloat16
    )
    parts = [own]
    outgoing = jnp.einsum(
        "ecl,lkf->eckf", picking, tile_set, preferred_element_type=jnp.float32
    ).astype(jnp.bfloat16)
    incoming = lax.all_to_all(outgoing, "seq", split_axis=0, concat_axis=0, tiled=True)
    fetched = incoming.reshape(seq_count * capacity, BLOCK, 2 * head_size)[my_slot]
    fetched = fetched.reshape(qblocks, head_count, top_count, BLOCK, 2 * head_size)
    for turn in range(top_count):
        parts.append(tile_partial(query_blocks, fetched[:, :, turn], scaling))
    result = merge_parts(parts)
    result = (
        result.transpose(0, 2, 1, 3)
        .reshape(qblocks * BLOCK, head_count * head_size)
        .astype(jnp.bfloat16)
    )
    return lax.all_to_all(result, ("heads", "sub"), split_axis=0, concat_axis=1, tiled=True)


STAT = 16
UNIT = 32767.0
LEAST = 1.2e-34
NEVER = -1.0e9
C2 = math.log2(math.e) * HD**-0.5


def scores_of(q, k, mask=None):
    s = lax.dot_general(k, q, (((1,), (1,)), ((), ())), preferred_element_type=jnp.float32)
    return s if mask is None else jnp.where(mask, s, -jnp.inf)


def weights_of(s):
    m = jnp.max(s, axis=0, keepdims=True)
    p = jnp.exp2((s - m) * C2)
    return p.astype(jnp.bfloat16), m * C2, jnp.sum(p, axis=0, keepdims=True)


def values_of(v, w, v_dim):
    return lax.dot_general(v, w, (((v_dim,), (0,)), ((), ())), preferred_element_type=jnp.float32)


def attend(tiles):
    count = len(tiles)
    s, w, parts = {}, {}, []
    for t in range(count + 2):
        if t < count:
            s[t] = tiles[t][0]()
        if 1 <= t <= count:
            w[t - 1] = weights_of(s.pop(t - 1))
        if t >= 2:
            weights, m, total = w.pop(t - 2)
            parts.append((tiles[t - 2][1](weights), m, total))
    return parts


def join(parts):
    top = functools.reduce(jnp.maximum, [m for _, m, _ in parts])
    factors = [jnp.exp2(m - top) for _, m, _ in parts]
    numer = sum(f * o for f, (o, _, _) in zip(factors, parts))
    denom = sum(f * t for f, (_, _, t) in zip(factors, parts))
    return numer, top, denom


def put(out_ref, heads):
    width, rows = len(heads) * HD, heads[0][0].shape[1]
    at = lax.broadcasted_iota(jnp.int32, (STAT, rows), 0)
    stats = jnp.zeros((STAT, rows), jnp.float32)
    for h, (numer, top, denom) in enumerate(heads):
        most = jnp.maximum(jnp.max(jnp.abs(numer), axis=0, keepdims=True), LEAST)
        code = jnp.round(numer * (UNIT / most))
        out_ref[h * HD : (h + 1) * HD, :] = code.astype(jnp.int32).astype(jnp.int16)
        for j, value in enumerate((top + jnp.log2(denom), jnp.log2(most / (UNIT * denom)))):
            whole = jnp.floor(value)
            stats = jnp.where(at == 4 * h + 2 * j, whole, stats)
            stats = jnp.where(at == 4 * h + 2 * j + 1, jnp.round((value - whole) * UNIT), stats)
    out_ref[width : width + STAT, :] = stats.astype(jnp.int32).astype(jnp.int16)


def take(ref, valid=None):
    width = ref.shape[0] - STAT
    stats = ref[width : width + STAT, :].astype(jnp.int32).astype(jnp.float32)
    heads = []
    for h in range(width // HD):
        code = ref[h * HD : (h + 1) * HD, :].astype(jnp.int32).astype(jnp.float32)
        weight = stats[4 * h : 4 * h + 1] + stats[4 * h + 1 : 4 * h + 2] * (1.0 / UNIT)
        unit = stats[4 * h + 2 : 4 * h + 3] + stats[4 * h + 3 : 4 * h + 4] * (1.0 / UNIT)
        if valid is not None:
            weight = jnp.where(valid, weight, NEVER)
        heads.append((code, weight, unit))
    return heads


def join_taken(taken):
    top = functools.reduce(jnp.maximum, [w for _, w, _ in taken])
    numer = sum(code * jnp.exp2(w - top + unit) for code, w, unit in taken)
    denom = sum(jnp.exp2(w - top) for _, w, _ in taken)
    return numer, top, denom


def cached_tiles(q_of, ck_ref, cvt_ref, h):
    cols = slice(h * HD, (h + 1) * HD)
    tiles = []
    for b in range(ck_ref.shape[0] // BLOCK):
        rows = slice(b * BLOCK, (b + 1) * BLOCK)
        tiles.append(
            (
                lambda rows=rows: scores_of(q_of(cols), ck_ref[rows, cols]),
                lambda w, rows=rows: values_of(cvt_ref[cols, rows], w, 1),
            )
        )
    return tiles


def attend_heads(tiles_of_heads):
    parts = attend([t for tiles in tiles_of_heads for t in tiles])
    heads = []
    for tiles in tiles_of_heads:
        heads.append(join(parts[: len(tiles)]))
        parts = parts[len(tiles) :]
    return heads


def cached_kernel(q_ref, ck_ref, cvt_ref, out_ref):
    heads = range(ck_ref.shape[1] // HD)
    q_of = lambda cols: q_ref[:, cols]
    put(out_ref, attend_heads([cached_tiles(q_of, ck_ref, cvt_ref, h) for h in heads]))


def either_kernel(middle_ref, a_ref, b_ref, ck_ref, cvt_ref, out_ref):
    middle = middle_ref[0] > 0
    heads = range(ck_ref.shape[1] // HD)
    q_of = lambda cols: jnp.where(middle, a_ref[:, cols], b_ref[:, cols])
    put(out_ref, attend_heads([cached_tiles(q_of, ck_ref, cvt_ref, h) for h in heads]))


def own_kernel(mine, order_ref, *refs):
    q_ref, *kv_refs, ck_ref, cvt_ref, out_ref = refs
    width = ck_ref.shape[1]
    rows = q_ref.shape[0]
    step = kv_refs[0].shape[0]

    def positions(shape, axis, pieces):
        at = lax.broadcasted_iota(jnp.int32, shape, axis)
        place = jnp.zeros(shape, jnp.int32)
        for i, d in enumerate(pieces):
            place = jnp.where(at // step == i, order_ref[d] * step + at % step, place)
        return place

    shape = (step * len(kv_refs), rows)
    mask = positions(shape, 1, mine) >= positions(shape, 0, range(len(kv_refs)))
    q_of = lambda cols: q_ref[:, cols]
    heads = []
    for h in range(width // HD):
        cols = slice(h * HD, (h + 1) * HD)
        vcols = slice(width + h * HD, width + (h + 1) * HD)
        own = (
            lambda cols=cols: scores_of(
                q_ref[:, cols], jnp.concatenate([r[:, cols] for r in kv_refs], axis=0), mask
            ),
            lambda w, vcols=vcols: values_of(
                jnp.concatenate([r[:, vcols] for r in kv_refs], axis=0), w, 0
            ),
        )
        heads.append([own] + cached_tiles(q_of, ck_ref, cvt_ref, h))
    put(out_ref, attend_heads(heads))


def merge_kernel(mine_ref, got_ref, out_ref):
    put(out_ref, [join_taken(pair) for pair in zip(take(mine_ref), take(got_ref))])


def middle_merge_kernel(middle_ref, mine_ref, got_ref, out_ref):
    taken = zip(take(mine_ref), take(got_ref, middle_ref[0] > 0))
    put(out_ref, [join_taken(pair) for pair in taken])


def final_kernel(own_ref, x_ref, y_ref, *out_refs):
    step = out_refs[0].shape[0]
    for h, taken in enumerate(zip(take(own_ref), take(x_ref), take(y_ref))):
        numer, _, denom = join_taken(taken)
        value = jnp.transpose(numer * (1.0 / denom)).astype(jnp.bfloat16)
        for i, out_ref in enumerate(out_refs):
            out_ref[:, h * HD : (h + 1) * HD] = value[i * step : (i + 1) * step]


def pick_kernel(pieces, order_ref, *refs):
    in_refs, out_refs = refs[: len(refs) - len(pieces)], refs[len(refs) - len(pieces) :]
    width = out_refs[0].shape[1] // len(in_refs)
    for d, out_ref in zip(pieces, out_refs):
        start = pl.multiple_of(order_ref[d] * width, width)
        for i, ref in enumerate(in_refs):
            out_ref[:, i * width : (i + 1) * width] = ref[:, pl.ds(start, width)]


def stack_kernel(*refs):
    *in_refs, out_ref = refs
    step = in_refs[0].shape[0]
    for i, ref in enumerate(in_refs):
        out_ref[i * step : (i + 1) * step, :] = ref[...]


def place_kernel(order_ref, *refs):
    *pieces, out_ref = refs
    width = pieces[0].shape[1]
    for d, piece in enumerate(pieces):
        start = pl.multiple_of(order_ref[d] * width, width)
        out_ref[:, pl.ds(start, width)] = piece[...]


def call(kernel, arrays, outs, flops=0, exps=0, scalars=None, unread=()):
    moved = sum(a.size * a.dtype.itemsize for a in arrays)
    moved += sum(math.prod(o.shape) * o.dtype.itemsize for o in outs)
    first = [] if scalars is None else [scalars]
    read = len(first) + len(arrays)

    def without_unread(*refs):
        kernel(*refs[:read], *refs[read + len(unread) :])

    return pl.pallas_call(
        without_unread,
        out_shape=outs,
        in_specs=[pl.BlockSpec(memory_space=pltpu.SMEM)] * len(first)
        + [pl.BlockSpec(memory_space=pltpu.VMEM)] * len(arrays)
        + [pl.BlockSpec(memory_space=pl.ANY)] * len(unread),
        out_specs=[pl.BlockSpec(memory_space=pltpu.VMEM)] * len(outs),
        compiler_params=pltpu.CompilerParams(vmem_limit_bytes=8 * 1024 * 1024),
        cost_estimate=pl.CostEstimate(flops=flops, bytes_accessed=moved, transcendentals=exps),
    )(*first, *arrays, *unread)


def after(x, unread):
    return call(stack_kernel, [x], [jax.ShapeDtypeStruct(x.shape, x.dtype)], unread=unread)[0]


def flip(x, bits):
    return lax.ppermute(x, "seq", [(i, i ^ bits) for i in range(4)])


def across(x):
    return lax.ppermute(x, "seq", [(1, 2), (2, 1)])


def outward(x):
    return lax.ppermute(x, "seq", [(1, 0), (2, 3)])


def inward(x):
    return lax.ppermute(x, "seq", [(0, 1), (3, 2)])


def dense_body(queries, new_keys, new_values, cache_keys, cache_values):
    s = lax.axis_index("seq")
    shares = lax.axis_size("heads") * lax.axis_size("sub")
    me = lax.axis_index("heads") * lax.axis_size("sub") + lax.axis_index("sub")
    step, width = queries.shape[0], queries.shape[1] // shares
    half, cached = shares // 2, cache_keys.shape[0]
    rows = half * step
    piece = jax.ShapeDtypeStruct((step, width), jnp.bfloat16)
    pair = jax.ShapeDtypeStruct((step, 2 * width), jnp.bfloat16)
    chunk = [jax.ShapeDtypeStruct((rows, width), jnp.bfloat16)]
    packed = [jax.ShapeDtypeStruct((width + STAT, rows), jnp.int16)]
    cost = {"flops": 4 * rows * cached * width, "exps": rows * cached * (width // HD)}
    middle = jnp.logical_and(s > 0, s < 3).astype(jnp.int32).reshape(1)
    order = jnp.stack([me ^ d for d in range(shares)]).astype(jnp.int32)
    pieces_a, pieces_b = range(half), range(half, shares)
    pick = functools.partial(pick_kernel, range(shares))
    cache_vt = cache_values.T
    context = [cache_keys, cache_vt]

    def swap(x, d):
        return lax.ppermute(x, ("heads", "sub"), [(i, i ^ d) for i in range(shares)]) if d else x

    def attend(q):
        return call(cached_kernel, [q, *context], packed, **cost)[0]

    def attend_either(in_middle, at_end):
        return call(either_kernel, [in_middle, at_end, *context], packed, scalars=middle, **cost)[0]

    def attend_own(q, pieces):
        more = {name: value * 3 // 2 for name, value in cost.items()}
        kernel = functools.partial(own_kernel, pieces)
        return call(kernel, [q, *kv, *context], packed, scalars=order, **more)[0]

    def merge(mine, got):
        return call(merge_kernel, [mine, got], packed)[0]

    def merge_in_middle(mine, got):
        return call(middle_merge_kernel, [mine, got], packed, scalars=middle)[0]

    def end(own, x, y, pieces):
        ended = call(final_kernel, [own, x, y], [piece] * half)
        return [swap(e, d) for e, d in zip(ended, pieces)]

    q = call(pick, [queries], [piece] * shares, scalars=order)
    a = call(stack_kernel, [swap(q[d], d) for d in pieces_a], chunk)[0]
    a3, a1 = flip(a, 3), flip(a, 1)
    b = call(stack_kernel, [swap(q[d], d) for d in pieces_b], chunk)[0]
    b2, b1 = flip(b, 2), flip(b, 1)
    kv = call(pick, [new_keys, new_values], [pair] * shares, scalars=order, unread=[b])
    kv = [swap(x, d) for d, x in enumerate(kv)]

    part_a3 = attend(a3)
    a2_end = outward(after(a3, [cache_vt]))
    b3 = flip(b2, 1)
    part_b2 = attend(b2)
    got_across, got_inward = across(part_b2), inward(part_b2)
    part_b1 = attend(b1)
    a2_middle = across(after(a1, [part_b2]))
    got_a2 = flip(after(part_a3, [part_b1, *kv[1:]]), 1)
    part_b3 = attend(b3)
    part_b3 = merge_in_middle(part_b3, got_inward)
    part_b1 = merge_in_middle(part_b1, got_across)
    from_b3, from_b1 = flip(part_b3, 3), flip(part_b1, 1)
    part_a2 = merge(attend_either(a2_middle, a2_end), after(got_a2, [part_b3, part_b1]))
    from_a2 = flip(part_a2, 2)
    part_a1 = attend(a1)
    from_a1 = flip(after(part_a1, [part_a2]), 1)

    out_b = end(attend_own(b, pieces_b), from_b3, from_b1, pieces_b)
    out_a = end(attend_own(a, pieces_a), from_a2, from_a1, pieces_a)
    out = jax.ShapeDtypeStruct((step, shares * width), jnp.bfloat16)
    return call(place_kernel, [*out_a, *out_b], [out], scalars=order)[0]


def power_of_two(n):
    return n & (n - 1) == 0


def body(queries, new_keys, new_values, cache_keys, cache_values, selection):
    qblocks, head_count, top_count = selection.shape
    seq_count = lax.axis_size("seq")
    shares = lax.axis_size("heads") * lax.axis_size("sub")
    every = top_count == cache_keys.shape[0] // BLOCK * seq_count and qblocks == 1
    fits = seq_count == 4 and power_of_two(shares) and shares > 1
    if every and fits and 4 * head_count <= STAT:
        return dense_body(queries, new_keys, new_values, cache_keys, cache_values)
    return sparse_body(queries, new_keys, new_values, cache_keys, cache_values, selection)


def solution(mesh):
    in_specs = (
        P(("groups", "seq", "heads", "sub"), None),
        P(("groups", "seq", "heads", "sub"), None),
        P(("groups", "seq", "heads", "sub"), None),
        P(("groups", "seq"), ("heads", "sub")),
        P(("groups", "seq"), ("heads", "sub")),
        P(("groups", "seq"), ("heads", "sub"), None),
    )
    out_specs = P(("groups", "seq", "heads", "sub"), None)
    return jax.shard_map(body, mesh=mesh, in_specs=in_specs, out_specs=out_specs, check_vma=False)
```

```python
import functools
import math

import jax
import jax.numpy as jnp
from jax import lax
from jax.experimental import pallas as pl
from jax.experimental.pallas import tpu as pltpu
from jax.sharding import PartitionSpec as P

HD = 128
BLOCK = 512


def order_ranks(owners):
    length = owners.shape[-1]
    counter = jnp.arange(length)
    earlier = counter[None, :] < counter[:, None]
    same_owner = owners[..., :, None] == owners[..., None, :]
    return jnp.sum(jnp.logical_and(same_owner, earlier), axis=-1)


def one_hot(values, length):
    return (values[..., None] == jnp.arange(length)).astype(jnp.float32)


def own_partial(query_blocks, key_blocks, value_blocks, scaling):
    scores = (
        jnp.einsum("bqhd,bkhd->bhqk", query_blocks, key_blocks, preferred_element_type=jnp.float32)
        * scaling
    )
    length = query_blocks.shape[1]
    causal = jnp.arange(length)[:, None] >= jnp.arange(length)[None, :]
    scores = jnp.where(causal, scores, -jnp.inf)
    highest = jnp.max(scores, axis=-1)
    weights = jnp.exp(scores - highest[..., None])
    totals = jnp.sum(weights, axis=-1)
    mixed = jnp.einsum(
        "bhqk,bkhd->bhqd",
        weights.astype(jnp.bfloat16),
        value_blocks,
        preferred_element_type=jnp.float32,
    )
    return (mixed, highest, totals)


def tile_partial(query_blocks, tile_pair, scaling):
    head_size = query_blocks.shape[-1]
    scores = (
        jnp.einsum(
            "bqhd,bhkd->bhqk",
            query_blocks,
            tile_pair[..., :head_size],
            preferred_element_type=jnp.float32,
        )
        * scaling
    )
    highest = jnp.max(scores, axis=-1)
    weights = jnp.exp(scores - highest[..., None])
    totals = jnp.sum(weights, axis=-1)
    mixed = jnp.einsum(
        "bhqk,bhkd->bhqd",
        weights.astype(jnp.bfloat16),
        tile_pair[..., head_size:],
        preferred_element_type=jnp.float32,
    )
    return (mixed, highest, totals)


def merge_parts(parts):
    top = parts[0][1]
    for part in parts[1:]:
        top = jnp.maximum(top, part[1])
    numer = jnp.zeros(parts[0][0].shape, jnp.float32)
    denom = jnp.zeros(parts[0][2].shape, jnp.float32)
    for part in parts:
        factor = jnp.exp(part[1] - top)
        numer = numer + factor[..., None] * part[0]
        denom = denom + factor * part[2]
    return numer / denom[..., None]


def sparse_body(queries, new_keys, new_values, cache_keys, cache_values, selection):
    heads_q, heads_k, heads_v = (
        lax.all_to_all(queries, ("heads", "sub"), split_axis=1, concat_axis=0, tiled=True),
        lax.all_to_all(new_keys, ("heads", "sub"), split_axis=1, concat_axis=0, tiled=True),
        lax.all_to_all(new_values, ("heads", "sub"), split_axis=1, concat_axis=0, tiled=True),
    )
    qblocks, head_count, top_count = selection.shape
    head_size = HD
    scaling = head_size ** (-0.5)
    shaped = (qblocks, BLOCK, head_count, head_size)
    query_blocks = heads_q.reshape(shaped)
    own = own_partial(query_blocks, heads_k.reshape(shaped), heads_v.reshape(shaped), scaling)
    seq_count = lax.axis_size("seq")
    myself = lax.axis_index("seq")
    cache_blocks = cache_keys.shape[0] // BLOCK
    tile_count = cache_blocks * head_count
    request_count = qblocks * head_count * top_count
    capacity = -(-request_count // seq_count)
    requests_all = lax.all_gather(selection, "seq", axis=0, tiled=True).reshape(
        seq_count, request_count
    )
    head_of = jnp.arange(request_count) // top_count % head_count
    my_requests = selection.reshape(request_count)
    my_owner = my_requests // cache_blocks
    my_slot = my_owner * capacity + order_ranks(my_owner)
    key_tiles = cache_keys.reshape(cache_blocks, BLOCK, head_count, head_size).transpose(0, 2, 1, 3)
    value_tiles = cache_values.reshape(cache_blocks, BLOCK, head_count, head_size).transpose(
        0, 2, 1, 3
    )
    tile_set = jnp.concatenate([key_tiles, value_tiles], axis=-1).reshape(
        tile_count, BLOCK, 2 * head_size
    )
    their_owner = requests_all // cache_blocks
    local_tile = requests_all % cache_blocks * head_count + head_of[None, :]
    served = (their_owner == myself).astype(jnp.float32)
    slot_pick = one_hot(order_ranks(their_owner), capacity) * served[..., None]
    picking = jnp.einsum("erc,erl->ecl", slot_pick, one_hot(local_tile, tile_count)).astype(
        jnp.bfloat16
    )
    parts = [own]
    outgoing = jnp.einsum(
        "ecl,lkf->eckf", picking, tile_set, preferred_element_type=jnp.float32
    ).astype(jnp.bfloat16)
    incoming = lax.all_to_all(outgoing, "seq", split_axis=0, concat_axis=0, tiled=True)
    fetched = incoming.reshape(seq_count * capacity, BLOCK, 2 * head_size)[my_slot]
    fetched = fetched.reshape(qblocks, head_count, top_count, BLOCK, 2 * head_size)
    for turn in range(top_count):
        parts.append(tile_partial(query_blocks, fetched[:, :, turn], scaling))
    result = merge_parts(parts)
    result = (
        result.transpose(0, 2, 1, 3)
        .reshape(qblocks * BLOCK, head_count * head_size)
        .astype(jnp.bfloat16)
    )
    return lax.all_to_all(result, ("heads", "sub"), split_axis=0, concat_axis=1, tiled=True)


STAT = 16
UNIT = 32767.0
LEAST = 1.2e-34
C2 = math.log2(math.e) * HD**-0.5


def scores_of(q, k, mask=None):
    s = lax.dot_general(k, q, (((1,), (1,)), ((), ())), preferred_element_type=jnp.float32)
    return s if mask is None else jnp.where(mask, s, -jnp.inf)


def weights_of(s):
    m = jnp.max(s, axis=0, keepdims=True)
    p = jnp.exp2((s - m) * C2)
    return p.astype(jnp.bfloat16), m * C2, jnp.sum(p, axis=0, keepdims=True)


def values_of(v, w, v_dim):
    return lax.dot_general(v, w, (((v_dim,), (0,)), ((), ())), preferred_element_type=jnp.float32)


def attend(tiles):
    count = len(tiles)
    s, w, parts = {}, {}, []
    for t in range(count + 2):
        if t < count:
            s[t] = tiles[t][0]()
        if 1 <= t <= count:
            w[t - 1] = weights_of(s.pop(t - 1))
        if t >= 2:
            weights, m, total = w.pop(t - 2)
            parts.append((tiles[t - 2][1](weights), m, total))
    return parts


def join(parts):
    top = functools.reduce(jnp.maximum, [m for _, m, _ in parts])
    factors = [jnp.exp2(m - top) for _, m, _ in parts]
    numer = sum(f * o for f, (o, _, _) in zip(factors, parts))
    denom = sum(f * t for f, (_, _, t) in zip(factors, parts))
    return numer, top, denom


def put(out_ref, heads):
    width, rows = len(heads) * HD, heads[0][0].shape[1]
    at = lax.broadcasted_iota(jnp.int32, (STAT, rows), 0)
    stats = jnp.zeros((STAT, rows), jnp.float32)
    for h, (numer, top, denom) in enumerate(heads):
        most = jnp.maximum(jnp.max(jnp.abs(numer), axis=0, keepdims=True), LEAST)
        code = jnp.round(numer * (UNIT / most))
        out_ref[h * HD : (h + 1) * HD, :] = code.astype(jnp.int32).astype(jnp.int16)
        for j, value in enumerate((top + jnp.log2(denom), jnp.log2(most / (UNIT * denom)))):
            whole = jnp.floor(value)
            stats = jnp.where(at == 4 * h + 2 * j, whole, stats)
            stats = jnp.where(at == 4 * h + 2 * j + 1, jnp.round((value - whole) * UNIT), stats)
    out_ref[width : width + STAT, :] = stats.astype(jnp.int32).astype(jnp.int16)


def take(ref):
    width = ref.shape[0] - STAT
    stats = ref[width : width + STAT, :].astype(jnp.int32).astype(jnp.float32)
    heads = []
    for h in range(width // HD):
        code = ref[h * HD : (h + 1) * HD, :].astype(jnp.int32).astype(jnp.float32)
        weight = stats[4 * h : 4 * h + 1] + stats[4 * h + 1 : 4 * h + 2] * (1.0 / UNIT)
        unit = stats[4 * h + 2 : 4 * h + 3] + stats[4 * h + 3 : 4 * h + 4] * (1.0 / UNIT)
        heads.append((code, weight, unit))
    return heads


def join_taken(taken):
    top = functools.reduce(jnp.maximum, [w for _, w, _ in taken])
    numer = sum(code * jnp.exp2(w - top + unit) for code, w, unit in taken)
    denom = sum(jnp.exp2(w - top) for _, w, _ in taken)
    return numer, top, denom


def cached_tiles(q_of, ck_ref, cvt_ref, h):
    cols = slice(h * HD, (h + 1) * HD)
    tiles = []
    for b in range(ck_ref.shape[0] // BLOCK):
        rows = slice(b * BLOCK, (b + 1) * BLOCK)
        tiles.append(
            (
                lambda rows=rows: scores_of(q_of(cols), ck_ref[rows, cols]),
                lambda w, rows=rows: values_of(cvt_ref[cols, rows], w, 1),
            )
        )
    return tiles


def attend_heads(tiles_of_heads):
    parts = attend([t for tiles in tiles_of_heads for t in tiles])
    heads = []
    for tiles in tiles_of_heads:
        heads.append(join(parts[: len(tiles)]))
        parts = parts[len(tiles) :]
    return heads


def cached_kernel(q_ref, ck_ref, cvt_ref, out_ref):
    heads = range(ck_ref.shape[1] // HD)
    q_of = lambda cols: q_ref[:, cols]
    put(out_ref, attend_heads([cached_tiles(q_of, ck_ref, cvt_ref, h) for h in heads]))


def own_kernel(mine, order_ref, *refs):
    q_ref, *kv_refs, ck_ref, cvt_ref, out_ref = refs
    width = ck_ref.shape[1]
    rows = q_ref.shape[0]
    step = kv_refs[0].shape[0]

    def positions(shape, axis, pieces):
        at = lax.broadcasted_iota(jnp.int32, shape, axis)
        place = jnp.zeros(shape, jnp.int32)
        for i, d in enumerate(pieces):
            place = jnp.where(at // step == i, order_ref[d] * step + at % step, place)
        return place

    shape = (step * len(kv_refs), rows)
    mask = positions(shape, 1, mine) >= positions(shape, 0, range(len(kv_refs)))
    q_of = lambda cols: q_ref[:, cols]
    heads = []
    for h in range(width // HD):
        cols = slice(h * HD, (h + 1) * HD)
        vcols = slice(width + h * HD, width + (h + 1) * HD)
        own = (
            lambda cols=cols: scores_of(
                q_ref[:, cols], jnp.concatenate([r[:, cols] for r in kv_refs], axis=0), mask
            ),
            lambda w, vcols=vcols: values_of(
                jnp.concatenate([r[:, vcols] for r in kv_refs], axis=0), w, 0
            ),
        )
        heads.append([own] + cached_tiles(q_of, ck_ref, cvt_ref, h))
    put(out_ref, attend_heads(heads))


def merge_kernel(*refs):
    *in_refs, out_ref = refs
    put(out_ref, [join_taken(taken) for taken in zip(*[take(r) for r in in_refs])])


def final_kernel(count, *refs):
    in_refs, out_refs = refs[:count], refs[count:]
    step = out_refs[0].shape[0]
    for h, taken in enumerate(zip(*[take(r) for r in in_refs])):
        numer, _, denom = join_taken(taken)
        value = jnp.transpose(numer * (1.0 / denom)).astype(jnp.bfloat16)
        for i, out_ref in enumerate(out_refs):
            out_ref[:, h * HD : (h + 1) * HD] = value[i * step : (i + 1) * step]


def pick_kernel(pieces, count, order_ref, *refs):
    in_refs, out_refs = refs[:count], refs[len(refs) - len(pieces) :]
    width = out_refs[0].shape[1] // len(in_refs)
    for d, out_ref in zip(pieces, out_refs):
        start = pl.multiple_of(order_ref[d] * width, width)
        for i, ref in enumerate(in_refs):
            out_ref[:, i * width : (i + 1) * width] = ref[:, pl.ds(start, width)]


def stack_kernel(count, *refs):
    out_ref = refs[-1]
    step = refs[0].shape[0]
    for i in range(count):
        out_ref[i * step : (i + 1) * step, :] = refs[i][...]


def place_kernel(order_ref, *refs):
    *pieces, out_ref = refs
    width = pieces[0].shape[1]
    for d, piece in enumerate(pieces):
        start = pl.multiple_of(order_ref[d] * width, width)
        out_ref[:, pl.ds(start, width)] = piece[...]


def call(kernel, arrays, outs, flops=0, exps=0, scalars=None, unread=()):
    moved = sum(a.size * a.dtype.itemsize for a in arrays)
    moved += sum(math.prod(o.shape) * o.dtype.itemsize for o in outs)
    first = [] if scalars is None else [scalars]
    return pl.pallas_call(
        kernel,
        out_shape=outs,
        in_specs=[pl.BlockSpec(memory_space=pltpu.SMEM)] * len(first)
        + [pl.BlockSpec(memory_space=pltpu.VMEM)] * len(arrays)
        + [pl.BlockSpec(memory_space=pl.ANY)] * len(unread),
        out_specs=[pl.BlockSpec(memory_space=pltpu.VMEM)] * len(outs),
        compiler_params=pltpu.CompilerParams(vmem_limit_bytes=16 * 1024 * 1024),
        cost_estimate=pl.CostEstimate(flops=flops, bytes_accessed=moved, transcendentals=exps),
    )(*first, *arrays, *unread)


def dense_body(queries, new_keys, new_values, cache_keys, cache_values):
    seq_count = lax.axis_size("seq")
    shares = lax.axis_size("heads") * lax.axis_size("sub")
    me = lax.axis_index("heads") * lax.axis_size("sub") + lax.axis_index("sub")
    step, width = queries.shape[0], queries.shape[1] // shares
    cached = cache_keys.shape[0]
    each = shares // CHUNKS
    rows = each * step
    chunk = jax.ShapeDtypeStruct((rows, width), jnp.bfloat16)
    piece = jax.ShapeDtypeStruct((step, width), jnp.bfloat16)
    pair = jax.ShapeDtypeStruct((step, 2 * width), jnp.bfloat16)
    packed = jax.ShapeDtypeStruct((width + STAT, rows), jnp.int16)
    tile_flops = 4 * rows * cached * width
    tile_exps = rows * cached * (width // HD)

    def swap(x, d):
        return lax.ppermute(x, ("heads", "sub"), [(i, i ^ d) for i in range(shares)])

    def along(x, bit):
        return lax.ppermute(x, "seq", [(i, i ^ bit) for i in range(seq_count)])

    def after(x, unread):
        like = jax.ShapeDtypeStruct(x.shape, x.dtype)
        return call(functools.partial(stack_kernel, 1), [x], [like], unread=unread)[0] if unread else x

    order = jnp.stack([me ^ d for d in range(shares)]).astype(jnp.int32)
    cache_vt = cache_values.T
    context = [cache_keys, cache_vt]

    def attend(q):
        return call(cached_kernel, [q, *context], [packed], tile_flops, tile_exps)[0]

    def attend_own(q, pieces):
        return call(
            functools.partial(own_kernel, pieces),
            [q, *kv, *context],
            [packed],
            tile_flops * 3 // 2,
            tile_exps * 3 // 2,
            order,
        )[0]

    def merge(mine, got):
        return call(merge_kernel, [mine, got], [packed])[0]

    def end(parts, pieces):
        ended = call(functools.partial(final_kernel, len(parts)), parts, [piece] * each)
        return [swap(x, d) if d else x for x, d in zip(ended, pieces)]

    pieces_a, pieces_b = range(each), range(each, shares)
    pick = functools.partial(pick_kernel, pieces_a, 1)
    q = call(pick, [queries], [piece] * each, scalars=order)
    q = [swap(x, d) if d else x for x, d in zip(q, pieces_a)]
    a = call(functools.partial(stack_kernel, each), q, [chunk])[0]
    a2, a1 = along(a, 2), along(a, 1)
    pick = functools.partial(pick_kernel, pieces_b, 1)
    q = call(pick, [queries], [piece] * each, scalars=order)
    q = [swap(x, d) for x, d in zip(q, pieces_b)]
    b = call(functools.partial(stack_kernel, each), q, [chunk])[0]
    b2, b1 = along(b, 2), along(b, 1)
    pick = functools.partial(pick_kernel, range(shares), 2)
    kv = call(pick, [new_keys, new_values], [pair] * shares, scalars=order, unread=[b])
    kv = [swap(x, d) if d else x for d, x in enumerate(kv)]
    part_a2, part_a1 = attend(a2), attend(a1)
    b3 = along(after(b2, [part_a2, part_a1]), 1)
    part_b2 = attend(b2)
    a3 = along(after(a2, [part_b2, b1, *kv[1:]]), 1)
    got_b2 = along(attend(b3), 1)
    got_a2 = along(attend(a3), 1)
    part_b2 = merge(part_b2, got_b2)
    from_b2 = along(part_b2, 2)
    from_b1 = along(after(attend(b1), [part_b2]), 1)
    part_a2 = merge(part_a2, got_a2)
    from_a2 = along(part_a2, 2)
    from_a1 = along(after(part_a1, [part_a2]), 1)
    out_b = end([attend_own(b, pieces_b), from_b2, from_b1], pieces_b)
    out_a = end([attend_own(a, pieces_a), from_a2, from_a1], pieces_a)
    results = [*out_a, *out_b]
    out = jax.ShapeDtypeStruct((step, shares * width), jnp.bfloat16)
    return call(place_kernel, results, [out], scalars=order)[0]


CHUNKS = 2


def power_of_two(n):
    return n & (n - 1) == 0


def body(queries, new_keys, new_values, cache_keys, cache_values, selection):
    qblocks, head_count, top_count = selection.shape
    seq_count = lax.axis_size("seq")
    shares = lax.axis_size("heads") * lax.axis_size("sub")
    every = top_count == cache_keys.shape[0] // BLOCK * seq_count and qblocks == 1
    fits = seq_count == 4 and power_of_two(shares) and shares % CHUNKS == 0
    if every and fits and 4 * head_count <= STAT:
        return dense_body(queries, new_keys, new_values, cache_keys, cache_values)
    return sparse_body(queries, new_keys, new_values, cache_keys, cache_values, selection)


def solution(mesh):
    in_specs = (
        P(("groups", "seq", "heads", "sub"), None),
        P(("groups", "seq", "heads", "sub"), None),
        P(("groups", "seq", "heads", "sub"), None),
        P(("groups", "seq"), ("heads", "sub")),
        P(("groups", "seq"), ("heads", "sub")),
        P(("groups", "seq"), ("heads", "sub"), None),
    )
    out_specs = P(("groups", "seq", "heads", "sub"), None)
    return jax.shard_map(body, mesh=mesh, in_specs=in_specs, out_specs=out_specs, check_vma=False)
```

```python
import functools
import math

import jax
import jax.numpy as jnp
from jax import lax
from jax.experimental import pallas as pl
from jax.experimental.pallas import tpu as pltpu
from jax.sharding import PartitionSpec as P

HD = 128
BLOCK = 512


def order_ranks(owners):
    length = owners.shape[-1]
    counter = jnp.arange(length)
    earlier = counter[None, :] < counter[:, None]
    same_owner = owners[..., :, None] == owners[..., None, :]
    return jnp.sum(jnp.logical_and(same_owner, earlier), axis=-1)


def one_hot(values, length):
    return (values[..., None] == jnp.arange(length)).astype(jnp.float32)


def own_partial(query_blocks, key_blocks, value_blocks, scaling):
    scores = (
        jnp.einsum("bqhd,bkhd->bhqk", query_blocks, key_blocks, preferred_element_type=jnp.float32)
        * scaling
    )
    length = query_blocks.shape[1]
    causal = jnp.arange(length)[:, None] >= jnp.arange(length)[None, :]
    scores = jnp.where(causal, scores, -jnp.inf)
    highest = jnp.max(scores, axis=-1)
    weights = jnp.exp(scores - highest[..., None])
    totals = jnp.sum(weights, axis=-1)
    mixed = jnp.einsum(
        "bhqk,bkhd->bhqd",
        weights.astype(jnp.bfloat16),
        value_blocks,
        preferred_element_type=jnp.float32,
    )
    return (mixed, highest, totals)


def tile_partial(query_blocks, tile_pair, scaling):
    head_size = query_blocks.shape[-1]
    scores = (
        jnp.einsum(
            "bqhd,bhkd->bhqk",
            query_blocks,
            tile_pair[..., :head_size],
            preferred_element_type=jnp.float32,
        )
        * scaling
    )
    highest = jnp.max(scores, axis=-1)
    weights = jnp.exp(scores - highest[..., None])
    totals = jnp.sum(weights, axis=-1)
    mixed = jnp.einsum(
        "bhqk,bhkd->bhqd",
        weights.astype(jnp.bfloat16),
        tile_pair[..., head_size:],
        preferred_element_type=jnp.float32,
    )
    return (mixed, highest, totals)


def merge_parts(parts):
    top = parts[0][1]
    for part in parts[1:]:
        top = jnp.maximum(top, part[1])
    numer = jnp.zeros(parts[0][0].shape, jnp.float32)
    denom = jnp.zeros(parts[0][2].shape, jnp.float32)
    for part in parts:
        factor = jnp.exp(part[1] - top)
        numer = numer + factor[..., None] * part[0]
        denom = denom + factor * part[2]
    return numer / denom[..., None]


def sparse_body(queries, new_keys, new_values, cache_keys, cache_values, selection):
    heads_q, heads_k, heads_v = (
        lax.all_to_all(queries, ("heads", "sub"), split_axis=1, concat_axis=0, tiled=True),
        lax.all_to_all(new_keys, ("heads", "sub"), split_axis=1, concat_axis=0, tiled=True),
        lax.all_to_all(new_values, ("heads", "sub"), split_axis=1, concat_axis=0, tiled=True),
    )
    qblocks, head_count, top_count = selection.shape
    head_size = HD
    scaling = head_size ** (-0.5)
    shaped = (qblocks, BLOCK, head_count, head_size)
    query_blocks = heads_q.reshape(shaped)
    own = own_partial(query_blocks, heads_k.reshape(shaped), heads_v.reshape(shaped), scaling)
    seq_count = lax.axis_size("seq")
    myself = lax.axis_index("seq")
    cache_blocks = cache_keys.shape[0] // BLOCK
    tile_count = cache_blocks * head_count
    request_count = qblocks * head_count * top_count
    capacity = -(-request_count // seq_count)
    requests_all = lax.all_gather(selection, "seq", axis=0, tiled=True).reshape(
        seq_count, request_count
    )
    head_of = jnp.arange(request_count) // top_count % head_count
    my_requests = selection.reshape(request_count)
    my_owner = my_requests // cache_blocks
    my_slot = my_owner * capacity + order_ranks(my_owner)
    key_tiles = cache_keys.reshape(cache_blocks, BLOCK, head_count, head_size).transpose(0, 2, 1, 3)
    value_tiles = cache_values.reshape(cache_blocks, BLOCK, head_count, head_size).transpose(
        0, 2, 1, 3
    )
    tile_set = jnp.concatenate([key_tiles, value_tiles], axis=-1).reshape(
        tile_count, BLOCK, 2 * head_size
    )
    their_owner = requests_all // cache_blocks
    local_tile = requests_all % cache_blocks * head_count + head_of[None, :]
    served = (their_owner == myself).astype(jnp.float32)
    slot_pick = one_hot(order_ranks(their_owner), capacity) * served[..., None]
    picking = jnp.einsum("erc,erl->ecl", slot_pick, one_hot(local_tile, tile_count)).astype(
        jnp.bfloat16
    )
    parts = [own]
    outgoing = jnp.einsum(
        "ecl,lkf->eckf", picking, tile_set, preferred_element_type=jnp.float32
    ).astype(jnp.bfloat16)
    incoming = lax.all_to_all(outgoing, "seq", split_axis=0, concat_axis=0, tiled=True)
    fetched = incoming.reshape(seq_count * capacity, BLOCK, 2 * head_size)[my_slot]
    fetched = fetched.reshape(qblocks, head_count, top_count, BLOCK, 2 * head_size)
    for turn in range(top_count):
        parts.append(tile_partial(query_blocks, fetched[:, :, turn], scaling))
    result = merge_parts(parts)
    result = (
        result.transpose(0, 2, 1, 3)
        .reshape(qblocks * BLOCK, head_count * head_size)
        .astype(jnp.bfloat16)
    )
    return lax.all_to_all(result, ("heads", "sub"), split_axis=0, concat_axis=1, tiled=True)


STAT = 16
UNIT = 32767.0
LEAST = 1.2e-34
C2 = math.log2(math.e) * HD**-0.5


def scores_of(q, k, mask=None):
    s = lax.dot_general(k, q, (((1,), (1,)), ((), ())), preferred_element_type=jnp.float32)
    return s if mask is None else jnp.where(mask, s, -jnp.inf)


def weights_of(s):
    m = jnp.max(s, axis=0, keepdims=True)
    p = jnp.exp2((s - m) * C2)
    return p.astype(jnp.bfloat16), m * C2, jnp.sum(p, axis=0, keepdims=True)


def values_of(v, w, v_dim):
    return lax.dot_general(v, w, (((v_dim,), (0,)), ((), ())), preferred_element_type=jnp.float32)


def attend(tiles):
    count = len(tiles)
    s, w, parts = {}, {}, []
    for t in range(count + 2):
        if t < count:
            s[t] = tiles[t][0]()
        if 1 <= t <= count:
            w[t - 1] = weights_of(s.pop(t - 1))
        if t >= 2:
            weights, m, total = w.pop(t - 2)
            parts.append((tiles[t - 2][1](weights), m, total))
    return parts


def join(parts):
    top = functools.reduce(jnp.maximum, [m for _, m, _ in parts])
    factors = [jnp.exp2(m - top) for _, m, _ in parts]
    numer = sum(f * o for f, (o, _, _) in zip(factors, parts))
    denom = sum(f * t for f, (_, _, t) in zip(factors, parts))
    return numer, top, denom


def put(out_ref, heads):
    width, rows = len(heads) * HD, heads[0][0].shape[1]
    at = lax.broadcasted_iota(jnp.int32, (STAT, rows), 0)
    stats = jnp.zeros((STAT, rows), jnp.float32)
    for h, (numer, top, denom) in enumerate(heads):
        most = jnp.maximum(jnp.max(jnp.abs(numer), axis=0, keepdims=True), LEAST)
        code = jnp.round(numer * (UNIT / most))
        out_ref[h * HD : (h + 1) * HD, :] = code.astype(jnp.int32).astype(jnp.int16)
        for j, value in enumerate((top + jnp.log2(denom), jnp.log2(most / (UNIT * denom)))):
            whole = jnp.floor(value)
            stats = jnp.where(at == 4 * h + 2 * j, whole, stats)
            stats = jnp.where(at == 4 * h + 2 * j + 1, jnp.round((value - whole) * UNIT), stats)
    out_ref[width : width + STAT, :] = stats.astype(jnp.int32).astype(jnp.int16)


def take(ref):
    width = ref.shape[0] - STAT
    stats = ref[width : width + STAT, :].astype(jnp.int32).astype(jnp.float32)
    heads = []
    for h in range(width // HD):
        code = ref[h * HD : (h + 1) * HD, :].astype(jnp.int32).astype(jnp.float32)
        weight = stats[4 * h : 4 * h + 1] + stats[4 * h + 1 : 4 * h + 2] * (1.0 / UNIT)
        unit = stats[4 * h + 2 : 4 * h + 3] + stats[4 * h + 3 : 4 * h + 4] * (1.0 / UNIT)
        heads.append((code, weight, unit))
    return heads


def join_taken(taken):
    top = functools.reduce(jnp.maximum, [w for _, w, _ in taken])
    numer = sum(code * jnp.exp2(w - top + unit) for code, w, unit in taken)
    denom = sum(jnp.exp2(w - top) for _, w, _ in taken)
    return numer, top, denom


def cached_tiles(q_of, ck_ref, cvt_ref, h):
    cols = slice(h * HD, (h + 1) * HD)
    tiles = []
    for b in range(ck_ref.shape[0] // BLOCK):
        rows = slice(b * BLOCK, (b + 1) * BLOCK)
        tiles.append(
            (
                lambda rows=rows: scores_of(q_of(cols), ck_ref[rows, cols]),
                lambda w, rows=rows: values_of(cvt_ref[cols, rows], w, 1),
            )
        )
    return tiles


def attend_heads(tiles_of_heads):
    parts = attend([t for tiles in tiles_of_heads for t in tiles])
    heads = []
    for tiles in tiles_of_heads:
        heads.append(join(parts[: len(tiles)]))
        parts = parts[len(tiles) :]
    return heads


def cached_kernel(q_ref, ck_ref, cvt_ref, out_ref):
    heads = range(ck_ref.shape[1] // HD)
    q_of = lambda cols: q_ref[:, cols]
    put(out_ref, attend_heads([cached_tiles(q_of, ck_ref, cvt_ref, h) for h in heads]))


def own_kernel(mine, order_ref, *refs):
    q_ref, *kv_refs, ck_ref, cvt_ref, out_ref = refs
    width = ck_ref.shape[1]
    rows = q_ref.shape[0]
    step = kv_refs[0].shape[0]

    def positions(shape, axis, pieces):
        at = lax.broadcasted_iota(jnp.int32, shape, axis)
        place = jnp.zeros(shape, jnp.int32)
        for i, d in enumerate(pieces):
            place = jnp.where(at // step == i, order_ref[d] * step + at % step, place)
        return place

    shape = (step * len(kv_refs), rows)
    mask = positions(shape, 1, mine) >= positions(shape, 0, range(len(kv_refs)))
    q_of = lambda cols: q_ref[:, cols]
    heads = []
    for h in range(width // HD):
        cols = slice(h * HD, (h + 1) * HD)
        vcols = slice(width + h * HD, width + (h + 1) * HD)
        own = (
            lambda cols=cols: scores_of(
                q_ref[:, cols], jnp.concatenate([r[:, cols] for r in kv_refs], axis=0), mask
            ),
            lambda w, vcols=vcols: values_of(
                jnp.concatenate([r[:, vcols] for r in kv_refs], axis=0), w, 0
            ),
        )
        heads.append([own] + cached_tiles(q_of, ck_ref, cvt_ref, h))
    put(out_ref, attend_heads(heads))


def merge_kernel(*refs):
    *in_refs, out_ref = refs
    put(out_ref, [join_taken(taken) for taken in zip(*[take(r) for r in in_refs])])


def final_kernel(count, *refs):
    in_refs, out_refs = refs[:count], refs[count:]
    step = out_refs[0].shape[0]
    for h, taken in enumerate(zip(*[take(r) for r in in_refs])):
        numer, _, denom = join_taken(taken)
        value = jnp.transpose(numer * (1.0 / denom)).astype(jnp.bfloat16)
        for i, out_ref in enumerate(out_refs):
            out_ref[:, h * HD : (h + 1) * HD] = value[i * step : (i + 1) * step]


def pick_kernel(pieces, count, order_ref, *refs):
    in_refs, out_refs = refs[:count], refs[len(refs) - len(pieces) :]
    width = out_refs[0].shape[1] // len(in_refs)
    for d, out_ref in zip(pieces, out_refs):
        start = pl.multiple_of(order_ref[d] * width, width)
        for i, ref in enumerate(in_refs):
            out_ref[:, i * width : (i + 1) * width] = ref[:, pl.ds(start, width)]


def stack_kernel(count, *refs):
    out_ref = refs[-1]
    step = refs[0].shape[0]
    for i in range(count):
        out_ref[i * step : (i + 1) * step, :] = refs[i][...]


def place_kernel(order_ref, *refs):
    *pieces, out_ref = refs
    width = pieces[0].shape[1]
    for d, piece in enumerate(pieces):
        start = pl.multiple_of(order_ref[d] * width, width)
        out_ref[:, pl.ds(start, width)] = piece[...]


def call(kernel, arrays, outs, flops=0, exps=0, scalars=None, unread=()):
    moved = sum(a.size * a.dtype.itemsize for a in arrays)
    moved += sum(math.prod(o.shape) * o.dtype.itemsize for o in outs)
    first = [] if scalars is None else [scalars]
    return pl.pallas_call(
        kernel,
        out_shape=outs,
        in_specs=[pl.BlockSpec(memory_space=pltpu.SMEM)] * len(first)
        + [pl.BlockSpec(memory_space=pltpu.VMEM)] * len(arrays)
        + [pl.BlockSpec(memory_space=pl.ANY)] * len(unread),
        out_specs=[pl.BlockSpec(memory_space=pltpu.VMEM)] * len(outs),
        compiler_params=pltpu.CompilerParams(vmem_limit_bytes=16 * 1024 * 1024),
        cost_estimate=pl.CostEstimate(flops=flops, bytes_accessed=moved, transcendentals=exps),
    )(*first, *arrays, *unread)


def dense_body(queries, new_keys, new_values, cache_keys, cache_values):
    seq_count = lax.axis_size("seq")
    shares = lax.axis_size("heads") * lax.axis_size("sub")
    me = lax.axis_index("heads") * lax.axis_size("sub") + lax.axis_index("sub")
    step, width = queries.shape[0], queries.shape[1] // shares
    cached = cache_keys.shape[0]
    each = shares // CHUNKS
    rows = each * step
    chunk = jax.ShapeDtypeStruct((rows, width), jnp.bfloat16)
    piece = jax.ShapeDtypeStruct((step, width), jnp.bfloat16)
    pair = jax.ShapeDtypeStruct((step, 2 * width), jnp.bfloat16)
    packed = jax.ShapeDtypeStruct((width + STAT, rows), jnp.int16)
    tile_flops = 4 * rows * cached * width
    tile_exps = rows * cached * (width // HD)

    def swap(x, d):
        return lax.ppermute(x, ("heads", "sub"), [(i, i ^ d) for i in range(shares)])

    def along(x, bit):
        return lax.ppermute(x, "seq", [(i, i ^ bit) for i in range(seq_count)])

    def after(x, unread):
        like = jax.ShapeDtypeStruct(x.shape, x.dtype)
        return call(functools.partial(stack_kernel, 1), [x], [like], unread=unread)[0] if unread else x

    order = jnp.stack([me ^ d for d in range(shares)]).astype(jnp.int32)
    cache_vt = cache_values.T
    context = [cache_keys, cache_vt]

    def attend(q):
        return call(cached_kernel, [q, *context], [packed], tile_flops, tile_exps)[0]

    def attend_own(q, pieces):
        return call(
            functools.partial(own_kernel, pieces),
            [q, *kv, *context],
            [packed],
            tile_flops * 3 // 2,
            tile_exps * 3 // 2,
            order,
        )[0]

    def merge(mine, got):
        return call(merge_kernel, [mine, got], [packed])[0]

    def end(parts, pieces):
        ended = call(functools.partial(final_kernel, len(parts)), parts, [piece] * each)
        return [swap(x, d) if d else x for x, d in zip(ended, pieces)]

    pieces_a, pieces_b = range(each), range(each, shares)
    pick = functools.partial(pick_kernel, pieces_a, 1)
    q = call(pick, [queries], [piece] * each, scalars=order)
    q = [swap(x, d) if d else x for x, d in zip(q, pieces_a)]
    a = call(functools.partial(stack_kernel, each), q, [chunk])[0]
    a2, a1 = along(a, 2), along(a, 1)
    pick = functools.partial(pick_kernel, pieces_b, 1)
    q = call(pick, [queries], [piece] * each, scalars=order)
    q = [swap(x if d == each else after(x, [cache_vt]), d) for x, d in zip(q, pieces_b)]
    b = call(functools.partial(stack_kernel, each), q, [chunk])[0]
    b2, b1 = along(b, 2), along(b, 1)
    pick = functools.partial(pick_kernel, range(shares), 2)
    kv = call(pick, [new_keys, new_values], [pair] * shares, scalars=order, unread=[b])
    kv = [swap(x, d) if d else x for d, x in enumerate(kv)]
    part_a2, part_a1 = attend(a2), attend(a1)
    b3 = along(after(b2, [part_a2, part_a1]), 1)
    part_b2 = attend(b2)
    a3 = along(after(a2, [part_b2, b3, b1, *kv[1:]]), 1)
    got_b2 = along(attend(b3), 1)
    got_a2 = along(attend(a3), 1)
    own_a, own_b = attend_own(a, pieces_a), attend_own(b, pieces_b)
    part_b2 = merge(part_b2, after(got_b2, [own_a, own_b]))
    from_b2 = along(part_b2, 2)
    from_b1 = along(after(attend(b1), [part_b2]), 1)
    part_a2 = merge(part_a2, got_a2)
    from_a2 = along(part_a2, 2)
    from_a1 = along(after(part_a1, [part_a2]), 1)
    out_b = end([own_b, from_b2, from_b1], pieces_b)
    out_a = end([own_a, from_a2, from_a1], pieces_a)
    results = [*out_a, *out_b]
    out = jax.ShapeDtypeStruct((step, shares * width), jnp.bfloat16)
    return call(place_kernel, results, [out], scalars=order)[0]


CHUNKS = 2


def power_of_two(n):
    return n & (n - 1) == 0


def body(queries, new_keys, new_values, cache_keys, cache_values, selection):
    qblocks, head_count, top_count = selection.shape
    seq_count = lax.axis_size("seq")
    shares = lax.axis_size("heads") * lax.axis_size("sub")
    every = top_count == cache_keys.shape[0] // BLOCK * seq_count and qblocks == 1
    fits = seq_count == 4 and power_of_two(shares) and shares % CHUNKS == 0
    if every and fits and 4 * head_count <= STAT:
        return dense_body(queries, new_keys, new_values, cache_keys, cache_values)
    return sparse_body(queries, new_keys, new_values, cache_keys, cache_values, selection)


def solution(mesh):
    in_specs = (
        P(("groups", "seq", "heads", "sub"), None),
        P(("groups", "seq", "heads", "sub"), None),
        P(("groups", "seq", "heads", "sub"), None),
        P(("groups", "seq"), ("heads", "sub")),
        P(("groups", "seq"), ("heads", "sub")),
        P(("groups", "seq"), ("heads", "sub"), None),
    )
    out_specs = P(("groups", "seq", "heads", "sub"), None)
    return jax.shard_map(body, mesh=mesh, in_specs=in_specs, out_specs=out_specs, check_vma=False)
```

```python
import functools
import math

import jax
import jax.numpy as jnp
from jax import lax
from jax.experimental import pallas as pl
from jax.experimental.pallas import tpu as pltpu
from jax.sharding import PartitionSpec as P

HD = 128
BLOCK = 512


def order_ranks(owners):
    length = owners.shape[-1]
    counter = jnp.arange(length)
    earlier = counter[None, :] < counter[:, None]
    same_owner = owners[..., :, None] == owners[..., None, :]
    return jnp.sum(jnp.logical_and(same_owner, earlier), axis=-1)


def one_hot(values, length):
    return (values[..., None] == jnp.arange(length)).astype(jnp.float32)


def own_partial(query_blocks, key_blocks, value_blocks, scaling):
    scores = (
        jnp.einsum("bqhd,bkhd->bhqk", query_blocks, key_blocks, preferred_element_type=jnp.float32)
        * scaling
    )
    length = query_blocks.shape[1]
    causal = jnp.arange(length)[:, None] >= jnp.arange(length)[None, :]
    scores = jnp.where(causal, scores, -jnp.inf)
    highest = jnp.max(scores, axis=-1)
    weights = jnp.exp(scores - highest[..., None])
    totals = jnp.sum(weights, axis=-1)
    mixed = jnp.einsum(
        "bhqk,bkhd->bhqd",
        weights.astype(jnp.bfloat16),
        value_blocks,
        preferred_element_type=jnp.float32,
    )
    return (mixed, highest, totals)


def tile_partial(query_blocks, tile_pair, scaling):
    head_size = query_blocks.shape[-1]
    scores = (
        jnp.einsum(
            "bqhd,bhkd->bhqk",
            query_blocks,
            tile_pair[..., :head_size],
            preferred_element_type=jnp.float32,
        )
        * scaling
    )
    highest = jnp.max(scores, axis=-1)
    weights = jnp.exp(scores - highest[..., None])
    totals = jnp.sum(weights, axis=-1)
    mixed = jnp.einsum(
        "bhqk,bhkd->bhqd",
        weights.astype(jnp.bfloat16),
        tile_pair[..., head_size:],
        preferred_element_type=jnp.float32,
    )
    return (mixed, highest, totals)


def merge_parts(parts):
    top = parts[0][1]
    for part in parts[1:]:
        top = jnp.maximum(top, part[1])
    numer = jnp.zeros(parts[0][0].shape, jnp.float32)
    denom = jnp.zeros(parts[0][2].shape, jnp.float32)
    for part in parts:
        factor = jnp.exp(part[1] - top)
        numer = numer + factor[..., None] * part[0]
        denom = denom + factor * part[2]
    return numer / denom[..., None]


def sparse_body(queries, new_keys, new_values, cache_keys, cache_values, selection):
    heads_q, heads_k, heads_v = (
        lax.all_to_all(queries, ("heads", "sub"), split_axis=1, concat_axis=0, tiled=True),
        lax.all_to_all(new_keys, ("heads", "sub"), split_axis=1, concat_axis=0, tiled=True),
        lax.all_to_all(new_values, ("heads", "sub"), split_axis=1, concat_axis=0, tiled=True),
    )
    qblocks, head_count, top_count = selection.shape
    head_size = HD
    scaling = head_size ** (-0.5)
    shaped = (qblocks, BLOCK, head_count, head_size)
    query_blocks = heads_q.reshape(shaped)
    own = own_partial(query_blocks, heads_k.reshape(shaped), heads_v.reshape(shaped), scaling)
    seq_count = lax.axis_size("seq")
    myself = lax.axis_index("seq")
    cache_blocks = cache_keys.shape[0] // BLOCK
    tile_count = cache_blocks * head_count
    request_count = qblocks * head_count * top_count
    capacity = -(-request_count // seq_count)
    requests_all = lax.all_gather(selection, "seq", axis=0, tiled=True).reshape(
        seq_count, request_count
    )
    head_of = jnp.arange(request_count) // top_count % head_count
    my_requests = selection.reshape(request_count)
    my_owner = my_requests // cache_blocks
    my_slot = my_owner * capacity + order_ranks(my_owner)
    key_tiles = cache_keys.reshape(cache_blocks, BLOCK, head_count, head_size).transpose(0, 2, 1, 3)
    value_tiles = cache_values.reshape(cache_blocks, BLOCK, head_count, head_size).transpose(
        0, 2, 1, 3
    )
    tile_set = jnp.concatenate([key_tiles, value_tiles], axis=-1).reshape(
        tile_count, BLOCK, 2 * head_size
    )
    their_owner = requests_all // cache_blocks
    local_tile = requests_all % cache_blocks * head_count + head_of[None, :]
    served = (their_owner == myself).astype(jnp.float32)
    slot_pick = one_hot(order_ranks(their_owner), capacity) * served[..., None]
    picking = jnp.einsum("erc,erl->ecl", slot_pick, one_hot(local_tile, tile_count)).astype(
        jnp.bfloat16
    )
    parts = [own]
    outgoing = jnp.einsum(
        "ecl,lkf->eckf", picking, tile_set, preferred_element_type=jnp.float32
    ).astype(jnp.bfloat16)
    incoming = lax.all_to_all(outgoing, "seq", split_axis=0, concat_axis=0, tiled=True)
    fetched = incoming.reshape(seq_count * capacity, BLOCK, 2 * head_size)[my_slot]
    fetched = fetched.reshape(qblocks, head_count, top_count, BLOCK, 2 * head_size)
    for turn in range(top_count):
        parts.append(tile_partial(query_blocks, fetched[:, :, turn], scaling))
    result = merge_parts(parts)
    result = (
        result.transpose(0, 2, 1, 3)
        .reshape(qblocks * BLOCK, head_count * head_size)
        .astype(jnp.bfloat16)
    )
    return lax.all_to_all(result, ("heads", "sub"), split_axis=0, concat_axis=1, tiled=True)


STAT = 16
UNIT = 32767.0
LEAST = 1.2e-34
C2 = math.log2(math.e) * HD**-0.5


def scores_of(q, k, mask=None):
    s = lax.dot_general(k, q, (((1,), (1,)), ((), ())), preferred_element_type=jnp.float32)
    return s if mask is None else jnp.where(mask, s, -jnp.inf)


def weights_of(s):
    m = jnp.max(s, axis=0, keepdims=True)
    p = jnp.exp2((s - m) * C2)
    return p.astype(jnp.bfloat16), m * C2, jnp.sum(p, axis=0, keepdims=True)


def values_of(v, w, v_dim):
    return lax.dot_general(v, w, (((v_dim,), (0,)), ((), ())), preferred_element_type=jnp.float32)


def attend(tiles):
    count = len(tiles)
    s, w, parts = {}, {}, []
    for t in range(count + 2):
        if t < count:
            s[t] = tiles[t][0]()
        if 1 <= t <= count:
            w[t - 1] = weights_of(s.pop(t - 1))
        if t >= 2:
            weights, m, total = w.pop(t - 2)
            parts.append((tiles[t - 2][1](weights), m, total))
    return parts


def join(parts):
    top = functools.reduce(jnp.maximum, [m for _, m, _ in parts])
    factors = [jnp.exp2(m - top) for _, m, _ in parts]
    numer = sum(f * o for f, (o, _, _) in zip(factors, parts))
    denom = sum(f * t for f, (_, _, t) in zip(factors, parts))
    return numer, top, denom


def put(out_ref, heads):
    width, rows = len(heads) * HD, heads[0][0].shape[1]
    at = lax.broadcasted_iota(jnp.int32, (STAT, rows), 0)
    stats = jnp.zeros((STAT, rows), jnp.float32)
    for h, (numer, top, denom) in enumerate(heads):
        most = jnp.maximum(jnp.max(jnp.abs(numer), axis=0, keepdims=True), LEAST)
        code = jnp.round(numer * (UNIT / most))
        out_ref[h * HD : (h + 1) * HD, :] = code.astype(jnp.int32).astype(jnp.int16)
        for j, value in enumerate((top + jnp.log2(denom), jnp.log2(most / (UNIT * denom)))):
            whole = jnp.floor(value)
            stats = jnp.where(at == 4 * h + 2 * j, whole, stats)
            stats = jnp.where(at == 4 * h + 2 * j + 1, jnp.round((value - whole) * UNIT), stats)
    out_ref[width : width + STAT, :] = stats.astype(jnp.int32).astype(jnp.int16)


def take(ref):
    width = ref.shape[0] - STAT
    stats = ref[width : width + STAT, :].astype(jnp.int32).astype(jnp.float32)
    heads = []
    for h in range(width // HD):
        code = ref[h * HD : (h + 1) * HD, :].astype(jnp.int32).astype(jnp.float32)
        weight = stats[4 * h : 4 * h + 1] + stats[4 * h + 1 : 4 * h + 2] * (1.0 / UNIT)
        unit = stats[4 * h + 2 : 4 * h + 3] + stats[4 * h + 3 : 4 * h + 4] * (1.0 / UNIT)
        heads.append((code, weight, unit))
    return heads


def join_taken(taken):
    top = functools.reduce(jnp.maximum, [w for _, w, _ in taken])
    numer = sum(code * jnp.exp2(w - top + unit) for code, w, unit in taken)
    denom = sum(jnp.exp2(w - top) for _, w, _ in taken)
    return numer, top, denom


def cached_tiles(q_of, ck_ref, cvt_ref, h):
    cols = slice(h * HD, (h + 1) * HD)
    tiles = []
    for b in range(ck_ref.shape[0] // BLOCK):
        rows = slice(b * BLOCK, (b + 1) * BLOCK)
        tiles.append(
            (
                lambda rows=rows: scores_of(q_of(cols), ck_ref[rows, cols]),
                lambda w, rows=rows: values_of(cvt_ref[cols, rows], w, 1),
            )
        )
    return tiles


def attend_heads(tiles_of_heads):
    parts = attend([t for tiles in tiles_of_heads for t in tiles])
    heads = []
    for tiles in tiles_of_heads:
        heads.append(join(parts[: len(tiles)]))
        parts = parts[len(tiles) :]
    return heads


def cached_kernel(q_ref, ck_ref, cvt_ref, out_ref):
    heads = range(ck_ref.shape[1] // HD)
    q_of = lambda cols: q_ref[:, cols]
    put(out_ref, attend_heads([cached_tiles(q_of, ck_ref, cvt_ref, h) for h in heads]))


def own_kernel(mine, order_ref, *refs):
    q_ref, *kv_refs, ck_ref, cvt_ref, out_ref = refs
    width = ck_ref.shape[1]
    rows = q_ref.shape[0]
    step = kv_refs[0].shape[0]

    def positions(shape, axis, pieces):
        at = lax.broadcasted_iota(jnp.int32, shape, axis)
        place = jnp.zeros(shape, jnp.int32)
        for i, d in enumerate(pieces):
            place = jnp.where(at // step == i, order_ref[d] * step + at % step, place)
        return place

    shape = (step * len(kv_refs), rows)
    mask = positions(shape, 1, mine) >= positions(shape, 0, range(len(kv_refs)))
    q_of = lambda cols: q_ref[:, cols]
    heads = []
    for h in range(width // HD):
        cols = slice(h * HD, (h + 1) * HD)
        vcols = slice(width + h * HD, width + (h + 1) * HD)
        own = (
            lambda cols=cols: scores_of(
                q_ref[:, cols], jnp.concatenate([r[:, cols] for r in kv_refs], axis=0), mask
            ),
            lambda w, vcols=vcols: values_of(
                jnp.concatenate([r[:, vcols] for r in kv_refs], axis=0), w, 0
            ),
        )
        heads.append([own] + cached_tiles(q_of, ck_ref, cvt_ref, h))
    put(out_ref, attend_heads(heads))


def merge_kernel(*refs):
    *in_refs, out_ref = refs
    put(out_ref, [join_taken(taken) for taken in zip(*[take(r) for r in in_refs])])


def final_kernel(count, *refs):
    in_refs, out_refs = refs[:count], refs[count:]
    step = out_refs[0].shape[0]
    for h, taken in enumerate(zip(*[take(r) for r in in_refs])):
        numer, _, denom = join_taken(taken)
        value = jnp.transpose(numer * (1.0 / denom)).astype(jnp.bfloat16)
        for i, out_ref in enumerate(out_refs):
            out_ref[:, h * HD : (h + 1) * HD] = value[i * step : (i + 1) * step]


def pick_kernel(pieces, count, order_ref, *refs):
    in_refs, out_refs = refs[:count], refs[len(refs) - len(pieces) :]
    width = out_refs[0].shape[1] // len(in_refs)
    for d, out_ref in zip(pieces, out_refs):
        start = pl.multiple_of(order_ref[d] * width, width)
        for i, ref in enumerate(in_refs):
            out_ref[:, i * width : (i + 1) * width] = ref[:, pl.ds(start, width)]


def stack_kernel(count, *refs):
    out_ref = refs[-1]
    step = refs[0].shape[0]
    for i in range(count):
        out_ref[i * step : (i + 1) * step, :] = refs[i][...]


def place_kernel(order_ref, *refs):
    *pieces, out_ref = refs
    width = pieces[0].shape[1]
    for d, piece in enumerate(pieces):
        start = pl.multiple_of(order_ref[d] * width, width)
        out_ref[:, pl.ds(start, width)] = piece[...]


def call(kernel, arrays, outs, flops=0, exps=0, scalars=None, unread=()):
    moved = sum(a.size * a.dtype.itemsize for a in arrays)
    moved += sum(math.prod(o.shape) * o.dtype.itemsize for o in outs)
    first = [] if scalars is None else [scalars]
    return pl.pallas_call(
        kernel,
        out_shape=outs,
        in_specs=[pl.BlockSpec(memory_space=pltpu.SMEM)] * len(first)
        + [pl.BlockSpec(memory_space=pltpu.VMEM)] * len(arrays)
        + [pl.BlockSpec(memory_space=pl.ANY)] * len(unread),
        out_specs=[pl.BlockSpec(memory_space=pltpu.VMEM)] * len(outs),
        compiler_params=pltpu.CompilerParams(vmem_limit_bytes=16 * 1024 * 1024),
        cost_estimate=pl.CostEstimate(flops=flops, bytes_accessed=moved, transcendentals=exps),
    )(*first, *arrays, *unread)


def dense_body(queries, new_keys, new_values, cache_keys, cache_values):
    seq_count = lax.axis_size("seq")
    shares = lax.axis_size("heads") * lax.axis_size("sub")
    me = lax.axis_index("heads") * lax.axis_size("sub") + lax.axis_index("sub")
    step, width = queries.shape[0], queries.shape[1] // shares
    cached = cache_keys.shape[0]
    each = shares // CHUNKS
    rows = each * step
    chunk = jax.ShapeDtypeStruct((rows, width), jnp.bfloat16)
    piece = jax.ShapeDtypeStruct((step, width), jnp.bfloat16)
    pair = jax.ShapeDtypeStruct((step, 2 * width), jnp.bfloat16)
    packed = jax.ShapeDtypeStruct((width + STAT, rows), jnp.int16)
    tile_flops = 4 * rows * cached * width
    tile_exps = rows * cached * (width // HD)

    def swap(x, d):
        return lax.ppermute(x, ("heads", "sub"), [(i, i ^ d) for i in range(shares)])

    def along(x, bit):
        return lax.ppermute(x, "seq", [(i, i ^ bit) for i in range(seq_count)])

    def after(x, unread):
        like = jax.ShapeDtypeStruct(x.shape, x.dtype)
        return call(functools.partial(stack_kernel, 1), [x], [like], unread=unread)[0] if unread else x

    order = jnp.stack([me ^ d for d in range(shares)]).astype(jnp.int32)
    cache_vt = cache_values.T
    context = [cache_keys, cache_vt]

    def attend(q):
        return call(cached_kernel, [q, *context], [packed], tile_flops, tile_exps)[0]

    def attend_own(q, pieces):
        return call(
            functools.partial(own_kernel, pieces),
            [q, *kv, *context],
            [packed],
            tile_flops * 3 // 2,
            tile_exps * 3 // 2,
            order,
        )[0]

    def merge(mine, got):
        return call(merge_kernel, [mine, got], [packed])[0]

    def end(parts, pieces):
        ended = call(functools.partial(final_kernel, len(parts)), parts, [piece] * each)
        return [swap(x, d) if d else x for x, d in zip(ended, pieces)]

    pieces_a, pieces_b = range(each), range(each, shares)
    pick = functools.partial(pick_kernel, pieces_a, 1)
    q = call(pick, [queries], [piece] * each, scalars=order)
    q = [swap(x, d) if d else x for x, d in zip(q, pieces_a)]
    a = call(functools.partial(stack_kernel, each), q, [chunk])[0]
    a2, a1 = along(a, 2), along(a, 1)
    pick = functools.partial(pick_kernel, pieces_b, 1)
    q = call(pick, [queries], [piece] * each, scalars=order)
    q = [swap(x if d == each else after(x, [cache_vt]), d) for x, d in zip(q, pieces_b)]
    b = call(functools.partial(stack_kernel, each), q, [chunk])[0]
    b2, b1 = along(b, 2), along(b, 1)
    pick = functools.partial(pick_kernel, range(shares), 2)
    kv = call(pick, [new_keys, new_values], [pair] * shares, scalars=order, unread=[b])
    kv = [swap(x, d) if d else x for d, x in enumerate(kv)]
    part_a2, part_a1 = attend(a2), attend(a1)
    b3 = along(after(b2, [part_a2, part_a1]), 1)
    part_b2 = attend(b2)
    own_a, own_b = attend_own(a, pieces_a), attend_own(b, pieces_b)
    a3 = along(after(a2, [part_b2, own_a, b3, b1]), 1)
    got_b2 = along(attend(b3), 1)
    got_a2 = along(after(attend(a3), [own_b]), 1)
    part_b2 = merge(part_b2, got_b2)
    from_b2 = along(part_b2, 2)
    from_b1 = along(after(attend(b1), [part_b2]), 1)
    part_a2 = merge(part_a2, got_a2)
    from_a2 = along(part_a2, 2)
    from_a1 = along(after(part_a1, [part_a2]), 1)
    out_b = end([own_b, from_b2, from_b1], pieces_b)
    out_a = end([own_a, from_a2, from_a1], pieces_a)
    results = [*out_a, *out_b]
    out = jax.ShapeDtypeStruct((step, shares * width), jnp.bfloat16)
    return call(place_kernel, results, [out], scalars=order)[0]


CHUNKS = 2


def power_of_two(n):
    return n & (n - 1) == 0


def body(queries, new_keys, new_values, cache_keys, cache_values, selection):
    qblocks, head_count, top_count = selection.shape
    seq_count = lax.axis_size("seq")
    shares = lax.axis_size("heads") * lax.axis_size("sub")
    every = top_count == cache_keys.shape[0] // BLOCK * seq_count and qblocks == 1
    fits = seq_count == 4 and power_of_two(shares) and shares % CHUNKS == 0
    if every and fits and 4 * head_count <= STAT:
        return dense_body(queries, new_keys, new_values, cache_keys, cache_values)
    return sparse_body(queries, new_keys, new_values, cache_keys, cache_values, selection)


def solution(mesh):
    in_specs = (
        P(("groups", "seq", "heads", "sub"), None),
        P(("groups", "seq", "heads", "sub"), None),
        P(("groups", "seq", "heads", "sub"), None),
        P(("groups", "seq"), ("heads", "sub")),
        P(("groups", "seq"), ("heads", "sub")),
        P(("groups", "seq"), ("heads", "sub"), None),
    )
    out_specs = P(("groups", "seq", "heads", "sub"), None)
    return jax.shard_map(body, mesh=mesh, in_specs=in_specs, out_specs=out_specs, check_vma=False)
```

```python
import functools
import math

import jax
import jax.numpy as jnp
from jax import lax
from jax.experimental import pallas as pl
from jax.experimental.pallas import tpu as pltpu
from jax.sharding import PartitionSpec as P

HD = 128
BLOCK = 512


def order_ranks(owners):
    length = owners.shape[-1]
    counter = jnp.arange(length)
    earlier = counter[None, :] < counter[:, None]
    same_owner = owners[..., :, None] == owners[..., None, :]
    return jnp.sum(jnp.logical_and(same_owner, earlier), axis=-1)


def one_hot(values, length):
    return (values[..., None] == jnp.arange(length)).astype(jnp.float32)


def own_partial(query_blocks, key_blocks, value_blocks, scaling):
    scores = (
        jnp.einsum("bqhd,bkhd->bhqk", query_blocks, key_blocks, preferred_element_type=jnp.float32)
        * scaling
    )
    length = query_blocks.shape[1]
    causal = jnp.arange(length)[:, None] >= jnp.arange(length)[None, :]
    scores = jnp.where(causal, scores, -jnp.inf)
    highest = jnp.max(scores, axis=-1)
    weights = jnp.exp(scores - highest[..., None])
    totals = jnp.sum(weights, axis=-1)
    mixed = jnp.einsum(
        "bhqk,bkhd->bhqd",
        weights.astype(jnp.bfloat16),
        value_blocks,
        preferred_element_type=jnp.float32,
    )
    return (mixed, highest, totals)


def tile_partial(query_blocks, tile_pair, scaling):
    head_size = query_blocks.shape[-1]
    scores = (
        jnp.einsum(
            "bqhd,bhkd->bhqk",
            query_blocks,
            tile_pair[..., :head_size],
            preferred_element_type=jnp.float32,
        )
        * scaling
    )
    highest = jnp.max(scores, axis=-1)
    weights = jnp.exp(scores - highest[..., None])
    totals = jnp.sum(weights, axis=-1)
    mixed = jnp.einsum(
        "bhqk,bhkd->bhqd",
        weights.astype(jnp.bfloat16),
        tile_pair[..., head_size:],
        preferred_element_type=jnp.float32,
    )
    return (mixed, highest, totals)


def merge_parts(parts):
    top = parts[0][1]
    for part in parts[1:]:
        top = jnp.maximum(top, part[1])
    numer = jnp.zeros(parts[0][0].shape, jnp.float32)
    denom = jnp.zeros(parts[0][2].shape, jnp.float32)
    for part in parts:
        factor = jnp.exp(part[1] - top)
        numer = numer + factor[..., None] * part[0]
        denom = denom + factor * part[2]
    return numer / denom[..., None]


def sparse_body(queries, new_keys, new_values, cache_keys, cache_values, selection):
    heads_q, heads_k, heads_v = (
        lax.all_to_all(queries, ("heads", "sub"), split_axis=1, concat_axis=0, tiled=True),
        lax.all_to_all(new_keys, ("heads", "sub"), split_axis=1, concat_axis=0, tiled=True),
        lax.all_to_all(new_values, ("heads", "sub"), split_axis=1, concat_axis=0, tiled=True),
    )
    qblocks, head_count, top_count = selection.shape
    head_size = HD
    scaling = head_size ** (-0.5)
    shaped = (qblocks, BLOCK, head_count, head_size)
    query_blocks = heads_q.reshape(shaped)
    own = own_partial(query_blocks, heads_k.reshape(shaped), heads_v.reshape(shaped), scaling)
    seq_count = lax.axis_size("seq")
    myself = lax.axis_index("seq")
    cache_blocks = cache_keys.shape[0] // BLOCK
    tile_count = cache_blocks * head_count
    request_count = qblocks * head_count * top_count
    capacity = -(-request_count // seq_count)
    requests_all = lax.all_gather(selection, "seq", axis=0, tiled=True).reshape(
        seq_count, request_count
    )
    head_of = jnp.arange(request_count) // top_count % head_count
    my_requests = selection.reshape(request_count)
    my_owner = my_requests // cache_blocks
    my_slot = my_owner * capacity + order_ranks(my_owner)
    key_tiles = cache_keys.reshape(cache_blocks, BLOCK, head_count, head_size).transpose(0, 2, 1, 3)
    value_tiles = cache_values.reshape(cache_blocks, BLOCK, head_count, head_size).transpose(
        0, 2, 1, 3
    )
    tile_set = jnp.concatenate([key_tiles, value_tiles], axis=-1).reshape(
        tile_count, BLOCK, 2 * head_size
    )
    their_owner = requests_all // cache_blocks
    local_tile = requests_all % cache_blocks * head_count + head_of[None, :]
    served = (their_owner == myself).astype(jnp.float32)
    slot_pick = one_hot(order_ranks(their_owner), capacity) * served[..., None]
    picking = jnp.einsum("erc,erl->ecl", slot_pick, one_hot(local_tile, tile_count)).astype(
        jnp.bfloat16
    )
    parts = [own]
    outgoing = jnp.einsum(
        "ecl,lkf->eckf", picking, tile_set, preferred_element_type=jnp.float32
    ).astype(jnp.bfloat16)
    incoming = lax.all_to_all(outgoing, "seq", split_axis=0, concat_axis=0, tiled=True)
    fetched = incoming.reshape(seq_count * capacity, BLOCK, 2 * head_size)[my_slot]
    fetched = fetched.reshape(qblocks, head_count, top_count, BLOCK, 2 * head_size)
    for turn in range(top_count):
        parts.append(tile_partial(query_blocks, fetched[:, :, turn], scaling))
    result = merge_parts(parts)
    result = (
        result.transpose(0, 2, 1, 3)
        .reshape(qblocks * BLOCK, head_count * head_size)
        .astype(jnp.bfloat16)
    )
    return lax.all_to_all(result, ("heads", "sub"), split_axis=0, concat_axis=1, tiled=True)


STAT = 16
UNIT = 32767.0
LEAST = 1.2e-34
NEVER = -1.0e9
C2 = math.log2(math.e) * HD**-0.5


def scores_of(q, k, mask=None):
    s = lax.dot_general(k, q, (((1,), (1,)), ((), ())), preferred_element_type=jnp.float32)
    return s if mask is None else jnp.where(mask, s, -jnp.inf)


def weights_of(s):
    m = jnp.max(s, axis=0, keepdims=True)
    p = jnp.exp2((s - m) * C2)
    return p.astype(jnp.bfloat16), m * C2, jnp.sum(p, axis=0, keepdims=True)


def values_of(v, w, v_dim):
    return lax.dot_general(v, w, (((v_dim,), (0,)), ((), ())), preferred_element_type=jnp.float32)


def attend(tiles):
    count = len(tiles)
    s, w, parts = {}, {}, []
    for t in range(count + 2):
        if t < count:
            s[t] = tiles[t][0]()
        if 1 <= t <= count:
            w[t - 1] = weights_of(s.pop(t - 1))
        if t >= 2:
            weights, m, total = w.pop(t - 2)
            parts.append((tiles[t - 2][1](weights), m, total))
    return parts


def join(parts):
    top = functools.reduce(jnp.maximum, [m for _, m, _ in parts])
    factors = [jnp.exp2(m - top) for _, m, _ in parts]
    numer = sum(f * o for f, (o, _, _) in zip(factors, parts))
    denom = sum(f * t for f, (_, _, t) in zip(factors, parts))
    return numer, top, denom


def put(out_ref, heads):
    width, rows = len(heads) * HD, heads[0][0].shape[1]
    at = lax.broadcasted_iota(jnp.int32, (STAT, rows), 0)
    stats = jnp.zeros((STAT, rows), jnp.float32)
    for h, (numer, top, denom) in enumerate(heads):
        most = jnp.maximum(jnp.max(jnp.abs(numer), axis=0, keepdims=True), LEAST)
        code = jnp.round(numer * (UNIT / most))
        out_ref[h * HD : (h + 1) * HD, :] = code.astype(jnp.int32).astype(jnp.int16)
        for j, value in enumerate((top + jnp.log2(denom), jnp.log2(most / (UNIT * denom)))):
            whole = jnp.floor(value)
            stats = jnp.where(at == 4 * h + 2 * j, whole, stats)
            stats = jnp.where(at == 4 * h + 2 * j + 1, jnp.round((value - whole) * UNIT), stats)
    out_ref[width : width + STAT, :] = stats.astype(jnp.int32).astype(jnp.int16)


def take(ref, valid=None):
    width = ref.shape[0] - STAT
    stats = ref[width : width + STAT, :].astype(jnp.int32).astype(jnp.float32)
    heads = []
    for h in range(width // HD):
        code = ref[h * HD : (h + 1) * HD, :].astype(jnp.int32).astype(jnp.float32)
        weight = stats[4 * h : 4 * h + 1] + stats[4 * h + 1 : 4 * h + 2] * (1.0 / UNIT)
        unit = stats[4 * h + 2 : 4 * h + 3] + stats[4 * h + 3 : 4 * h + 4] * (1.0 / UNIT)
        if valid is not None:
            weight = jnp.where(valid, weight, NEVER)
        heads.append((code, weight, unit))
    return heads


def join_taken(taken):
    top = functools.reduce(jnp.maximum, [w for _, w, _ in taken])
    numer = sum(code * jnp.exp2(w - top + unit) for code, w, unit in taken)
    denom = sum(jnp.exp2(w - top) for _, w, _ in taken)
    return numer, top, denom


def cached_tiles(q_of, ck_ref, cvt_ref, h):
    cols = slice(h * HD, (h + 1) * HD)
    tiles = []
    for b in range(ck_ref.shape[0] // BLOCK):
        rows = slice(b * BLOCK, (b + 1) * BLOCK)
        tiles.append(
            (
                lambda rows=rows: scores_of(q_of(cols), ck_ref[rows, cols]),
                lambda w, rows=rows: values_of(cvt_ref[cols, rows], w, 1),
            )
        )
    return tiles


def attend_heads(tiles_of_heads):
    parts = attend([t for tiles in tiles_of_heads for t in tiles])
    heads = []
    for tiles in tiles_of_heads:
        heads.append(join(parts[: len(tiles)]))
        parts = parts[len(tiles) :]
    return heads


def cached_kernel(q_ref, ck_ref, cvt_ref, out_ref):
    heads = range(ck_ref.shape[1] // HD)
    q_of = lambda cols: q_ref[:, cols]
    put(out_ref, attend_heads([cached_tiles(q_of, ck_ref, cvt_ref, h) for h in heads]))


def either_kernel(middle_ref, a_ref, b_ref, ck_ref, cvt_ref, out_ref):
    middle = middle_ref[0] > 0
    heads = range(ck_ref.shape[1] // HD)
    q_of = lambda cols: jnp.where(middle, a_ref[:, cols], b_ref[:, cols])
    put(out_ref, attend_heads([cached_tiles(q_of, ck_ref, cvt_ref, h) for h in heads]))


def own_kernel(mine, order_ref, *refs):
    q_ref, *kv_refs, ck_ref, cvt_ref, out_ref = refs
    width = ck_ref.shape[1]
    rows = q_ref.shape[0]
    step = kv_refs[0].shape[0]

    def positions(shape, axis, pieces):
        at = lax.broadcasted_iota(jnp.int32, shape, axis)
        place = jnp.zeros(shape, jnp.int32)
        for i, d in enumerate(pieces):
            place = jnp.where(at // step == i, order_ref[d] * step + at % step, place)
        return place

    shape = (step * len(kv_refs), rows)
    mask = positions(shape, 1, mine) >= positions(shape, 0, range(len(kv_refs)))
    q_of = lambda cols: q_ref[:, cols]
    heads = []
    for h in range(width // HD):
        cols = slice(h * HD, (h + 1) * HD)
        vcols = slice(width + h * HD, width + (h + 1) * HD)
        own = (
            lambda cols=cols: scores_of(
                q_ref[:, cols], jnp.concatenate([r[:, cols] for r in kv_refs], axis=0), mask
            ),
            lambda w, vcols=vcols: values_of(
                jnp.concatenate([r[:, vcols] for r in kv_refs], axis=0), w, 0
            ),
        )
        heads.append([own] + cached_tiles(q_of, ck_ref, cvt_ref, h))
    put(out_ref, attend_heads(heads))


def merge_kernel(mine_ref, got_ref, out_ref):
    put(out_ref, [join_taken(pair) for pair in zip(take(mine_ref), take(got_ref))])


def middle_merge_kernel(middle_ref, mine_ref, got_ref, out_ref):
    taken = zip(take(mine_ref), take(got_ref, middle_ref[0] > 0))
    put(out_ref, [join_taken(pair) for pair in taken])


def final_kernel(own_ref, x_ref, y_ref, *out_refs):
    step = out_refs[0].shape[0]
    for h, taken in enumerate(zip(take(own_ref), take(x_ref), take(y_ref))):
        numer, _, denom = join_taken(taken)
        value = jnp.transpose(numer * (1.0 / denom)).astype(jnp.bfloat16)
        for i, out_ref in enumerate(out_refs):
            out_ref[:, h * HD : (h + 1) * HD] = value[i * step : (i + 1) * step]


def pick_kernel(pieces, order_ref, *refs):
    in_refs, out_refs = refs[: len(refs) - len(pieces)], refs[len(refs) - len(pieces) :]
    width = out_refs[0].shape[1] // len(in_refs)
    for d, out_ref in zip(pieces, out_refs):
        start = pl.multiple_of(order_ref[d] * width, width)
        for i, ref in enumerate(in_refs):
            out_ref[:, i * width : (i + 1) * width] = ref[:, pl.ds(start, width)]


def stack_kernel(*refs):
    *in_refs, out_ref = refs
    step = in_refs[0].shape[0]
    for i, ref in enumerate(in_refs):
        out_ref[i * step : (i + 1) * step, :] = ref[...]


def place_kernel(order_ref, *refs):
    *pieces, out_ref = refs
    width = pieces[0].shape[1]
    for d, piece in enumerate(pieces):
        start = pl.multiple_of(order_ref[d] * width, width)
        out_ref[:, pl.ds(start, width)] = piece[...]


def call(kernel, arrays, outs, flops=0, exps=0, scalars=None, unread=()):
    moved = sum(a.size * a.dtype.itemsize for a in arrays)
    moved += sum(math.prod(o.shape) * o.dtype.itemsize for o in outs)
    first = [] if scalars is None else [scalars]
    read = len(first) + len(arrays)

    def without_unread(*refs):
        kernel(*refs[:read], *refs[read + len(unread) :])

    return pl.pallas_call(
        without_unread,
        out_shape=outs,
        in_specs=[pl.BlockSpec(memory_space=pltpu.SMEM)] * len(first)
        + [pl.BlockSpec(memory_space=pltpu.VMEM)] * len(arrays)
        + [pl.BlockSpec(memory_space=pl.ANY)] * len(unread),
        out_specs=[pl.BlockSpec(memory_space=pltpu.VMEM)] * len(outs),
        compiler_params=pltpu.CompilerParams(vmem_limit_bytes=16 * 1024 * 1024),
        cost_estimate=pl.CostEstimate(flops=flops, bytes_accessed=moved, transcendentals=exps),
    )(*first, *arrays, *unread)


def after(x, unread):
    return call(stack_kernel, [x], [jax.ShapeDtypeStruct(x.shape, x.dtype)], unread=unread)[0]


def flip(x, bits):
    return lax.ppermute(x, "seq", [(i, i ^ bits) for i in range(4)])


def across(x):
    return lax.ppermute(x, "seq", [(1, 2), (2, 1)])


def outward(x):
    return lax.ppermute(x, "seq", [(1, 0), (2, 3)])


def inward(x):
    return lax.ppermute(x, "seq", [(0, 1), (3, 2)])


def dense_body(queries, new_keys, new_values, cache_keys, cache_values):
    s = lax.axis_index("seq")
    shares = lax.axis_size("heads") * lax.axis_size("sub")
    me = lax.axis_index("heads") * lax.axis_size("sub") + lax.axis_index("sub")
    step, width = queries.shape[0], queries.shape[1] // shares
    half, cached = shares // 2, cache_keys.shape[0]
    rows = half * step
    piece = jax.ShapeDtypeStruct((step, width), jnp.bfloat16)
    pair = jax.ShapeDtypeStruct((step, 2 * width), jnp.bfloat16)
    chunk = [jax.ShapeDtypeStruct((rows, width), jnp.bfloat16)]
    packed = [jax.ShapeDtypeStruct((width + STAT, rows), jnp.int16)]
    cost = {"flops": 4 * rows * cached * width, "exps": rows * cached * (width // HD)}
    middle = jnp.logical_and(s > 0, s < 3).astype(jnp.int32).reshape(1)
    order = jnp.stack([me ^ d for d in range(shares)]).astype(jnp.int32)
    pieces_a, pieces_b = range(half), range(half, shares)
    pick = functools.partial(pick_kernel, range(shares))
    cache_vt = cache_values.T
    context = [cache_keys, cache_vt]

    def swap(x, d):
        return lax.ppermute(x, ("heads", "sub"), [(i, i ^ d) for i in range(shares)]) if d else x

    def attend(q):
        return call(cached_kernel, [q, *context], packed, **cost)[0]

    def attend_either(in_middle, at_end, unread):
        arrays = [in_middle, at_end, *context]
        return call(either_kernel, arrays, packed, scalars=middle, unread=unread, **cost)[0]

    def attend_own(q, pieces, unread):
        more = {name: value * 3 // 2 for name, value in cost.items()}
        kernel = functools.partial(own_kernel, pieces)
        arrays = [q, *kv, *context]
        return call(kernel, arrays, packed, scalars=order, unread=unread, **more)[0]

    def merge(mine, got):
        return call(merge_kernel, [mine, got], packed)[0]

    def merge_in_middle(mine, got):
        return call(middle_merge_kernel, [mine, got], packed, scalars=middle)[0]

    def end(own, x, y, pieces):
        ended = call(final_kernel, [own, x, y], [piece] * half)
        return [swap(e, d) for e, d in zip(ended, pieces)]

    pick_some = lambda pieces: functools.partial(pick_kernel, pieces)
    q = call(pick_some(pieces_a), [queries], [piece] * half, scalars=order)
    a = call(stack_kernel, [swap(x, d) for x, d in zip(q, pieces_a)], chunk)[0]
    a3, a1 = flip(a, 3), flip(a, 1)
    q = call(pick_some(pieces_b), [queries], [piece] * half, scalars=order)
    q = [x if d == half else after(x, [cache_vt]) for x, d in zip(q, pieces_b)]
    b = call(stack_kernel, [swap(x, d) for x, d in zip(q, pieces_b)], chunk)[0]
    b2, b1 = flip(b, 2), flip(b, 1)
    kv = call(pick, [new_keys, new_values], [pair] * shares, scalars=order, unread=[b])
    kv = [swap(x, d) for d, x in enumerate(kv)]

    part_a3, part_a1 = attend(a3), attend(a1)
    b3 = flip(after(b2, [part_a3, part_a1]), 1)
    a2_middle, a2_end = across(after(a1, [b2])), outward(after(a3, [b2]))
    part_b2 = attend(b2)
    got_inward, got_across = inward(part_b2), across(part_b2)
    part_b1 = attend(b1)
    got_a2 = flip(after(part_a3, [part_b1, *kv[1:]]), 1)
    part_b3 = merge_in_middle(attend(b3), got_inward)
    from_b3 = flip(part_b3, 3)
    part_b1 = merge_in_middle(part_b1, got_across)
    from_b1 = flip(part_b1, 1)
    own_a, own_b = attend_own(a, pieces_a, [part_b1]), attend_own(b, pieces_b, [part_b1])
    part_a2 = merge(attend_either(a2_middle, a2_end, [part_b3]), after(got_a2, [own_b]))
    from_a2 = flip(part_a2, 2)
    from_a1 = flip(after(part_a1, [part_a2]), 1)

    out_b = end(own_b, from_b3, from_b1, pieces_b)
    out_a = end(own_a, from_a2, from_a1, pieces_a)
    out = jax.ShapeDtypeStruct((step, shares * width), jnp.bfloat16)
    return call(place_kernel, [*out_a, *out_b], [out], scalars=order)[0]


def power_of_two(n):
    return n & (n - 1) == 0


def body(queries, new_keys, new_values, cache_keys, cache_values, selection):
    qblocks, head_count, top_count = selection.shape
    seq_count = lax.axis_size("seq")
    shares = lax.axis_size("heads") * lax.axis_size("sub")
    every = top_count == cache_keys.shape[0] // BLOCK * seq_count and qblocks == 1
    fits = seq_count == 4 and power_of_two(shares) and shares > 1
    if every and fits and 4 * head_count <= STAT:
        return dense_body(queries, new_keys, new_values, cache_keys, cache_values)
    return sparse_body(queries, new_keys, new_values, cache_keys, cache_values, selection)


def solution(mesh):
    in_specs = (
        P(("groups", "seq", "heads", "sub"), None),
        P(("groups", "seq", "heads", "sub"), None),
        P(("groups", "seq", "heads", "sub"), None),
        P(("groups", "seq"), ("heads", "sub")),
        P(("groups", "seq"), ("heads", "sub")),
        P(("groups", "seq"), ("heads", "sub"), None),
    )
    out_specs = P(("groups", "seq", "heads", "sub"), None)
    return jax.shard_map(body, mesh=mesh, in_specs=in_specs, out_specs=out_specs, check_vma=False)
```

```python
import functools
import math

import jax
import jax.numpy as jnp
from jax import lax
from jax.experimental import pallas as pl
from jax.experimental.pallas import tpu as pltpu
from jax.sharding import PartitionSpec as P

HD = 128
BLOCK = 512


def order_ranks(owners):
    length = owners.shape[-1]
    counter = jnp.arange(length)
    earlier = counter[None, :] < counter[:, None]
    same_owner = owners[..., :, None] == owners[..., None, :]
    return jnp.sum(jnp.logical_and(same_owner, earlier), axis=-1)


def one_hot(values, length):
    return (values[..., None] == jnp.arange(length)).astype(jnp.float32)


def own_partial(query_blocks, key_blocks, value_blocks, scaling):
    scores = (
        jnp.einsum("bqhd,bkhd->bhqk", query_blocks, key_blocks, preferred_element_type=jnp.float32)
        * scaling
    )
    length = query_blocks.shape[1]
    causal = jnp.arange(length)[:, None] >= jnp.arange(length)[None, :]
    scores = jnp.where(causal, scores, -jnp.inf)
    highest = jnp.max(scores, axis=-1)
    weights = jnp.exp(scores - highest[..., None])
    totals = jnp.sum(weights, axis=-1)
    mixed = jnp.einsum(
        "bhqk,bkhd->bhqd",
        weights.astype(jnp.bfloat16),
        value_blocks,
        preferred_element_type=jnp.float32,
    )
    return (mixed, highest, totals)


def tile_partial(query_blocks, tile_pair, scaling):
    head_size = query_blocks.shape[-1]
    scores = (
        jnp.einsum(
            "bqhd,bhkd->bhqk",
            query_blocks,
            tile_pair[..., :head_size],
            preferred_element_type=jnp.float32,
        )
        * scaling
    )
    highest = jnp.max(scores, axis=-1)
    weights = jnp.exp(scores - highest[..., None])
    totals = jnp.sum(weights, axis=-1)
    mixed = jnp.einsum(
        "bhqk,bhkd->bhqd",
        weights.astype(jnp.bfloat16),
        tile_pair[..., head_size:],
        preferred_element_type=jnp.float32,
    )
    return (mixed, highest, totals)


def merge_parts(parts):
    top = parts[0][1]
    for part in parts[1:]:
        top = jnp.maximum(top, part[1])
    numer = jnp.zeros(parts[0][0].shape, jnp.float32)
    denom = jnp.zeros(parts[0][2].shape, jnp.float32)
    for part in parts:
        factor = jnp.exp(part[1] - top)
        numer = numer + factor[..., None] * part[0]
        denom = denom + factor * part[2]
    return numer / denom[..., None]


def sparse_body(queries, new_keys, new_values, cache_keys, cache_values, selection):
    heads_q, heads_k, heads_v = (
        lax.all_to_all(queries, ("heads", "sub"), split_axis=1, concat_axis=0, tiled=True),
        lax.all_to_all(new_keys, ("heads", "sub"), split_axis=1, concat_axis=0, tiled=True),
        lax.all_to_all(new_values, ("heads", "sub"), split_axis=1, concat_axis=0, tiled=True),
    )
    qblocks, head_count, top_count = selection.shape
    head_size = HD
    scaling = head_size ** (-0.5)
    shaped = (qblocks, BLOCK, head_count, head_size)
    query_blocks = heads_q.reshape(shaped)
    own = own_partial(query_blocks, heads_k.reshape(shaped), heads_v.reshape(shaped), scaling)
    seq_count = lax.axis_size("seq")
    myself = lax.axis_index("seq")
    cache_blocks = cache_keys.shape[0] // BLOCK
    tile_count = cache_blocks * head_count
    request_count = qblocks * head_count * top_count
    capacity = -(-request_count // seq_count)
    requests_all = lax.all_gather(selection, "seq", axis=0, tiled=True).reshape(
        seq_count, request_count
    )
    head_of = jnp.arange(request_count) // top_count % head_count
    my_requests = selection.reshape(request_count)
    my_owner = my_requests // cache_blocks
    my_slot = my_owner * capacity + order_ranks(my_owner)
    key_tiles = cache_keys.reshape(cache_blocks, BLOCK, head_count, head_size).transpose(0, 2, 1, 3)
    value_tiles = cache_values.reshape(cache_blocks, BLOCK, head_count, head_size).transpose(
        0, 2, 1, 3
    )
    tile_set = jnp.concatenate([key_tiles, value_tiles], axis=-1).reshape(
        tile_count, BLOCK, 2 * head_size
    )
    their_owner = requests_all // cache_blocks
    local_tile = requests_all % cache_blocks * head_count + head_of[None, :]
    served = (their_owner == myself).astype(jnp.float32)
    slot_pick = one_hot(order_ranks(their_owner), capacity) * served[..., None]
    picking = jnp.einsum("erc,erl->ecl", slot_pick, one_hot(local_tile, tile_count)).astype(
        jnp.bfloat16
    )
    parts = [own]
    outgoing = jnp.einsum(
        "ecl,lkf->eckf", picking, tile_set, preferred_element_type=jnp.float32
    ).astype(jnp.bfloat16)
    incoming = lax.all_to_all(outgoing, "seq", split_axis=0, concat_axis=0, tiled=True)
    fetched = incoming.reshape(seq_count * capacity, BLOCK, 2 * head_size)[my_slot]
    fetched = fetched.reshape(qblocks, head_count, top_count, BLOCK, 2 * head_size)
    for turn in range(top_count):
        parts.append(tile_partial(query_blocks, fetched[:, :, turn], scaling))
    result = merge_parts(parts)
    result = (
        result.transpose(0, 2, 1, 3)
        .reshape(qblocks * BLOCK, head_count * head_size)
        .astype(jnp.bfloat16)
    )
    return lax.all_to_all(result, ("heads", "sub"), split_axis=0, concat_axis=1, tiled=True)


STAT = 16
UNIT = 32767.0
LEAST = 1.2e-34
NEVER = -1.0e9
C2 = math.log2(math.e) * HD**-0.5


def scores_of(q, k, mask=None):
    s = lax.dot_general(k, q, (((1,), (1,)), ((), ())), preferred_element_type=jnp.float32)
    return s if mask is None else jnp.where(mask, s, -jnp.inf)


def weights_of(s):
    m = jnp.max(s, axis=0, keepdims=True)
    p = jnp.exp2((s - m) * C2)
    return p.astype(jnp.bfloat16), m * C2, jnp.sum(p, axis=0, keepdims=True)


def values_of(v, w, v_dim):
    return lax.dot_general(v, w, (((v_dim,), (0,)), ((), ())), preferred_element_type=jnp.float32)


def attend(tiles):
    count = len(tiles)
    s, w, parts = {}, {}, []
    for t in range(count + 2):
        if t < count:
            s[t] = tiles[t][0]()
        if 1 <= t <= count:
            w[t - 1] = weights_of(s.pop(t - 1))
        if t >= 2:
            weights, m, total = w.pop(t - 2)
            parts.append((tiles[t - 2][1](weights), m, total))
    return parts


def join(parts):
    top = functools.reduce(jnp.maximum, [m for _, m, _ in parts])
    factors = [jnp.exp2(m - top) for _, m, _ in parts]
    numer = sum(f * o for f, (o, _, _) in zip(factors, parts))
    denom = sum(f * t for f, (_, _, t) in zip(factors, parts))
    return numer, top, denom


def put(out_ref, heads):
    width, rows = len(heads) * HD, heads[0][0].shape[1]
    at = lax.broadcasted_iota(jnp.int32, (STAT, rows), 0)
    stats = jnp.zeros((STAT, rows), jnp.float32)
    for h, (numer, top, denom) in enumerate(heads):
        most = jnp.maximum(jnp.max(jnp.abs(numer), axis=0, keepdims=True), LEAST)
        code = jnp.round(numer * (UNIT / most))
        out_ref[h * HD : (h + 1) * HD, :] = code.astype(jnp.int32).astype(jnp.int16)
        for j, value in enumerate((top + jnp.log2(denom), jnp.log2(most / (UNIT * denom)))):
            whole = jnp.floor(value)
            stats = jnp.where(at == 4 * h + 2 * j, whole, stats)
            stats = jnp.where(at == 4 * h + 2 * j + 1, jnp.round((value - whole) * UNIT), stats)
    out_ref[width : width + STAT, :] = stats.astype(jnp.int32).astype(jnp.int16)


def take(ref, valid=None):
    width = ref.shape[0] - STAT
    stats = ref[width : width + STAT, :].astype(jnp.int32).astype(jnp.float32)
    heads = []
    for h in range(width // HD):
        code = ref[h * HD : (h + 1) * HD, :].astype(jnp.int32).astype(jnp.float32)
        weight = stats[4 * h : 4 * h + 1] + stats[4 * h + 1 : 4 * h + 2] * (1.0 / UNIT)
        unit = stats[4 * h + 2 : 4 * h + 3] + stats[4 * h + 3 : 4 * h + 4] * (1.0 / UNIT)
        if valid is not None:
            weight = jnp.where(valid, weight, NEVER)
        heads.append((code, weight, unit))
    return heads


def join_taken(taken):
    top = functools.reduce(jnp.maximum, [w for _, w, _ in taken])
    numer = sum(code * jnp.exp2(w - top + unit) for code, w, unit in taken)
    denom = sum(jnp.exp2(w - top) for _, w, _ in taken)
    return numer, top, denom


def cached_tiles(q_of, ck_ref, cvt_ref, h):
    cols = slice(h * HD, (h + 1) * HD)
    tiles = []
    for b in range(ck_ref.shape[0] // BLOCK):
        rows = slice(b * BLOCK, (b + 1) * BLOCK)
        tiles.append(
            (
                lambda rows=rows: scores_of(q_of(cols), ck_ref[rows, cols]),
                lambda w, rows=rows: values_of(cvt_ref[cols, rows], w, 1),
            )
        )
    return tiles


def attend_heads(tiles_of_heads):
    parts = attend([t for tiles in tiles_of_heads for t in tiles])
    heads = []
    for tiles in tiles_of_heads:
        heads.append(join(parts[: len(tiles)]))
        parts = parts[len(tiles) :]
    return heads


def cached_kernel(q_ref, ck_ref, cvt_ref, out_ref):
    heads = range(ck_ref.shape[1] // HD)
    q_of = lambda cols: q_ref[:, cols]
    put(out_ref, attend_heads([cached_tiles(q_of, ck_ref, cvt_ref, h) for h in heads]))


def either_kernel(middle_ref, a_ref, b_ref, ck_ref, cvt_ref, out_ref):
    middle = middle_ref[0] > 0
    heads = range(ck_ref.shape[1] // HD)
    q_of = lambda cols: jnp.where(middle, a_ref[:, cols], b_ref[:, cols])
    put(out_ref, attend_heads([cached_tiles(q_of, ck_ref, cvt_ref, h) for h in heads]))


def own_kernel(mine, order_ref, *refs):
    q_ref, *kv_refs, ck_ref, cvt_ref, out_ref = refs
    width = ck_ref.shape[1]
    rows = q_ref.shape[0]
    step = kv_refs[0].shape[0]

    def positions(shape, axis, pieces):
        at = lax.broadcasted_iota(jnp.int32, shape, axis)
        place = jnp.zeros(shape, jnp.int32)
        for i, d in enumerate(pieces):
            place = jnp.where(at // step == i, order_ref[d] * step + at % step, place)
        return place

    shape = (step * len(kv_refs), rows)
    mask = positions(shape, 1, mine) >= positions(shape, 0, range(len(kv_refs)))
    q_of = lambda cols: q_ref[:, cols]
    heads = []
    for h in range(width // HD):
        cols = slice(h * HD, (h + 1) * HD)
        vcols = slice(width + h * HD, width + (h + 1) * HD)
        own = (
            lambda cols=cols: scores_of(
                q_ref[:, cols], jnp.concatenate([r[:, cols] for r in kv_refs], axis=0), mask
            ),
            lambda w, vcols=vcols: values_of(
                jnp.concatenate([r[:, vcols] for r in kv_refs], axis=0), w, 0
            ),
        )
        heads.append([own] + cached_tiles(q_of, ck_ref, cvt_ref, h))
    put(out_ref, attend_heads(heads))


def merge_kernel(mine_ref, got_ref, out_ref):
    put(out_ref, [join_taken(pair) for pair in zip(take(mine_ref), take(got_ref))])


def middle_merge_kernel(middle_ref, mine_ref, got_ref, out_ref):
    taken = zip(take(mine_ref), take(got_ref, middle_ref[0] > 0))
    put(out_ref, [join_taken(pair) for pair in taken])


def final_kernel(own_ref, x_ref, y_ref, *out_refs):
    step = out_refs[0].shape[0]
    for h, taken in enumerate(zip(take(own_ref), take(x_ref), take(y_ref))):
        numer, _, denom = join_taken(taken)
        value = jnp.transpose(numer * (1.0 / denom)).astype(jnp.bfloat16)
        for i, out_ref in enumerate(out_refs):
            out_ref[:, h * HD : (h + 1) * HD] = value[i * step : (i + 1) * step]


def pick_kernel(pieces, order_ref, *refs):
    in_refs, out_refs = refs[: len(refs) - len(pieces)], refs[len(refs) - len(pieces) :]
    width = out_refs[0].shape[1] // len(in_refs)
    for d, out_ref in zip(pieces, out_refs):
        start = pl.multiple_of(order_ref[d] * width, width)
        for i, ref in enumerate(in_refs):
            out_ref[:, i * width : (i + 1) * width] = ref[:, pl.ds(start, width)]


def stack_kernel(*refs):
    *in_refs, out_ref = refs
    step = in_refs[0].shape[0]
    for i, ref in enumerate(in_refs):
        out_ref[i * step : (i + 1) * step, :] = ref[...]


def place_kernel(order_ref, *refs):
    *pieces, out_ref = refs
    width = pieces[0].shape[1]
    for d, piece in enumerate(pieces):
        start = pl.multiple_of(order_ref[d] * width, width)
        out_ref[:, pl.ds(start, width)] = piece[...]


def call(kernel, arrays, outs, flops=0, exps=0, scalars=None, unread=()):
    moved = sum(a.size * a.dtype.itemsize for a in arrays)
    moved += sum(math.prod(o.shape) * o.dtype.itemsize for o in outs)
    first = [] if scalars is None else [scalars]
    read = len(first) + len(arrays)

    def without_unread(*refs):
        kernel(*refs[:read], *refs[read + len(unread) :])

    return pl.pallas_call(
        without_unread,
        out_shape=outs,
        in_specs=[pl.BlockSpec(memory_space=pltpu.SMEM)] * len(first)
        + [pl.BlockSpec(memory_space=pltpu.VMEM)] * len(arrays)
        + [pl.BlockSpec(memory_space=pl.ANY)] * len(unread),
        out_specs=[pl.BlockSpec(memory_space=pltpu.VMEM)] * len(outs),
        compiler_params=pltpu.CompilerParams(vmem_limit_bytes=16 * 1024 * 1024),
        cost_estimate=pl.CostEstimate(flops=flops, bytes_accessed=moved, transcendentals=exps),
    )(*first, *arrays, *unread)


def after(x, unread):
    return call(stack_kernel, [x], [jax.ShapeDtypeStruct(x.shape, x.dtype)], unread=unread)[0]


def last_after(x, unread):
    return pl.pallas_call(
        lambda *refs: None,
        out_shape=jax.ShapeDtypeStruct(x.shape, x.dtype),
        in_specs=[pl.BlockSpec(memory_space=pl.ANY)] * (1 + len(unread)),
        out_specs=pl.BlockSpec(memory_space=pl.ANY),
        input_output_aliases={0: 0},
        cost_estimate=pl.CostEstimate(flops=0, bytes_accessed=0, transcendentals=0),
    )(x, *unread)


def flip(x, bits):
    return lax.ppermute(x, "seq", [(i, i ^ bits) for i in range(4)])


def across(x):
    return lax.ppermute(x, "seq", [(1, 2), (2, 1)])


def outward(x):
    return lax.ppermute(x, "seq", [(1, 0), (2, 3)])


def inward(x):
    return lax.ppermute(x, "seq", [(0, 1), (3, 2)])


def dense_body(queries, new_keys, new_values, cache_keys, cache_values):
    s = lax.axis_index("seq")
    shares = lax.axis_size("heads") * lax.axis_size("sub")
    me = lax.axis_index("heads") * lax.axis_size("sub") + lax.axis_index("sub")
    step, width = queries.shape[0], queries.shape[1] // shares
    half, cached = shares // 2, cache_keys.shape[0]
    rows = half * step
    piece = jax.ShapeDtypeStruct((step, width), jnp.bfloat16)
    pair = jax.ShapeDtypeStruct((step, 2 * width), jnp.bfloat16)
    chunk = [jax.ShapeDtypeStruct((rows, width), jnp.bfloat16)]
    packed = [jax.ShapeDtypeStruct((width + STAT, rows), jnp.int16)]
    cost = {"flops": 4 * rows * cached * width, "exps": rows * cached * (width // HD)}
    middle = jnp.logical_and(s > 0, s < 3).astype(jnp.int32).reshape(1)
    order = jnp.stack([me ^ d for d in range(shares)]).astype(jnp.int32)
    pieces_a, pieces_b = range(half), range(half, shares)
    pick = functools.partial(pick_kernel, range(shares))
    cache_vt = cache_values.T
    context = [cache_keys, cache_vt]

    def swap(x, d):
        return lax.ppermute(x, ("heads", "sub"), [(i, i ^ d) for i in range(shares)]) if d else x

    def attend(q):
        return call(cached_kernel, [q, *context], packed, **cost)[0]

    def attend_either(in_middle, at_end, unread):
        arrays = [in_middle, at_end, *context]
        return call(either_kernel, arrays, packed, scalars=middle, unread=unread, **cost)[0]

    def attend_own(q, pieces, unread):
        more = {name: value * 3 // 2 for name, value in cost.items()}
        kernel = functools.partial(own_kernel, pieces)
        arrays = [q, *kv, *context]
        return call(kernel, arrays, packed, scalars=order, unread=unread, **more)[0]

    def merge(mine, got):
        return call(merge_kernel, [mine, got], packed)[0]

    def merge_in_middle(mine, got):
        return call(middle_merge_kernel, [mine, got], packed, scalars=middle)[0]

    def end(own, x, y, pieces):
        ended = call(final_kernel, [own, x, y], [piece] * half)
        return [swap(e, d) for e, d in zip(ended, pieces)]

    pick_some = lambda pieces: functools.partial(pick_kernel, pieces)
    q = call(pick_some(pieces_a), [queries], [piece] * half, scalars=order)
    a = call(stack_kernel, [swap(x, d) for x, d in zip(q, pieces_a)], chunk)[0]
    a3, a1 = flip(a, 3), flip(a, 1)
    q = call(pick_some(pieces_b), [queries], [piece] * half, scalars=order, unread=[a])
    b = call(stack_kernel, [swap(x, d) for x, d in zip(q, pieces_b)], chunk)[0]
    b2 = flip(b, 2)
    b_again = after(b, [cache_vt])
    b1 = flip(b_again, 1)
    kv = call(pick, [new_keys, new_values], [pair] * shares, scalars=order, unread=[b_again])
    kv = [swap(x, d) for d, x in enumerate(kv)]

    part_a3, part_a1 = attend(a3), attend(a1)
    b3 = flip(after(b2, [part_a3, part_a1]), 1)
    a2_middle = across(last_after(a1, [b2, part_a1]))
    a2_end = outward(last_after(a3, [b2, part_a3]))
    part_b2 = attend(b2)
    got_inward, got_across = inward(part_b2), across(part_b2)
    part_b1 = attend(b1)
    got_a2 = flip(last_after(part_a3, [part_b1, b3, *kv[1:]]), 1)
    part_b3 = merge_in_middle(attend(b3), got_inward)
    from_b3 = flip(part_b3, 3)
    part_b1 = merge_in_middle(part_b1, got_across)
    from_b1 = flip(part_b1, 1)
    part_a2 = merge(attend_either(a2_middle, a2_end, [part_b3, part_b1]), got_a2)
    from_a2 = flip(part_a2, 2)
    from_a1 = flip(last_after(part_a1, [part_a2]), 1)

    out_b = end(attend_own(b, pieces_b, [part_b1]), from_b3, from_b1, pieces_b)
    out_a = end(attend_own(a, pieces_a, [part_b1]), from_a2, from_a1, pieces_a)
    out = jax.ShapeDtypeStruct((step, shares * width), jnp.bfloat16)
    return call(place_kernel, [*out_a, *out_b], [out], scalars=order)[0]


def power_of_two(n):
    return n & (n - 1) == 0


def body(queries, new_keys, new_values, cache_keys, cache_values, selection):
    qblocks, head_count, top_count = selection.shape
    seq_count = lax.axis_size("seq")
    shares = lax.axis_size("heads") * lax.axis_size("sub")
    every = top_count == cache_keys.shape[0] // BLOCK * seq_count and qblocks == 1
    fits = seq_count == 4 and power_of_two(shares) and shares > 1
    if every and fits and 4 * head_count <= STAT:
        return dense_body(queries, new_keys, new_values, cache_keys, cache_values)
    return sparse_body(queries, new_keys, new_values, cache_keys, cache_values, selection)


def solution(mesh):
    in_specs = (
        P(("groups", "seq", "heads", "sub"), None),
        P(("groups", "seq", "heads", "sub"), None),
        P(("groups", "seq", "heads", "sub"), None),
        P(("groups", "seq"), ("heads", "sub")),
        P(("groups", "seq"), ("heads", "sub")),
        P(("groups", "seq"), ("heads", "sub"), None),
    )
    out_specs = P(("groups", "seq", "heads", "sub"), None)
    return jax.shard_map(body, mesh=mesh, in_specs=in_specs, out_specs=out_specs, check_vma=False)
```

```python
import functools
import math

import jax
import jax.numpy as jnp
from jax import lax
from jax.experimental import pallas as pl
from jax.experimental.pallas import tpu as pltpu
from jax.sharding import PartitionSpec as P

HD = 128
BLOCK = 512


def order_ranks(owners):
    length = owners.shape[-1]
    counter = jnp.arange(length)
    earlier = counter[None, :] < counter[:, None]
    same_owner = owners[..., :, None] == owners[..., None, :]
    return jnp.sum(jnp.logical_and(same_owner, earlier), axis=-1)


def one_hot(values, length):
    return (values[..., None] == jnp.arange(length)).astype(jnp.float32)


def own_partial(query_blocks, key_blocks, value_blocks, scaling):
    scores = (
        jnp.einsum("bqhd,bkhd->bhqk", query_blocks, key_blocks, preferred_element_type=jnp.float32)
        * scaling
    )
    length = query_blocks.shape[1]
    causal = jnp.arange(length)[:, None] >= jnp.arange(length)[None, :]
    scores = jnp.where(causal, scores, -jnp.inf)
    highest = jnp.max(scores, axis=-1)
    weights = jnp.exp(scores - highest[..., None])
    totals = jnp.sum(weights, axis=-1)
    mixed = jnp.einsum(
        "bhqk,bkhd->bhqd",
        weights.astype(jnp.bfloat16),
        value_blocks,
        preferred_element_type=jnp.float32,
    )
    return (mixed, highest, totals)


def tile_partial(query_blocks, tile_pair, scaling):
    head_size = query_blocks.shape[-1]
    scores = (
        jnp.einsum(
            "bqhd,bhkd->bhqk",
            query_blocks,
            tile_pair[..., :head_size],
            preferred_element_type=jnp.float32,
        )
        * scaling
    )
    highest = jnp.max(scores, axis=-1)
    weights = jnp.exp(scores - highest[..., None])
    totals = jnp.sum(weights, axis=-1)
    mixed = jnp.einsum(
        "bhqk,bhkd->bhqd",
        weights.astype(jnp.bfloat16),
        tile_pair[..., head_size:],
        preferred_element_type=jnp.float32,
    )
    return (mixed, highest, totals)


def merge_parts(parts):
    top = parts[0][1]
    for part in parts[1:]:
        top = jnp.maximum(top, part[1])
    numer = jnp.zeros(parts[0][0].shape, jnp.float32)
    denom = jnp.zeros(parts[0][2].shape, jnp.float32)
    for part in parts:
        factor = jnp.exp(part[1] - top)
        numer = numer + factor[..., None] * part[0]
        denom = denom + factor * part[2]
    return numer / denom[..., None]


def sparse_body(queries, new_keys, new_values, cache_keys, cache_values, selection):
    heads_q, heads_k, heads_v = (
        lax.all_to_all(queries, ("heads", "sub"), split_axis=1, concat_axis=0, tiled=True),
        lax.all_to_all(new_keys, ("heads", "sub"), split_axis=1, concat_axis=0, tiled=True),
        lax.all_to_all(new_values, ("heads", "sub"), split_axis=1, concat_axis=0, tiled=True),
    )
    qblocks, head_count, top_count = selection.shape
    head_size = HD
    scaling = head_size ** (-0.5)
    shaped = (qblocks, BLOCK, head_count, head_size)
    query_blocks = heads_q.reshape(shaped)
    own = own_partial(query_blocks, heads_k.reshape(shaped), heads_v.reshape(shaped), scaling)
    seq_count = lax.axis_size("seq")
    myself = lax.axis_index("seq")
    cache_blocks = cache_keys.shape[0] // BLOCK
    tile_count = cache_blocks * head_count
    request_count = qblocks * head_count * top_count
    capacity = -(-request_count // seq_count)
    requests_all = lax.all_gather(selection, "seq", axis=0, tiled=True).reshape(
        seq_count, request_count
    )
    head_of = jnp.arange(request_count) // top_count % head_count
    my_requests = selection.reshape(request_count)
    my_owner = my_requests // cache_blocks
    my_slot = my_owner * capacity + order_ranks(my_owner)
    key_tiles = cache_keys.reshape(cache_blocks, BLOCK, head_count, head_size).transpose(0, 2, 1, 3)
    value_tiles = cache_values.reshape(cache_blocks, BLOCK, head_count, head_size).transpose(
        0, 2, 1, 3
    )
    tile_set = jnp.concatenate([key_tiles, value_tiles], axis=-1).reshape(
        tile_count, BLOCK, 2 * head_size
    )
    their_owner = requests_all // cache_blocks
    local_tile = requests_all % cache_blocks * head_count + head_of[None, :]
    served = (their_owner == myself).astype(jnp.float32)
    slot_pick = one_hot(order_ranks(their_owner), capacity) * served[..., None]
    picking = jnp.einsum("erc,erl->ecl", slot_pick, one_hot(local_tile, tile_count)).astype(
        jnp.bfloat16
    )
    parts = [own]
    outgoing = jnp.einsum(
        "ecl,lkf->eckf", picking, tile_set, preferred_element_type=jnp.float32
    ).astype(jnp.bfloat16)
    incoming = lax.all_to_all(outgoing, "seq", split_axis=0, concat_axis=0, tiled=True)
    fetched = incoming.reshape(seq_count * capacity, BLOCK, 2 * head_size)[my_slot]
    fetched = fetched.reshape(qblocks, head_count, top_count, BLOCK, 2 * head_size)
    for turn in range(top_count):
        parts.append(tile_partial(query_blocks, fetched[:, :, turn], scaling))
    result = merge_parts(parts)
    result = (
        result.transpose(0, 2, 1, 3)
        .reshape(qblocks * BLOCK, head_count * head_size)
        .astype(jnp.bfloat16)
    )
    return lax.all_to_all(result, ("heads", "sub"), split_axis=0, concat_axis=1, tiled=True)


STAT = 16
UNIT = 32767.0
LEAST = 1.2e-34
C2 = math.log2(math.e) * HD**-0.5


def scores_of(q, k, mask=None):
    s = lax.dot_general(k, q, (((1,), (1,)), ((), ())), preferred_element_type=jnp.float32)
    return s if mask is None else jnp.where(mask, s, -jnp.inf)


def weights_of(s):
    m = jnp.max(s, axis=0, keepdims=True)
    p = jnp.exp2((s - m) * C2)
    return p.astype(jnp.bfloat16), m * C2, jnp.sum(p, axis=0, keepdims=True)


def values_of(v, w, v_dim):
    return lax.dot_general(v, w, (((v_dim,), (0,)), ((), ())), preferred_element_type=jnp.float32)


def attend(tiles):
    count = len(tiles)
    s, w, parts = {}, {}, []
    for t in range(count + 2):
        if t < count:
            s[t] = tiles[t][0]()
        if 1 <= t <= count:
            w[t - 1] = weights_of(s.pop(t - 1))
        if t >= 2:
            weights, m, total = w.pop(t - 2)
            parts.append((tiles[t - 2][1](weights), m, total))
    return parts


def join(parts):
    top = functools.reduce(jnp.maximum, [m for _, m, _ in parts])
    factors = [jnp.exp2(m - top) for _, m, _ in parts]
    numer = sum(f * o for f, (o, _, _) in zip(factors, parts))
    denom = sum(f * t for f, (_, _, t) in zip(factors, parts))
    return numer, top, denom


def put(out_ref, heads):
    width, rows = len(heads) * HD, heads[0][0].shape[1]
    at = lax.broadcasted_iota(jnp.int32, (STAT, rows), 0)
    stats = jnp.zeros((STAT, rows), jnp.float32)
    for h, (numer, top, denom) in enumerate(heads):
        most = jnp.maximum(jnp.max(jnp.abs(numer), axis=0, keepdims=True), LEAST)
        code = jnp.round(numer * (UNIT / most))
        out_ref[h * HD : (h + 1) * HD, :] = code.astype(jnp.int32).astype(jnp.int16)
        for j, value in enumerate((top + jnp.log2(denom), jnp.log2(most / (UNIT * denom)))):
            whole = jnp.floor(value)
            stats = jnp.where(at == 4 * h + 2 * j, whole, stats)
            stats = jnp.where(at == 4 * h + 2 * j + 1, jnp.round((value - whole) * UNIT), stats)
    out_ref[width : width + STAT, :] = stats.astype(jnp.int32).astype(jnp.int16)


def take(ref):
    width = ref.shape[0] - STAT
    stats = ref[width : width + STAT, :].astype(jnp.int32).astype(jnp.float32)
    heads = []
    for h in range(width // HD):
        code = ref[h * HD : (h + 1) * HD, :].astype(jnp.int32).astype(jnp.float32)
        weight = stats[4 * h : 4 * h + 1] + stats[4 * h + 1 : 4 * h + 2] * (1.0 / UNIT)
        unit = stats[4 * h + 2 : 4 * h + 3] + stats[4 * h + 3 : 4 * h + 4] * (1.0 / UNIT)
        heads.append((code, weight, unit))
    return heads


def join_taken(taken):
    top = functools.reduce(jnp.maximum, [w for _, w, _ in taken])
    numer = sum(code * jnp.exp2(w - top + unit) for code, w, unit in taken)
    denom = sum(jnp.exp2(w - top) for _, w, _ in taken)
    return numer, top, denom


def cached_tiles(q_of, ck_ref, cvt_ref, h):
    cols = slice(h * HD, (h + 1) * HD)
    tiles = []
    for b in range(ck_ref.shape[0] // BLOCK):
        rows = slice(b * BLOCK, (b + 1) * BLOCK)
        tiles.append(
            (
                lambda rows=rows: scores_of(q_of(cols), ck_ref[rows, cols]),
                lambda w, rows=rows: values_of(cvt_ref[cols, rows], w, 1),
            )
        )
    return tiles


def attend_heads(tiles_of_heads):
    parts = attend([t for tiles in tiles_of_heads for t in tiles])
    heads = []
    for tiles in tiles_of_heads:
        heads.append(join(parts[: len(tiles)]))
        parts = parts[len(tiles) :]
    return heads


def cached_kernel(q_ref, ck_ref, cvt_ref, out_ref):
    heads = range(ck_ref.shape[1] // HD)
    q_of = lambda cols: q_ref[:, cols]
    put(out_ref, attend_heads([cached_tiles(q_of, ck_ref, cvt_ref, h) for h in heads]))


def own_kernel(mine, order_ref, *refs):
    q_ref, *kv_refs, ck_ref, cvt_ref, out_ref = refs
    width = ck_ref.shape[1]
    rows = q_ref.shape[0]
    step = kv_refs[0].shape[0]

    def positions(shape, axis, pieces):
        at = lax.broadcasted_iota(jnp.int32, shape, axis)
        place = jnp.zeros(shape, jnp.int32)
        for i, d in enumerate(pieces):
            place = jnp.where(at // step == i, order_ref[d] * step + at % step, place)
        return place

    shape = (step * len(kv_refs), rows)
    mask = positions(shape, 1, mine) >= positions(shape, 0, range(len(kv_refs)))
    q_of = lambda cols: q_ref[:, cols]
    heads = []
    for h in range(width // HD):
        cols = slice(h * HD, (h + 1) * HD)
        vcols = slice(width + h * HD, width + (h + 1) * HD)
        own = (
            lambda cols=cols: scores_of(
                q_ref[:, cols], jnp.concatenate([r[:, cols] for r in kv_refs], axis=0), mask
            ),
            lambda w, vcols=vcols: values_of(
                jnp.concatenate([r[:, vcols] for r in kv_refs], axis=0), w, 0
            ),
        )
        heads.append([own] + cached_tiles(q_of, ck_ref, cvt_ref, h))
    put(out_ref, attend_heads(heads))


def merge_kernel(*refs):
    *in_refs, out_ref = refs
    put(out_ref, [join_taken(taken) for taken in zip(*[take(r) for r in in_refs])])


def final_kernel(count, *refs):
    in_refs, out_refs = refs[:count], refs[count:]
    step = out_refs[0].shape[0]
    for h, taken in enumerate(zip(*[take(r) for r in in_refs])):
        numer, _, denom = join_taken(taken)
        value = jnp.transpose(numer * (1.0 / denom)).astype(jnp.bfloat16)
        for i, out_ref in enumerate(out_refs):
            out_ref[:, h * HD : (h + 1) * HD] = value[i * step : (i + 1) * step]


def pick_kernel(pieces, count, order_ref, *refs):
    in_refs, out_refs, done = refs[:count], refs[count:-1], refs[-1]
    width = out_refs[0].shape[1] // count
    copies = []
    for d, out_ref in zip(pieces, out_refs):
        start = pl.multiple_of(order_ref[d] * width, width)
        for i, ref in enumerate(in_refs):
            source, target = ref.at[:, pl.ds(start, width)], out_ref.at[:, i * width : (i + 1) * width]
            copies.append(pltpu.make_async_copy(source, target, done.at[len(copies)]))
            copies[-1].start()
    for copy in copies:
        copy.wait()


def stack_kernel(count, *refs):
    out_ref = refs[-1]
    step = refs[0].shape[0]
    for i in range(count):
        out_ref[i * step : (i + 1) * step, :] = refs[i][...]


def place_kernel(order_ref, *refs):
    *pieces, out_ref, done = refs
    width = pieces[0].shape[1]
    copies = []
    for d, piece in enumerate(pieces):
        start = pl.multiple_of(order_ref[d] * width, width)
        copies.append(pltpu.make_async_copy(piece, out_ref.at[:, pl.ds(start, width)], done.at[d]))
        copies[-1].start()
    for copy in copies:
        copy.wait()


def move(kernel, copies, scalars, arrays, outs, out_space, unread=()):
    read = 1 + len(arrays)

    def without_unread(*refs):
        kernel(*refs[:read], *refs[read + len(unread) :])

    return pl.pallas_call(
        without_unread,
        out_shape=outs,
        in_specs=[pl.BlockSpec(memory_space=pltpu.SMEM)]
        + [pl.BlockSpec(memory_space=pl.ANY)] * (len(arrays) + len(unread)),
        out_specs=[pl.BlockSpec(memory_space=out_space)] * len(outs),
        scratch_shapes=[pltpu.SemaphoreType.DMA((copies,))],
        cost_estimate=pl.CostEstimate(flops=0, bytes_accessed=2 * 4 * outs[0].size, transcendentals=0),
    )(scalars, *arrays, *unread)


def call(kernel, arrays, outs, flops=0, exps=0, scalars=None, unread=()):
    moved = sum(a.size * a.dtype.itemsize for a in arrays)
    moved += sum(math.prod(o.shape) * o.dtype.itemsize for o in outs)
    first = [] if scalars is None else [scalars]
    return pl.pallas_call(
        kernel,
        out_shape=outs,
        in_specs=[pl.BlockSpec(memory_space=pltpu.SMEM)] * len(first)
        + [pl.BlockSpec(memory_space=pltpu.VMEM)] * len(arrays)
        + [pl.BlockSpec(memory_space=pl.ANY)] * len(unread),
        out_specs=[pl.BlockSpec(memory_space=pltpu.VMEM)] * len(outs),
        compiler_params=pltpu.CompilerParams(vmem_limit_bytes=16 * 1024 * 1024),
        cost_estimate=pl.CostEstimate(flops=flops, bytes_accessed=moved, transcendentals=exps),
    )(*first, *arrays, *unread)


def dense_body(queries, new_keys, new_values, cache_keys, cache_values):
    seq_count = lax.axis_size("seq")
    shares = lax.axis_size("heads") * lax.axis_size("sub")
    me = lax.axis_index("heads") * lax.axis_size("sub") + lax.axis_index("sub")
    step, width = queries.shape[0], queries.shape[1] // shares
    cached = cache_keys.shape[0]
    each = shares // CHUNKS
    rows = each * step
    chunk = jax.ShapeDtypeStruct((rows, width), jnp.bfloat16)
    piece = jax.ShapeDtypeStruct((step, width), jnp.bfloat16)
    pair = jax.ShapeDtypeStruct((step, 2 * width), jnp.bfloat16)
    packed = jax.ShapeDtypeStruct((width + STAT, rows), jnp.int16)
    tile_flops = 4 * rows * cached * width
    tile_exps = rows * cached * (width // HD)

    def swap(x, d):
        return lax.ppermute(x, ("heads", "sub"), [(i, i ^ d) for i in range(shares)])

    def along(x, bit):
        return lax.ppermute(x, "seq", [(i, i ^ bit) for i in range(seq_count)])

    def after(x, unread):
        like = jax.ShapeDtypeStruct(x.shape, x.dtype)
        return call(functools.partial(stack_kernel, 1), [x], [like], unread=unread)[0] if unread else x

    order = jnp.stack([me ^ d for d in range(shares)]).astype(jnp.int32)
    cache_vt = cache_values.T
    context = [cache_keys, cache_vt]

    def attend(q):
        return call(cached_kernel, [q, *context], [packed], tile_flops, tile_exps)[0]

    def attend_own(q, pieces):
        return call(
            functools.partial(own_kernel, pieces),
            [q, *kv, *context],
            [packed],
            tile_flops * 3 // 2,
            tile_exps * 3 // 2,
            order,
        )[0]

    def merge(mine, got):
        return call(merge_kernel, [mine, got], [packed])[0]

    def end(parts, pieces):
        ended = call(functools.partial(final_kernel, len(parts)), parts, [piece] * each)
        return [swap(x, d) if d else x for x, d in zip(ended, pieces)]

    pieces_a, pieces_b = range(each), range(each, shares)

    def pick(arrays, pieces, out, unread=()):
        kernel = functools.partial(pick_kernel, pieces, len(arrays))
        count = len(pieces)
        return move(kernel, count * len(arrays), order, arrays, [out] * count, pltpu.VMEM, unread)

    q = [swap(x, d) if d else x for x, d in zip(pick([queries], pieces_a, piece), pieces_a)]
    a = call(functools.partial(stack_kernel, each), q, [chunk])[0]
    a2, a1 = along(a, 2), along(a, 1)
    q = [swap(x, d) for x, d in zip(pick([queries], pieces_b, piece), pieces_b)]
    b = call(functools.partial(stack_kernel, each), q, [chunk])[0]
    b2, b1 = along(b, 2), along(b, 1)
    kv = pick([new_keys, new_values], range(shares), pair, [b, cache_vt])
    kv = [swap(x, d) if d else x for d, x in enumerate(kv)]
    part_a2, part_a1 = attend(a2), attend(a1)
    b3 = along(after(b2, [part_a2, part_a1]), 1)
    part_b2 = attend(b2)
    a3 = along(after(a2, [part_b2, b1, *kv[1:]]), 1)
    got_b2 = along(attend(b3), 1)
    got_a2 = along(attend(a3), 1)
    part_b2 = merge(part_b2, got_b2)
    from_b2 = along(part_b2, 2)
    from_b1 = along(after(attend(b1), [part_b2]), 1)
    part_a2 = merge(part_a2, got_a2)
    from_a2 = along(part_a2, 2)
    from_a1 = along(after(part_a1, [part_a2]), 1)
    out_b = end([attend_own(b, pieces_b), from_b2, from_b1], pieces_b)
    out_a = end([attend_own(a, pieces_a), from_a2, from_a1], pieces_a)
    results = [*out_a, *out_b]
    out = jax.ShapeDtypeStruct((step, shares * width), jnp.bfloat16)
    return move(place_kernel, shares, order, results, [out], pl.ANY)[0]


CHUNKS = 2


def power_of_two(n):
    return n & (n - 1) == 0


def body(queries, new_keys, new_values, cache_keys, cache_values, selection):
    qblocks, head_count, top_count = selection.shape
    seq_count = lax.axis_size("seq")
    shares = lax.axis_size("heads") * lax.axis_size("sub")
    every = top_count == cache_keys.shape[0] // BLOCK * seq_count and qblocks == 1
    fits = seq_count == 4 and power_of_two(shares) and shares % CHUNKS == 0
    if every and fits and 4 * head_count <= STAT:
        return dense_body(queries, new_keys, new_values, cache_keys, cache_values)
    return sparse_body(queries, new_keys, new_values, cache_keys, cache_values, selection)


def solution(mesh):
    in_specs = (
        P(("groups", "seq", "heads", "sub"), None),
        P(("groups", "seq", "heads", "sub"), None),
        P(("groups", "seq", "heads", "sub"), None),
        P(("groups", "seq"), ("heads", "sub")),
        P(("groups", "seq"), ("heads", "sub")),
        P(("groups", "seq"), ("heads", "sub"), None),
    )
    out_specs = P(("groups", "seq", "heads", "sub"), None)
    return jax.shard_map(body, mesh=mesh, in_specs=in_specs, out_specs=out_specs, check_vma=False)
```

```python
import functools
import math

import jax
import jax.numpy as jnp
from jax import lax
from jax.experimental import pallas as pl
from jax.experimental.pallas import tpu as pltpu
from jax.sharding import PartitionSpec as P

HD = 128
BLOCK = 512


def order_ranks(owners):
    length = owners.shape[-1]
    counter = jnp.arange(length)
    earlier = counter[None, :] < counter[:, None]
    same_owner = owners[..., :, None] == owners[..., None, :]
    return jnp.sum(jnp.logical_and(same_owner, earlier), axis=-1)


def one_hot(values, length):
    return (values[..., None] == jnp.arange(length)).astype(jnp.float32)


def own_partial(query_blocks, key_blocks, value_blocks, scaling):
    scores = (
        jnp.einsum("bqhd,bkhd->bhqk", query_blocks, key_blocks, preferred_element_type=jnp.float32)
        * scaling
    )
    length = query_blocks.shape[1]
    causal = jnp.arange(length)[:, None] >= jnp.arange(length)[None, :]
    scores = jnp.where(causal, scores, -jnp.inf)
    highest = jnp.max(scores, axis=-1)
    weights = jnp.exp(scores - highest[..., None])
    totals = jnp.sum(weights, axis=-1)
    mixed = jnp.einsum(
        "bhqk,bkhd->bhqd",
        weights.astype(jnp.bfloat16),
        value_blocks,
        preferred_element_type=jnp.float32,
    )
    return (mixed, highest, totals)


def tile_partial(query_blocks, tile_pair, scaling):
    head_size = query_blocks.shape[-1]
    scores = (
        jnp.einsum(
            "bqhd,bhkd->bhqk",
            query_blocks,
            tile_pair[..., :head_size],
            preferred_element_type=jnp.float32,
        )
        * scaling
    )
    highest = jnp.max(scores, axis=-1)
    weights = jnp.exp(scores - highest[..., None])
    totals = jnp.sum(weights, axis=-1)
    mixed = jnp.einsum(
        "bhqk,bhkd->bhqd",
        weights.astype(jnp.bfloat16),
        tile_pair[..., head_size:],
        preferred_element_type=jnp.float32,
    )
    return (mixed, highest, totals)


def merge_parts(parts):
    top = parts[0][1]
    for part in parts[1:]:
        top = jnp.maximum(top, part[1])
    numer = jnp.zeros(parts[0][0].shape, jnp.float32)
    denom = jnp.zeros(parts[0][2].shape, jnp.float32)
    for part in parts:
        factor = jnp.exp(part[1] - top)
        numer = numer + factor[..., None] * part[0]
        denom = denom + factor * part[2]
    return numer / denom[..., None]


def sparse_body(queries, new_keys, new_values, cache_keys, cache_values, selection):
    heads_q, heads_k, heads_v = (
        lax.all_to_all(queries, ("heads", "sub"), split_axis=1, concat_axis=0, tiled=True),
        lax.all_to_all(new_keys, ("heads", "sub"), split_axis=1, concat_axis=0, tiled=True),
        lax.all_to_all(new_values, ("heads", "sub"), split_axis=1, concat_axis=0, tiled=True),
    )
    qblocks, head_count, top_count = selection.shape
    head_size = HD
    scaling = head_size ** (-0.5)
    shaped = (qblocks, BLOCK, head_count, head_size)
    query_blocks = heads_q.reshape(shaped)
    own = own_partial(query_blocks, heads_k.reshape(shaped), heads_v.reshape(shaped), scaling)
    seq_count = lax.axis_size("seq")
    myself = lax.axis_index("seq")
    cache_blocks = cache_keys.shape[0] // BLOCK
    tile_count = cache_blocks * head_count
    request_count = qblocks * head_count * top_count
    capacity = -(-request_count // seq_count)
    requests_all = lax.all_gather(selection, "seq", axis=0, tiled=True).reshape(
        seq_count, request_count
    )
    head_of = jnp.arange(request_count) // top_count % head_count
    my_requests = selection.reshape(request_count)
    my_owner = my_requests // cache_blocks
    my_slot = my_owner * capacity + order_ranks(my_owner)
    key_tiles = cache_keys.reshape(cache_blocks, BLOCK, head_count, head_size).transpose(0, 2, 1, 3)
    value_tiles = cache_values.reshape(cache_blocks, BLOCK, head_count, head_size).transpose(
        0, 2, 1, 3
    )
    tile_set = jnp.concatenate([key_tiles, value_tiles], axis=-1).reshape(
        tile_count, BLOCK, 2 * head_size
    )
    their_owner = requests_all // cache_blocks
    local_tile = requests_all % cache_blocks * head_count + head_of[None, :]
    served = (their_owner == myself).astype(jnp.float32)
    slot_pick = one_hot(order_ranks(their_owner), capacity) * served[..., None]
    picking = jnp.einsum("erc,erl->ecl", slot_pick, one_hot(local_tile, tile_count)).astype(
        jnp.bfloat16
    )
    parts = [own]
    outgoing = jnp.einsum(
        "ecl,lkf->eckf", picking, tile_set, preferred_element_type=jnp.float32
    ).astype(jnp.bfloat16)
    incoming = lax.all_to_all(outgoing, "seq", split_axis=0, concat_axis=0, tiled=True)
    fetched = incoming.reshape(seq_count * capacity, BLOCK, 2 * head_size)[my_slot]
    fetched = fetched.reshape(qblocks, head_count, top_count, BLOCK, 2 * head_size)
    for turn in range(top_count):
        parts.append(tile_partial(query_blocks, fetched[:, :, turn], scaling))
    result = merge_parts(parts)
    result = (
        result.transpose(0, 2, 1, 3)
        .reshape(qblocks * BLOCK, head_count * head_size)
        .astype(jnp.bfloat16)
    )
    return lax.all_to_all(result, ("heads", "sub"), split_axis=0, concat_axis=1, tiled=True)


STAT = 16
UNIT = 32767.0
LEAST = 1.2e-34
C2 = math.log2(math.e) * HD**-0.5


def scores_of(q, k, mask=None):
    s = lax.dot_general(k, q, (((1,), (1,)), ((), ())), preferred_element_type=jnp.float32)
    return s if mask is None else jnp.where(mask, s, -jnp.inf)


def weights_of(s):
    m = jnp.max(s, axis=0, keepdims=True)
    p = jnp.exp2((s - m) * C2)
    return p.astype(jnp.bfloat16), m * C2, jnp.sum(p, axis=0, keepdims=True)


def values_of(v, w, v_dim):
    return lax.dot_general(v, w, (((v_dim,), (0,)), ((), ())), preferred_element_type=jnp.float32)


def attend(tiles):
    count = len(tiles)
    s, w, parts = {}, {}, []
    for t in range(count + 2):
        if t < count:
            s[t] = tiles[t][0]()
        if 1 <= t <= count:
            w[t - 1] = weights_of(s.pop(t - 1))
        if t >= 2:
            weights, m, total = w.pop(t - 2)
            parts.append((tiles[t - 2][1](weights), m, total))
    return parts


def join(parts):
    top = functools.reduce(jnp.maximum, [m for _, m, _ in parts])
    factors = [jnp.exp2(m - top) for _, m, _ in parts]
    numer = sum(f * o for f, (o, _, _) in zip(factors, parts))
    denom = sum(f * t for f, (_, _, t) in zip(factors, parts))
    return numer, top, denom


def put(out_ref, heads):
    width, rows = len(heads) * HD, heads[0][0].shape[1]
    at = lax.broadcasted_iota(jnp.int32, (STAT, rows), 0)
    stats = jnp.zeros((STAT, rows), jnp.float32)
    for h, (numer, top, denom) in enumerate(heads):
        most = jnp.maximum(jnp.max(jnp.abs(numer), axis=0, keepdims=True), LEAST)
        code = jnp.round(numer * (UNIT / most))
        out_ref[h * HD : (h + 1) * HD, :] = code.astype(jnp.int32).astype(jnp.int16)
        for j, value in enumerate((top + jnp.log2(denom), jnp.log2(most / (UNIT * denom)))):
            whole = jnp.floor(value)
            stats = jnp.where(at == 4 * h + 2 * j, whole, stats)
            stats = jnp.where(at == 4 * h + 2 * j + 1, jnp.round((value - whole) * UNIT), stats)
    out_ref[width : width + STAT, :] = stats.astype(jnp.int32).astype(jnp.int16)


def take(ref):
    width = ref.shape[0] - STAT
    stats = ref[width : width + STAT, :].astype(jnp.int32).astype(jnp.float32)
    heads = []
    for h in range(width // HD):
        code = ref[h * HD : (h + 1) * HD, :].astype(jnp.int32).astype(jnp.float32)
        weight = stats[4 * h : 4 * h + 1] + stats[4 * h + 1 : 4 * h + 2] * (1.0 / UNIT)
        unit = stats[4 * h + 2 : 4 * h + 3] + stats[4 * h + 3 : 4 * h + 4] * (1.0 / UNIT)
        heads.append((code, weight, unit))
    return heads


def join_taken(taken):
    top = functools.reduce(jnp.maximum, [w for _, w, _ in taken])
    numer = sum(code * jnp.exp2(w - top + unit) for code, w, unit in taken)
    denom = sum(jnp.exp2(w - top) for _, w, _ in taken)
    return numer, top, denom


def cached_tiles(q_of, ck_ref, cvt_ref, h):
    cols = slice(h * HD, (h + 1) * HD)
    tiles = []
    for b in range(ck_ref.shape[0] // BLOCK):
        rows = slice(b * BLOCK, (b + 1) * BLOCK)
        tiles.append(
            (
                lambda rows=rows: scores_of(q_of(cols), ck_ref[rows, cols]),
                lambda w, rows=rows: values_of(cvt_ref[cols, rows], w, 1),
            )
        )
    return tiles


def attend_heads(tiles_of_heads):
    parts = attend([t for tiles in tiles_of_heads for t in tiles])
    heads = []
    for tiles in tiles_of_heads:
        heads.append(join(parts[: len(tiles)]))
        parts = parts[len(tiles) :]
    return heads


def cached_kernel(q_ref, ck_ref, cvt_ref, out_ref):
    heads = range(ck_ref.shape[1] // HD)
    q_of = lambda cols: q_ref[:, cols]
    put(out_ref, attend_heads([cached_tiles(q_of, ck_ref, cvt_ref, h) for h in heads]))


def own_kernel(mine, order_ref, *refs):
    q_ref, *kv_refs, ck_ref, cvt_ref, out_ref = refs
    width = ck_ref.shape[1]
    rows = q_ref.shape[0]
    step = kv_refs[0].shape[0]

    def positions(shape, axis, pieces):
        at = lax.broadcasted_iota(jnp.int32, shape, axis)
        place = jnp.zeros(shape, jnp.int32)
        for i, d in enumerate(pieces):
            place = jnp.where(at // step == i, order_ref[d] * step + at % step, place)
        return place

    shape = (step * len(kv_refs), rows)
    mask = positions(shape, 1, mine) >= positions(shape, 0, range(len(kv_refs)))
    q_of = lambda cols: q_ref[:, cols]
    heads = []
    for h in range(width // HD):
        cols = slice(h * HD, (h + 1) * HD)
        vcols = slice(width + h * HD, width + (h + 1) * HD)
        own = (
            lambda cols=cols: scores_of(
                q_ref[:, cols], jnp.concatenate([r[:, cols] for r in kv_refs], axis=0), mask
            ),
            lambda w, vcols=vcols: values_of(
                jnp.concatenate([r[:, vcols] for r in kv_refs], axis=0), w, 0
            ),
        )
        heads.append([own] + cached_tiles(q_of, ck_ref, cvt_ref, h))
    put(out_ref, attend_heads(heads))


def merge_kernel(*refs):
    *in_refs, out_ref = refs
    put(out_ref, [join_taken(taken) for taken in zip(*[take(r) for r in in_refs])])


def final_kernel(count, *refs):
    in_refs, out_refs = refs[:count], refs[count:]
    step = out_refs[0].shape[0]
    for h, taken in enumerate(zip(*[take(r) for r in in_refs])):
        numer, _, denom = join_taken(taken)
        value = jnp.transpose(numer * (1.0 / denom)).astype(jnp.bfloat16)
        for i, out_ref in enumerate(out_refs):
            out_ref[:, h * HD : (h + 1) * HD] = value[i * step : (i + 1) * step]


def pick_kernel(pieces, count, order_ref, *refs):
    in_refs, out_refs, done = refs[:count], refs[count:-1], refs[-1]
    width = out_refs[0].shape[1] // count
    copies = []
    for d, out_ref in zip(pieces, out_refs):
        start = pl.multiple_of(order_ref[d] * width, width)
        for i, ref in enumerate(in_refs):
            source, target = ref.at[:, pl.ds(start, width)], out_ref.at[:, i * width : (i + 1) * width]
            copies.append(pltpu.make_async_copy(source, target, done.at[len(copies)]))
            copies[-1].start()
    for copy in copies:
        copy.wait()


def slice_kernel(pieces, order_ref, ref, *out_refs):
    width = out_refs[0].shape[1]
    for d, out_ref in zip(pieces, out_refs):
        out_ref[...] = ref[:, pl.ds(pl.multiple_of(order_ref[d] * width, width), width)]


def stack_kernel(count, *refs):
    out_ref = refs[-1]
    step = refs[0].shape[0]
    for i in range(count):
        out_ref[i * step : (i + 1) * step, :] = refs[i][...]


def place_kernel(order_ref, *refs):
    *pieces, out_ref = refs
    width = pieces[0].shape[1]
    for d, piece in enumerate(pieces):
        start = pl.multiple_of(order_ref[d] * width, width)
        out_ref[:, pl.ds(start, width)] = piece[...]


def move(kernel, copies, scalars, arrays, outs, unread=()):
    read = 1 + len(arrays)

    def without_unread(*refs):
        kernel(*refs[:read], *refs[read + len(unread) :])

    return pl.pallas_call(
        without_unread,
        out_shape=outs,
        in_specs=[pl.BlockSpec(memory_space=pltpu.SMEM)]
        + [pl.BlockSpec(memory_space=pl.ANY)] * (len(arrays) + len(unread)),
        out_specs=[pl.BlockSpec(memory_space=pltpu.VMEM)] * len(outs),
        scratch_shapes=[pltpu.SemaphoreType.DMA((copies,))],
        cost_estimate=pl.CostEstimate(flops=0, bytes_accessed=2 * 4 * outs[0].size, transcendentals=0),
    )(scalars, *arrays, *unread)


def call(kernel, arrays, outs, flops=0, exps=0, scalars=None, unread=()):
    moved = sum(a.size * a.dtype.itemsize for a in arrays)
    moved += sum(math.prod(o.shape) * o.dtype.itemsize for o in outs)
    first = [] if scalars is None else [scalars]
    return pl.pallas_call(
        kernel,
        out_shape=outs,
        in_specs=[pl.BlockSpec(memory_space=pltpu.SMEM)] * len(first)
        + [pl.BlockSpec(memory_space=pltpu.VMEM)] * len(arrays)
        + [pl.BlockSpec(memory_space=pl.ANY)] * len(unread),
        out_specs=[pl.BlockSpec(memory_space=pltpu.VMEM)] * len(outs),
        compiler_params=pltpu.CompilerParams(vmem_limit_bytes=16 * 1024 * 1024),
        cost_estimate=pl.CostEstimate(flops=flops, bytes_accessed=moved, transcendentals=exps),
    )(*first, *arrays, *unread)


def dense_body(queries, new_keys, new_values, cache_keys, cache_values):
    seq_count = lax.axis_size("seq")
    shares = lax.axis_size("heads") * lax.axis_size("sub")
    me = lax.axis_index("heads") * lax.axis_size("sub") + lax.axis_index("sub")
    step, width = queries.shape[0], queries.shape[1] // shares
    cached = cache_keys.shape[0]
    each = shares // CHUNKS
    rows = each * step
    chunk = jax.ShapeDtypeStruct((rows, width), jnp.bfloat16)
    piece = jax.ShapeDtypeStruct((step, width), jnp.bfloat16)
    pair = jax.ShapeDtypeStruct((step, 2 * width), jnp.bfloat16)
    packed = jax.ShapeDtypeStruct((width + STAT, rows), jnp.int16)
    tile_flops = 4 * rows * cached * width
    tile_exps = rows * cached * (width // HD)

    def swap(x, d):
        return lax.ppermute(x, ("heads", "sub"), [(i, i ^ d) for i in range(shares)])

    def along(x, bit):
        return lax.ppermute(x, "seq", [(i, i ^ bit) for i in range(seq_count)])

    def after(x, unread):
        like = jax.ShapeDtypeStruct(x.shape, x.dtype)
        return call(functools.partial(stack_kernel, 1), [x], [like], unread=unread)[0] if unread else x

    order = jnp.stack([me ^ d for d in range(shares)]).astype(jnp.int32)
    cache_vt = cache_values.T
    context = [cache_keys, cache_vt]

    def attend(q):
        return call(cached_kernel, [q, *context], [packed], tile_flops, tile_exps)[0]

    def attend_own(q, pieces):
        return call(
            functools.partial(own_kernel, pieces),
            [q, *kv, *context],
            [packed],
            tile_flops * 3 // 2,
            tile_exps * 3 // 2,
            order,
        )[0]

    def merge(mine, got):
        return call(merge_kernel, [mine, got], [packed])[0]

    def end(parts, pieces):
        ended = call(functools.partial(final_kernel, len(parts)), parts, [piece] * each)
        return [swap(x, d) if d else x for x, d in zip(ended, pieces)]

    pieces_a, pieces_b = range(each), range(each, shares)

    def pick(arrays, pieces, out, unread=()):
        kernel = functools.partial(pick_kernel, pieces, len(arrays))
        count = len(pieces)
        return move(kernel, count * len(arrays), order, arrays, [out] * count, unread)

    def slices(pieces):
        kernel = functools.partial(slice_kernel, pieces)
        return call(kernel, [queries], [piece] * each, scalars=order)

    q = [swap(x, d) if d else x for x, d in zip(slices(pieces_a), pieces_a)]
    a = call(functools.partial(stack_kernel, each), q, [chunk])[0]
    q = slices(pieces_b)
    a2, a1 = along(a, 2), along(a, 1)
    q = [swap(x, d) for x, d in zip(q, pieces_b)]
    b = call(functools.partial(stack_kernel, each), q, [chunk])[0]
    b2, b1 = along(b, 2), along(b, 1)
    kv = pick([new_keys, new_values], range(shares), pair, [b, cache_vt])
    kv = [swap(x, d) if d else x for d, x in enumerate(kv)]
    part_a2, part_a1 = attend(a2), attend(a1)
    b3 = along(after(b2, [part_a2, part_a1]), 1)
    part_b2 = attend(b2)
    a3 = along(after(a2, [part_b2, b1, *kv[1:]]), 1)
    got_b2 = along(attend(b3), 1)
    got_a2 = along(attend(a3), 1)
    part_b2 = merge(part_b2, got_b2)
    from_b2 = along(part_b2, 2)
    from_b1 = along(after(attend(b1), [part_b2]), 1)
    part_a2 = merge(part_a2, got_a2)
    from_a2 = along(part_a2, 2)
    from_a1 = along(after(part_a1, [part_a2]), 1)
    out_b = end([attend_own(b, pieces_b), from_b2, from_b1], pieces_b)
    out_a = end([attend_own(a, pieces_a), from_a2, from_a1], pieces_a)
    results = [*out_a, *out_b]
    out = jax.ShapeDtypeStruct((step, shares * width), jnp.bfloat16)
    return call(place_kernel, results, [out], scalars=order)[0]


CHUNKS = 2


def power_of_two(n):
    return n & (n - 1) == 0


def body(queries, new_keys, new_values, cache_keys, cache_values, selection):
    qblocks, head_count, top_count = selection.shape
    seq_count = lax.axis_size("seq")
    shares = lax.axis_size("heads") * lax.axis_size("sub")
    every = top_count == cache_keys.shape[0] // BLOCK * seq_count and qblocks == 1
    fits = seq_count == 4 and power_of_two(shares) and shares % CHUNKS == 0
    if every and fits and 4 * head_count <= STAT:
        return dense_body(queries, new_keys, new_values, cache_keys, cache_values)
    return sparse_body(queries, new_keys, new_values, cache_keys, cache_values, selection)


def solution(mesh):
    in_specs = (
        P(("groups", "seq", "heads", "sub"), None),
        P(("groups", "seq", "heads", "sub"), None),
        P(("groups", "seq", "heads", "sub"), None),
        P(("groups", "seq"), ("heads", "sub")),
        P(("groups", "seq"), ("heads", "sub")),
        P(("groups", "seq"), ("heads", "sub"), None),
    )
    out_specs = P(("groups", "seq", "heads", "sub"), None)
    return jax.shard_map(body, mesh=mesh, in_specs=in_specs, out_specs=out_specs, check_vma=False)
```

```python
import functools
import math

import jax
import jax.numpy as jnp
from jax import lax
from jax.experimental import pallas as pl
from jax.experimental.pallas import tpu as pltpu
from jax.sharding import PartitionSpec as P

HD = 128
BLOCK = 512


def order_ranks(owners):
    length = owners.shape[-1]
    counter = jnp.arange(length)
    earlier = counter[None, :] < counter[:, None]
    same_owner = owners[..., :, None] == owners[..., None, :]
    return jnp.sum(jnp.logical_and(same_owner, earlier), axis=-1)


def one_hot(values, length):
    return (values[..., None] == jnp.arange(length)).astype(jnp.float32)


def own_partial(query_blocks, key_blocks, value_blocks, scaling):
    scores = (
        jnp.einsum("bqhd,bkhd->bhqk", query_blocks, key_blocks, preferred_element_type=jnp.float32)
        * scaling
    )
    length = query_blocks.shape[1]
    causal = jnp.arange(length)[:, None] >= jnp.arange(length)[None, :]
    scores = jnp.where(causal, scores, -jnp.inf)
    highest = jnp.max(scores, axis=-1)
    weights = jnp.exp(scores - highest[..., None])
    totals = jnp.sum(weights, axis=-1)
    mixed = jnp.einsum(
        "bhqk,bkhd->bhqd",
        weights.astype(jnp.bfloat16),
        value_blocks,
        preferred_element_type=jnp.float32,
    )
    return (mixed, highest, totals)


def tile_partial(query_blocks, tile_pair, scaling):
    head_size = query_blocks.shape[-1]
    scores = (
        jnp.einsum(
            "bqhd,bhkd->bhqk",
            query_blocks,
            tile_pair[..., :head_size],
            preferred_element_type=jnp.float32,
        )
        * scaling
    )
    highest = jnp.max(scores, axis=-1)
    weights = jnp.exp(scores - highest[..., None])
    totals = jnp.sum(weights, axis=-1)
    mixed = jnp.einsum(
        "bhqk,bhkd->bhqd",
        weights.astype(jnp.bfloat16),
        tile_pair[..., head_size:],
        preferred_element_type=jnp.float32,
    )
    return (mixed, highest, totals)


def merge_parts(parts):
    top = parts[0][1]
    for part in parts[1:]:
        top = jnp.maximum(top, part[1])
    numer = jnp.zeros(parts[0][0].shape, jnp.float32)
    denom = jnp.zeros(parts[0][2].shape, jnp.float32)
    for part in parts:
        factor = jnp.exp(part[1] - top)
        numer = numer + factor[..., None] * part[0]
        denom = denom + factor * part[2]
    return numer / denom[..., None]


def sparse_body(queries, new_keys, new_values, cache_keys, cache_values, selection):
    heads_q, heads_k, heads_v = (
        lax.all_to_all(queries, ("heads", "sub"), split_axis=1, concat_axis=0, tiled=True),
        lax.all_to_all(new_keys, ("heads", "sub"), split_axis=1, concat_axis=0, tiled=True),
        lax.all_to_all(new_values, ("heads", "sub"), split_axis=1, concat_axis=0, tiled=True),
    )
    qblocks, head_count, top_count = selection.shape
    head_size = HD
    scaling = head_size ** (-0.5)
    shaped = (qblocks, BLOCK, head_count, head_size)
    query_blocks = heads_q.reshape(shaped)
    own = own_partial(query_blocks, heads_k.reshape(shaped), heads_v.reshape(shaped), scaling)
    seq_count = lax.axis_size("seq")
    myself = lax.axis_index("seq")
    cache_blocks = cache_keys.shape[0] // BLOCK
    tile_count = cache_blocks * head_count
    request_count = qblocks * head_count * top_count
    capacity = -(-request_count // seq_count)
    requests_all = lax.all_gather(selection, "seq", axis=0, tiled=True).reshape(
        seq_count, request_count
    )
    head_of = jnp.arange(request_count) // top_count % head_count
    my_requests = selection.reshape(request_count)
    my_owner = my_requests // cache_blocks
    my_slot = my_owner * capacity + order_ranks(my_owner)
    key_tiles = cache_keys.reshape(cache_blocks, BLOCK, head_count, head_size).transpose(0, 2, 1, 3)
    value_tiles = cache_values.reshape(cache_blocks, BLOCK, head_count, head_size).transpose(
        0, 2, 1, 3
    )
    tile_set = jnp.concatenate([key_tiles, value_tiles], axis=-1).reshape(
        tile_count, BLOCK, 2 * head_size
    )
    their_owner = requests_all // cache_blocks
    local_tile = requests_all % cache_blocks * head_count + head_of[None, :]
    served = (their_owner == myself).astype(jnp.float32)
    slot_pick = one_hot(order_ranks(their_owner), capacity) * served[..., None]
    picking = jnp.einsum("erc,erl->ecl", slot_pick, one_hot(local_tile, tile_count)).astype(
        jnp.bfloat16
    )
    parts = [own]
    outgoing = jnp.einsum(
        "ecl,lkf->eckf", picking, tile_set, preferred_element_type=jnp.float32
    ).astype(jnp.bfloat16)
    incoming = lax.all_to_all(outgoing, "seq", split_axis=0, concat_axis=0, tiled=True)
    fetched = incoming.reshape(seq_count * capacity, BLOCK, 2 * head_size)[my_slot]
    fetched = fetched.reshape(qblocks, head_count, top_count, BLOCK, 2 * head_size)
    for turn in range(top_count):
        parts.append(tile_partial(query_blocks, fetched[:, :, turn], scaling))
    result = merge_parts(parts)
    result = (
        result.transpose(0, 2, 1, 3)
        .reshape(qblocks * BLOCK, head_count * head_size)
        .astype(jnp.bfloat16)
    )
    return lax.all_to_all(result, ("heads", "sub"), split_axis=0, concat_axis=1, tiled=True)


STAT = 16
UNIT = 32767.0
LEAST = 1.2e-34
C2 = math.log2(math.e) * HD**-0.5


def scores_of(q, k, mask=None):
    s = lax.dot_general(k, q, (((1,), (1,)), ((), ())), preferred_element_type=jnp.float32)
    return s if mask is None else jnp.where(mask, s, -jnp.inf)


def weights_of(s):
    m = jnp.max(s, axis=0, keepdims=True)
    p = jnp.exp2((s - m) * C2)
    return p.astype(jnp.bfloat16), m * C2, jnp.sum(p, axis=0, keepdims=True)


def values_of(v, w, v_dim):
    return lax.dot_general(v, w, (((v_dim,), (0,)), ((), ())), preferred_element_type=jnp.float32)


def attend(tiles):
    count = len(tiles)
    s, w, parts = {}, {}, []
    for t in range(count + 2):
        if t < count:
            s[t] = tiles[t][0]()
        if 1 <= t <= count:
            w[t - 1] = weights_of(s.pop(t - 1))
        if t >= 2:
            weights, m, total = w.pop(t - 2)
            parts.append((tiles[t - 2][1](weights), m, total))
    return parts


def join(parts):
    top = functools.reduce(jnp.maximum, [m for _, m, _ in parts])
    factors = [jnp.exp2(m - top) for _, m, _ in parts]
    numer = sum(f * o for f, (o, _, _) in zip(factors, parts))
    denom = sum(f * t for f, (_, _, t) in zip(factors, parts))
    return numer, top, denom


def put(out_ref, heads):
    width, rows = len(heads) * HD, heads[0][0].shape[1]
    at = lax.broadcasted_iota(jnp.int32, (STAT, rows), 0)
    stats = jnp.zeros((STAT, rows), jnp.float32)
    for h, (numer, top, denom) in enumerate(heads):
        most = jnp.maximum(jnp.max(jnp.abs(numer), axis=0, keepdims=True), LEAST)
        code = jnp.round(numer * (UNIT / most))
        out_ref[h * HD : (h + 1) * HD, :] = code.astype(jnp.int32).astype(jnp.int16)
        for j, value in enumerate((top + jnp.log2(denom), jnp.log2(most / (UNIT * denom)))):
            whole = jnp.floor(value)
            stats = jnp.where(at == 4 * h + 2 * j, whole, stats)
            stats = jnp.where(at == 4 * h + 2 * j + 1, jnp.round((value - whole) * UNIT), stats)
    out_ref[width : width + STAT, :] = stats.astype(jnp.int32).astype(jnp.int16)


def take(ref):
    width = ref.shape[0] - STAT
    stats = ref[width : width + STAT, :].astype(jnp.int32).astype(jnp.float32)
    heads = []
    for h in range(width // HD):
        code = ref[h * HD : (h + 1) * HD, :].astype(jnp.int32).astype(jnp.float32)
        weight = stats[4 * h : 4 * h + 1] + stats[4 * h + 1 : 4 * h + 2] * (1.0 / UNIT)
        unit = stats[4 * h + 2 : 4 * h + 3] + stats[4 * h + 3 : 4 * h + 4] * (1.0 / UNIT)
        heads.append((code, weight, unit))
    return heads


def join_taken(taken):
    top = functools.reduce(jnp.maximum, [w for _, w, _ in taken])
    numer = sum(code * jnp.exp2(w - top + unit) for code, w, unit in taken)
    denom = sum(jnp.exp2(w - top) for _, w, _ in taken)
    return numer, top, denom


def cached_tiles(q_of, ck_ref, cvt_ref, h):
    cols = slice(h * HD, (h + 1) * HD)
    tiles = []
    for b in range(ck_ref.shape[0] // BLOCK):
        rows = slice(b * BLOCK, (b + 1) * BLOCK)
        tiles.append(
            (
                lambda rows=rows: scores_of(q_of(cols), ck_ref[rows, cols]),
                lambda w, rows=rows: values_of(cvt_ref[cols, rows], w, 1),
            )
        )
    return tiles


def attend_heads(tiles_of_heads):
    parts = attend([t for tiles in tiles_of_heads for t in tiles])
    heads = []
    for tiles in tiles_of_heads:
        heads.append(join(parts[: len(tiles)]))
        parts = parts[len(tiles) :]
    return heads


def cached_kernel(q_ref, ck_ref, cvt_ref, out_ref):
    heads = range(ck_ref.shape[1] // HD)
    q_of = lambda cols: q_ref[:, cols]
    put(out_ref, attend_heads([cached_tiles(q_of, ck_ref, cvt_ref, h) for h in heads]))


def own_kernel(mine, order_ref, *refs):
    q_ref, *kv_refs, ck_ref, cvt_ref, out_ref = refs
    width = ck_ref.shape[1]
    rows = q_ref.shape[0]
    step = kv_refs[0].shape[0]

    def positions(shape, axis, pieces):
        at = lax.broadcasted_iota(jnp.int32, shape, axis)
        place = jnp.zeros(shape, jnp.int32)
        for i, d in enumerate(pieces):
            place = jnp.where(at // step == i, order_ref[d] * step + at % step, place)
        return place

    shape = (step * len(kv_refs), rows)
    mask = positions(shape, 1, mine) >= positions(shape, 0, range(len(kv_refs)))
    q_of = lambda cols: q_ref[:, cols]
    heads = []
    for h in range(width // HD):
        cols = slice(h * HD, (h + 1) * HD)
        vcols = slice(width + h * HD, width + (h + 1) * HD)
        own = (
            lambda cols=cols: scores_of(
                q_ref[:, cols], jnp.concatenate([r[:, cols] for r in kv_refs], axis=0), mask
            ),
            lambda w, vcols=vcols: values_of(
                jnp.concatenate([r[:, vcols] for r in kv_refs], axis=0), w, 0
            ),
        )
        heads.append([own] + cached_tiles(q_of, ck_ref, cvt_ref, h))
    put(out_ref, attend_heads(heads))


def merge_kernel(*refs):
    *in_refs, out_ref = refs
    put(out_ref, [join_taken(taken) for taken in zip(*[take(r) for r in in_refs])])


def final_kernel(count, *refs):
    in_refs, out_refs = refs[:count], refs[count:]
    step = out_refs[0].shape[0]
    for h, taken in enumerate(zip(*[take(r) for r in in_refs])):
        numer, _, denom = join_taken(taken)
        value = jnp.transpose(numer * (1.0 / denom)).astype(jnp.bfloat16)
        for i, out_ref in enumerate(out_refs):
            out_ref[:, h * HD : (h + 1) * HD] = value[i * step : (i + 1) * step]


def pick_kernel(pieces, count, order_ref, *refs):
    in_refs, out_refs, done = refs[:count], refs[count:-1], refs[-1]
    width = out_refs[0].shape[1] // count
    copies = []
    for d, out_ref in zip(pieces, out_refs):
        start = pl.multiple_of(order_ref[d] * width, width)
        for i, ref in enumerate(in_refs):
            source, target = ref.at[:, pl.ds(start, width)], out_ref.at[:, i * width : (i + 1) * width]
            copies.append(pltpu.make_async_copy(source, target, done.at[len(copies)]))
            copies[-1].start()
    for copy in copies:
        copy.wait()


def slice_kernel(pieces, order_ref, ref, *out_refs):
    width = out_refs[0].shape[1]
    for d, out_ref in zip(pieces, out_refs):
        out_ref[...] = ref[:, pl.ds(pl.multiple_of(order_ref[d] * width, width), width)]


def stack_kernel(count, *refs):
    out_ref = refs[-1]
    step = refs[0].shape[0]
    for i in range(count):
        out_ref[i * step : (i + 1) * step, :] = refs[i][...]


def place_kernel(order_ref, *refs):
    *pieces, out_ref = refs
    width = pieces[0].shape[1]
    for d, piece in enumerate(pieces):
        start = pl.multiple_of(order_ref[d] * width, width)
        out_ref[:, pl.ds(start, width)] = piece[...]


def move(kernel, copies, scalars, arrays, outs, unread=()):
    read = 1 + len(arrays)

    def without_unread(*refs):
        kernel(*refs[:read], *refs[read + len(unread) :])

    return pl.pallas_call(
        without_unread,
        out_shape=outs,
        in_specs=[pl.BlockSpec(memory_space=pltpu.SMEM)]
        + [pl.BlockSpec(memory_space=pl.ANY)] * (len(arrays) + len(unread)),
        out_specs=[pl.BlockSpec(memory_space=pltpu.VMEM)] * len(outs),
        scratch_shapes=[pltpu.SemaphoreType.DMA((copies,))],
        cost_estimate=pl.CostEstimate(flops=0, bytes_accessed=2 * 4 * outs[0].size, transcendentals=0),
    )(scalars, *arrays, *unread)


def call(kernel, arrays, outs, flops=0, exps=0, scalars=None, unread=()):
    moved = sum(a.size * a.dtype.itemsize for a in arrays)
    moved += sum(math.prod(o.shape) * o.dtype.itemsize for o in outs)
    first = [] if scalars is None else [scalars]
    read = len(first) + len(arrays)

    def without_unread(*refs):
        kernel(*refs[:read], *refs[read + len(unread) :])

    return pl.pallas_call(
        without_unread,
        out_shape=outs,
        in_specs=[pl.BlockSpec(memory_space=pltpu.SMEM)] * len(first)
        + [pl.BlockSpec(memory_space=pltpu.VMEM)] * len(arrays)
        + [pl.BlockSpec(memory_space=pl.ANY)] * len(unread),
        out_specs=[pl.BlockSpec(memory_space=pltpu.VMEM)] * len(outs),
        compiler_params=pltpu.CompilerParams(vmem_limit_bytes=16 * 1024 * 1024),
        cost_estimate=pl.CostEstimate(flops=flops, bytes_accessed=moved, transcendentals=exps),
    )(*first, *arrays, *unread)


def dense_body(queries, new_keys, new_values, cache_keys, cache_values):
    seq_count = lax.axis_size("seq")
    shares = lax.axis_size("heads") * lax.axis_size("sub")
    me = lax.axis_index("heads") * lax.axis_size("sub") + lax.axis_index("sub")
    step, width = queries.shape[0], queries.shape[1] // shares
    cached = cache_keys.shape[0]
    each = shares // CHUNKS
    rows = each * step
    chunk = jax.ShapeDtypeStruct((rows, width), jnp.bfloat16)
    piece = jax.ShapeDtypeStruct((step, width), jnp.bfloat16)
    pair = jax.ShapeDtypeStruct((step, 2 * width), jnp.bfloat16)
    packed = jax.ShapeDtypeStruct((width + STAT, rows), jnp.int16)
    tile_flops = 4 * rows * cached * width
    tile_exps = rows * cached * (width // HD)

    def swap(x, d):
        return lax.ppermute(x, ("heads", "sub"), [(i, i ^ d) for i in range(shares)])

    def along(x, bit):
        return lax.ppermute(x, "seq", [(i, i ^ bit) for i in range(seq_count)])

    def after(x, unread):
        like = jax.ShapeDtypeStruct(x.shape, x.dtype)
        return call(functools.partial(stack_kernel, 1), [x], [like], unread=unread)[0] if unread else x

    order = jnp.stack([me ^ d for d in range(shares)]).astype(jnp.int32)
    cache_vt = cache_values.T
    context = [cache_keys, cache_vt]

    def attend(q):
        return call(cached_kernel, [q, *context], [packed], tile_flops, tile_exps)[0]

    def attend_own(q, pieces, unread):
        return call(
            functools.partial(own_kernel, pieces),
            [q, *kv, *context],
            [packed],
            tile_flops * 3 // 2,
            tile_exps * 3 // 2,
            order,
            unread,
        )[0]

    def merge(mine, got):
        return call(merge_kernel, [mine, got], [packed])[0]

    def end(parts, pieces):
        ended = call(functools.partial(final_kernel, len(parts)), parts, [piece] * each)
        return [swap(x, d) if d else x for x, d in zip(ended, pieces)]

    pieces_a, pieces_b = range(each), range(each, shares)

    def pick(arrays, pieces, out, unread=()):
        kernel = functools.partial(pick_kernel, pieces, len(arrays))
        count = len(pieces)
        return move(kernel, count * len(arrays), order, arrays, [out] * count, unread)

    def slices(pieces):
        kernel = functools.partial(slice_kernel, pieces)
        return call(kernel, [queries], [piece] * each, scalars=order)

    q = [swap(x, d) if d else x for x, d in zip(slices(pieces_a), pieces_a)]
    a = call(functools.partial(stack_kernel, each), q, [chunk])[0]
    q = slices(pieces_b)
    a2, a1 = along(a, 2), along(a, 1)
    q = [swap(x, d) for x, d in zip(q, pieces_b)]
    b = call(functools.partial(stack_kernel, each), q, [chunk])[0]
    b2, b1 = along(b, 2), along(b, 1)
    kv = pick([new_keys, new_values], range(shares), pair, [b, cache_vt])
    kv = [swap(x, d) if d else x for d, x in enumerate(kv)]
    part_a2, part_a1 = attend(a2), attend(a1)
    b3 = along(after(b2, [part_a2, part_a1]), 1)
    part_b2 = attend(b2)
    a3 = along(after(a2, [part_b2, b1, *kv[1:]]), 1)
    got_b2 = along(attend(b3), 1)
    got_a2 = along(attend(a3), 1)
    part_b2 = merge(part_b2, got_b2)
    from_b2 = along(part_b2, 2)
    from_b1 = along(after(attend(b1), [part_b2]), 1)
    own_b, own_a = [attend_own(*x, [part_b2]) for x in ((b, pieces_b), (a, pieces_a))]
    part_a2 = merge(part_a2, after(got_a2, [own_a, own_b]))
    from_a2 = along(part_a2, 2)
    from_a1 = along(after(part_a1, [part_a2]), 1)
    out_b = end([own_b, from_b2, from_b1], pieces_b)
    out_a = end([own_a, from_a2, from_a1], pieces_a)
    results = [*out_a, *out_b]
    out = jax.ShapeDtypeStruct((step, shares * width), jnp.bfloat16)
    return call(place_kernel, results, [out], scalars=order)[0]


CHUNKS = 2


def power_of_two(n):
    return n & (n - 1) == 0


def body(queries, new_keys, new_values, cache_keys, cache_values, selection):
    qblocks, head_count, top_count = selection.shape
    seq_count = lax.axis_size("seq")
    shares = lax.axis_size("heads") * lax.axis_size("sub")
    every = top_count == cache_keys.shape[0] // BLOCK * seq_count and qblocks == 1
    fits = seq_count == 4 and power_of_two(shares) and shares % CHUNKS == 0
    if every and fits and 4 * head_count <= STAT:
        return dense_body(queries, new_keys, new_values, cache_keys, cache_values)
    return sparse_body(queries, new_keys, new_values, cache_keys, cache_values, selection)


def solution(mesh):
    in_specs = (
        P(("groups", "seq", "heads", "sub"), None),
        P(("groups", "seq", "heads", "sub"), None),
        P(("groups", "seq", "heads", "sub"), None),
        P(("groups", "seq"), ("heads", "sub")),
        P(("groups", "seq"), ("heads", "sub")),
        P(("groups", "seq"), ("heads", "sub"), None),
    )
    out_specs = P(("groups", "seq", "heads", "sub"), None)
    return jax.shard_map(body, mesh=mesh, in_specs=in_specs, out_specs=out_specs, check_vma=False)
```

```python
import functools
import math

import jax
import jax.numpy as jnp
from jax import lax
from jax.experimental import pallas as pl
from jax.experimental.pallas import tpu as pltpu
from jax.sharding import PartitionSpec as P

HD = 128
BLOCK = 512


def order_ranks(owners):
    length = owners.shape[-1]
    counter = jnp.arange(length)
    earlier = counter[None, :] < counter[:, None]
    same_owner = owners[..., :, None] == owners[..., None, :]
    return jnp.sum(jnp.logical_and(same_owner, earlier), axis=-1)


def one_hot(values, length):
    return (values[..., None] == jnp.arange(length)).astype(jnp.float32)


def own_partial(query_blocks, key_blocks, value_blocks, scaling):
    scores = (
        jnp.einsum("bqhd,bkhd->bhqk", query_blocks, key_blocks, preferred_element_type=jnp.float32)
        * scaling
    )
    length = query_blocks.shape[1]
    causal = jnp.arange(length)[:, None] >= jnp.arange(length)[None, :]
    scores = jnp.where(causal, scores, -jnp.inf)
    highest = jnp.max(scores, axis=-1)
    weights = jnp.exp(scores - highest[..., None])
    totals = jnp.sum(weights, axis=-1)
    mixed = jnp.einsum(
        "bhqk,bkhd->bhqd",
        weights.astype(jnp.bfloat16),
        value_blocks,
        preferred_element_type=jnp.float32,
    )
    return (mixed, highest, totals)


def tile_partial(query_blocks, tile_pair, scaling):
    head_size = query_blocks.shape[-1]
    scores = (
        jnp.einsum(
            "bqhd,bhkd->bhqk",
            query_blocks,
            tile_pair[..., :head_size],
            preferred_element_type=jnp.float32,
        )
        * scaling
    )
    highest = jnp.max(scores, axis=-1)
    weights = jnp.exp(scores - highest[..., None])
    totals = jnp.sum(weights, axis=-1)
    mixed = jnp.einsum(
        "bhqk,bhkd->bhqd",
        weights.astype(jnp.bfloat16),
        tile_pair[..., head_size:],
        preferred_element_type=jnp.float32,
    )
    return (mixed, highest, totals)


def merge_parts(parts):
    top = parts[0][1]
    for part in parts[1:]:
        top = jnp.maximum(top, part[1])
    numer = jnp.zeros(parts[0][0].shape, jnp.float32)
    denom = jnp.zeros(parts[0][2].shape, jnp.float32)
    for part in parts:
        factor = jnp.exp(part[1] - top)
        numer = numer + factor[..., None] * part[0]
        denom = denom + factor * part[2]
    return numer / denom[..., None]


def sparse_body(queries, new_keys, new_values, cache_keys, cache_values, selection):
    heads_q, heads_k, heads_v = (
        lax.all_to_all(queries, ("heads", "sub"), split_axis=1, concat_axis=0, tiled=True),
        lax.all_to_all(new_keys, ("heads", "sub"), split_axis=1, concat_axis=0, tiled=True),
        lax.all_to_all(new_values, ("heads", "sub"), split_axis=1, concat_axis=0, tiled=True),
    )
    qblocks, head_count, top_count = selection.shape
    head_size = HD
    scaling = head_size ** (-0.5)
    shaped = (qblocks, BLOCK, head_count, head_size)
    query_blocks = heads_q.reshape(shaped)
    own = own_partial(query_blocks, heads_k.reshape(shaped), heads_v.reshape(shaped), scaling)
    seq_count = lax.axis_size("seq")
    myself = lax.axis_index("seq")
    cache_blocks = cache_keys.shape[0] // BLOCK
    tile_count = cache_blocks * head_count
    request_count = qblocks * head_count * top_count
    capacity = -(-request_count // seq_count)
    requests_all = lax.all_gather(selection, "seq", axis=0, tiled=True).reshape(
        seq_count, request_count
    )
    head_of = jnp.arange(request_count) // top_count % head_count
    my_requests = selection.reshape(request_count)
    my_owner = my_requests // cache_blocks
    my_slot = my_owner * capacity + order_ranks(my_owner)
    key_tiles = cache_keys.reshape(cache_blocks, BLOCK, head_count, head_size).transpose(0, 2, 1, 3)
    value_tiles = cache_values.reshape(cache_blocks, BLOCK, head_count, head_size).transpose(
        0, 2, 1, 3
    )
    tile_set = jnp.concatenate([key_tiles, value_tiles], axis=-1).reshape(
        tile_count, BLOCK, 2 * head_size
    )
    their_owner = requests_all // cache_blocks
    local_tile = requests_all % cache_blocks * head_count + head_of[None, :]
    served = (their_owner == myself).astype(jnp.float32)
    slot_pick = one_hot(order_ranks(their_owner), capacity) * served[..., None]
    picking = jnp.einsum("erc,erl->ecl", slot_pick, one_hot(local_tile, tile_count)).astype(
        jnp.bfloat16
    )
    parts = [own]
    outgoing = jnp.einsum(
        "ecl,lkf->eckf", picking, tile_set, preferred_element_type=jnp.float32
    ).astype(jnp.bfloat16)
    incoming = lax.all_to_all(outgoing, "seq", split_axis=0, concat_axis=0, tiled=True)
    fetched = incoming.reshape(seq_count * capacity, BLOCK, 2 * head_size)[my_slot]
    fetched = fetched.reshape(qblocks, head_count, top_count, BLOCK, 2 * head_size)
    for turn in range(top_count):
        parts.append(tile_partial(query_blocks, fetched[:, :, turn], scaling))
    result = merge_parts(parts)
    result = (
        result.transpose(0, 2, 1, 3)
        .reshape(qblocks * BLOCK, head_count * head_size)
        .astype(jnp.bfloat16)
    )
    return lax.all_to_all(result, ("heads", "sub"), split_axis=0, concat_axis=1, tiled=True)


STAT = 16
UNIT = 32767.0
LEAST = 1.2e-34
C2 = math.log2(math.e) * HD**-0.5


def scores_of(q, k, mask=None):
    s = lax.dot_general(k, q, (((1,), (1,)), ((), ())), preferred_element_type=jnp.float32)
    return s if mask is None else jnp.where(mask, s, -jnp.inf)


def weights_of(s):
    m = jnp.max(s, axis=0, keepdims=True)
    p = jnp.exp2((s - m) * C2)
    return p.astype(jnp.bfloat16), m * C2, jnp.sum(p, axis=0, keepdims=True)


def values_of(v, w, v_dim):
    return lax.dot_general(v, w, (((v_dim,), (0,)), ((), ())), preferred_element_type=jnp.float32)


def attend(tiles):
    count = len(tiles)
    s, w, parts = {}, {}, []
    for t in range(count + 2):
        if t < count:
            s[t] = tiles[t][0]()
        if 1 <= t <= count:
            w[t - 1] = weights_of(s.pop(t - 1))
        if t >= 2:
            weights, m, total = w.pop(t - 2)
            parts.append((tiles[t - 2][1](weights), m, total))
    return parts


def join(parts):
    top = functools.reduce(jnp.maximum, [m for _, m, _ in parts])
    factors = [jnp.exp2(m - top) for _, m, _ in parts]
    numer = sum(f * o for f, (o, _, _) in zip(factors, parts))
    denom = sum(f * t for f, (_, _, t) in zip(factors, parts))
    return numer, top, denom


def put(out_ref, heads):
    width, rows = len(heads) * HD, heads[0][0].shape[1]
    at = lax.broadcasted_iota(jnp.int32, (STAT, rows), 0)
    stats = jnp.zeros((STAT, rows), jnp.float32)
    for h, (numer, top, denom) in enumerate(heads):
        most = jnp.maximum(jnp.max(jnp.abs(numer), axis=0, keepdims=True), LEAST)
        code = jnp.round(numer * (UNIT / most))
        out_ref[h * HD : (h + 1) * HD, :] = code.astype(jnp.int32).astype(jnp.int16)
        for j, value in enumerate((top + jnp.log2(denom), jnp.log2(most / (UNIT * denom)))):
            whole = jnp.floor(value)
            stats = jnp.where(at == 4 * h + 2 * j, whole, stats)
            stats = jnp.where(at == 4 * h + 2 * j + 1, jnp.round((value - whole) * UNIT), stats)
    out_ref[width : width + STAT, :] = stats.astype(jnp.int32).astype(jnp.int16)


def take(ref):
    width = ref.shape[0] - STAT
    stats = ref[width : width + STAT, :].astype(jnp.int32).astype(jnp.float32)
    heads = []
    for h in range(width // HD):
        code = ref[h * HD : (h + 1) * HD, :].astype(jnp.int32).astype(jnp.float32)
        weight = stats[4 * h : 4 * h + 1] + stats[4 * h + 1 : 4 * h + 2] * (1.0 / UNIT)
        unit = stats[4 * h + 2 : 4 * h + 3] + stats[4 * h + 3 : 4 * h + 4] * (1.0 / UNIT)
        heads.append((code, weight, unit))
    return heads


def join_taken(taken):
    top = functools.reduce(jnp.maximum, [w for _, w, _ in taken])
    numer = sum(code * jnp.exp2(w - top + unit) for code, w, unit in taken)
    denom = sum(jnp.exp2(w - top) for _, w, _ in taken)
    return numer, top, denom


def cached_tiles(q_of, ck_ref, cvt_ref, h):
    cols = slice(h * HD, (h + 1) * HD)
    tiles = []
    for b in range(ck_ref.shape[0] // BLOCK):
        rows = slice(b * BLOCK, (b + 1) * BLOCK)
        tiles.append(
            (
                lambda rows=rows: scores_of(q_of(cols), ck_ref[rows, cols]),
                lambda w, rows=rows: values_of(cvt_ref[cols, rows], w, 1),
            )
        )
    return tiles


def attend_heads(tiles_of_heads):
    parts = attend([t for tiles in tiles_of_heads for t in tiles])
    heads = []
    for tiles in tiles_of_heads:
        heads.append(join(parts[: len(tiles)]))
        parts = parts[len(tiles) :]
    return heads


def cached_kernel(q_ref, ck_ref, cvt_ref, out_ref):
    heads = range(ck_ref.shape[1] // HD)
    q_of = lambda cols: q_ref[:, cols]
    put(out_ref, attend_heads([cached_tiles(q_of, ck_ref, cvt_ref, h) for h in heads]))


def own_kernel(mine, order_ref, *refs):
    q_ref, *kv_refs, ck_ref, cvt_ref, out_ref = refs
    width = ck_ref.shape[1]
    rows = q_ref.shape[0]
    step = kv_refs[0].shape[0]

    def positions(shape, axis, pieces):
        at = lax.broadcasted_iota(jnp.int32, shape, axis)
        place = jnp.zeros(shape, jnp.int32)
        for i, d in enumerate(pieces):
            place = jnp.where(at // step == i, order_ref[d] * step + at % step, place)
        return place

    shape = (step * len(kv_refs), rows)
    mask = positions(shape, 1, mine) >= positions(shape, 0, range(len(kv_refs)))
    q_of = lambda cols: q_ref[:, cols]
    heads = []
    for h in range(width // HD):
        cols = slice(h * HD, (h + 1) * HD)
        vcols = slice(width + h * HD, width + (h + 1) * HD)
        own = (
            lambda cols=cols: scores_of(
                q_ref[:, cols], jnp.concatenate([r[:, cols] for r in kv_refs], axis=0), mask
            ),
            lambda w, vcols=vcols: values_of(
                jnp.concatenate([r[:, vcols] for r in kv_refs], axis=0), w, 0
            ),
        )
        heads.append([own] + cached_tiles(q_of, ck_ref, cvt_ref, h))
    put(out_ref, attend_heads(heads))


def merge_kernel(*refs):
    *in_refs, out_ref = refs
    put(out_ref, [join_taken(taken) for taken in zip(*[take(r) for r in in_refs])])


def final_kernel(count, *refs):
    in_refs, out_refs = refs[:count], refs[count:]
    step = out_refs[0].shape[0]
    for h, taken in enumerate(zip(*[take(r) for r in in_refs])):
        numer, _, denom = join_taken(taken)
        value = jnp.transpose(numer * (1.0 / denom)).astype(jnp.bfloat16)
        for i, out_ref in enumerate(out_refs):
            out_ref[:, h * HD : (h + 1) * HD] = value[i * step : (i + 1) * step]


def pick_kernel(pieces, count, order_ref, *refs):
    in_refs, out_refs, done = refs[:count], refs[count:-1], refs[-1]
    width = out_refs[0].shape[1] // count
    copies = []
    for d, out_ref in zip(pieces, out_refs):
        start = pl.multiple_of(order_ref[d] * width, width)
        for i, ref in enumerate(in_refs):
            source, target = ref.at[:, pl.ds(start, width)], out_ref.at[:, i * width : (i + 1) * width]
            copies.append(pltpu.make_async_copy(source, target, done.at[len(copies)]))
            copies[-1].start()
    for copy in copies:
        copy.wait()


def slice_kernel(pieces, order_ref, ref, *out_refs):
    width = out_refs[0].shape[1]
    for d, out_ref in zip(pieces, out_refs):
        out_ref[...] = ref[:, pl.ds(pl.multiple_of(order_ref[d] * width, width), width)]


def stack_kernel(count, *refs):
    out_ref = refs[-1]
    step = refs[0].shape[0]
    for i in range(count):
        out_ref[i * step : (i + 1) * step, :] = refs[i][...]


def place_kernel(order_ref, *refs):
    *pieces, out_ref = refs
    width = pieces[0].shape[1]
    for d, piece in enumerate(pieces):
        start = pl.multiple_of(order_ref[d] * width, width)
        out_ref[:, pl.ds(start, width)] = piece[...]


def move(kernel, copies, scalars, arrays, outs, unread=()):
    read = 1 + len(arrays)

    def without_unread(*refs):
        kernel(*refs[:read], *refs[read + len(unread) :])

    return pl.pallas_call(
        without_unread,
        out_shape=outs,
        in_specs=[pl.BlockSpec(memory_space=pltpu.SMEM)]
        + [pl.BlockSpec(memory_space=pl.ANY)] * (len(arrays) + len(unread)),
        out_specs=[pl.BlockSpec(memory_space=pltpu.VMEM)] * len(outs),
        scratch_shapes=[pltpu.SemaphoreType.DMA((copies,))],
        cost_estimate=pl.CostEstimate(flops=0, bytes_accessed=2 * 4 * outs[0].size, transcendentals=0),
    )(scalars, *arrays, *unread)


def call(kernel, arrays, outs, flops=0, exps=0, scalars=None, unread=()):
    moved = sum(a.size * a.dtype.itemsize for a in arrays)
    moved += sum(math.prod(o.shape) * o.dtype.itemsize for o in outs)
    first = [] if scalars is None else [scalars]
    return pl.pallas_call(
        kernel,
        out_shape=outs,
        in_specs=[pl.BlockSpec(memory_space=pltpu.SMEM)] * len(first)
        + [pl.BlockSpec(memory_space=pltpu.VMEM)] * len(arrays)
        + [pl.BlockSpec(memory_space=pl.ANY)] * len(unread),
        out_specs=[pl.BlockSpec(memory_space=pltpu.VMEM)] * len(outs),
        compiler_params=pltpu.CompilerParams(vmem_limit_bytes=16 * 1024 * 1024),
        cost_estimate=pl.CostEstimate(flops=flops, bytes_accessed=moved, transcendentals=exps),
    )(*first, *arrays, *unread)


def dense_body(queries, new_keys, new_values, cache_keys, cache_values):
    seq_count = lax.axis_size("seq")
    shares = lax.axis_size("heads") * lax.axis_size("sub")
    me = lax.axis_index("heads") * lax.axis_size("sub") + lax.axis_index("sub")
    step, width = queries.shape[0], queries.shape[1] // shares
    cached = cache_keys.shape[0]
    each = shares // CHUNKS
    rows = each * step
    chunk = jax.ShapeDtypeStruct((rows, width), jnp.bfloat16)
    piece = jax.ShapeDtypeStruct((step, width), jnp.bfloat16)
    pair = jax.ShapeDtypeStruct((step, 2 * width), jnp.bfloat16)
    packed = jax.ShapeDtypeStruct((width + STAT, rows), jnp.int16)
    tile_flops = 4 * rows * cached * width
    tile_exps = rows * cached * (width // HD)

    def swap(x, d):
        return lax.ppermute(x, ("heads", "sub"), [(i, i ^ d) for i in range(shares)])

    def along(x, bit):
        return lax.ppermute(x, "seq", [(i, i ^ bit) for i in range(seq_count)])

    def after(x, unread):
        like = jax.ShapeDtypeStruct(x.shape, x.dtype)
        return call(functools.partial(stack_kernel, 1), [x], [like], unread=unread)[0] if unread else x

    order = jnp.stack([me ^ d for d in range(shares)]).astype(jnp.int32)
    cache_vt = cache_values.T
    context = [cache_keys, cache_vt]

    def attend(q):
        return call(cached_kernel, [q, *context], [packed], tile_flops, tile_exps)[0]

    def attend_own(q, pieces):
        return call(
            functools.partial(own_kernel, pieces),
            [q, *kv, *context],
            [packed],
            tile_flops * 3 // 2,
            tile_exps * 3 // 2,
            order,
        )[0]

    def merge(mine, got):
        return call(merge_kernel, [mine, got], [packed])[0]

    def end(parts, pieces):
        ended = call(functools.partial(final_kernel, len(parts)), parts, [piece] * each)
        return [swap(x, d) if d else x for x, d in zip(ended, pieces)]

    pieces_a, pieces_b = range(each), range(each, shares)

    def pick(arrays, pieces, out, unread=()):
        kernel = functools.partial(pick_kernel, pieces, len(arrays))
        count = len(pieces)
        return move(kernel, count * len(arrays), order, arrays, [out] * count, unread)

    def slices(pieces):
        kernel = functools.partial(slice_kernel, pieces)
        return call(kernel, [queries], [piece] * each, scalars=order)

    q = [swap(x, d) if d else x for x, d in zip(slices(pieces_a), pieces_a)]
    a = call(functools.partial(stack_kernel, each), q, [chunk])[0]
    q = slices(pieces_b)
    a2, a1 = along(a, 2), along(a, 1)
    q = [swap(x, d) for x, d in zip(q, pieces_b)]
    kv = pick([new_keys, new_values], range(shares), pair)
    b = call(functools.partial(stack_kernel, each), q, [chunk], unread=[kv[0], cache_vt])[0]
    b2, b1 = along(b, 2), along(b, 1)
    kv = [swap(after(x, [b]), d) if d else x for d, x in enumerate(kv)]
    part_a2, part_a1 = attend(a2), attend(a1)
    b3 = along(after(b2, [part_a2, part_a1, b1]), 1)
    part_b2 = attend(b2)
    a3 = along(after(a2, [part_b2, b1, *kv[1:]]), 1)
    got_b2 = along(attend(b3), 1)
    got_a2 = along(attend(a3), 1)
    part_b2 = merge(part_b2, got_b2)
    from_b2 = along(part_b2, 2)
    from_b1 = along(after(attend(b1), [part_b2]), 1)
    part_a2 = merge(part_a2, got_a2)
    from_a2 = along(part_a2, 2)
    from_a1 = along(after(part_a1, [part_a2]), 1)
    out_b = end([attend_own(b, pieces_b), from_b2, from_b1], pieces_b)
    out_a = end([attend_own(a, pieces_a), from_a2, from_a1], pieces_a)
    results = [*out_a, *out_b]
    out = jax.ShapeDtypeStruct((step, shares * width), jnp.bfloat16)
    return call(place_kernel, results, [out], scalars=order)[0]


CHUNKS = 2


def power_of_two(n):
    return n & (n - 1) == 0


def body(queries, new_keys, new_values, cache_keys, cache_values, selection):
    qblocks, head_count, top_count = selection.shape
    seq_count = lax.axis_size("seq")
    shares = lax.axis_size("heads") * lax.axis_size("sub")
    every = top_count == cache_keys.shape[0] // BLOCK * seq_count and qblocks == 1
    fits = seq_count == 4 and power_of_two(shares) and shares % CHUNKS == 0
    if every and fits and 4 * head_count <= STAT:
        return dense_body(queries, new_keys, new_values, cache_keys, cache_values)
    return sparse_body(queries, new_keys, new_values, cache_keys, cache_values, selection)


def solution(mesh):
    in_specs = (
        P(("groups", "seq", "heads", "sub"), None),
        P(("groups", "seq", "heads", "sub"), None),
        P(("groups", "seq", "heads", "sub"), None),
        P(("groups", "seq"), ("heads", "sub")),
        P(("groups", "seq"), ("heads", "sub")),
        P(("groups", "seq"), ("heads", "sub"), None),
    )
    out_specs = P(("groups", "seq", "heads", "sub"), None)
    return jax.shard_map(body, mesh=mesh, in_specs=in_specs, out_specs=out_specs, check_vma=False)
```

```python
import functools
import math

import jax
import jax.numpy as jnp
from jax import lax
from jax.experimental import pallas as pl
from jax.experimental.pallas import tpu as pltpu
from jax.sharding import PartitionSpec as P

HD = 128
BLOCK = 512


def order_ranks(owners):
    length = owners.shape[-1]
    counter = jnp.arange(length)
    earlier = counter[None, :] < counter[:, None]
    same_owner = owners[..., :, None] == owners[..., None, :]
    return jnp.sum(jnp.logical_and(same_owner, earlier), axis=-1)


def one_hot(values, length):
    return (values[..., None] == jnp.arange(length)).astype(jnp.float32)


def own_partial(query_blocks, key_blocks, value_blocks, scaling):
    scores = (
        jnp.einsum("bqhd,bkhd->bhqk", query_blocks, key_blocks, preferred_element_type=jnp.float32)
        * scaling
    )
    length = query_blocks.shape[1]
    causal = jnp.arange(length)[:, None] >= jnp.arange(length)[None, :]
    scores = jnp.where(causal, scores, -jnp.inf)
    highest = jnp.max(scores, axis=-1)
    weights = jnp.exp(scores - highest[..., None])
    totals = jnp.sum(weights, axis=-1)
    mixed = jnp.einsum(
        "bhqk,bkhd->bhqd",
        weights.astype(jnp.bfloat16),
        value_blocks,
        preferred_element_type=jnp.float32,
    )
    return (mixed, highest, totals)


def tile_partial(query_blocks, tile_pair, scaling):
    head_size = query_blocks.shape[-1]
    scores = (
        jnp.einsum(
            "bqhd,bhkd->bhqk",
            query_blocks,
            tile_pair[..., :head_size],
            preferred_element_type=jnp.float32,
        )
        * scaling
    )
    highest = jnp.max(scores, axis=-1)
    weights = jnp.exp(scores - highest[..., None])
    totals = jnp.sum(weights, axis=-1)
    mixed = jnp.einsum(
        "bhqk,bhkd->bhqd",
        weights.astype(jnp.bfloat16),
        tile_pair[..., head_size:],
        preferred_element_type=jnp.float32,
    )
    return (mixed, highest, totals)


def merge_parts(parts):
    top = parts[0][1]
    for part in parts[1:]:
        top = jnp.maximum(top, part[1])
    numer = jnp.zeros(parts[0][0].shape, jnp.float32)
    denom = jnp.zeros(parts[0][2].shape, jnp.float32)
    for part in parts:
        factor = jnp.exp(part[1] - top)
        numer = numer + factor[..., None] * part[0]
        denom = denom + factor * part[2]
    return numer / denom[..., None]


def sparse_body(queries, new_keys, new_values, cache_keys, cache_values, selection):
    heads_q, heads_k, heads_v = (
        lax.all_to_all(queries, ("heads", "sub"), split_axis=1, concat_axis=0, tiled=True),
        lax.all_to_all(new_keys, ("heads", "sub"), split_axis=1, concat_axis=0, tiled=True),
        lax.all_to_all(new_values, ("heads", "sub"), split_axis=1, concat_axis=0, tiled=True),
    )
    qblocks, head_count, top_count = selection.shape
    head_size = HD
    scaling = head_size ** (-0.5)
    shaped = (qblocks, BLOCK, head_count, head_size)
    query_blocks = heads_q.reshape(shaped)
    own = own_partial(query_blocks, heads_k.reshape(shaped), heads_v.reshape(shaped), scaling)
    seq_count = lax.axis_size("seq")
    myself = lax.axis_index("seq")
    cache_blocks = cache_keys.shape[0] // BLOCK
    tile_count = cache_blocks * head_count
    request_count = qblocks * head_count * top_count
    capacity = -(-request_count // seq_count)
    requests_all = lax.all_gather(selection, "seq", axis=0, tiled=True).reshape(
        seq_count, request_count
    )
    head_of = jnp.arange(request_count) // top_count % head_count
    my_requests = selection.reshape(request_count)
    my_owner = my_requests // cache_blocks
    my_slot = my_owner * capacity + order_ranks(my_owner)
    key_tiles = cache_keys.reshape(cache_blocks, BLOCK, head_count, head_size).transpose(0, 2, 1, 3)
    value_tiles = cache_values.reshape(cache_blocks, BLOCK, head_count, head_size).transpose(
        0, 2, 1, 3
    )
    tile_set = jnp.concatenate([key_tiles, value_tiles], axis=-1).reshape(
        tile_count, BLOCK, 2 * head_size
    )
    their_owner = requests_all // cache_blocks
    local_tile = requests_all % cache_blocks * head_count + head_of[None, :]
    served = (their_owner == myself).astype(jnp.float32)
    slot_pick = one_hot(order_ranks(their_owner), capacity) * served[..., None]
    picking = jnp.einsum("erc,erl->ecl", slot_pick, one_hot(local_tile, tile_count)).astype(
        jnp.bfloat16
    )
    parts = [own]
    outgoing = jnp.einsum(
        "ecl,lkf->eckf", picking, tile_set, preferred_element_type=jnp.float32
    ).astype(jnp.bfloat16)
    incoming = lax.all_to_all(outgoing, "seq", split_axis=0, concat_axis=0, tiled=True)
    fetched = incoming.reshape(seq_count * capacity, BLOCK, 2 * head_size)[my_slot]
    fetched = fetched.reshape(qblocks, head_count, top_count, BLOCK, 2 * head_size)
    for turn in range(top_count):
        parts.append(tile_partial(query_blocks, fetched[:, :, turn], scaling))
    result = merge_parts(parts)
    result = (
        result.transpose(0, 2, 1, 3)
        .reshape(qblocks * BLOCK, head_count * head_size)
        .astype(jnp.bfloat16)
    )
    return lax.all_to_all(result, ("heads", "sub"), split_axis=0, concat_axis=1, tiled=True)


STAT = 16
UNIT = 32767.0
LEAST = 1.2e-34
NEVER = -1.0e9
C2 = math.log2(math.e) * HD**-0.5


def scores_of(q, k, mask=None):
    s = lax.dot_general(k, q, (((1,), (1,)), ((), ())), preferred_element_type=jnp.float32)
    return s if mask is None else jnp.where(mask, s, -jnp.inf)


def weights_of(s):
    m = jnp.max(s, axis=0, keepdims=True)
    p = jnp.exp2((s - m) * C2)
    return p.astype(jnp.bfloat16), m * C2, jnp.sum(p, axis=0, keepdims=True)


def values_of(v, w, v_dim):
    return lax.dot_general(v, w, (((v_dim,), (0,)), ((), ())), preferred_element_type=jnp.float32)


def attend(tiles):
    count = len(tiles)
    s, w, parts = {}, {}, []
    for t in range(count + 2):
        if t < count:
            s[t] = tiles[t][0]()
        if 1 <= t <= count:
            w[t - 1] = weights_of(s.pop(t - 1))
        if t >= 2:
            weights, m, total = w.pop(t - 2)
            parts.append((tiles[t - 2][1](weights), m, total))
    return parts


def join(parts):
    top = functools.reduce(jnp.maximum, [m for _, m, _ in parts])
    factors = [jnp.exp2(m - top) for _, m, _ in parts]
    numer = sum(f * o for f, (o, _, _) in zip(factors, parts))
    denom = sum(f * t for f, (_, _, t) in zip(factors, parts))
    return numer, top, denom


def put(out_ref, heads):
    width, rows = len(heads) * HD, heads[0][0].shape[1]
    at = lax.broadcasted_iota(jnp.int32, (STAT, rows), 0)
    stats = jnp.zeros((STAT, rows), jnp.float32)
    for h, (numer, top, denom) in enumerate(heads):
        most = jnp.maximum(jnp.max(jnp.abs(numer), axis=0, keepdims=True), LEAST)
        code = jnp.round(numer * (UNIT / most))
        out_ref[h * HD : (h + 1) * HD, :] = code.astype(jnp.int32).astype(jnp.int16)
        for j, value in enumerate((top + jnp.log2(denom), jnp.log2(most / (UNIT * denom)))):
            whole = jnp.floor(value)
            stats = jnp.where(at == 4 * h + 2 * j, whole, stats)
            stats = jnp.where(at == 4 * h + 2 * j + 1, jnp.round((value - whole) * UNIT), stats)
    out_ref[width : width + STAT, :] = stats.astype(jnp.int32).astype(jnp.int16)


def take(ref, valid=None):
    width = ref.shape[0] - STAT
    stats = ref[width : width + STAT, :].astype(jnp.int32).astype(jnp.float32)
    heads = []
    for h in range(width // HD):
        code = ref[h * HD : (h + 1) * HD, :].astype(jnp.int32).astype(jnp.float32)
        weight = stats[4 * h : 4 * h + 1] + stats[4 * h + 1 : 4 * h + 2] * (1.0 / UNIT)
        unit = stats[4 * h + 2 : 4 * h + 3] + stats[4 * h + 3 : 4 * h + 4] * (1.0 / UNIT)
        if valid is not None:
            weight = jnp.where(valid, weight, NEVER)
        heads.append((code, weight, unit))
    return heads


def join_taken(taken):
    top = functools.reduce(jnp.maximum, [w for _, w, _ in taken])
    numer = sum(code * jnp.exp2(w - top + unit) for code, w, unit in taken)
    denom = sum(jnp.exp2(w - top) for _, w, _ in taken)
    return numer, top, denom


def cached_tiles(q_of, ck_ref, cvt_ref, h):
    cols = slice(h * HD, (h + 1) * HD)
    tiles = []
    for b in range(ck_ref.shape[0] // BLOCK):
        rows = slice(b * BLOCK, (b + 1) * BLOCK)
        tiles.append(
            (
                lambda rows=rows: scores_of(q_of(cols), ck_ref[rows, cols]),
                lambda w, rows=rows: values_of(cvt_ref[cols, rows], w, 1),
            )
        )
    return tiles


def attend_heads(tiles_of_heads):
    parts = attend([t for tiles in tiles_of_heads for t in tiles])
    heads = []
    for tiles in tiles_of_heads:
        heads.append(join(parts[: len(tiles)]))
        parts = parts[len(tiles) :]
    return heads


def cached_kernel(q_ref, ck_ref, cvt_ref, out_ref):
    heads = range(ck_ref.shape[1] // HD)
    q_of = lambda cols: q_ref[:, cols]
    put(out_ref, attend_heads([cached_tiles(q_of, ck_ref, cvt_ref, h) for h in heads]))


def either_kernel(middle_ref, a_ref, b_ref, ck_ref, cvt_ref, out_ref):
    middle = middle_ref[0] > 0
    heads = range(ck_ref.shape[1] // HD)
    q_of = lambda cols: jnp.where(middle, a_ref[:, cols], b_ref[:, cols])
    put(out_ref, attend_heads([cached_tiles(q_of, ck_ref, cvt_ref, h) for h in heads]))


def own_kernel(mine, order_ref, *refs):
    q_ref, *kv_refs, ck_ref, cvt_ref, out_ref = refs
    width = ck_ref.shape[1]
    rows = q_ref.shape[0]
    step = kv_refs[0].shape[0]

    def positions(shape, axis, pieces):
        at = lax.broadcasted_iota(jnp.int32, shape, axis)
        place = jnp.zeros(shape, jnp.int32)
        for i, d in enumerate(pieces):
            place = jnp.where(at // step == i, order_ref[d] * step + at % step, place)
        return place

    shape = (step * len(kv_refs), rows)
    mask = positions(shape, 1, mine) >= positions(shape, 0, range(len(kv_refs)))
    q_of = lambda cols: q_ref[:, cols]
    heads = []
    for h in range(width // HD):
        cols = slice(h * HD, (h + 1) * HD)
        vcols = slice(width + h * HD, width + (h + 1) * HD)
        own = (
            lambda cols=cols: scores_of(
                q_ref[:, cols], jnp.concatenate([r[:, cols] for r in kv_refs], axis=0), mask
            ),
            lambda w, vcols=vcols: values_of(
                jnp.concatenate([r[:, vcols] for r in kv_refs], axis=0), w, 0
            ),
        )
        heads.append([own] + cached_tiles(q_of, ck_ref, cvt_ref, h))
    put(out_ref, attend_heads(heads))


def merge_kernel(*refs):
    *in_refs, out_ref = refs
    put(out_ref, [join_taken(taken) for taken in zip(*[take(r) for r in in_refs])])


def middle_merge_kernel(middle_ref, mine_ref, got_ref, out_ref):
    taken = zip(take(mine_ref), take(got_ref, middle_ref[0] > 0))
    put(out_ref, [join_taken(pair) for pair in taken])


def final_kernel(count, middle_ref, *refs):
    in_refs, out_refs = refs[:count], refs[count:]
    step = out_refs[0].shape[0]
    taken_of = [take(r) for r in in_refs[:3]] + [take(r, middle_ref[0] > 0) for r in in_refs[3:]]
    for h, taken in enumerate(zip(*taken_of)):
        numer, _, denom = join_taken(taken)
        value = jnp.transpose(numer * (1.0 / denom)).astype(jnp.bfloat16)
        for i, out_ref in enumerate(out_refs):
            out_ref[:, h * HD : (h + 1) * HD] = value[i * step : (i + 1) * step]


def pick_kernel(pieces, count, order_ref, *refs):
    in_refs, out_refs, done = refs[:count], refs[count:-1], refs[-1]
    width = out_refs[0].shape[1] // count
    copies = []
    for d, out_ref in zip(pieces, out_refs):
        start = pl.multiple_of(order_ref[d] * width, width)
        for i, ref in enumerate(in_refs):
            source, target = ref.at[:, pl.ds(start, width)], out_ref.at[:, i * width : (i + 1) * width]
            copies.append(pltpu.make_async_copy(source, target, done.at[len(copies)]))
            copies[-1].start()
    for copy in copies:
        copy.wait()


def slice_kernel(pieces, order_ref, ref, *out_refs):
    width = out_refs[0].shape[1]
    for d, out_ref in zip(pieces, out_refs):
        out_ref[...] = ref[:, pl.ds(pl.multiple_of(order_ref[d] * width, width), width)]


def stack_kernel(count, *refs):
    out_ref = refs[-1]
    step = refs[0].shape[0]
    for i in range(count):
        out_ref[i * step : (i + 1) * step, :] = refs[i][...]


def place_kernel(order_ref, *refs):
    *pieces, out_ref = refs
    width = pieces[0].shape[1]
    for d, piece in enumerate(pieces):
        start = pl.multiple_of(order_ref[d] * width, width)
        out_ref[:, pl.ds(start, width)] = piece[...]


def move(kernel, copies, scalars, arrays, outs, unread=()):
    read = 1 + len(arrays)

    def without_unread(*refs):
        kernel(*refs[:read], *refs[read + len(unread) :])

    return pl.pallas_call(
        without_unread,
        out_shape=outs,
        in_specs=[pl.BlockSpec(memory_space=pltpu.SMEM)]
        + [pl.BlockSpec(memory_space=pl.ANY)] * (len(arrays) + len(unread)),
        out_specs=[pl.BlockSpec(memory_space=pltpu.VMEM)] * len(outs),
        scratch_shapes=[pltpu.SemaphoreType.DMA((copies,))],
        cost_estimate=pl.CostEstimate(flops=0, bytes_accessed=2 * 4 * outs[0].size, transcendentals=0),
    )(scalars, *arrays, *unread)


def call(kernel, arrays, outs, flops=0, exps=0, scalars=None, unread=()):
    moved = sum(a.size * a.dtype.itemsize for a in arrays)
    moved += sum(math.prod(o.shape) * o.dtype.itemsize for o in outs)
    first = [] if scalars is None else [scalars]
    read = len(first) + len(arrays)

    def without_unread(*refs):
        kernel(*refs[:read], *refs[read + len(unread) :])

    return pl.pallas_call(
        without_unread,
        out_shape=outs,
        in_specs=[pl.BlockSpec(memory_space=pltpu.SMEM)] * len(first)
        + [pl.BlockSpec(memory_space=pltpu.VMEM)] * len(arrays)
        + [pl.BlockSpec(memory_space=pl.ANY)] * len(unread),
        out_specs=[pl.BlockSpec(memory_space=pltpu.VMEM)] * len(outs),
        compiler_params=pltpu.CompilerParams(vmem_limit_bytes=16 * 1024 * 1024),
        cost_estimate=pl.CostEstimate(flops=flops, bytes_accessed=moved, transcendentals=exps),
    )(*first, *arrays, *unread)


def dense_body(queries, new_keys, new_values, cache_keys, cache_values):
    seq_count = lax.axis_size("seq")
    shares = lax.axis_size("heads") * lax.axis_size("sub")
    me = lax.axis_index("heads") * lax.axis_size("sub") + lax.axis_index("sub")
    step, width = queries.shape[0], queries.shape[1] // shares
    cached = cache_keys.shape[0]
    each = shares // CHUNKS
    rows = each * step
    chunk = jax.ShapeDtypeStruct((rows, width), jnp.bfloat16)
    piece = jax.ShapeDtypeStruct((step, width), jnp.bfloat16)
    pair = jax.ShapeDtypeStruct((step, 2 * width), jnp.bfloat16)
    packed = jax.ShapeDtypeStruct((width + STAT, rows), jnp.int16)
    tile_flops = 4 * rows * cached * width
    tile_exps = rows * cached * (width // HD)

    def swap(x, d):
        return lax.ppermute(x, ("heads", "sub"), [(i, i ^ d) for i in range(shares)])

    def along(x, bit):
        return lax.ppermute(x, "seq", [(i, i ^ bit) for i in range(seq_count)])

    def after(x, unread):
        like = jax.ShapeDtypeStruct(x.shape, x.dtype)
        return call(functools.partial(stack_kernel, 1), [x], [like], unread=unread)[0] if unread else x

    order = jnp.stack([me ^ d for d in range(shares)]).astype(jnp.int32)
    cache_vt = cache_values.T
    context = [cache_keys, cache_vt]

    def attend(q):
        return call(cached_kernel, [q, *context], [packed], tile_flops, tile_exps)[0]

    def attend_own(q, pieces):
        return call(
            functools.partial(own_kernel, pieces),
            [q, *kv, *context],
            [packed],
            tile_flops * 3 // 2,
            tile_exps * 3 // 2,
            order,
        )[0]

    def merge(mine, got):
        return call(merge_kernel, [mine, got], [packed])[0]

    def end(parts, pieces):
        kernel = functools.partial(final_kernel, len(parts))
        ended = call(kernel, parts, [piece] * each, scalars=middle)
        return [swap(x, d) if d else x for x, d in zip(ended, pieces)]

    s = lax.axis_index("seq")
    middle = jnp.logical_and(s > 0, s < 3).astype(jnp.int32).reshape(1)

    pieces_a, pieces_b = range(each), range(each, shares)

    def pick(arrays, pieces, out, unread=()):
        kernel = functools.partial(pick_kernel, pieces, len(arrays))
        count = len(pieces)
        return move(kernel, count * len(arrays), order, arrays, [out] * count, unread)

    def slices(pieces):
        kernel = functools.partial(slice_kernel, pieces)
        return call(kernel, [queries], [piece] * each, scalars=order)

    q = [swap(x, d) if d else x for x, d in zip(slices(pieces_a), pieces_a)]
    a = call(functools.partial(stack_kernel, each), q, [chunk])[0]
    q = slices(pieces_b)
    a2, a1 = along(a, 2), along(a, 1)
    q = [swap(x, d) for x, d in zip(q, pieces_b)]
    b = call(functools.partial(stack_kernel, each), q, [chunk])[0]
    b2, b1 = along(b, 2), along(b, 1)
    kv = pick([new_keys, new_values], range(shares), pair, [b, cache_vt])
    kv = [swap(x, d) if d else x for d, x in enumerate(kv)]
    part_a2, part_a1 = attend(a2), attend(a1)
    b3 = along(after(b2, [part_a2, part_a1]), 1)
    part_b2 = attend(b2)
    a3_end = lax.ppermute(after(a2, [part_b2, b1, *kv[1:]]), "seq", [(1, 0), (2, 3)])
    a3_middle = lax.ppermute(after(a, [part_b2]), "seq", [(1, 2), (2, 1)])
    got_b2 = along(attend(b3), 1)
    arrays = [a3_middle, a3_end, *context]
    part_a3 = call(either_kernel, arrays, [packed], tile_flops, tile_exps, middle)[0]
    got_a2 = lax.ppermute(part_a3, "seq", [(0, 1), (3, 2)])
    part_b2 = merge(part_b2, got_b2)
    from_b2 = along(part_b2, 2)
    from_b1 = along(after(attend(b1), [part_b2]), 1)
    part_a2 = call(middle_merge_kernel, [part_a2, got_a2], [packed], scalars=middle)[0]
    from_a3 = lax.ppermute(after(part_a3, [part_b2]), "seq", [(1, 2), (2, 1)])
    from_a2 = along(part_a2, 2)
    from_a1 = along(after(part_a1, [part_a2]), 1)
    out_b = end([attend_own(b, pieces_b), from_b2, from_b1], pieces_b)
    out_a = end([attend_own(a, pieces_a), from_a2, from_a1, from_a3], pieces_a)
    results = [*out_a, *out_b]
    out = jax.ShapeDtypeStruct((step, shares * width), jnp.bfloat16)
    return call(place_kernel, results, [out], scalars=order)[0]


CHUNKS = 2


def power_of_two(n):
    return n & (n - 1) == 0


def body(queries, new_keys, new_values, cache_keys, cache_values, selection):
    qblocks, head_count, top_count = selection.shape
    seq_count = lax.axis_size("seq")
    shares = lax.axis_size("heads") * lax.axis_size("sub")
    every = top_count == cache_keys.shape[0] // BLOCK * seq_count and qblocks == 1
    fits = seq_count == 4 and power_of_two(shares) and shares % CHUNKS == 0
    if every and fits and 4 * head_count <= STAT:
        return dense_body(queries, new_keys, new_values, cache_keys, cache_values)
    return sparse_body(queries, new_keys, new_values, cache_keys, cache_values, selection)


def solution(mesh):
    in_specs = (
        P(("groups", "seq", "heads", "sub"), None),
        P(("groups", "seq", "heads", "sub"), None),
        P(("groups", "seq", "heads", "sub"), None),
        P(("groups", "seq"), ("heads", "sub")),
        P(("groups", "seq"), ("heads", "sub")),
        P(("groups", "seq"), ("heads", "sub"), None),
    )
    out_specs = P(("groups", "seq", "heads", "sub"), None)
    return jax.shard_map(body, mesh=mesh, in_specs=in_specs, out_specs=out_specs, check_vma=False)
```

```python
import functools
import math

import jax
import jax.numpy as jnp
from jax import lax
from jax.experimental import pallas as pl
from jax.experimental.pallas import tpu as pltpu
from jax.sharding import PartitionSpec as P

HD = 128
BLOCK = 512


def order_ranks(owners):
    length = owners.shape[-1]
    counter = jnp.arange(length)
    earlier = counter[None, :] < counter[:, None]
    same_owner = owners[..., :, None] == owners[..., None, :]
    return jnp.sum(jnp.logical_and(same_owner, earlier), axis=-1)


def one_hot(values, length):
    return (values[..., None] == jnp.arange(length)).astype(jnp.float32)


def own_partial(query_blocks, key_blocks, value_blocks, scaling):
    scores = (
        jnp.einsum("bqhd,bkhd->bhqk", query_blocks, key_blocks, preferred_element_type=jnp.float32)
        * scaling
    )
    length = query_blocks.shape[1]
    causal = jnp.arange(length)[:, None] >= jnp.arange(length)[None, :]
    scores = jnp.where(causal, scores, -jnp.inf)
    highest = jnp.max(scores, axis=-1)
    weights = jnp.exp(scores - highest[..., None])
    totals = jnp.sum(weights, axis=-1)
    mixed = jnp.einsum(
        "bhqk,bkhd->bhqd",
        weights.astype(jnp.bfloat16),
        value_blocks,
        preferred_element_type=jnp.float32,
    )
    return (mixed, highest, totals)


def tile_partial(query_blocks, tile_pair, scaling):
    head_size = query_blocks.shape[-1]
    scores = (
        jnp.einsum(
            "bqhd,bhkd->bhqk",
            query_blocks,
            tile_pair[..., :head_size],
            preferred_element_type=jnp.float32,
        )
        * scaling
    )
    highest = jnp.max(scores, axis=-1)
    weights = jnp.exp(scores - highest[..., None])
    totals = jnp.sum(weights, axis=-1)
    mixed = jnp.einsum(
        "bhqk,bhkd->bhqd",
        weights.astype(jnp.bfloat16),
        tile_pair[..., head_size:],
        preferred_element_type=jnp.float32,
    )
    return (mixed, highest, totals)


def merge_parts(parts):
    top = parts[0][1]
    for part in parts[1:]:
        top = jnp.maximum(top, part[1])
    numer = jnp.zeros(parts[0][0].shape, jnp.float32)
    denom = jnp.zeros(parts[0][2].shape, jnp.float32)
    for part in parts:
        factor = jnp.exp(part[1] - top)
        numer = numer + factor[..., None] * part[0]
        denom = denom + factor * part[2]
    return numer / denom[..., None]


def sparse_body(queries, new_keys, new_values, cache_keys, cache_values, selection):
    heads_q, heads_k, heads_v = (
        lax.all_to_all(queries, ("heads", "sub"), split_axis=1, concat_axis=0, tiled=True),
        lax.all_to_all(new_keys, ("heads", "sub"), split_axis=1, concat_axis=0, tiled=True),
        lax.all_to_all(new_values, ("heads", "sub"), split_axis=1, concat_axis=0, tiled=True),
    )
    qblocks, head_count, top_count = selection.shape
    head_size = HD
    scaling = head_size ** (-0.5)
    shaped = (qblocks, BLOCK, head_count, head_size)
    query_blocks = heads_q.reshape(shaped)
    own = own_partial(query_blocks, heads_k.reshape(shaped), heads_v.reshape(shaped), scaling)
    seq_count = lax.axis_size("seq")
    myself = lax.axis_index("seq")
    cache_blocks = cache_keys.shape[0] // BLOCK
    tile_count = cache_blocks * head_count
    request_count = qblocks * head_count * top_count
    capacity = -(-request_count // seq_count)
    requests_all = lax.all_gather(selection, "seq", axis=0, tiled=True).reshape(
        seq_count, request_count
    )
    head_of = jnp.arange(request_count) // top_count % head_count
    my_requests = selection.reshape(request_count)
    my_owner = my_requests // cache_blocks
    my_slot = my_owner * capacity + order_ranks(my_owner)
    key_tiles = cache_keys.reshape(cache_blocks, BLOCK, head_count, head_size).transpose(0, 2, 1, 3)
    value_tiles = cache_values.reshape(cache_blocks, BLOCK, head_count, head_size).transpose(
        0, 2, 1, 3
    )
    tile_set = jnp.concatenate([key_tiles, value_tiles], axis=-1).reshape(
        tile_count, BLOCK, 2 * head_size
    )
    their_owner = requests_all // cache_blocks
    local_tile = requests_all % cache_blocks * head_count + head_of[None, :]
    served = (their_owner == myself).astype(jnp.float32)
    slot_pick = one_hot(order_ranks(their_owner), capacity) * served[..., None]
    picking = jnp.einsum("erc,erl->ecl", slot_pick, one_hot(local_tile, tile_count)).astype(
        jnp.bfloat16
    )
    parts = [own]
    outgoing = jnp.einsum(
        "ecl,lkf->eckf", picking, tile_set, preferred_element_type=jnp.float32
    ).astype(jnp.bfloat16)
    incoming = lax.all_to_all(outgoing, "seq", split_axis=0, concat_axis=0, tiled=True)
    fetched = incoming.reshape(seq_count * capacity, BLOCK, 2 * head_size)[my_slot]
    fetched = fetched.reshape(qblocks, head_count, top_count, BLOCK, 2 * head_size)
    for turn in range(top_count):
        parts.append(tile_partial(query_blocks, fetched[:, :, turn], scaling))
    result = merge_parts(parts)
    result = (
        result.transpose(0, 2, 1, 3)
        .reshape(qblocks * BLOCK, head_count * head_size)
        .astype(jnp.bfloat16)
    )
    return lax.all_to_all(result, ("heads", "sub"), split_axis=0, concat_axis=1, tiled=True)


STAT = 16
UNIT = 32767.0
LEAST = 1.2e-34
C2 = math.log2(math.e) * HD**-0.5


def scores_of(q, k, mask=None):
    s = lax.dot_general(k, q, (((1,), (1,)), ((), ())), preferred_element_type=jnp.float32)
    return s if mask is None else jnp.where(mask, s, -jnp.inf)


def weights_of(s):
    m = jnp.max(s, axis=0, keepdims=True)
    p = jnp.exp2((s - m) * C2)
    return p.astype(jnp.bfloat16), m * C2, jnp.sum(p, axis=0, keepdims=True)


def values_of(v, w, v_dim):
    return lax.dot_general(v, w, (((v_dim,), (0,)), ((), ())), preferred_element_type=jnp.float32)


def attend(tiles):
    count = len(tiles)
    s, w, parts = {}, {}, []
    for t in range(count + 2):
        if t < count:
            s[t] = tiles[t][0]()
        if 1 <= t <= count:
            w[t - 1] = weights_of(s.pop(t - 1))
        if t >= 2:
            weights, m, total = w.pop(t - 2)
            parts.append((tiles[t - 2][1](weights), m, total))
    return parts


def join(parts):
    top = functools.reduce(jnp.maximum, [m for _, m, _ in parts])
    factors = [jnp.exp2(m - top) for _, m, _ in parts]
    numer = sum(f * o for f, (o, _, _) in zip(factors, parts))
    denom = sum(f * t for f, (_, _, t) in zip(factors, parts))
    return numer, top, denom


def put(out_ref, heads):
    width, rows = len(heads) * HD, heads[0][0].shape[1]
    at = lax.broadcasted_iota(jnp.int32, (STAT, rows), 0)
    stats = jnp.zeros((STAT, rows), jnp.float32)
    for h, (numer, top, denom) in enumerate(heads):
        most = jnp.maximum(jnp.max(jnp.abs(numer), axis=0, keepdims=True), LEAST)
        code = jnp.round(numer * (UNIT / most))
        out_ref[h * HD : (h + 1) * HD, :] = code.astype(jnp.int32).astype(jnp.int16)
        weight = jnp.log2(denom)
        for j, value in enumerate((top + weight, jnp.log2(most) - math.log2(UNIT) - weight)):
            whole = jnp.floor(value)
            stats = jnp.where(at == 4 * h + 2 * j, whole, stats)
            stats = jnp.where(at == 4 * h + 2 * j + 1, jnp.round((value - whole) * UNIT), stats)
    out_ref[width : width + STAT, :] = stats.astype(jnp.int32).astype(jnp.int16)


def take(ref):
    width = ref.shape[0] - STAT
    stats = ref[width : width + STAT, :].astype(jnp.int32).astype(jnp.float32)
    heads = []
    for h in range(width // HD):
        code = ref[h * HD : (h + 1) * HD, :].astype(jnp.int32).astype(jnp.float32)
        weight = stats[4 * h : 4 * h + 1] + stats[4 * h + 1 : 4 * h + 2] * (1.0 / UNIT)
        unit = stats[4 * h + 2 : 4 * h + 3] + stats[4 * h + 3 : 4 * h + 4] * (1.0 / UNIT)
        heads.append((code, weight, unit))
    return heads


def join_taken(taken):
    top = functools.reduce(jnp.maximum, [w for _, w, _ in taken])
    numer = sum(code * jnp.exp2(w - top + unit) for code, w, unit in taken)
    denom = sum(jnp.exp2(w - top) for _, w, _ in taken)
    return numer, top, denom


def cached_tiles(q_of, ck_ref, cvt_ref, h):
    cols = slice(h * HD, (h + 1) * HD)
    tiles = []
    for b in range(ck_ref.shape[0] // BLOCK):
        rows = slice(b * BLOCK, (b + 1) * BLOCK)
        tiles.append(
            (
                lambda rows=rows: scores_of(q_of(cols), ck_ref[rows, cols]),
                lambda w, rows=rows: values_of(cvt_ref[cols, rows], w, 1),
            )
        )
    return tiles


def attend_heads(tiles_of_heads):
    parts = attend([t for tiles in tiles_of_heads for t in tiles])
    heads = []
    for tiles in tiles_of_heads:
        heads.append(join(parts[: len(tiles)]))
        parts = parts[len(tiles) :]
    return heads


def cached_kernel(q_ref, ck_ref, cvt_ref, out_ref):
    heads = range(ck_ref.shape[1] // HD)
    q_of = lambda cols: q_ref[:, cols]
    put(out_ref, attend_heads([cached_tiles(q_of, ck_ref, cvt_ref, h) for h in heads]))


def own_kernel(mine, order_ref, *refs):
    q_ref, *kv_refs, ck_ref, cvt_ref, out_ref = refs
    width = ck_ref.shape[1]
    rows = q_ref.shape[0]
    step = kv_refs[0].shape[0]

    def positions(shape, axis, pieces):
        at = lax.broadcasted_iota(jnp.int32, shape, axis)
        place = jnp.zeros(shape, jnp.int32)
        for i, d in enumerate(pieces):
            place = jnp.where(at // step == i, order_ref[d] * step + at % step, place)
        return place

    shape = (step * len(kv_refs), rows)
    mask = positions(shape, 1, mine) >= positions(shape, 0, range(len(kv_refs)))
    q_of = lambda cols: q_ref[:, cols]
    heads = []
    for h in range(width // HD):
        cols = slice(h * HD, (h + 1) * HD)
        vcols = slice(width + h * HD, width + (h + 1) * HD)
        own = (
            lambda cols=cols: scores_of(
                q_ref[:, cols], jnp.concatenate([r[:, cols] for r in kv_refs], axis=0), mask
            ),
            lambda w, vcols=vcols: values_of(
                jnp.concatenate([r[:, vcols] for r in kv_refs], axis=0), w, 0
            ),
        )
        heads.append([own] + cached_tiles(q_of, ck_ref, cvt_ref, h))
    put(out_ref, attend_heads(heads))


def merge_kernel(*refs):
    *in_refs, out_ref = refs
    put(out_ref, [join_taken(taken) for taken in zip(*[take(r) for r in in_refs])])


def final_kernel(count, *refs):
    in_refs, out_refs = refs[:count], refs[count:]
    step = out_refs[0].shape[0]
    for h, taken in enumerate(zip(*[take(r) for r in in_refs])):
        numer, _, denom = join_taken(taken)
        value = jnp.transpose(numer * (1.0 / denom)).astype(jnp.bfloat16)
        for i, out_ref in enumerate(out_refs):
            out_ref[:, h * HD : (h + 1) * HD] = value[i * step : (i + 1) * step]


def pick_kernel(pieces, count, order_ref, *refs):
    in_refs, out_refs, done = refs[:count], refs[count:-1], refs[-1]
    width = out_refs[0].shape[1] // count
    copies = []
    for d, out_ref in zip(pieces, out_refs):
        start = pl.multiple_of(order_ref[d] * width, width)
        for i, ref in enumerate(in_refs):
            source, target = ref.at[:, pl.ds(start, width)], out_ref.at[:, i * width : (i + 1) * width]
            copies.append(pltpu.make_async_copy(source, target, done.at[len(copies)]))
            copies[-1].start()
    for copy in copies:
        copy.wait()


def slice_kernel(pieces, order_ref, ref, *out_refs):
    width = out_refs[0].shape[1]
    for d, out_ref in zip(pieces, out_refs):
        out_ref[...] = ref[:, pl.ds(pl.multiple_of(order_ref[d] * width, width), width)]


def stack_kernel(count, *refs):
    out_ref = refs[-1]
    step = refs[0].shape[0]
    for i in range(count):
        out_ref[i * step : (i + 1) * step, :] = refs[i][...]


def place_kernel(order_ref, *refs):
    *pieces, out_ref = refs
    width = pieces[0].shape[1]
    for d, piece in enumerate(pieces):
        start = pl.multiple_of(order_ref[d] * width, width)
        out_ref[:, pl.ds(start, width)] = piece[...]


def move(kernel, copies, scalars, arrays, outs, unread=()):
    read = 1 + len(arrays)

    def without_unread(*refs):
        kernel(*refs[:read], *refs[read + len(unread) :])

    return pl.pallas_call(
        without_unread,
        out_shape=outs,
        in_specs=[pl.BlockSpec(memory_space=pltpu.SMEM)]
        + [pl.BlockSpec(memory_space=pl.ANY)] * (len(arrays) + len(unread)),
        out_specs=[pl.BlockSpec(memory_space=pltpu.VMEM)] * len(outs),
        scratch_shapes=[pltpu.SemaphoreType.DMA((copies,))],
        cost_estimate=pl.CostEstimate(flops=0, bytes_accessed=2 * 4 * outs[0].size, transcendentals=0),
    )(scalars, *arrays, *unread)


def call(kernel, arrays, outs, flops=0, exps=0, scalars=None, unread=()):
    moved = sum(a.size * a.dtype.itemsize for a in arrays)
    moved += sum(math.prod(o.shape) * o.dtype.itemsize for o in outs)
    first = [] if scalars is None else [scalars]
    return pl.pallas_call(
        kernel,
        out_shape=outs,
        in_specs=[pl.BlockSpec(memory_space=pltpu.SMEM)] * len(first)
        + [pl.BlockSpec(memory_space=pltpu.VMEM)] * len(arrays)
        + [pl.BlockSpec(memory_space=pl.ANY)] * len(unread),
        out_specs=[pl.BlockSpec(memory_space=pltpu.VMEM)] * len(outs),
        compiler_params=pltpu.CompilerParams(vmem_limit_bytes=16 * 1024 * 1024),
        cost_estimate=pl.CostEstimate(flops=flops, bytes_accessed=moved, transcendentals=exps),
    )(*first, *arrays, *unread)


def dense_body(queries, new_keys, new_values, cache_keys, cache_values):
    seq_count = lax.axis_size("seq")
    shares = lax.axis_size("heads") * lax.axis_size("sub")
    me = lax.axis_index("heads") * lax.axis_size("sub") + lax.axis_index("sub")
    step, width = queries.shape[0], queries.shape[1] // shares
    cached = cache_keys.shape[0]
    each = shares // CHUNKS
    rows = each * step
    chunk = jax.ShapeDtypeStruct((rows, width), jnp.bfloat16)
    piece = jax.ShapeDtypeStruct((step, width), jnp.bfloat16)
    pair = jax.ShapeDtypeStruct((step, 2 * width), jnp.bfloat16)
    packed = jax.ShapeDtypeStruct((width + STAT, rows), jnp.int16)
    tile_flops = 4 * rows * cached * width
    tile_exps = rows * cached * (width // HD)

    def swap(x, d):
        return lax.ppermute(x, ("heads", "sub"), [(i, i ^ d) for i in range(shares)])

    def along(x, bit):
        return lax.ppermute(x, "seq", [(i, i ^ bit) for i in range(seq_count)])

    def after(x, unread):
        like = jax.ShapeDtypeStruct(x.shape, x.dtype)
        return call(functools.partial(stack_kernel, 1), [x], [like], unread=unread)[0] if unread else x

    order = jnp.stack([me ^ d for d in range(shares)]).astype(jnp.int32)
    cache_vt = cache_values.T
    context = [cache_keys, cache_vt]

    def attend(q):
        return call(cached_kernel, [q, *context], [packed], tile_flops, tile_exps)[0]

    def attend_own(q, pieces):
        return call(
            functools.partial(own_kernel, pieces),
            [q, *kv, *context],
            [packed],
            tile_flops * 3 // 2,
            tile_exps * 3 // 2,
            order,
        )[0]

    def merge(mine, got):
        return call(merge_kernel, [mine, got], [packed])[0]

    def end(parts, pieces):
        ended = call(functools.partial(final_kernel, len(parts)), parts, [piece] * each)
        return [swap(x, d) if d else x for x, d in zip(ended, pieces)]

    pieces_a, pieces_b = range(each), range(each, shares)

    def pick(arrays, pieces, out, unread=()):
        kernel = functools.partial(pick_kernel, pieces, len(arrays))
        count = len(pieces)
        return move(kernel, count * len(arrays), order, arrays, [out] * count, unread)

    def slices(pieces):
        kernel = functools.partial(slice_kernel, pieces)
        return call(kernel, [queries], [piece] * each, scalars=order)

    q = [swap(x, d) if d else x for x, d in zip(slices(pieces_a), pieces_a)]
    a = call(functools.partial(stack_kernel, each), q, [chunk])[0]
    q = slices(pieces_b)
    a2, a1 = along(a, 2), along(a, 1)
    q = [swap(x, d) for x, d in zip(q, pieces_b)]
    b = call(functools.partial(stack_kernel, each), q, [chunk])[0]
    b2, b1 = along(b, 2), along(b, 1)
    kv = pick([new_keys, new_values], range(shares), pair, [b, cache_vt])
    kv = [swap(x, d) if d else x for d, x in enumerate(kv)]
    part_a2, part_a1 = attend(a2), attend(a1)
    b3 = along(after(b2, [part_a2, part_a1]), 1)
    part_b2 = attend(b2)
    a3 = along(after(a2, [part_b2, b1, *kv[1:]]), 1)
    got_b2 = along(attend(b3), 1)
    got_a2 = along(attend(a3), 1)
    part_b2 = merge(part_b2, got_b2)
    from_b2 = along(part_b2, 2)
    from_b1 = along(after(attend(b1), [part_b2]), 1)
    part_a2 = merge(part_a2, got_a2)
    from_a2 = along(part_a2, 2)
    from_a1 = along(after(part_a1, [part_a2]), 1)
    out_b = end([attend_own(b, pieces_b), from_b2, from_b1], pieces_b)
    out_a = end([attend_own(a, pieces_a), from_a2, from_a1], pieces_a)
    results = [*out_a, *out_b]
    out = jax.ShapeDtypeStruct((step, shares * width), jnp.bfloat16)
    return call(place_kernel, results, [out], scalars=order)[0]


CHUNKS = 2


def power_of_two(n):
    return n & (n - 1) == 0


def body(queries, new_keys, new_values, cache_keys, cache_values, selection):
    qblocks, head_count, top_count = selection.shape
    seq_count = lax.axis_size("seq")
    shares = lax.axis_size("heads") * lax.axis_size("sub")
    every = top_count == cache_keys.shape[0] // BLOCK * seq_count and qblocks == 1
    fits = seq_count == 4 and power_of_two(shares) and shares % CHUNKS == 0
    if every and fits and 4 * head_count <= STAT:
        return dense_body(queries, new_keys, new_values, cache_keys, cache_values)
    return sparse_body(queries, new_keys, new_values, cache_keys, cache_values, selection)


def solution(mesh):
    in_specs = (
        P(("groups", "seq", "heads", "sub"), None),
        P(("groups", "seq", "heads", "sub"), None),
        P(("groups", "seq", "heads", "sub"), None),
        P(("groups", "seq"), ("heads", "sub")),
        P(("groups", "seq"), ("heads", "sub")),
        P(("groups", "seq"), ("heads", "sub"), None),
    )
    out_specs = P(("groups", "seq", "heads", "sub"), None)
    return jax.shard_map(body, mesh=mesh, in_specs=in_specs, out_specs=out_specs, check_vma=False)
```

```python
import functools
import math

import jax
import jax.numpy as jnp
from jax import lax
from jax.experimental import pallas as pl
from jax.experimental.pallas import tpu as pltpu
from jax.sharding import PartitionSpec as P

HD = 128
BLOCK = 512


def order_ranks(owners):
    length = owners.shape[-1]
    counter = jnp.arange(length)
    earlier = counter[None, :] < counter[:, None]
    same_owner = owners[..., :, None] == owners[..., None, :]
    return jnp.sum(jnp.logical_and(same_owner, earlier), axis=-1)


def one_hot(values, length):
    return (values[..., None] == jnp.arange(length)).astype(jnp.float32)


def own_partial(query_blocks, key_blocks, value_blocks, scaling):
    scores = (
        jnp.einsum("bqhd,bkhd->bhqk", query_blocks, key_blocks, preferred_element_type=jnp.float32)
        * scaling
    )
    length = query_blocks.shape[1]
    causal = jnp.arange(length)[:, None] >= jnp.arange(length)[None, :]
    scores = jnp.where(causal, scores, -jnp.inf)
    highest = jnp.max(scores, axis=-1)
    weights = jnp.exp(scores - highest[..., None])
    totals = jnp.sum(weights, axis=-1)
    mixed = jnp.einsum(
        "bhqk,bkhd->bhqd",
        weights.astype(jnp.bfloat16),
        value_blocks,
        preferred_element_type=jnp.float32,
    )
    return (mixed, highest, totals)


def tile_partial(query_blocks, tile_pair, scaling):
    head_size = query_blocks.shape[-1]
    scores = (
        jnp.einsum(
            "bqhd,bhkd->bhqk",
            query_blocks,
            tile_pair[..., :head_size],
            preferred_element_type=jnp.float32,
        )
        * scaling
    )
    highest = jnp.max(scores, axis=-1)
    weights = jnp.exp(scores - highest[..., None])
    totals = jnp.sum(weights, axis=-1)
    mixed = jnp.einsum(
        "bhqk,bhkd->bhqd",
        weights.astype(jnp.bfloat16),
        tile_pair[..., head_size:],
        preferred_element_type=jnp.float32,
    )
    return (mixed, highest, totals)


def merge_parts(parts):
    top = parts[0][1]
    for part in parts[1:]:
        top = jnp.maximum(top, part[1])
    numer = jnp.zeros(parts[0][0].shape, jnp.float32)
    denom = jnp.zeros(parts[0][2].shape, jnp.float32)
    for part in parts:
        factor = jnp.exp(part[1] - top)
        numer = numer + factor[..., None] * part[0]
        denom = denom + factor * part[2]
    return numer / denom[..., None]


def sparse_body(queries, new_keys, new_values, cache_keys, cache_values, selection):
    heads_q, heads_k, heads_v = (
        lax.all_to_all(queries, ("heads", "sub"), split_axis=1, concat_axis=0, tiled=True),
        lax.all_to_all(new_keys, ("heads", "sub"), split_axis=1, concat_axis=0, tiled=True),
        lax.all_to_all(new_values, ("heads", "sub"), split_axis=1, concat_axis=0, tiled=True),
    )
    qblocks, head_count, top_count = selection.shape
    head_size = HD
    scaling = head_size ** (-0.5)
    shaped = (qblocks, BLOCK, head_count, head_size)
    query_blocks = heads_q.reshape(shaped)
    own = own_partial(query_blocks, heads_k.reshape(shaped), heads_v.reshape(shaped), scaling)
    seq_count = lax.axis_size("seq")
    myself = lax.axis_index("seq")
    cache_blocks = cache_keys.shape[0] // BLOCK
    tile_count = cache_blocks * head_count
    request_count = qblocks * head_count * top_count
    capacity = -(-request_count // seq_count)
    requests_all = lax.all_gather(selection, "seq", axis=0, tiled=True).reshape(
        seq_count, request_count
    )
    head_of = jnp.arange(request_count) // top_count % head_count
    my_requests = selection.reshape(request_count)
    my_owner = my_requests // cache_blocks
    my_slot = my_owner * capacity + order_ranks(my_owner)
    key_tiles = cache_keys.reshape(cache_blocks, BLOCK, head_count, head_size).transpose(0, 2, 1, 3)
    value_tiles = cache_values.reshape(cache_blocks, BLOCK, head_count, head_size).transpose(
        0, 2, 1, 3
    )
    tile_set = jnp.concatenate([key_tiles, value_tiles], axis=-1).reshape(
        tile_count, BLOCK, 2 * head_size
    )
    their_owner = requests_all // cache_blocks
    local_tile = requests_all % cache_blocks * head_count + head_of[None, :]
    served = (their_owner == myself).astype(jnp.float32)
    slot_pick = one_hot(order_ranks(their_owner), capacity) * served[..., None]
    picking = jnp.einsum("erc,erl->ecl", slot_pick, one_hot(local_tile, tile_count)).astype(
        jnp.bfloat16
    )
    parts = [own]
    outgoing = jnp.einsum(
        "ecl,lkf->eckf", picking, tile_set, preferred_element_type=jnp.float32
    ).astype(jnp.bfloat16)
    incoming = lax.all_to_all(outgoing, "seq", split_axis=0, concat_axis=0, tiled=True)
    fetched = incoming.reshape(seq_count * capacity, BLOCK, 2 * head_size)[my_slot]
    fetched = fetched.reshape(qblocks, head_count, top_count, BLOCK, 2 * head_size)
    for turn in range(top_count):
        parts.append(tile_partial(query_blocks, fetched[:, :, turn], scaling))
    result = merge_parts(parts)
    result = (
        result.transpose(0, 2, 1, 3)
        .reshape(qblocks * BLOCK, head_count * head_size)
        .astype(jnp.bfloat16)
    )
    return lax.all_to_all(result, ("heads", "sub"), split_axis=0, concat_axis=1, tiled=True)


STAT = 16
UNIT = 32767.0
LEAST = 1.2e-34
C2 = math.log2(math.e) * HD**-0.5


def scores_of(q, k, mask=None):
    s = lax.dot_general(k, q, (((1,), (1,)), ((), ())), preferred_element_type=jnp.float32)
    return s if mask is None else jnp.where(mask, s, -jnp.inf)


def weights_of(s):
    m = jnp.max(s, axis=0, keepdims=True)
    p = jnp.exp2((s - m) * C2)
    return p.astype(jnp.bfloat16), m * C2, jnp.sum(p, axis=0, keepdims=True)


def values_of(v, w, v_dim):
    return lax.dot_general(v, w, (((v_dim,), (0,)), ((), ())), preferred_element_type=jnp.float32)


def attend(tiles):
    count = len(tiles)
    s, w, parts = {}, {}, []
    for t in range(count + 2):
        if t < count:
            s[t] = tiles[t][0]()
        if 1 <= t <= count:
            w[t - 1] = weights_of(s.pop(t - 1))
        if t >= 2:
            weights, m, total = w.pop(t - 2)
            parts.append((tiles[t - 2][1](weights), m, total))
    return parts


def join(parts):
    top = functools.reduce(jnp.maximum, [m for _, m, _ in parts])
    factors = [jnp.exp2(m - top) for _, m, _ in parts]
    numer = sum(f * o for f, (o, _, _) in zip(factors, parts))
    denom = sum(f * t for f, (_, _, t) in zip(factors, parts))
    return numer, top, denom


def put(out_ref, heads):
    width, rows = len(heads) * HD, heads[0][0].shape[1]
    at = lax.broadcasted_iota(jnp.int32, (STAT, rows), 0)
    stats = jnp.zeros((STAT, rows), jnp.float32)
    for h, (numer, top, denom) in enumerate(heads):
        most = jnp.maximum(jnp.max(jnp.abs(numer), axis=0, keepdims=True), LEAST)
        code = jnp.round(numer * (UNIT / most))
        out_ref[h * HD : (h + 1) * HD, :] = code.astype(jnp.int32).astype(jnp.int16)
        weight = jnp.log2(denom)
        for j, value in enumerate((top + weight, jnp.log2(most) - math.log2(UNIT) - weight)):
            whole = jnp.floor(value)
            stats = jnp.where(at == 4 * h + 2 * j, whole, stats)
            stats = jnp.where(at == 4 * h + 2 * j + 1, jnp.round((value - whole) * UNIT), stats)
    out_ref[width : width + STAT, :] = stats.astype(jnp.int32).astype(jnp.int16)


def take(ref):
    width = ref.shape[0] - STAT
    stats = ref[width : width + STAT, :].astype(jnp.int32).astype(jnp.float32)
    heads = []
    for h in range(width // HD):
        code = ref[h * HD : (h + 1) * HD, :].astype(jnp.int32).astype(jnp.float32)
        weight = stats[4 * h : 4 * h + 1] + stats[4 * h + 1 : 4 * h + 2] * (1.0 / UNIT)
        unit = stats[4 * h + 2 : 4 * h + 3] + stats[4 * h + 3 : 4 * h + 4] * (1.0 / UNIT)
        heads.append((code, weight, unit))
    return heads


def join_taken(taken):
    top = functools.reduce(jnp.maximum, [w for _, w, _ in taken])
    numer = sum(code * jnp.exp2(w - top + unit) for code, w, unit in taken)
    denom = sum(jnp.exp2(w - top) for _, w, _ in taken)
    return numer, top, denom


def cached_tiles(q_of, ck_ref, cvt_ref, h):
    cols = slice(h * HD, (h + 1) * HD)
    tiles = []
    for b in range(ck_ref.shape[0] // BLOCK):
        rows = slice(b * BLOCK, (b + 1) * BLOCK)
        tiles.append(
            (
                lambda rows=rows: scores_of(q_of(cols), ck_ref[rows, cols]),
                lambda w, rows=rows: values_of(cvt_ref[cols, rows], w, 1),
            )
        )
    return tiles


def attend_heads(tiles_of_heads):
    parts = attend([t for tiles in tiles_of_heads for t in tiles])
    heads = []
    for tiles in tiles_of_heads:
        heads.append(join(parts[: len(tiles)]))
        parts = parts[len(tiles) :]
    return heads


def cached_kernel(q_ref, ck_ref, cvt_ref, out_ref):
    heads = range(ck_ref.shape[1] // HD)
    q_of = lambda cols: q_ref[:, cols]
    put(out_ref, attend_heads([cached_tiles(q_of, ck_ref, cvt_ref, h) for h in heads]))


def own_kernel(mine, order_ref, *refs):
    q_ref, *kv_refs, ck_ref, cvt_ref, out_ref = refs
    width = ck_ref.shape[1]
    rows = q_ref.shape[0]
    step = kv_refs[0].shape[0]

    def positions(shape, axis, pieces):
        at = lax.broadcasted_iota(jnp.int32, shape, axis)
        place = jnp.zeros(shape, jnp.int32)
        for i, d in enumerate(pieces):
            place = jnp.where(at // step == i, order_ref[d] * step + at % step, place)
        return place

    shape = (step * len(kv_refs), rows)
    mask = positions(shape, 1, mine) >= positions(shape, 0, range(len(kv_refs)))
    q_of = lambda cols: q_ref[:, cols]
    heads = []
    for h in range(width // HD):
        cols = slice(h * HD, (h + 1) * HD)
        vcols = slice(width + h * HD, width + (h + 1) * HD)
        own = (
            lambda cols=cols: scores_of(
                q_ref[:, cols], jnp.concatenate([r[:, cols] for r in kv_refs], axis=0), mask
            ),
            lambda w, vcols=vcols: values_of(
                jnp.concatenate([r[:, vcols] for r in kv_refs], axis=0), w, 0
            ),
        )
        heads.append([own] + cached_tiles(q_of, ck_ref, cvt_ref, h))
    put(out_ref, attend_heads(heads))


def merge_kernel(*refs):
    *in_refs, out_ref = refs
    put(out_ref, [join_taken(taken) for taken in zip(*[take(r) for r in in_refs])])


def final_kernel(count, *refs):
    in_refs, out_refs = refs[:count], refs[count:]
    step = out_refs[0].shape[0]
    for h, taken in enumerate(zip(*[take(r) for r in in_refs])):
        numer, _, denom = join_taken(taken)
        value = jnp.transpose(numer * (1.0 / denom)).astype(jnp.bfloat16)
        for i, out_ref in enumerate(out_refs):
            out_ref[:, h * HD : (h + 1) * HD] = value[i * step : (i + 1) * step]


def pick_kernel(pieces, count, order_ref, *refs):
    in_refs, out_refs, done = refs[:count], refs[count:-1], refs[-1]
    width = out_refs[0].shape[1] // count
    copies = []
    for d, out_ref in zip(pieces, out_refs):
        start = pl.multiple_of(order_ref[d] * width, width)
        for i, ref in enumerate(in_refs):
            source, target = ref.at[:, pl.ds(start, width)], out_ref.at[:, i * width : (i + 1) * width]
            copies.append(pltpu.make_async_copy(source, target, done.at[len(copies)]))
            copies[-1].start()
    for copy in copies:
        copy.wait()


def slice_kernel(pieces, order_ref, ref, *out_refs):
    width = out_refs[0].shape[1]
    for d, out_ref in zip(pieces, out_refs):
        out_ref[...] = ref[:, pl.ds(pl.multiple_of(order_ref[d] * width, width), width)]


def stack_kernel(count, *refs):
    out_ref = refs[-1]
    step = refs[0].shape[0]
    for i in range(count):
        out_ref[i * step : (i + 1) * step, :] = refs[i][...]


def place_kernel(order_ref, *refs):
    *pieces, out_ref = refs
    width = pieces[0].shape[1]
    for d, piece in enumerate(pieces):
        start = pl.multiple_of(order_ref[d] * width, width)
        out_ref[:, pl.ds(start, width)] = piece[...]


def move(kernel, copies, scalars, arrays, outs, unread=()):
    read = 1 + len(arrays)

    def without_unread(*refs):
        kernel(*refs[:read], *refs[read + len(unread) :])

    return pl.pallas_call(
        without_unread,
        out_shape=outs,
        in_specs=[pl.BlockSpec(memory_space=pltpu.SMEM)]
        + [pl.BlockSpec(memory_space=pl.ANY)] * (len(arrays) + len(unread)),
        out_specs=[pl.BlockSpec(memory_space=pltpu.VMEM)] * len(outs),
        scratch_shapes=[pltpu.SemaphoreType.DMA((copies,))],
        cost_estimate=pl.CostEstimate(flops=0, bytes_accessed=2 * 4 * outs[0].size, transcendentals=0),
    )(scalars, *arrays, *unread)


def call(kernel, arrays, outs, flops=0, exps=0, scalars=None, unread=()):
    moved = sum(a.size * a.dtype.itemsize for a in arrays)
    moved += sum(math.prod(o.shape) * o.dtype.itemsize for o in outs)
    first = [] if scalars is None else [scalars]
    read = len(first) + len(arrays)

    def without_unread(*refs):
        kernel(*refs[:read], *refs[read + len(unread) :])

    return pl.pallas_call(
        without_unread,
        out_shape=outs,
        in_specs=[pl.BlockSpec(memory_space=pltpu.SMEM)] * len(first)
        + [pl.BlockSpec(memory_space=pltpu.VMEM)] * len(arrays)
        + [pl.BlockSpec(memory_space=pl.ANY)] * len(unread),
        out_specs=[pl.BlockSpec(memory_space=pltpu.VMEM)] * len(outs),
        compiler_params=pltpu.CompilerParams(vmem_limit_bytes=16 * 1024 * 1024),
        cost_estimate=pl.CostEstimate(flops=flops, bytes_accessed=moved, transcendentals=exps),
    )(*first, *arrays, *unread)


def dense_body(queries, new_keys, new_values, cache_keys, cache_values):
    seq_count = lax.axis_size("seq")
    shares = lax.axis_size("heads") * lax.axis_size("sub")
    me = lax.axis_index("heads") * lax.axis_size("sub") + lax.axis_index("sub")
    step, width = queries.shape[0], queries.shape[1] // shares
    cached = cache_keys.shape[0]
    each = shares // CHUNKS
    rows = each * step
    chunk = jax.ShapeDtypeStruct((rows, width), jnp.bfloat16)
    piece = jax.ShapeDtypeStruct((step, width), jnp.bfloat16)
    pair = jax.ShapeDtypeStruct((step, 2 * width), jnp.bfloat16)
    packed = jax.ShapeDtypeStruct((width + STAT, rows), jnp.int16)
    tile_flops = 4 * rows * cached * width
    tile_exps = rows * cached * (width // HD)

    def swap(x, d):
        return lax.ppermute(x, ("heads", "sub"), [(i, i ^ d) for i in range(shares)])

    def along(x, bit):
        return lax.ppermute(x, "seq", [(i, i ^ bit) for i in range(seq_count)])

    def after(x, unread):
        like = jax.ShapeDtypeStruct(x.shape, x.dtype)
        return call(functools.partial(stack_kernel, 1), [x], [like], unread=unread)[0] if unread else x

    order = jnp.stack([me ^ d for d in range(shares)]).astype(jnp.int32)
    cache_vt = cache_values.T
    context = [cache_keys, cache_vt]

    def attend(q):
        return call(cached_kernel, [q, *context], [packed], tile_flops, tile_exps)[0]

    def attend_own(q, pieces, unread):
        return call(
            functools.partial(own_kernel, pieces),
            [q, *kv, *context],
            [packed],
            tile_flops * 3 // 2,
            tile_exps * 3 // 2,
            order,
            unread,
        )[0]

    def merge(mine, got):
        return call(merge_kernel, [mine, got], [packed])[0]

    def end(parts, pieces):
        ended = call(functools.partial(final_kernel, len(parts)), parts, [piece] * each)
        return [swap(x, d) if d else x for x, d in zip(ended, pieces)]

    pieces_a, pieces_b = range(each), range(each, shares)

    def pick(arrays, pieces, out, unread=()):
        kernel = functools.partial(pick_kernel, pieces, len(arrays))
        count = len(pieces)
        return move(kernel, count * len(arrays), order, arrays, [out] * count, unread)

    def slices(pieces):
        kernel = functools.partial(slice_kernel, pieces)
        return call(kernel, [queries], [piece] * each, scalars=order)

    q = [swap(x, d) if d else x for x, d in zip(slices(pieces_a), pieces_a)]
    a = call(functools.partial(stack_kernel, each), q, [chunk])[0]
    q = slices(pieces_b)
    a2, a1 = along(a, 2), along(a, 1)
    q = [swap(x, d) for x, d in zip(q, pieces_b)]
    b = call(functools.partial(stack_kernel, each), q, [chunk])[0]
    b2, b1 = along(b, 2), along(b, 1)
    kv = pick([new_keys, new_values], range(shares), pair, [b, cache_vt])
    kv = [swap(x, d) if d else x for d, x in enumerate(kv)]
    part_a2, part_a1 = attend(a2), attend(a1)
    b3 = along(after(b2, [part_a2, part_a1]), 1)
    part_b2 = attend(b2)
    a3 = along(after(a2, [part_b2, b1, *kv[1:]]), 1)
    got_b2 = along(attend(b3), 1)
    got_a2 = along(attend(a3), 1)
    part_b2 = merge(part_b2, got_b2)
    from_b2 = along(part_b2, 2)
    from_b1 = along(after(attend(b1), [part_b2]), 1)
    own_b, own_a = attend_own(b, pieces_b, [part_b2]), attend_own(a, pieces_a, [part_b2])
    part_a2 = after(merge(part_a2, got_a2), [from_b2, own_a, own_b])
    from_a2 = along(part_a2, 2)
    from_a1 = along(after(part_a1, [part_a2]), 1)
    out_b = end([own_b, from_b2, from_b1], pieces_b)
    out_a = end([own_a, from_a2, from_a1], pieces_a)
    results = [*out_a, *out_b]
    out = jax.ShapeDtypeStruct((step, shares * width), jnp.bfloat16)
    return call(place_kernel, results, [out], scalars=order)[0]


CHUNKS = 2


def power_of_two(n):
    return n & (n - 1) == 0


def body(queries, new_keys, new_values, cache_keys, cache_values, selection):
    qblocks, head_count, top_count = selection.shape
    seq_count = lax.axis_size("seq")
    shares = lax.axis_size("heads") * lax.axis_size("sub")
    every = top_count == cache_keys.shape[0] // BLOCK * seq_count and qblocks == 1
    fits = seq_count == 4 and power_of_two(shares) and shares % CHUNKS == 0
    if every and fits and 4 * head_count <= STAT:
        return dense_body(queries, new_keys, new_values, cache_keys, cache_values)
    return sparse_body(queries, new_keys, new_values, cache_keys, cache_values, selection)


def solution(mesh):
    in_specs = (
        P(("groups", "seq", "heads", "sub"), None),
        P(("groups", "seq", "heads", "sub"), None),
        P(("groups", "seq", "heads", "sub"), None),
        P(("groups", "seq"), ("heads", "sub")),
        P(("groups", "seq"), ("heads", "sub")),
        P(("groups", "seq"), ("heads", "sub"), None),
    )
    out_specs = P(("groups", "seq", "heads", "sub"), None)
    return jax.shard_map(body, mesh=mesh, in_specs=in_specs, out_specs=out_specs, check_vma=False)
```

```python
import functools
import math

import jax
import jax.numpy as jnp
from jax import lax
from jax.experimental import pallas as pl
from jax.experimental.pallas import tpu as pltpu
from jax.sharding import PartitionSpec as P

HD = 128
BLOCK = 512


def order_ranks(owners):
    length = owners.shape[-1]
    counter = jnp.arange(length)
    earlier = counter[None, :] < counter[:, None]
    same_owner = owners[..., :, None] == owners[..., None, :]
    return jnp.sum(jnp.logical_and(same_owner, earlier), axis=-1)


def one_hot(values, length):
    return (values[..., None] == jnp.arange(length)).astype(jnp.float32)


def own_partial(query_blocks, key_blocks, value_blocks, scaling):
    scores = (
        jnp.einsum("bqhd,bkhd->bhqk", query_blocks, key_blocks, preferred_element_type=jnp.float32)
        * scaling
    )
    length = query_blocks.shape[1]
    causal = jnp.arange(length)[:, None] >= jnp.arange(length)[None, :]
    scores = jnp.where(causal, scores, -jnp.inf)
    highest = jnp.max(scores, axis=-1)
    weights = jnp.exp(scores - highest[..., None])
    totals = jnp.sum(weights, axis=-1)
    mixed = jnp.einsum(
        "bhqk,bkhd->bhqd",
        weights.astype(jnp.bfloat16),
        value_blocks,
        preferred_element_type=jnp.float32,
    )
    return (mixed, highest, totals)


def tile_partial(query_blocks, tile_pair, scaling):
    head_size = query_blocks.shape[-1]
    scores = (
        jnp.einsum(
            "bqhd,bhkd->bhqk",
            query_blocks,
            tile_pair[..., :head_size],
            preferred_element_type=jnp.float32,
        )
        * scaling
    )
    highest = jnp.max(scores, axis=-1)
    weights = jnp.exp(scores - highest[..., None])
    totals = jnp.sum(weights, axis=-1)
    mixed = jnp.einsum(
        "bhqk,bhkd->bhqd",
        weights.astype(jnp.bfloat16),
        tile_pair[..., head_size:],
        preferred_element_type=jnp.float32,
    )
    return (mixed, highest, totals)


def merge_parts(parts):
    top = parts[0][1]
    for part in parts[1:]:
        top = jnp.maximum(top, part[1])
    numer = jnp.zeros(parts[0][0].shape, jnp.float32)
    denom = jnp.zeros(parts[0][2].shape, jnp.float32)
    for part in parts:
        factor = jnp.exp(part[1] - top)
        numer = numer + factor[..., None] * part[0]
        denom = denom + factor * part[2]
    return numer / denom[..., None]


def sparse_body(queries, new_keys, new_values, cache_keys, cache_values, selection):
    heads_q, heads_k, heads_v = (
        lax.all_to_all(queries, ("heads", "sub"), split_axis=1, concat_axis=0, tiled=True),
        lax.all_to_all(new_keys, ("heads", "sub"), split_axis=1, concat_axis=0, tiled=True),
        lax.all_to_all(new_values, ("heads", "sub"), split_axis=1, concat_axis=0, tiled=True),
    )
    qblocks, head_count, top_count = selection.shape
    head_size = HD
    scaling = head_size ** (-0.5)
    shaped = (qblocks, BLOCK, head_count, head_size)
    query_blocks = heads_q.reshape(shaped)
    own = own_partial(query_blocks, heads_k.reshape(shaped), heads_v.reshape(shaped), scaling)
    seq_count = lax.axis_size("seq")
    myself = lax.axis_index("seq")
    cache_blocks = cache_keys.shape[0] // BLOCK
    tile_count = cache_blocks * head_count
    request_count = qblocks * head_count * top_count
    capacity = -(-request_count // seq_count)
    requests_all = lax.all_gather(selection, "seq", axis=0, tiled=True).reshape(
        seq_count, request_count
    )
    head_of = jnp.arange(request_count) // top_count % head_count
    my_requests = selection.reshape(request_count)
    my_owner = my_requests // cache_blocks
    my_slot = my_owner * capacity + order_ranks(my_owner)
    key_tiles = cache_keys.reshape(cache_blocks, BLOCK, head_count, head_size).transpose(0, 2, 1, 3)
    value_tiles = cache_values.reshape(cache_blocks, BLOCK, head_count, head_size).transpose(
        0, 2, 1, 3
    )
    tile_set = jnp.concatenate([key_tiles, value_tiles], axis=-1).reshape(
        tile_count, BLOCK, 2 * head_size
    )
    their_owner = requests_all // cache_blocks
    local_tile = requests_all % cache_blocks * head_count + head_of[None, :]
    served = (their_owner == myself).astype(jnp.float32)
    slot_pick = one_hot(order_ranks(their_owner), capacity) * served[..., None]
    picking = jnp.einsum("erc,erl->ecl", slot_pick, one_hot(local_tile, tile_count)).astype(
        jnp.bfloat16
    )
    parts = [own]
    outgoing = jnp.einsum(
        "ecl,lkf->eckf", picking, tile_set, preferred_element_type=jnp.float32
    ).astype(jnp.bfloat16)
    incoming = lax.all_to_all(outgoing, "seq", split_axis=0, concat_axis=0, tiled=True)
    fetched = incoming.reshape(seq_count * capacity, BLOCK, 2 * head_size)[my_slot]
    fetched = fetched.reshape(qblocks, head_count, top_count, BLOCK, 2 * head_size)
    for turn in range(top_count):
        parts.append(tile_partial(query_blocks, fetched[:, :, turn], scaling))
    result = merge_parts(parts)
    result = (
        result.transpose(0, 2, 1, 3)
        .reshape(qblocks * BLOCK, head_count * head_size)
        .astype(jnp.bfloat16)
    )
    return lax.all_to_all(result, ("heads", "sub"), split_axis=0, concat_axis=1, tiled=True)


STAT = 16
UNIT = 32767.0
LEAST = 1.2e-34
C2 = math.log2(math.e) * HD**-0.5


def scores_of(q, k, mask=None):
    s = lax.dot_general(k, q, (((1,), (1,)), ((), ())), preferred_element_type=jnp.float32)
    return s if mask is None else jnp.where(mask, s, -jnp.inf)


def weights_of(s):
    m = jnp.max(s, axis=0, keepdims=True)
    p = jnp.exp2((s - m) * C2)
    return p.astype(jnp.bfloat16), m * C2, jnp.sum(p, axis=0, keepdims=True)


def values_of(v, w, v_dim):
    return lax.dot_general(v, w, (((v_dim,), (0,)), ((), ())), preferred_element_type=jnp.float32)


def attend(tiles):
    count = len(tiles)
    s, w, parts = {}, {}, []
    for t in range(count + 2):
        if t < count:
            s[t] = tiles[t][0]()
        if 1 <= t <= count:
            w[t - 1] = weights_of(s.pop(t - 1))
        if t >= 2:
            weights, m, total = w.pop(t - 2)
            parts.append((tiles[t - 2][1](weights), m, total))
    return parts


def join(parts):
    top = functools.reduce(jnp.maximum, [m for _, m, _ in parts])
    factors = [jnp.exp2(m - top) for _, m, _ in parts]
    numer = sum(f * o for f, (o, _, _) in zip(factors, parts))
    denom = sum(f * t for f, (_, _, t) in zip(factors, parts))
    return numer, top, denom


def put(out_ref, heads):
    width, rows = len(heads) * HD, heads[0][0].shape[1]
    at = lax.broadcasted_iota(jnp.int32, (STAT, rows), 0)
    stats = jnp.zeros((STAT, rows), jnp.float32)
    for h, (numer, top, denom) in enumerate(heads):
        most = jnp.maximum(jnp.max(jnp.abs(numer), axis=0, keepdims=True), LEAST)
        code = jnp.round(numer * (UNIT / most))
        out_ref[h * HD : (h + 1) * HD, :] = code.astype(jnp.int32).astype(jnp.int16)
        weight = jnp.log2(denom)
        for j, value in enumerate((top + weight, jnp.log2(most) - math.log2(UNIT) - weight)):
            whole = jnp.floor(value)
            stats = jnp.where(at == 4 * h + 2 * j, whole, stats)
            stats = jnp.where(at == 4 * h + 2 * j + 1, jnp.round((value - whole) * UNIT), stats)
    out_ref[width : width + STAT, :] = stats.astype(jnp.int32).astype(jnp.int16)


def take(ref):
    width = ref.shape[0] - STAT
    stats = ref[width : width + STAT, :].astype(jnp.int32).astype(jnp.float32)
    heads = []
    for h in range(width // HD):
        code = ref[h * HD : (h + 1) * HD, :].astype(jnp.int32).astype(jnp.float32)
        weight = stats[4 * h : 4 * h + 1] + stats[4 * h + 1 : 4 * h + 2] * (1.0 / UNIT)
        unit = stats[4 * h + 2 : 4 * h + 3] + stats[4 * h + 3 : 4 * h + 4] * (1.0 / UNIT)
        heads.append((code, weight, unit))
    return heads


def join_taken(taken):
    top = functools.reduce(jnp.maximum, [w for _, w, _ in taken])
    numer = sum(code * jnp.exp2(w - top + unit) for code, w, unit in taken)
    denom = sum(jnp.exp2(w - top) for _, w, _ in taken)
    return numer, top, denom


def cached_tiles(q_of, ck_ref, cvt_ref, h):
    cols = slice(h * HD, (h + 1) * HD)
    tiles = []
    for b in range(ck_ref.shape[0] // BLOCK):
        rows = slice(b * BLOCK, (b + 1) * BLOCK)
        tiles.append(
            (
                lambda rows=rows: scores_of(q_of(cols), ck_ref[rows, cols]),
                lambda w, rows=rows: values_of(cvt_ref[cols, rows], w, 1),
            )
        )
    return tiles


def attend_heads(tiles_of_heads):
    parts = attend([t for tiles in tiles_of_heads for t in tiles])
    heads = []
    for tiles in tiles_of_heads:
        heads.append(join(parts[: len(tiles)]))
        parts = parts[len(tiles) :]
    return heads


def cached_kernel(q_ref, ck_ref, cvt_ref, out_ref):
    heads = range(ck_ref.shape[1] // HD)
    q_of = lambda cols: q_ref[:, cols]
    put(out_ref, attend_heads([cached_tiles(q_of, ck_ref, cvt_ref, h) for h in heads]))


def own_kernel(mine, order_ref, *refs):
    q_ref, *kv_refs, ck_ref, cvt_ref, out_ref = refs
    width = ck_ref.shape[1]
    rows = q_ref.shape[0]
    step = kv_refs[0].shape[0]

    def positions(shape, axis, pieces):
        at = lax.broadcasted_iota(jnp.int32, shape, axis)
        place = jnp.zeros(shape, jnp.int32)
        for i, d in enumerate(pieces):
            place = jnp.where(at // step == i, order_ref[d] * step + at % step, place)
        return place

    shape = (step * len(kv_refs), rows)
    mask = positions(shape, 1, mine) >= positions(shape, 0, range(len(kv_refs)))
    q_of = lambda cols: q_ref[:, cols]
    heads = []
    for h in range(width // HD):
        cols = slice(h * HD, (h + 1) * HD)
        vcols = slice(width + h * HD, width + (h + 1) * HD)
        own = (
            lambda cols=cols: scores_of(
                q_ref[:, cols], jnp.concatenate([r[:, cols] for r in kv_refs], axis=0), mask
            ),
            lambda w, vcols=vcols: values_of(
                jnp.concatenate([r[:, vcols] for r in kv_refs], axis=0), w, 0
            ),
        )
        heads.append([own] + cached_tiles(q_of, ck_ref, cvt_ref, h))
    put(out_ref, attend_heads(heads))


def merge_kernel(*refs):
    *in_refs, out_ref = refs
    put(out_ref, [join_taken(taken) for taken in zip(*[take(r) for r in in_refs])])


def final_kernel(count, *refs):
    in_refs, out_refs = refs[:count], refs[count:]
    step = out_refs[0].shape[0]
    for h, taken in enumerate(zip(*[take(r) for r in in_refs])):
        numer, _, denom = join_taken(taken)
        value = jnp.transpose(numer * (1.0 / denom)).astype(jnp.bfloat16)
        for i, out_ref in enumerate(out_refs):
            out_ref[:, h * HD : (h + 1) * HD] = value[i * step : (i + 1) * step]


def pick_kernel(pieces, count, order_ref, *refs):
    in_refs, out_refs, done = refs[:count], refs[count:-1], refs[-1]
    width = out_refs[0].shape[1] // count
    copies = []
    for d, out_ref in zip(pieces, out_refs):
        start = pl.multiple_of(order_ref[d] * width, width)
        for i, ref in enumerate(in_refs):
            source, target = ref.at[:, pl.ds(start, width)], out_ref.at[:, i * width : (i + 1) * width]
            copies.append(pltpu.make_async_copy(source, target, done.at[len(copies)]))
            copies[-1].start()
    for copy in copies:
        copy.wait()


def slice_kernel(pieces, order_ref, ref, *out_refs):
    width = out_refs[0].shape[1]
    for d, out_ref in zip(pieces, out_refs):
        out_ref[...] = ref[:, pl.ds(pl.multiple_of(order_ref[d] * width, width), width)]


def stack_kernel(count, *refs):
    out_ref = refs[-1]
    step = refs[0].shape[0]
    for i in range(count):
        out_ref[i * step : (i + 1) * step, :] = refs[i][...]


def place_kernel(order_ref, *refs):
    *pieces, out_ref = refs
    width = pieces[0].shape[1]
    for d, piece in enumerate(pieces):
        start = pl.multiple_of(order_ref[d] * width, width)
        out_ref[:, pl.ds(start, width)] = piece[...]


def move(kernel, copies, scalars, arrays, outs, unread=()):
    read = 1 + len(arrays)

    def without_unread(*refs):
        kernel(*refs[:read], *refs[read + len(unread) :])

    return pl.pallas_call(
        without_unread,
        out_shape=outs,
        in_specs=[pl.BlockSpec(memory_space=pltpu.SMEM)]
        + [pl.BlockSpec(memory_space=pl.ANY)] * (len(arrays) + len(unread)),
        out_specs=[pl.BlockSpec(memory_space=pltpu.VMEM)] * len(outs),
        scratch_shapes=[pltpu.SemaphoreType.DMA((copies,))],
        cost_estimate=pl.CostEstimate(flops=0, bytes_accessed=2 * 4 * outs[0].size, transcendentals=0),
    )(scalars, *arrays, *unread)


def call(kernel, arrays, outs, flops=0, exps=0, scalars=None, unread=()):
    moved = sum(a.size * a.dtype.itemsize for a in arrays)
    moved += sum(math.prod(o.shape) * o.dtype.itemsize for o in outs)
    first = [] if scalars is None else [scalars]
    read = len(first) + len(arrays)

    def without_unread(*refs):
        kernel(*refs[:read], *refs[read + len(unread) :])

    return pl.pallas_call(
        without_unread,
        out_shape=outs,
        in_specs=[pl.BlockSpec(memory_space=pltpu.SMEM)] * len(first)
        + [pl.BlockSpec(memory_space=pltpu.VMEM)] * len(arrays)
        + [pl.BlockSpec(memory_space=pl.ANY)] * len(unread),
        out_specs=[pl.BlockSpec(memory_space=pltpu.VMEM)] * len(outs),
        compiler_params=pltpu.CompilerParams(vmem_limit_bytes=16 * 1024 * 1024),
        cost_estimate=pl.CostEstimate(flops=flops, bytes_accessed=moved, transcendentals=exps),
    )(*first, *arrays, *unread)


def dense_body(queries, new_keys, new_values, cache_keys, cache_values):
    seq_count = lax.axis_size("seq")
    shares = lax.axis_size("heads") * lax.axis_size("sub")
    me = lax.axis_index("heads") * lax.axis_size("sub") + lax.axis_index("sub")
    step, width = queries.shape[0], queries.shape[1] // shares
    cached = cache_keys.shape[0]
    each = shares // CHUNKS
    rows = each * step
    chunk = jax.ShapeDtypeStruct((rows, width), jnp.bfloat16)
    piece = jax.ShapeDtypeStruct((step, width), jnp.bfloat16)
    pair = jax.ShapeDtypeStruct((step, 2 * width), jnp.bfloat16)
    packed = jax.ShapeDtypeStruct((width + STAT, rows), jnp.int16)
    tile_flops = 4 * rows * cached * width
    tile_exps = rows * cached * (width // HD)

    def swap(x, d):
        return lax.ppermute(x, ("heads", "sub"), [(i, i ^ d) for i in range(shares)])

    def along(x, bit):
        return lax.ppermute(x, "seq", [(i, i ^ bit) for i in range(seq_count)])

    def after(x, unread):
        like = jax.ShapeDtypeStruct(x.shape, x.dtype)
        return call(functools.partial(stack_kernel, 1), [x], [like], unread=unread)[0] if unread else x

    order = jnp.stack([me ^ d for d in range(shares)]).astype(jnp.int32)
    cache_vt = cache_values.T
    context = [cache_keys, cache_vt]

    def attend(q):
        return call(cached_kernel, [q, *context], [packed], tile_flops, tile_exps)[0]

    def attend_own(q, pieces, unread):
        return call(
            functools.partial(own_kernel, pieces),
            [q, *kv, *context],
            [packed],
            tile_flops * 3 // 2,
            tile_exps * 3 // 2,
            order,
            unread,
        )[0]

    def merge(mine, got):
        return call(merge_kernel, [mine, got], [packed])[0]

    def end(parts, pieces):
        ended = call(functools.partial(final_kernel, len(parts)), parts, [piece] * each)
        return [swap(x, d) if d else x for x, d in zip(ended, pieces)]

    pieces_a, pieces_b = range(each), range(each, shares)

    def pick(arrays, pieces, out, unread=()):
        kernel = functools.partial(pick_kernel, pieces, len(arrays))
        count = len(pieces)
        return move(kernel, count * len(arrays), order, arrays, [out] * count, unread)

    def slices(pieces):
        kernel = functools.partial(slice_kernel, pieces)
        return call(kernel, [queries], [piece] * each, scalars=order)

    q = [swap(x, d) if d else x for x, d in zip(slices(pieces_a), pieces_a)]
    a = call(functools.partial(stack_kernel, each), q, [chunk])[0]
    q = slices(pieces_b)
    a2, a1 = along(a, 2), along(a, 1)
    q = [swap(x, d) for x, d in zip(q, pieces_b)]
    b = call(functools.partial(stack_kernel, each), q, [chunk])[0]
    b2, b1 = along(b, 2), along(b, 1)
    kv = pick([new_keys, new_values], range(shares), pair, [b, cache_vt])
    kv = [swap(x, d) if d else x for d, x in enumerate(kv)]
    part_a2, part_a1 = attend(a2), attend(a1)
    b3 = along(after(b2, [part_a2, part_a1]), 1)
    part_b2 = attend(b2)
    a3 = along(after(a2, [part_b2, b1, *kv[1:]]), 1)
    got_b2 = along(attend(b3), 1)
    got_a2 = along(attend(a3), 1)
    part_b1 = attend(b1)
    part_b2 = merge(part_b2, after(got_b2, [part_b1]))
    from_b2 = along(part_b2, 2)
    from_b1 = along(after(part_b1, [part_b2]), 1)
    own_b, own_a = attend_own(b, pieces_b, [part_b2]), attend_own(a, pieces_a, [part_b2])
    part_a2 = after(merge(part_a2, got_a2), [from_b2, own_a, own_b])
    from_a2 = along(part_a2, 2)
    from_a1 = along(after(part_a1, [part_a2]), 1)
    out_b = end([own_b, from_b2, from_b1], pieces_b)
    out_a = end([own_a, from_a2, from_a1], pieces_a)
    results = [*out_a, *out_b]
    out = jax.ShapeDtypeStruct((step, shares * width), jnp.bfloat16)
    return call(place_kernel, results, [out], scalars=order)[0]


CHUNKS = 2


def power_of_two(n):
    return n & (n - 1) == 0


def body(queries, new_keys, new_values, cache_keys, cache_values, selection):
    qblocks, head_count, top_count = selection.shape
    seq_count = lax.axis_size("seq")
    shares = lax.axis_size("heads") * lax.axis_size("sub")
    every = top_count == cache_keys.shape[0] // BLOCK * seq_count and qblocks == 1
    fits = seq_count == 4 and power_of_two(shares) and shares % CHUNKS == 0
    if every and fits and 4 * head_count <= STAT:
        return dense_body(queries, new_keys, new_values, cache_keys, cache_values)
    return sparse_body(queries, new_keys, new_values, cache_keys, cache_values, selection)


def solution(mesh):
    in_specs = (
        P(("groups", "seq", "heads", "sub"), None),
        P(("groups", "seq", "heads", "sub"), None),
        P(("groups", "seq", "heads", "sub"), None),
        P(("groups", "seq"), ("heads", "sub")),
        P(("groups", "seq"), ("heads", "sub")),
        P(("groups", "seq"), ("heads", "sub"), None),
    )
    out_specs = P(("groups", "seq", "heads", "sub"), None)
    return jax.shard_map(body, mesh=mesh, in_specs=in_specs, out_specs=out_specs, check_vma=False)
```

```python
import functools
import math

import jax
import jax.numpy as jnp
from jax import lax
from jax.experimental import pallas as pl
from jax.experimental.pallas import tpu as pltpu
from jax.sharding import PartitionSpec as P

HD = 128
BLOCK = 512


def order_ranks(owners):
    length = owners.shape[-1]
    counter = jnp.arange(length)
    earlier = counter[None, :] < counter[:, None]
    same_owner = owners[..., :, None] == owners[..., None, :]
    return jnp.sum(jnp.logical_and(same_owner, earlier), axis=-1)


def one_hot(values, length):
    return (values[..., None] == jnp.arange(length)).astype(jnp.float32)


def own_partial(query_blocks, key_blocks, value_blocks, scaling):
    scores = (
        jnp.einsum("bqhd,bkhd->bhqk", query_blocks, key_blocks, preferred_element_type=jnp.float32)
        * scaling
    )
    length = query_blocks.shape[1]
    causal = jnp.arange(length)[:, None] >= jnp.arange(length)[None, :]
    scores = jnp.where(causal, scores, -jnp.inf)
    highest = jnp.max(scores, axis=-1)
    weights = jnp.exp(scores - highest[..., None])
    totals = jnp.sum(weights, axis=-1)
    mixed = jnp.einsum(
        "bhqk,bkhd->bhqd",
        weights.astype(jnp.bfloat16),
        value_blocks,
        preferred_element_type=jnp.float32,
    )
    return (mixed, highest, totals)


def tile_partial(query_blocks, tile_pair, scaling):
    head_size = query_blocks.shape[-1]
    scores = (
        jnp.einsum(
            "bqhd,bhkd->bhqk",
            query_blocks,
            tile_pair[..., :head_size],
            preferred_element_type=jnp.float32,
        )
        * scaling
    )
    highest = jnp.max(scores, axis=-1)
    weights = jnp.exp(scores - highest[..., None])
    totals = jnp.sum(weights, axis=-1)
    mixed = jnp.einsum(
        "bhqk,bhkd->bhqd",
        weights.astype(jnp.bfloat16),
        tile_pair[..., head_size:],
        preferred_element_type=jnp.float32,
    )
    return (mixed, highest, totals)


def merge_parts(parts):
    top = parts[0][1]
    for part in parts[1:]:
        top = jnp.maximum(top, part[1])
    numer = jnp.zeros(parts[0][0].shape, jnp.float32)
    denom = jnp.zeros(parts[0][2].shape, jnp.float32)
    for part in parts:
        factor = jnp.exp(part[1] - top)
        numer = numer + factor[..., None] * part[0]
        denom = denom + factor * part[2]
    return numer / denom[..., None]


def sparse_body(queries, new_keys, new_values, cache_keys, cache_values, selection):
    heads_q, heads_k, heads_v = (
        lax.all_to_all(queries, ("heads", "sub"), split_axis=1, concat_axis=0, tiled=True),
        lax.all_to_all(new_keys, ("heads", "sub"), split_axis=1, concat_axis=0, tiled=True),
        lax.all_to_all(new_values, ("heads", "sub"), split_axis=1, concat_axis=0, tiled=True),
    )
    qblocks, head_count, top_count = selection.shape
    head_size = HD
    scaling = head_size ** (-0.5)
    shaped = (qblocks, BLOCK, head_count, head_size)
    query_blocks = heads_q.reshape(shaped)
    own = own_partial(query_blocks, heads_k.reshape(shaped), heads_v.reshape(shaped), scaling)
    seq_count = lax.axis_size("seq")
    myself = lax.axis_index("seq")
    cache_blocks = cache_keys.shape[0] // BLOCK
    tile_count = cache_blocks * head_count
    request_count = qblocks * head_count * top_count
    capacity = -(-request_count // seq_count)
    requests_all = lax.all_gather(selection, "seq", axis=0, tiled=True).reshape(
        seq_count, request_count
    )
    head_of = jnp.arange(request_count) // top_count % head_count
    my_requests = selection.reshape(request_count)
    my_owner = my_requests // cache_blocks
    my_slot = my_owner * capacity + order_ranks(my_owner)
    key_tiles = cache_keys.reshape(cache_blocks, BLOCK, head_count, head_size).transpose(0, 2, 1, 3)
    value_tiles = cache_values.reshape(cache_blocks, BLOCK, head_count, head_size).transpose(
        0, 2, 1, 3
    )
    tile_set = jnp.concatenate([key_tiles, value_tiles], axis=-1).reshape(
        tile_count, BLOCK, 2 * head_size
    )
    their_owner = requests_all // cache_blocks
    local_tile = requests_all % cache_blocks * head_count + head_of[None, :]
    served = (their_owner == myself).astype(jnp.float32)
    slot_pick = one_hot(order_ranks(their_owner), capacity) * served[..., None]
    picking = jnp.einsum("erc,erl->ecl", slot_pick, one_hot(local_tile, tile_count)).astype(
        jnp.bfloat16
    )
    parts = [own]
    outgoing = jnp.einsum(
        "ecl,lkf->eckf", picking, tile_set, preferred_element_type=jnp.float32
    ).astype(jnp.bfloat16)
    incoming = lax.all_to_all(outgoing, "seq", split_axis=0, concat_axis=0, tiled=True)
    fetched = incoming.reshape(seq_count * capacity, BLOCK, 2 * head_size)[my_slot]
    fetched = fetched.reshape(qblocks, head_count, top_count, BLOCK, 2 * head_size)
    for turn in range(top_count):
        parts.append(tile_partial(query_blocks, fetched[:, :, turn], scaling))
    result = merge_parts(parts)
    result = (
        result.transpose(0, 2, 1, 3)
        .reshape(qblocks * BLOCK, head_count * head_size)
        .astype(jnp.bfloat16)
    )
    return lax.all_to_all(result, ("heads", "sub"), split_axis=0, concat_axis=1, tiled=True)


STAT = 16
UNIT = 32767.0
LEAST = 1.2e-34
C2 = math.log2(math.e) * HD**-0.5


def scores_of(q, k, mask=None):
    s = lax.dot_general(k, q, (((1,), (1,)), ((), ())), preferred_element_type=jnp.float32)
    return s if mask is None else jnp.where(mask, s, -jnp.inf)


def weights_of(s):
    m = jnp.max(s, axis=0, keepdims=True)
    p = jnp.exp2((s - m) * C2)
    return p.astype(jnp.bfloat16), m * C2, jnp.sum(p, axis=0, keepdims=True)


def values_of(v, w, v_dim):
    return lax.dot_general(v, w, (((v_dim,), (0,)), ((), ())), preferred_element_type=jnp.float32)


def attend(tiles):
    count = len(tiles)
    s, w, parts = {}, {}, []
    for t in range(count + 2):
        if t < count:
            s[t] = tiles[t][0]()
        if 1 <= t <= count:
            w[t - 1] = weights_of(s.pop(t - 1))
        if t >= 2:
            weights, m, total = w.pop(t - 2)
            parts.append((tiles[t - 2][1](weights), m, total))
    return parts


def join(parts):
    top = functools.reduce(jnp.maximum, [m for _, m, _ in parts])
    factors = [jnp.exp2(m - top) for _, m, _ in parts]
    numer = sum(f * o for f, (o, _, _) in zip(factors, parts))
    denom = sum(f * t for f, (_, _, t) in zip(factors, parts))
    return numer, top, denom


def put(out_ref, heads):
    width, rows = len(heads) * HD, heads[0][0].shape[1]
    at = lax.broadcasted_iota(jnp.int32, (STAT, rows), 0)
    stats = jnp.zeros((STAT, rows), jnp.float32)
    for h, (numer, top, denom) in enumerate(heads):
        most = jnp.maximum(jnp.max(jnp.abs(numer), axis=0, keepdims=True), LEAST)
        code = jnp.round(numer * (UNIT / most))
        out_ref[h * HD : (h + 1) * HD, :] = code.astype(jnp.int32).astype(jnp.int16)
        weight = jnp.log2(denom)
        for j, value in enumerate((top + weight, jnp.log2(most) - math.log2(UNIT) - weight)):
            whole = jnp.floor(value)
            stats = jnp.where(at == 4 * h + 2 * j, whole, stats)
            stats = jnp.where(at == 4 * h + 2 * j + 1, jnp.round((value - whole) * UNIT), stats)
    out_ref[width : width + STAT, :] = stats.astype(jnp.int32).astype(jnp.int16)


def take(ref):
    width = ref.shape[0] - STAT
    stats = ref[width : width + STAT, :].astype(jnp.int32).astype(jnp.float32)
    heads = []
    for h in range(width // HD):
        code = ref[h * HD : (h + 1) * HD, :].astype(jnp.int32).astype(jnp.float32)
        weight = stats[4 * h : 4 * h + 1] + stats[4 * h + 1 : 4 * h + 2] * (1.0 / UNIT)
        unit = stats[4 * h + 2 : 4 * h + 3] + stats[4 * h + 3 : 4 * h + 4] * (1.0 / UNIT)
        heads.append((code, weight, unit))
    return heads


def join_taken(taken):
    top = functools.reduce(jnp.maximum, [w for _, w, _ in taken])
    numer = sum(code * jnp.exp2(w - top + unit) for code, w, unit in taken)
    denom = sum(jnp.exp2(w - top) for _, w, _ in taken)
    return numer, top, denom


def cached_tiles(q_of, ck_ref, cvt_ref, h):
    cols = slice(h * HD, (h + 1) * HD)
    tiles = []
    for b in range(ck_ref.shape[0] // BLOCK):
        rows = slice(b * BLOCK, (b + 1) * BLOCK)
        tiles.append(
            (
                lambda rows=rows: scores_of(q_of(cols), ck_ref[rows, cols]),
                lambda w, rows=rows: values_of(cvt_ref[cols, rows], w, 1),
            )
        )
    return tiles


def attend_heads(tiles_of_heads):
    parts = attend([t for tiles in tiles_of_heads for t in tiles])
    heads = []
    for tiles in tiles_of_heads:
        heads.append(join(parts[: len(tiles)]))
        parts = parts[len(tiles) :]
    return heads


def cached_kernel(q_ref, ck_ref, cvt_ref, out_ref):
    heads = range(ck_ref.shape[1] // HD)
    q_of = lambda cols: q_ref[:, cols]
    put(out_ref, attend_heads([cached_tiles(q_of, ck_ref, cvt_ref, h) for h in heads]))


def own_kernel(mine, order_ref, *refs):
    q_ref, *kv_refs, ck_ref, cvt_ref, out_ref = refs
    width = ck_ref.shape[1]
    rows = q_ref.shape[0]
    step = kv_refs[0].shape[0]

    def positions(shape, axis, pieces):
        at = lax.broadcasted_iota(jnp.int32, shape, axis)
        place = jnp.zeros(shape, jnp.int32)
        for i, d in enumerate(pieces):
            place = jnp.where(at // step == i, order_ref[d] * step + at % step, place)
        return place

    shape = (step * len(kv_refs), rows)
    mask = positions(shape, 1, mine) >= positions(shape, 0, range(len(kv_refs)))
    q_of = lambda cols: q_ref[:, cols]
    heads = []
    for h in range(width // HD):
        cols = slice(h * HD, (h + 1) * HD)
        vcols = slice(width + h * HD, width + (h + 1) * HD)
        own = (
            lambda cols=cols: scores_of(
                q_ref[:, cols], jnp.concatenate([r[:, cols] for r in kv_refs], axis=0), mask
            ),
            lambda w, vcols=vcols: values_of(
                jnp.concatenate([r[:, vcols] for r in kv_refs], axis=0), w, 0
            ),
        )
        heads.append([own] + cached_tiles(q_of, ck_ref, cvt_ref, h))
    put(out_ref, attend_heads(heads))


def merge_kernel(*refs):
    *in_refs, out_ref = refs
    put(out_ref, [join_taken(taken) for taken in zip(*[take(r) for r in in_refs])])


def final_kernel(count, *refs):
    in_refs, out_refs = refs[:count], refs[count:]
    step = out_refs[0].shape[0]
    for h, taken in enumerate(zip(*[take(r) for r in in_refs])):
        numer, _, denom = join_taken(taken)
        value = jnp.transpose(numer * (1.0 / denom)).astype(jnp.bfloat16)
        for i, out_ref in enumerate(out_refs):
            out_ref[:, h * HD : (h + 1) * HD] = value[i * step : (i + 1) * step]


def pick_kernel(pieces, count, order_ref, *refs):
    in_refs, out_refs, done = refs[:count], refs[count:-1], refs[-1]
    width = out_refs[0].shape[1] // count
    copies = []
    for d, out_ref in zip(pieces, out_refs):
        start = pl.multiple_of(order_ref[d] * width, width)
        for i, ref in enumerate(in_refs):
            source, target = ref.at[:, pl.ds(start, width)], out_ref.at[:, i * width : (i + 1) * width]
            copies.append(pltpu.make_async_copy(source, target, done.at[len(copies)]))
            copies[-1].start()
    for copy in copies:
        copy.wait()


def slice_kernel(pieces, order_ref, ref, *out_refs):
    width = out_refs[0].shape[1]
    for d, out_ref in zip(pieces, out_refs):
        out_ref[...] = ref[:, pl.ds(pl.multiple_of(order_ref[d] * width, width), width)]


def stack_kernel(count, *refs):
    out_ref = refs[-1]
    step = refs[0].shape[0]
    for i in range(count):
        out_ref[i * step : (i + 1) * step, :] = refs[i][...]


def place_kernel(order_ref, *refs):
    *pieces, out_ref = refs
    width = pieces[0].shape[1]
    for d, piece in enumerate(pieces):
        start = pl.multiple_of(order_ref[d] * width, width)
        out_ref[:, pl.ds(start, width)] = piece[...]


def move(kernel, copies, scalars, arrays, outs, unread=()):
    read = 1 + len(arrays)

    def without_unread(*refs):
        kernel(*refs[:read], *refs[read + len(unread) :])

    return pl.pallas_call(
        without_unread,
        out_shape=outs,
        in_specs=[pl.BlockSpec(memory_space=pltpu.SMEM)]
        + [pl.BlockSpec(memory_space=pl.ANY)] * (len(arrays) + len(unread)),
        out_specs=[pl.BlockSpec(memory_space=pltpu.VMEM)] * len(outs),
        scratch_shapes=[pltpu.SemaphoreType.DMA((copies,))],
        cost_estimate=pl.CostEstimate(flops=0, bytes_accessed=2 * 4 * outs[0].size, transcendentals=0),
    )(scalars, *arrays, *unread)


def call(kernel, arrays, outs, flops=0, exps=0, scalars=None, unread=()):
    moved = sum(a.size * a.dtype.itemsize for a in arrays)
    moved += sum(math.prod(o.shape) * o.dtype.itemsize for o in outs)
    first = [] if scalars is None else [scalars]
    read = len(first) + len(arrays)

    def without_unread(*refs):
        kernel(*refs[:read], *refs[read + len(unread) :])

    return pl.pallas_call(
        without_unread,
        out_shape=outs,
        in_specs=[pl.BlockSpec(memory_space=pltpu.SMEM)] * len(first)
        + [pl.BlockSpec(memory_space=pltpu.VMEM)] * len(arrays)
        + [pl.BlockSpec(memory_space=pl.ANY)] * len(unread),
        out_specs=[pl.BlockSpec(memory_space=pltpu.VMEM)] * len(outs),
        compiler_params=pltpu.CompilerParams(vmem_limit_bytes=16 * 1024 * 1024),
        cost_estimate=pl.CostEstimate(flops=flops, bytes_accessed=moved, transcendentals=exps),
    )(*first, *arrays, *unread)


def dense_body(queries, new_keys, new_values, cache_keys, cache_values):
    seq_count = lax.axis_size("seq")
    shares = lax.axis_size("heads") * lax.axis_size("sub")
    me = lax.axis_index("heads") * lax.axis_size("sub") + lax.axis_index("sub")
    step, width = queries.shape[0], queries.shape[1] // shares
    cached = cache_keys.shape[0]
    each = shares // CHUNKS
    rows = each * step
    chunk = jax.ShapeDtypeStruct((rows, width), jnp.bfloat16)
    piece = jax.ShapeDtypeStruct((step, width), jnp.bfloat16)
    pair = jax.ShapeDtypeStruct((step, 2 * width), jnp.bfloat16)
    packed = jax.ShapeDtypeStruct((width + STAT, rows), jnp.int16)
    tile_flops = 4 * rows * cached * width
    tile_exps = rows * cached * (width // HD)

    def swap(x, d):
        return lax.ppermute(x, ("heads", "sub"), [(i, i ^ d) for i in range(shares)])

    def along(x, bit):
        return lax.ppermute(x, "seq", [(i, i ^ bit) for i in range(seq_count)])

    def after(x, unread):
        like = jax.ShapeDtypeStruct(x.shape, x.dtype)
        return call(functools.partial(stack_kernel, 1), [x], [like], unread=unread)[0] if unread else x

    order = jnp.stack([me ^ d for d in range(shares)]).astype(jnp.int32)
    cache_vt = cache_values.T
    context = [cache_keys, cache_vt]

    def attend(q):
        return call(cached_kernel, [q, *context], [packed], tile_flops, tile_exps)[0]

    def attend_own(q, pieces, unread):
        return call(
            functools.partial(own_kernel, pieces),
            [q, *kv, *context],
            [packed],
            tile_flops * 3 // 2,
            tile_exps * 3 // 2,
            order,
            unread,
        )[0]

    def merge(mine, got):
        return call(merge_kernel, [mine, got], [packed])[0]

    def end(parts, pieces):
        ended = call(functools.partial(final_kernel, len(parts)), parts, [piece] * each)
        return [swap(x, d) if d else x for x, d in zip(ended, pieces)]

    pieces_a, pieces_b = range(each), range(each, shares)

    def pick(arrays, pieces, out, unread=()):
        kernel = functools.partial(pick_kernel, pieces, len(arrays))
        count = len(pieces)
        return move(kernel, count * len(arrays), order, arrays, [out] * count, unread)

    def slices(pieces):
        kernel = functools.partial(slice_kernel, pieces)
        return call(kernel, [queries], [piece] * each, scalars=order)

    q = [swap(x, d) if d else x for x, d in zip(slices(pieces_a), pieces_a)]
    a = call(functools.partial(stack_kernel, each), q, [chunk])[0]
    q = slices(pieces_b)
    a2, a1 = along(a, 2), along(a, 1)
    q = [swap(x if d == each else after(x, [cache_vt]), d) for x, d in zip(q, pieces_b)]
    b = call(functools.partial(stack_kernel, each), q, [chunk])[0]
    b2, b1 = along(b, 2), along(b, 1)
    kv = pick([new_keys, new_values], range(shares), pair, [b])
    kv = [swap(x, d) if d else x for d, x in enumerate(kv)]
    part_a2, part_a1 = attend(a2), attend(a1)
    b3 = along(after(b2, [part_a2, part_a1]), 1)
    part_b2 = attend(b2)
    a3 = along(after(a2, [part_b2, b1, *kv[1:]]), 1)
    got_b2 = along(attend(b3), 1)
    got_a2 = along(attend(a3), 1)
    part_b1 = attend(b1)
    part_b2 = merge(part_b2, after(got_b2, [part_b1]))
    from_b2 = along(part_b2, 2)
    from_b1 = along(after(part_b1, [part_b2]), 1)
    own_b, own_a = attend_own(b, pieces_b, [part_b2]), attend_own(a, pieces_a, [part_b2])
    part_a2 = after(merge(part_a2, got_a2), [from_b2, own_a, own_b])
    from_a2 = along(part_a2, 2)
    from_a1 = along(after(part_a1, [part_a2]), 1)
    out_b = end([own_b, from_b2, from_b1], pieces_b)
    out_a = end([own_a, from_a2, from_a1], pieces_a)
    results = [*out_a, *out_b]
    out = jax.ShapeDtypeStruct((step, shares * width), jnp.bfloat16)
    return call(place_kernel, results, [out], scalars=order)[0]


CHUNKS = 2


def power_of_two(n):
    return n & (n - 1) == 0


def body(queries, new_keys, new_values, cache_keys, cache_values, selection):
    qblocks, head_count, top_count = selection.shape
    seq_count = lax.axis_size("seq")
    shares = lax.axis_size("heads") * lax.axis_size("sub")
    every = top_count == cache_keys.shape[0] // BLOCK * seq_count and qblocks == 1
    fits = seq_count == 4 and power_of_two(shares) and shares % CHUNKS == 0
    if every and fits and 4 * head_count <= STAT:
        return dense_body(queries, new_keys, new_values, cache_keys, cache_values)
    return sparse_body(queries, new_keys, new_values, cache_keys, cache_values, selection)


def solution(mesh):
    in_specs = (
        P(("groups", "seq", "heads", "sub"), None),
        P(("groups", "seq", "heads", "sub"), None),
        P(("groups", "seq", "heads", "sub"), None),
        P(("groups", "seq"), ("heads", "sub")),
        P(("groups", "seq"), ("heads", "sub")),
        P(("groups", "seq"), ("heads", "sub"), None),
    )
    out_specs = P(("groups", "seq", "heads", "sub"), None)
    return jax.shard_map(body, mesh=mesh, in_specs=in_specs, out_specs=out_specs, check_vma=False)
```

```python
import functools
import math

import jax
import jax.numpy as jnp
from jax import lax
from jax.experimental import pallas as pl
from jax.experimental.pallas import tpu as pltpu
from jax.sharding import PartitionSpec as P

HD = 128
BLOCK = 512


def order_ranks(owners):
    length = owners.shape[-1]
    counter = jnp.arange(length)
    earlier = counter[None, :] < counter[:, None]
    same_owner = owners[..., :, None] == owners[..., None, :]
    return jnp.sum(jnp.logical_and(same_owner, earlier), axis=-1)


def one_hot(values, length):
    return (values[..., None] == jnp.arange(length)).astype(jnp.float32)


def own_partial(query_blocks, key_blocks, value_blocks, scaling):
    scores = (
        jnp.einsum("bqhd,bkhd->bhqk", query_blocks, key_blocks, preferred_element_type=jnp.float32)
        * scaling
    )
    length = query_blocks.shape[1]
    causal = jnp.arange(length)[:, None] >= jnp.arange(length)[None, :]
    scores = jnp.where(causal, scores, -jnp.inf)
    highest = jnp.max(scores, axis=-1)
    weights = jnp.exp(scores - highest[..., None])
    totals = jnp.sum(weights, axis=-1)
    mixed = jnp.einsum(
        "bhqk,bkhd->bhqd",
        weights.astype(jnp.bfloat16),
        value_blocks,
        preferred_element_type=jnp.float32,
    )
    return (mixed, highest, totals)


def tile_partial(query_blocks, tile_pair, scaling):
    head_size = query_blocks.shape[-1]
    scores = (
        jnp.einsum(
            "bqhd,bhkd->bhqk",
            query_blocks,
            tile_pair[..., :head_size],
            preferred_element_type=jnp.float32,
        )
        * scaling
    )
    highest = jnp.max(scores, axis=-1)
    weights = jnp.exp(scores - highest[..., None])
    totals = jnp.sum(weights, axis=-1)
    mixed = jnp.einsum(
        "bhqk,bhkd->bhqd",
        weights.astype(jnp.bfloat16),
        tile_pair[..., head_size:],
        preferred_element_type=jnp.float32,
    )
    return (mixed, highest, totals)


def merge_parts(parts):
    top = parts[0][1]
    for part in parts[1:]:
        top = jnp.maximum(top, part[1])
    numer = jnp.zeros(parts[0][0].shape, jnp.float32)
    denom = jnp.zeros(parts[0][2].shape, jnp.float32)
    for part in parts:
        factor = jnp.exp(part[1] - top)
        numer = numer + factor[..., None] * part[0]
        denom = denom + factor * part[2]
    return numer / denom[..., None]


def sparse_body(queries, new_keys, new_values, cache_keys, cache_values, selection):
    heads_q, heads_k, heads_v = (
        lax.all_to_all(queries, ("heads", "sub"), split_axis=1, concat_axis=0, tiled=True),
        lax.all_to_all(new_keys, ("heads", "sub"), split_axis=1, concat_axis=0, tiled=True),
        lax.all_to_all(new_values, ("heads", "sub"), split_axis=1, concat_axis=0, tiled=True),
    )
    qblocks, head_count, top_count = selection.shape
    head_size = HD
    scaling = head_size ** (-0.5)
    shaped = (qblocks, BLOCK, head_count, head_size)
    query_blocks = heads_q.reshape(shaped)
    own = own_partial(query_blocks, heads_k.reshape(shaped), heads_v.reshape(shaped), scaling)
    seq_count = lax.axis_size("seq")
    myself = lax.axis_index("seq")
    cache_blocks = cache_keys.shape[0] // BLOCK
    tile_count = cache_blocks * head_count
    request_count = qblocks * head_count * top_count
    capacity = -(-request_count // seq_count)
    requests_all = lax.all_gather(selection, "seq", axis=0, tiled=True).reshape(
        seq_count, request_count
    )
    head_of = jnp.arange(request_count) // top_count % head_count
    my_requests = selection.reshape(request_count)
    my_owner = my_requests // cache_blocks
    my_slot = my_owner * capacity + order_ranks(my_owner)
    key_tiles = cache_keys.reshape(cache_blocks, BLOCK, head_count, head_size).transpose(0, 2, 1, 3)
    value_tiles = cache_values.reshape(cache_blocks, BLOCK, head_count, head_size).transpose(
        0, 2, 1, 3
    )
    tile_set = jnp.concatenate([key_tiles, value_tiles], axis=-1).reshape(
        tile_count, BLOCK, 2 * head_size
    )
    their_owner = requests_all // cache_blocks
    local_tile = requests_all % cache_blocks * head_count + head_of[None, :]
    served = (their_owner == myself).astype(jnp.float32)
    slot_pick = one_hot(order_ranks(their_owner), capacity) * served[..., None]
    picking = jnp.einsum("erc,erl->ecl", slot_pick, one_hot(local_tile, tile_count)).astype(
        jnp.bfloat16
    )
    parts = [own]
    outgoing = jnp.einsum(
        "ecl,lkf->eckf", picking, tile_set, preferred_element_type=jnp.float32
    ).astype(jnp.bfloat16)
    incoming = lax.all_to_all(outgoing, "seq", split_axis=0, concat_axis=0, tiled=True)
    fetched = incoming.reshape(seq_count * capacity, BLOCK, 2 * head_size)[my_slot]
    fetched = fetched.reshape(qblocks, head_count, top_count, BLOCK, 2 * head_size)
    for turn in range(top_count):
        parts.append(tile_partial(query_blocks, fetched[:, :, turn], scaling))
    result = merge_parts(parts)
    result = (
        result.transpose(0, 2, 1, 3)
        .reshape(qblocks * BLOCK, head_count * head_size)
        .astype(jnp.bfloat16)
    )
    return lax.all_to_all(result, ("heads", "sub"), split_axis=0, concat_axis=1, tiled=True)


STAT = 16
UNIT = 32767.0
LEAST = 1.2e-34
C2 = math.log2(math.e) * HD**-0.5


def scores_of(q, k, mask=None):
    s = lax.dot_general(k, q, (((1,), (1,)), ((), ())), preferred_element_type=jnp.float32)
    return s if mask is None else jnp.where(mask, s, -jnp.inf)


def weights_of(s):
    m = jnp.max(s, axis=0, keepdims=True)
    p = jnp.exp2((s - m) * C2)
    return p.astype(jnp.bfloat16), m * C2, jnp.sum(p, axis=0, keepdims=True)


def values_of(v, w, v_dim):
    return lax.dot_general(v, w, (((v_dim,), (0,)), ((), ())), preferred_element_type=jnp.float32)


def attend(tiles):
    count = len(tiles)
    s, w, parts = {}, {}, []
    for t in range(count + 2):
        if t < count:
            s[t] = tiles[t][0]()
        if 1 <= t <= count:
            w[t - 1] = weights_of(s.pop(t - 1))
        if t >= 2:
            weights, m, total = w.pop(t - 2)
            parts.append((tiles[t - 2][1](weights), m, total))
    return parts


def join(parts):
    top = functools.reduce(jnp.maximum, [m for _, m, _ in parts])
    factors = [jnp.exp2(m - top) for _, m, _ in parts]
    numer = sum(f * o for f, (o, _, _) in zip(factors, parts))
    denom = sum(f * t for f, (_, _, t) in zip(factors, parts))
    return numer, top, denom


def put(out_ref, heads):
    width, rows = len(heads) * HD, heads[0][0].shape[1]
    at = lax.broadcasted_iota(jnp.int32, (STAT, rows), 0)
    stats = jnp.zeros((STAT, rows), jnp.float32)
    for h, (numer, top, denom) in enumerate(heads):
        most = jnp.maximum(jnp.max(jnp.abs(numer), axis=0, keepdims=True), LEAST)
        code = jnp.round(numer * (UNIT / most))
        out_ref[h * HD : (h + 1) * HD, :] = code.astype(jnp.int32).astype(jnp.int16)
        weight = jnp.log2(denom)
        for j, value in enumerate((top + weight, jnp.log2(most) - math.log2(UNIT) - weight)):
            whole = jnp.floor(value)
            stats = jnp.where(at == 4 * h + 2 * j, whole, stats)
            stats = jnp.where(at == 4 * h + 2 * j + 1, jnp.round((value - whole) * UNIT), stats)
    out_ref[width : width + STAT, :] = stats.astype(jnp.int32).astype(jnp.int16)


def take(ref):
    width = ref.shape[0] - STAT
    stats = ref[width : width + STAT, :].astype(jnp.int32).astype(jnp.float32)
    heads = []
    for h in range(width // HD):
        code = ref[h * HD : (h + 1) * HD, :].astype(jnp.int32).astype(jnp.float32)
        weight = stats[4 * h : 4 * h + 1] + stats[4 * h + 1 : 4 * h + 2] * (1.0 / UNIT)
        unit = stats[4 * h + 2 : 4 * h + 3] + stats[4 * h + 3 : 4 * h + 4] * (1.0 / UNIT)
        heads.append((code, weight, unit))
    return heads


def join_taken(taken):
    top = functools.reduce(jnp.maximum, [w for _, w, _ in taken])
    numer = sum(code * jnp.exp2(w - top + unit) for code, w, unit in taken)
    denom = sum(jnp.exp2(w - top) for _, w, _ in taken)
    return numer, top, denom


def cached_tiles(q_of, ck_ref, cvt_ref, h):
    cols = slice(h * HD, (h + 1) * HD)
    tiles = []
    for b in range(ck_ref.shape[0] // BLOCK):
        rows = slice(b * BLOCK, (b + 1) * BLOCK)
        tiles.append(
            (
                lambda rows=rows: scores_of(q_of(cols), ck_ref[rows, cols]),
                lambda w, rows=rows: values_of(cvt_ref[cols, rows], w, 1),
            )
        )
    return tiles


def attend_heads(tiles_of_heads):
    parts = attend([t for tiles in tiles_of_heads for t in tiles])
    heads = []
    for tiles in tiles_of_heads:
        heads.append(join(parts[: len(tiles)]))
        parts = parts[len(tiles) :]
    return heads


def cached_kernel(q_ref, ck_ref, cvt_ref, out_ref):
    heads = range(ck_ref.shape[1] // HD)
    q_of = lambda cols: q_ref[:, cols]
    put(out_ref, attend_heads([cached_tiles(q_of, ck_ref, cvt_ref, h) for h in heads]))


def own_kernel(mine, order_ref, *refs):
    q_ref, *kv_refs, ck_ref, cvt_ref, out_ref = refs
    width = ck_ref.shape[1]
    rows = q_ref.shape[0]
    step = kv_refs[0].shape[0]

    def positions(shape, axis, pieces):
        at = lax.broadcasted_iota(jnp.int32, shape, axis)
        place = jnp.zeros(shape, jnp.int32)
        for i, d in enumerate(pieces):
            place = jnp.where(at // step == i, order_ref[d] * step + at % step, place)
        return place

    shape = (step * len(kv_refs), rows)
    mask = positions(shape, 1, mine) >= positions(shape, 0, range(len(kv_refs)))
    q_of = lambda cols: q_ref[:, cols]
    heads = []
    for h in range(width // HD):
        cols = slice(h * HD, (h + 1) * HD)
        vcols = slice(width + h * HD, width + (h + 1) * HD)
        own = (
            lambda cols=cols: scores_of(
                q_ref[:, cols], jnp.concatenate([r[:, cols] for r in kv_refs], axis=0), mask
            ),
            lambda w, vcols=vcols: values_of(
                jnp.concatenate([r[:, vcols] for r in kv_refs], axis=0), w, 0
            ),
        )
        heads.append([own] + cached_tiles(q_of, ck_ref, cvt_ref, h))
    put(out_ref, attend_heads(heads))


def merge_kernel(*refs):
    *in_refs, out_ref = refs
    put(out_ref, [join_taken(taken) for taken in zip(*[take(r) for r in in_refs])])


def final_kernel(count, *refs):
    in_refs, out_refs = refs[:count], refs[count:]
    step = out_refs[0].shape[0]
    for h, taken in enumerate(zip(*[take(r) for r in in_refs])):
        numer, _, denom = join_taken(taken)
        value = jnp.transpose(numer * (1.0 / denom)).astype(jnp.bfloat16)
        for i, out_ref in enumerate(out_refs):
            out_ref[:, h * HD : (h + 1) * HD] = value[i * step : (i + 1) * step]


def pick_kernel(pieces, count, order_ref, *refs):
    in_refs, out_refs, done = refs[:count], refs[count:-1], refs[-1]
    width = out_refs[0].shape[1] // count
    copies = []
    for d, out_ref in zip(pieces, out_refs):
        start = pl.multiple_of(order_ref[d] * width, width)
        for i, ref in enumerate(in_refs):
            source, target = ref.at[:, pl.ds(start, width)], out_ref.at[:, i * width : (i + 1) * width]
            copies.append(pltpu.make_async_copy(source, target, done.at[len(copies)]))
            copies[-1].start()
    for copy in copies:
        copy.wait()


def slice_kernel(pieces, order_ref, ref, *out_refs):
    width = out_refs[0].shape[1]
    for d, out_ref in zip(pieces, out_refs):
        out_ref[...] = ref[:, pl.ds(pl.multiple_of(order_ref[d] * width, width), width)]


def stack_kernel(count, *refs):
    out_ref = refs[-1]
    step = refs[0].shape[0]
    for i in range(count):
        out_ref[i * step : (i + 1) * step, :] = refs[i][...]


def place_kernel(order_ref, *refs):
    *pieces, out_ref = refs
    width = pieces[0].shape[1]
    for d, piece in enumerate(pieces):
        start = pl.multiple_of(order_ref[d] * width, width)
        out_ref[:, pl.ds(start, width)] = piece[...]


def move(kernel, copies, scalars, arrays, outs, unread=()):
    read = 1 + len(arrays)

    def without_unread(*refs):
        kernel(*refs[:read], *refs[read + len(unread) :])

    return pl.pallas_call(
        without_unread,
        out_shape=outs,
        in_specs=[pl.BlockSpec(memory_space=pltpu.SMEM)]
        + [pl.BlockSpec(memory_space=pl.ANY)] * (len(arrays) + len(unread)),
        out_specs=[pl.BlockSpec(memory_space=pltpu.VMEM)] * len(outs),
        scratch_shapes=[pltpu.SemaphoreType.DMA((copies,))],
        cost_estimate=pl.CostEstimate(flops=0, bytes_accessed=2 * 4 * outs[0].size, transcendentals=0),
    )(scalars, *arrays, *unread)


def call(kernel, arrays, outs, flops=0, exps=0, scalars=None, unread=()):
    moved = sum(a.size * a.dtype.itemsize for a in arrays)
    moved += sum(math.prod(o.shape) * o.dtype.itemsize for o in outs)
    first = [] if scalars is None else [scalars]
    read = len(first) + len(arrays)

    def without_unread(*refs):
        kernel(*refs[:read], *refs[read + len(unread) :])

    return pl.pallas_call(
        without_unread,
        out_shape=outs,
        in_specs=[pl.BlockSpec(memory_space=pltpu.SMEM)] * len(first)
        + [pl.BlockSpec(memory_space=pltpu.VMEM)] * len(arrays)
        + [pl.BlockSpec(memory_space=pl.ANY)] * len(unread),
        out_specs=[pl.BlockSpec(memory_space=pltpu.VMEM)] * len(outs),
        compiler_params=pltpu.CompilerParams(vmem_limit_bytes=16 * 1024 * 1024),
        cost_estimate=pl.CostEstimate(flops=flops, bytes_accessed=moved, transcendentals=exps),
    )(*first, *arrays, *unread)


def dense_body(queries, new_keys, new_values, cache_keys, cache_values):
    seq_count = lax.axis_size("seq")
    shares = lax.axis_size("heads") * lax.axis_size("sub")
    me = lax.axis_index("heads") * lax.axis_size("sub") + lax.axis_index("sub")
    step, width = queries.shape[0], queries.shape[1] // shares
    cached = cache_keys.shape[0]
    each = shares // CHUNKS
    rows = each * step
    chunk = jax.ShapeDtypeStruct((rows, width), jnp.bfloat16)
    piece = jax.ShapeDtypeStruct((step, width), jnp.bfloat16)
    pair = jax.ShapeDtypeStruct((step, 2 * width), jnp.bfloat16)
    packed = jax.ShapeDtypeStruct((width + STAT, rows), jnp.int16)
    tile_flops = 4 * rows * cached * width
    tile_exps = rows * cached * (width // HD)

    def swap(x, d):
        return lax.ppermute(x, ("heads", "sub"), [(i, i ^ d) for i in range(shares)])

    def along(x, bit):
        return lax.ppermute(x, "seq", [(i, i ^ bit) for i in range(seq_count)])

    def after(x, unread):
        like = jax.ShapeDtypeStruct(x.shape, x.dtype)
        return call(functools.partial(stack_kernel, 1), [x], [like], unread=unread)[0] if unread else x

    order = jnp.stack([me ^ d for d in range(shares)]).astype(jnp.int32)
    cache_vt = cache_values.T
    context = [cache_keys, cache_vt]

    def attend(q):
        return call(cached_kernel, [q, *context], [packed], tile_flops, tile_exps)[0]

    def attend_own(q, pieces, unread):
        return call(
            functools.partial(own_kernel, pieces),
            [q, *kv, *context],
            [packed],
            tile_flops * 3 // 2,
            tile_exps * 3 // 2,
            order,
            unread,
        )[0]

    def merge(mine, got):
        return call(merge_kernel, [mine, got], [packed])[0]

    def end(parts, pieces):
        ended = call(functools.partial(final_kernel, len(parts)), parts, [piece] * each)
        return [swap(x, d) if d else x for x, d in zip(ended, pieces)]

    pieces_a, pieces_b = range(each), range(each, shares)

    def pick(arrays, pieces, out, unread=()):
        kernel = functools.partial(pick_kernel, pieces, len(arrays))
        count = len(pieces)
        return move(kernel, count * len(arrays), order, arrays, [out] * count, unread)

    def slices(pieces):
        kernel = functools.partial(slice_kernel, pieces)
        return call(kernel, [queries], [piece] * each, scalars=order)

    q = [swap(x, d) if d else x for x, d in zip(slices(pieces_a), pieces_a)]
    a = call(functools.partial(stack_kernel, each), q, [chunk])[0]
    q = slices(pieces_b)
    a2, a1 = along(a, 2), along(a, 1)
    q = [swap(x, d) for x, d in zip(q, pieces_b)]
    b = call(functools.partial(stack_kernel, each), q, [chunk])[0]
    b2, b1 = along(b, 2), along(b, 1)
    kv = pick([new_keys, new_values], range(shares), pair, [b, cache_vt])
    kv = [swap(x, d) if d else x for d, x in enumerate(kv)]
    part_a2, part_a1 = attend(a2), attend(a1)
    b3 = along(after(b2, [part_a2, part_a1]), 1)
    part_b2 = attend(b2)
    a3 = along(after(a2, [part_b2, b1, *kv[1:]]), 1)
    got_b2 = along(attend(b3), 1)
    got_a2 = along(attend(a3), 1)
    part_b1 = attend(b1)
    part_b2 = merge(part_b2, after(got_b2, [part_b1]))
    from_b2 = along(part_b2, 2)
    own_b = attend_own(b, pieces_b, [part_b2])
    from_b1 = along(after(part_b1, [own_b]), 1)
    own_a = attend_own(a, pieces_a, [part_b2])
    part_a2 = after(merge(part_a2, got_a2), [from_b2, own_a, own_b])
    from_a2 = along(part_a2, 2)
    from_a1 = along(after(part_a1, [part_a2]), 1)
    out_b = end([own_b, from_b2, from_b1], pieces_b)
    out_a = end([own_a, from_a2, from_a1], pieces_a)
    results = [*out_a, *out_b]
    out = jax.ShapeDtypeStruct((step, shares * width), jnp.bfloat16)
    return call(place_kernel, results, [out], scalars=order)[0]


CHUNKS = 2


def power_of_two(n):
    return n & (n - 1) == 0


def body(queries, new_keys, new_values, cache_keys, cache_values, selection):
    qblocks, head_count, top_count = selection.shape
    seq_count = lax.axis_size("seq")
    shares = lax.axis_size("heads") * lax.axis_size("sub")
    every = top_count == cache_keys.shape[0] // BLOCK * seq_count and qblocks == 1
    fits = seq_count == 4 and power_of_two(shares) and shares % CHUNKS == 0
    if every and fits and 4 * head_count <= STAT:
        return dense_body(queries, new_keys, new_values, cache_keys, cache_values)
    return sparse_body(queries, new_keys, new_values, cache_keys, cache_values, selection)


def solution(mesh):
    in_specs = (
        P(("groups", "seq", "heads", "sub"), None),
        P(("groups", "seq", "heads", "sub"), None),
        P(("groups", "seq", "heads", "sub"), None),
        P(("groups", "seq"), ("heads", "sub")),
        P(("groups", "seq"), ("heads", "sub")),
        P(("groups", "seq"), ("heads", "sub"), None),
    )
    out_specs = P(("groups", "seq", "heads", "sub"), None)
    return jax.shard_map(body, mesh=mesh, in_specs=in_specs, out_specs=out_specs, check_vma=False)
```
